32 devices in a mesh: member: 2 (over x), lateral: 8 (over z, y), radial: 2 (over core).
Axes of the slice: x: 2, y: 2, z: 4, core: 2. Of those that a mesh axis runs over, the one named last changes fastest.
Arguments:
- initial_displacement: float32 [6, 8, 256, 2048], P('member', 'radial', 'lateral'), parts along dimension 0, may hold values from -6 to 6
- force: float32 [6, 8, 256, 2048], P('member', 'radial', 'lateral'), parts along dimension 0, may hold values from -12 to 12
- viscosity: float32 [32], P('member'), parts along dimension 0, may hold values from 0.1 to 10
- layer_index: int32 [8, 256, 2048], P('radial', 'lateral'), may hold values from 0 to 15
- response: float32 [512, 1024], P(None, 'lateral'), may hold values from 0.2 to 2
- ocean_mask: int32 [256, 2048], P('lateral'), may hold values 0 or 1
Outputs:
- displacement: float32 [6, 8, 256, 2048], P('member', 'radial', 'lateral'), parts along dimension 0
- coefficients: float32 [1024, 1024], P('member', ('lateral', 'radial')), parts along dimension 0
- sea_load: float32 [256, 4096], P('lateral', 'member'), parts along dimension 1
The draws below stay inside these ranges and needn't reach their ends.
There are 2 independent parts, one for each index of `member`. The reference program is written for one: setup_inputs(seed, part) draws one part's arguments, and reference() takes and returns one part's arrays. A program takes and returns all parts, laid end to end along the dimension named above; an argument that names none is the same for every part. Nothing has to cross between parts.
All inputs are finite; a program needn't handle non-finite values. No bound on the sum of `ocean_mask` on one device may be relied on, other than what follows from the above.
Results may differ from the reference program's by a relative error of at most 0.000073.
Values sent between devices are 32-bit elements; how exact they have to be, the bound alone decides.
No kernel may reach another device: no remote copies, remote signals or barrier semaphores. Data moves between devices by JAX's collectives and lax.ppermute only.
A program may use at most 128 MiB of HBM per device.

```python
import math
import jax
import jax.numpy as jnp
from jax import lax

SHELLS = 8
NLON = 2048
MODES = 512
LAYERS = 16
SWEEPS = 2
NLAT = 256


def with_ends(values, own_key, low, top_value):
    dims = values.shape
    spot = [jax.random.randint(jax.random.fold_in(own_key, axis), (), 0, dims[axis]) for axis in range(len(dims))]
    values = values.at[tuple(spot)].set(low)
    longest = dims.index(max(dims))
    spot[longest] = (spot[longest] + 1) % dims[longest]
    return values.at[tuple(spot)].set(top_value)


def levels(stream_key, shape, cuts, least, largest):
    factor_of, own = 1.0, jax.random.fold_in(stream_key, 6)
    for position, shards_of in cuts:
        draws = jnp.exp(jax.random.uniform(jax.random.fold_in(own, position), (shards_of,), jnp.float32, least / len(cuts), largest / len(cuts)))
        factor_of = factor_of * jnp.repeat(draws, shape[position] // shards_of).reshape([-1 if axis == position else 1 for axis in range(len(shape))])
    return factor_of


def noise(key, dims, deviation, limit, split=(), kind=jnp.bfloat16):
    loudness = levels(key, dims, split, -0.22, 0.18) if split else 1.0
    values = jax.random.normal(key, dims, jnp.float32) * deviation * loudness
    return jnp.minimum(jnp.maximum(values, -limit), limit).astype(kind)


def setup_inputs(seed: int = 0, part: int = 0) -> dict:
    seeds = jax.random.split(jax.random.key(seed), 7)
    own_keys = jax.random.split(jax.random.fold_in(seeds[6], part), 7)
    initial_displacement = noise(own_keys[0], (3, SHELLS, NLAT, NLON), 1.0, 6.0, ((1, 2), (2, 8)), jnp.float32)
    force = noise(own_keys[1], (3, SHELLS, NLAT, NLON), 2.0, 12.0, ((1, 2), (2, 8)), jnp.float32)
    viscosity = jnp.clip(jnp.exp(jax.random.uniform(own_keys[2], (LAYERS,), jnp.float32, math.log(0.1), math.log(10.0))), 0.1, 10.0)
    layer_index = with_ends(jax.random.randint(seeds[3], (SHELLS, NLAT, NLON), 0, LAYERS), jax.random.fold_in(seeds[3], 1), 0, LAYERS - 1).astype(jnp.int32)
    response = jnp.clip(jnp.exp(math.log(2.0) - 2.3025851 * jax.random.uniform(seeds[4], (MODES, 2 * MODES), jnp.float32) ** levels(seeds[4], (MODES, 2 * MODES), ((1, 8),), -0.2, 0.2)), 0.2, 2.0)
    ocean_mask = with_ends((jax.random.randint(seeds[5], (NLAT, NLON), 0, 10) < 7).astype(jnp.int32), jax.random.fold_in(seeds[5], 1), 0, 1)
    return dict(initial_displacement=initial_displacement, force=force, viscosity=viscosity, layer_index=layer_index, response=response, ocean_mask=ocean_mask)


highest = lax.Precision.HIGHEST
relaxation = 0.8

def layer_lookup(layer_index, viscosity):
    result = jnp.zeros(layer_index.shape, jnp.float32)
    for layer_number in range(viscosity.shape[0]):
        result = result + jnp.where(layer_index == layer_number, viscosity[layer_number], jnp.zeros((), viscosity.dtype))
    return result

def longitude_table(count, columns, modes):
    points = jnp.arange(count, dtype=jnp.int32)[:, None]
    orders = (columns % modes)[None, :]
    phase = points * orders % count
    angle = 2.0 * math.pi / count * phase.astype(jnp.float32)
    table = jnp.where(columns[None, :] >= modes, jnp.sin(angle), jnp.cos(angle))
    return table * math.sqrt(2.0 / count)

def colatitude_table(count, modes):
    points = jnp.arange(count, dtype=jnp.int32)[:, None]
    waves = jnp.arange(modes, dtype=jnp.int32)[None, :]
    phase = waves * (2 * points + 1) % (4 * count)
    angle = math.pi / (2 * count) * phase.astype(jnp.float32)
    return jnp.cos(angle) * math.sqrt(2.0 / count)

def sweep(padded, eta_padded, force):
    eta_mid = eta_padded[1:-1, 1:-1]
    middle = padded[:, 1:-1, 1:-1]
    beside_eta = [eta_padded[2:, 1:-1], eta_padded[:-2, 1:-1], eta_padded[1:-1, 2:], eta_padded[1:-1, :-2], jnp.roll(eta_mid, 1, axis=-1), jnp.roll(eta_mid, -1, axis=-1)]
    beside_field = [padded[:, 2:, 1:-1], padded[:, :-2, 1:-1], padded[:, 1:-1, 2:], padded[:, 1:-1, :-2], jnp.roll(middle, 1, axis=-1), jnp.roll(middle, -1, axis=-1)]
    diagonal = jnp.ones(eta_mid.shape, eta_mid.dtype)
    pulled = jnp.zeros(middle.shape, middle.dtype)
    for other_eta, other_field in zip(beside_eta, beside_field):
        weight = 0.5 * (eta_mid + other_eta)
        diagonal = diagonal + weight
        pulled = pulled + weight[None] * other_field
    remainder = force - (diagonal[None] * middle - pulled)
    return middle + relaxation * remainder / diagonal[None]

def reference(initial_displacement, force, viscosity, layer_index, response, ocean_mask):
    eta = layer_lookup(layer_index, viscosity)
    eta_padded = jnp.pad(eta, ((1, 1), (1, 1), (0, 0)))
    displacement = initial_displacement
    for sweep_number in range(SWEEPS):
        padded = jnp.pad(displacement, ((0, 0), (1, 1), (1, 1), (0, 0)))
        displacement = sweep(padded, eta_padded, force)
    surface = displacement[0, SHELLS - 1]
    columns = jnp.arange(2 * MODES, dtype=jnp.int32)
    longitude = longitude_table(NLON, columns, MODES)
    colatitude = colatitude_table(NLAT, MODES)
    fourier = jnp.dot(surface, longitude, precision=highest)
    coefficients = jnp.dot(colatitude.T, fourier, precision=highest)
    load_spectrum = response * coefficients
    load_rows = jnp.dot(colatitude, load_spectrum, precision=highest)
    sea_load = ocean_mask.astype(jnp.float32) * jnp.dot(load_rows, longitude.T, precision=highest)
    return (displacement, coefficients, sea_load)
```

```python
import functools
import math

import jax
import jax.numpy as jnp
import ml_dtypes
import numpy as np
from jax import lax
from jax.experimental import pallas as pl
from jax.experimental.pallas import tpu as pltpu
from jax.sharding import PartitionSpec as P

MODES = 512
RELAXATION = 0.8
TILE = 8
MIB = 1 << 20
ANY = pl.BlockSpec(memory_space=pl.ANY)
SMEM = pl.BlockSpec(memory_space=pltpu.SMEM)
VMEM = pl.BlockSpec(memory_space=pltpu.VMEM)


def params(mib):
    return pltpu.CompilerParams(vmem_limit_bytes=mib * MIB)


def halves(table):
    high = table.astype(ml_dtypes.bfloat16)
    low = (table - high.astype(np.float64)).astype(ml_dtypes.bfloat16)
    return high, low


@functools.lru_cache
def longitude_tables(count, modes):
    points = np.arange(count // 2, dtype=np.int64)[:, None]
    orders = np.arange(modes, dtype=np.int64)[None, :]
    angle = (2.0 * math.pi / count) * (points * orders % count)
    table = np.concatenate([np.cos(angle), np.sin(angle)], axis=1) * math.sqrt(2.0 / count)
    return halves(table)


@functools.lru_cache
def colatitude_tables(count, modes):
    points = np.arange(count, dtype=np.int64)[:, None]
    waves = np.arange(modes, dtype=np.int64)[None, :]
    phase = waves * (2 * points + 1) % (4 * count)
    return halves(np.cos(math.pi / (2 * count) * phase) * math.sqrt(2.0 / count))


def split(values):
    high = values.astype(jnp.bfloat16)
    return high, (values - high.astype(jnp.float32)).astype(jnp.bfloat16)


def dot(a, b):
    return jnp.dot(a, b, preferred_element_type=jnp.float32)


def half_viscosity(index, viscosity_ref):
    values = [0.5 * viscosity_ref[k] for k in range(viscosity_ref.shape[0])]
    bit = 1
    while len(values) > 1:
        odd = (index & bit) != 0
        if len(values) % 2:
            values.append(values[-1])
        values = [jnp.where(odd, b, a) for a, b in zip(values[::2], values[1::2])]
        bit *= 2
    return values[0]


def row_number(shape):
    return lax.broadcasted_iota(jnp.int32, shape, 0)


def north_of(above, middle):
    return pltpu.roll(jnp.where(row_number(middle.shape) == TILE - 1, above, middle), 1, 0)


def south_of(below, middle):
    return pltpu.roll(jnp.where(row_number(middle.shape) == 0, below, middle), TILE - 1, 0)


def east_of(values):
    return pltpu.roll(values, values.shape[-1] - 1, values.ndim - 1)


def west_of(values):
    return pltpu.roll(values, 1, values.ndim - 1)


def relax_weights(middle, others):
    weights = [middle + other for other in others]
    diagonal = 1.0 + functools.reduce(jnp.add, weights)
    return weights, RELAXATION / diagonal


def relax(weights, factor, middle, others, force):
    total = force
    for weight, other in zip(weights, others):
        total = total + weight * other
    return (1.0 - RELAXATION) * middle + factor * total


def around(ref, lead, shell, start):
    rows = lambda first: pl.ds(pl.multiple_of(first, TILE), TILE)
    middle = ref[(*lead, shell, rows(start))]
    return middle, [
        ref[(*lead, shell + 1, rows(start))],
        ref[(*lead, shell - 1, rows(start))],
        south_of(ref[(*lead, shell, rows(start + TILE))], middle),
        north_of(ref[(*lead, shell, rows(start - TILE))], middle),
        west_of(middle),
        east_of(middle),
    ]


def surface_message_kernel(viscosity, d7, d6, f7, i7, i6, d7_end, d6_end, f7_end, i7_end, i6_end, up, down):
    sides = ((down, 0, (d7, d6, f7, i7, i6)), (up, TILE - 1, (d7_end, d6_end, f7_end, i7_end, i6_end)))
    for message, near, (a7, a6, g7, k7, k6) in sides:
        far = 1 if near == 0 else near - 1
        h7, h6 = half_viscosity(k7[...], viscosity), half_viscosity(k6[...], viscosity)
        rows = (a7[far], a7[near], a6[near], h7[far], h7[near], h6[near], g7[near])
        for place, row in enumerate(rows):
            message[place] = row
        message[len(rows)] = jnp.zeros_like(rows[0])


def main_message_kernel(viscosity, d, f, index, h, up, down, ring, tops, ends, force_tops, force_ends, sems):
    shells, rows = h.shape[0], h.shape[1]
    components = d.shape[0]
    last = pl.ds(rows - TILE, TILE)
    shell = jnp.where(lax.axis_index("radial") == 0, shells - 1, 0)
    copies = [
        pltpu.make_async_copy(d.at[:, :, pl.ds(0, TILE)], tops, sems.at[0]),
        pltpu.make_async_copy(d.at[:, :, last], ends, sems.at[1]),
        pltpu.make_async_copy(f.at[:, :, pl.ds(0, TILE)], force_tops, sems.at[2]),
        pltpu.make_async_copy(f.at[:, :, last], force_ends, sems.at[3]),
        pltpu.make_async_copy(d.at[:, shell], ring.at[pl.ds(0, components)], sems.at[4]),
    ]
    for copy in copies:
        copy.start()

    def lookup(step, _):
        s, start = step // (rows // TILE), pl.multiple_of(step % (rows // TILE) * TILE, TILE)
        h[s, pl.ds(start, TILE)] = half_viscosity(index[s, pl.ds(start, TILE)], viscosity)
        return 0

    lax.fori_loop(0, shells * (rows // TILE), lookup, 0)
    eta_copy = pltpu.make_async_copy(h.at[shell], ring.at[components], sems.at[5])
    eta_copy.start()
    for copy in copies[:4]:
        copy.wait()
    for message, near, a, g in ((down, 0, tops, force_tops), (up, TILE - 1, ends, force_ends)):
        far = 1 if near == 0 else near - 1
        h_near, h_far = (0, 1) if near == 0 else (rows - 1, rows - 2)
        for s in range(shells):
            for c in range(components):
                message[c * shells + s] = a[c, s, far]
                message[(components + c) * shells + s] = a[c, s, near]
                message[(2 * components + c) * shells + s] = g[c, s, near]
            message[3 * components * shells + s] = h[s, h_far]
            message[(3 * components + 1) * shells + s] = h[s, h_near]
    copies[4].wait()
    eta_copy.wait()


def surface_kernel(d, f, h, before, after, high, low, out, field, force, eta, smoothed, sems):
    shells, rows, count = h.shape
    top = lax.axis_size("radial") - 1

    @pl.when(lax.axis_index("radial") == top)
    def _():
        inner = pl.ds(TILE, rows)
        copies = [
            pltpu.make_async_copy(d.at[0, pl.ds(shells - 3, 3)], field.at[pl.ds(0, 3), inner], sems.at[0]),
            pltpu.make_async_copy(h.at[pl.ds(shells - 3, 3)], eta.at[pl.ds(0, 3), inner], sems.at[1]),
            pltpu.make_async_copy(f.at[0, pl.ds(shells - 2, 2)], force, sems.at[2]),
        ]
        for copy in copies:
            copy.start()
        zeros = jnp.zeros((rows, count), jnp.float32)
        field[3, inner] = zeros
        eta[3, inner] = zeros
        smoothed[2, inner] = zeros
        for message, place in ((before, TILE - 1), (after, rows + TILE)):
            field[2, place] = message[1]
            field[1, place] = message[2]
            eta[2, place] = message[4]
            eta[1, place] = message[5]
        for copy in copies:
            copy.wait()
        lateral = lax.axis_index("lateral")
        inside = (lateral > 0, lateral < lax.axis_size("lateral") - 1)
        for message, own, place, there in (
            (before, TILE, TILE - 1, inside[0]),
            (after, rows + TILE - 1, rows + TILE, inside[1]),
        ):
            row = lambda k: message[pl.ds(k, 1)]
            own_row = lambda ref: ref[2, pl.ds(own, 1)]
            none = jnp.zeros((1, count), jnp.float32)
            weights, factor = relax_weights(
                row(4), [none, row(5), row(3), own_row(eta), west_of(row(4)), east_of(row(4))]
            )
            edge = relax(
                weights,
                factor,
                row(1),
                [none, row(2), row(0), own_row(field), west_of(row(1)), east_of(row(1))],
                row(6),
            )
            smoothed[1, pl.ds(place, 1)] = jnp.where(there, edge, none)

        def first(step, _):
            start = pl.multiple_of(step * TILE, TILE)
            for s in (1, 2):
                weights, factor = relax_weights(*around(eta, (), s, start + TILE))
                middle, others = around(field, (), s, start + TILE)
                smoothed[s - 1, pl.ds(start + TILE, TILE)] = relax(
                    weights, factor, middle, others, force[s - 1, pl.ds(start, TILE)]
                )
            return 0

        lax.fori_loop(0, rows // TILE, first, 0)

        def second(step, _):
            start = pl.multiple_of(step * TILE, TILE)
            weights, factor = relax_weights(*around(eta, (), 2, start + TILE))
            middle, others = around(smoothed, (), 1, start + TILE)
            field[0, pl.ds(start, TILE)] = relax(weights, factor, middle, others, force[1, pl.ds(start, TILE)])
            return 0

        lax.fori_loop(0, rows // TILE, second, 0)
        half = count // 2
        left, right = field[0, pl.ds(0, rows), :half], field[0, pl.ds(0, rows), half:]
        near, far = split(jnp.concatenate([left + right, left - right], axis=0))
        total = dot(jnp.concatenate([near, far], axis=0), high[...])
        total = total[: 2 * rows] + total[2 * rows :] + dot(near, low[...])
        odd = lax.broadcasted_iota(jnp.int32, (rows, total.shape[1]), 1) % 2 == 1
        fourier = jnp.where(odd, total[rows:], total[:rows])
        blocks, width = out.shape[0], out.shape[2]
        for block in range(blocks):
            out[block] = fourier[:, block * width : (block + 1) * width]


def load_tiles(parts, sems, place):
    copies = [pltpu.make_async_copy(source, target, sems.at[place + k]) for k, (source, target) in enumerate(parts)]
    for copy in copies:
        copy.start()
    return copies


def sweep_shells(d, f, h, ring_field, ring_eta, out, field, eta, force, result, sems, after_shell):
    components, shells, rows, count = d.shape
    inner = pl.ds(TILE, rows)
    lower = lax.axis_index("radial") == 0
    ring, nothing = jnp.where(lower, shells + 1, 0), jnp.where(lower, 0, shells + 1)
    halo = [
        pltpu.make_async_copy(source, field.at[c, ring, inner], sems.at[0, c])
        for c, source in enumerate(ring_field)
    ] + [pltpu.make_async_copy(ring_eta, eta.at[ring, inner], sems.at[0, components])]
    for copy in halo:
        copy.start()
    loads = []
    for s in range(shells):
        loads.append(
            [
                pltpu.make_async_copy(d.at[:, s], field.at[:, s + 1, inner], sems.at[s + 1, 0]),
                pltpu.make_async_copy(h.at[s], eta.at[s + 1, inner], sems.at[s + 1, 1]),
                pltpu.make_async_copy(f.at[:, s], force.at[:, s], sems.at[s + 1, 2]),
            ]
        )
        for copy in loads[s]:
            copy.start()
    zeros = jnp.zeros((rows, count), jnp.float32)
    for c in range(components):
        field[c, nothing, inner] = zeros
    eta[nothing, inner] = zeros
    for copy in halo + loads[0]:
        copy.wait()
    stores = []
    for s in range(shells):
        if s + 1 < shells:
            for copy in loads[s + 1]:
                copy.wait()

        def tile(step, _):
            start = pl.multiple_of(step * TILE, TILE)
            weights, factor = relax_weights(*around(eta, (), s + 1, start + TILE))
            for c in range(components):
                middle, others = around(field, (c,), s + 1, start + TILE)
                result[c, s, pl.ds(start, TILE)] = relax(
                    weights, factor, middle, others, force[c, s, pl.ds(start, TILE)]
                )
            return 0

        lax.fori_loop(0, rows // TILE, tile, 0)
        stores.append(pltpu.make_async_copy(result.at[:, s], out.at[:, s], sems.at[s + 1, 3]))
        stores[-1].start()
        after_shell(s)
    for copy in stores:
        copy.wait()


def set_edge(ref, lead, shells, rows, before, after):
    for s in range(shells):
        ref[(*lead, s + 1, TILE - 1)] = before(s)
        ref[(*lead, s + 1, rows + TILE)] = after(s)


def first_kernel(d, f, h, ring, before, after, out, ring_out, field, eta, force, result, edges, sems, ring_sems):
    components, shells, rows, _ = d.shape
    lower = lax.axis_index("radial") == 0
    row = lambda message, kind: lambda s: message[kind * shells + s]
    for c in range(components):
        set_edge(field, (c,), shells, rows, row(before, components + c), row(after, components + c))
    kind = 3 * components + 1
    set_edge(eta, (), shells, rows, row(before, kind), row(after, kind))
    for side, message in enumerate((before, after)):
        for place, k in enumerate([components + c for c in range(components)] + [kind]):
            low, high = message[pl.ds(k * shells, 1)], message[pl.ds((k + 1) * shells - 1, 1)]
            edges[pl.ds(side * (components + 1) + place, 1)] = jnp.where(lower, high, low)
    edge_copy = pltpu.make_async_copy(edges, ring_out.at[pl.ds(components * rows, edges.shape[0])], ring_sems.at[0])
    edge_copy.start()

    def ring_copies(s):
        return [
            pltpu.make_async_copy(result.at[c, s], ring_out.at[pl.ds(c * rows, rows)], ring_sems.at[c + 1])
            for c in range(components)
        ]

    def after_shell(s):
        if s in (0, shells - 1):

            @pl.when(lower if s else jnp.logical_not(lower))
            def _():
                for copy in ring_copies(s):
                    copy.start()

    sweep_shells(
        d, f, h, [ring.at[c] for c in range(components)], ring.at[components],
        out, field, eta, force, result, sems, after_shell,
    )
    for copy in ring_copies(0):
        copy.wait()
    edge_copy.wait()


def second_kernel(
    d, f, h, ring, ring_two, before, after, own_up, own_down, out, field, eta, force, result, edges, sems, ring_sems
):
    components, shells, rows, count = d.shape
    lower = lax.axis_index("radial") == 0
    lateral = lax.axis_index("lateral")
    fetch = pltpu.make_async_copy(ring_two.at[pl.ds(components * rows, edges.shape[0])], edges, ring_sems.at[0])
    fetch.start()
    kind = 3 * components + 1
    row = lambda message, kind: lambda s: message[kind * shells + s]
    set_edge(eta, (), shells, rows, row(before, kind), row(after, kind))
    fetch.wait()
    place = row_number((2 * shells, count))
    pair = lambda a, b, k: jnp.concatenate([a[k * shells : (k + 1) * shells], b[k * shells : (k + 1) * shells]], axis=0)

    def neighbours(inner, outer, part):
        middle = pair(before, after, inner)
        beyond = [edges[pl.ds(side * (components + 1) + part, 1)] for side in range(2)]
        beyond = jnp.where(place < shells, beyond[0], beyond[1])
        none = jnp.zeros_like(beyond)
        above = pltpu.roll(middle, 2 * shells - 1, 0)
        below = pltpu.roll(middle, 1, 0)
        return middle, [
            jnp.where(place % shells == shells - 1, jnp.where(lower, beyond, none), above),
            jnp.where(place % shells == 0, jnp.where(lower, none, beyond), below),
            pair(before, after, outer),
            pair(own_down, own_up, inner),
            west_of(middle),
            east_of(middle),
        ]

    weights, factor = relax_weights(*neighbours(kind, kind - 1, components))
    inside = jnp.where(place < shells, lateral, lax.axis_size("lateral") - 1 - lateral) > 0
    for c in range(components):
        middle, others = neighbours(components + c, c, c)
        edge = relax(weights, factor, middle, others, pair(before, after, 2 * components + c))
        edge = jnp.where(inside, edge, jnp.zeros_like(edge))
        set_edge(field, (c,), shells, rows, lambda s: edge[s], lambda s: edge[shells + s])
    sweep_shells(
        d, f, h, [ring_two.at[pl.ds(c * rows, rows)] for c in range(components)], ring.at[components],
        out, field, eta, force, result, sems, lambda s: None,
    )


def spectrum_kernel(orders, response, wave_high, wave_low, point_high, point_low, coefficients, out):
    radial = lax.axis_size("radial")
    bands, rows, width = orders.shape[0] // radial, orders.shape[1], orders.shape[2]
    fourier = jnp.concatenate([orders[band * radial + radial - 1] for band in range(bands)], axis=0)
    high, low = split(fourier)
    spectrum = dot(wave_high[...], high) + dot(wave_high[...], low) + dot(wave_low[...], high)
    coefficients[...] = spectrum
    own = response[:, :width]
    for place in range(1, radial):
        own = jnp.where(
            lax.axis_index("radial") == place, response[:, place * width : (place + 1) * width], own
        )
    high, low = split(own * spectrum)
    load = dot(point_high[...], high) + dot(point_high[...], low) + dot(point_low[...], high)
    for band in range(bands):
        for place in range(radial):
            out[band * radial + place] = load[band * rows : (band + 1) * rows]


def load_kernel(load, mask, high, low, out):
    blocks, rows, width = load.shape
    half = out.shape[1] // 2
    values = jnp.concatenate([load[block] for block in range(blocks)], axis=1)
    odd = lax.broadcasted_iota(jnp.int32, values.shape, 1) % 2 == 1
    near, far = split(jnp.concatenate([values, jnp.where(odd, -values, values)], axis=0))
    total = dot(jnp.concatenate([near, far], axis=0), high[...])
    total = total[: 2 * rows] + total[2 * rows :] + dot(near, low[...])
    out[:, :half] = total[:rows] * mask[:, :half].astype(jnp.float32)
    out[:, half:] = total[rows:] * mask[:, half:].astype(jnp.float32)


def tile_spec(block, *index):
    return pl.BlockSpec(block, lambda _: index)


def shards(initial_displacement, force, viscosity, layer_index, response, ocean_mask):
    components, shells, rows, count = initial_displacement.shape
    radial, lateral = lax.axis_size("radial"), lax.axis_size("lateral")
    f32 = functools.partial(jax.ShapeDtypeStruct, dtype=jnp.float32)
    scratch = lambda *shape: pltpu.VMEM(shape, jnp.float32)
    width = 2 * MODES // (lateral * radial)
    up = [(i, i + 1) for i in range(lateral - 1)]
    down = [(j, i) for i, j in up]
    top_only = lambda pairs: [(i * radial + radial - 1, j * radial + radial - 1) for i, j in pairs]

    last = rows // TILE - 1
    block4, block3 = (None, None, TILE, count), (None, TILE, count)
    row_specs = [
        [
            tile_spec(block4, 0, shells - 1, row, 0),
            tile_spec(block4, 0, shells - 2, row, 0),
            tile_spec(block4, 0, shells - 1, row, 0),
            tile_spec(block3, shells - 1, row, 0),
            tile_spec(block3, shells - 2, row, 0),
        ]
        for row in (0, last)
    ]
    tensors = (initial_displacement, initial_displacement, force, layer_index, layer_index)
    surface_up, surface_down = pl.pallas_call(
        surface_message_kernel,
        grid=(1,),
        in_specs=[SMEM, *row_specs[0], *row_specs[1]],
        out_specs=[VMEM, VMEM],
        out_shape=[f32((TILE, count))] * 2,
        compiler_params=params(8),
    )(viscosity, *tensors, *tensors)
    both = ("lateral", "radial")
    surface_before = lax.ppermute(surface_up, both, top_only(up))
    surface_after = lax.ppermute(surface_down, both, top_only(down))

    fields = -(-(3 * components + 2) * shells // TILE) * TILE
    edge_rows = scratch(components, shells, TILE, count)
    eta, own_up, own_down, ring = pl.pallas_call(
        main_message_kernel,
        in_specs=[SMEM, ANY, ANY, VMEM],
        out_specs=[VMEM, VMEM, VMEM, ANY],
        out_shape=[
            f32((shells, rows, count)),
            f32((fields, count)),
            f32((fields, count)),
            f32((components + 1, rows, count)),
        ],
        scratch_shapes=[edge_rows] * 4 + [pltpu.SemaphoreType.DMA((6,))],
        compiler_params=params(16),
    )(viscosity, initial_displacement, force, layer_index)
    swap = [(i, radial - 1 - i) for i in range(radial)]
    ring = lax.ppermute(ring, "radial", swap)
    before = lax.ppermute(own_up, "lateral", up)
    after = lax.ppermute(own_down, "lateral", down)

    high, low = longitude_tables(count, MODES)
    orders = pl.pallas_call(
        surface_kernel,
        in_specs=[ANY, ANY, ANY, VMEM, VMEM, VMEM, VMEM],
        out_specs=VMEM,
        out_shape=f32((lateral * radial, rows, width)),
        scratch_shapes=[
            scratch(4, rows + 2 * TILE, count),
            scratch(2, rows, count),
            scratch(4, rows + 2 * TILE, count),
            scratch(3, rows + 2 * TILE, count),
            pltpu.SemaphoreType.DMA((3,)),
        ],
        compiler_params=params(24),
    )(initial_displacement, force, eta, surface_before, surface_after, high, low)
    orders = lax.all_to_all(orders, both, split_axis=0, concat_axis=0, tiled=True)

    sweep_scratch = [
        scratch(components, shells + 2, rows + 2 * TILE, count),
        scratch(shells + 2, rows + 2 * TILE, count),
        scratch(components, shells, rows, count),
        scratch(components, shells, rows, count),
        scratch(2 * (components + 1), count),
        pltpu.SemaphoreType.DMA((shells + 1, 4)),
        pltpu.SemaphoreType.DMA((components + 1,)),
    ]
    cost = pl.CostEstimate(flops=200 * 3 * shells * rows * count, bytes_accessed=16 * MIB, transcendentals=0)
    smoothed, ring_two = pl.pallas_call(
        first_kernel,
        in_specs=[ANY, ANY, ANY, ANY, VMEM, VMEM],
        out_specs=[ANY, ANY],
        out_shape=[
            f32(initial_displacement.shape),
            f32((components * rows + 2 * (components + 1), count)),
        ],
        scratch_shapes=sweep_scratch,
        compiler_params=params(28),
        cost_estimate=cost,
    )(initial_displacement, force, eta, ring, before, after)
    ring_two = lax.ppermute(ring_two, "radial", swap)

    point_high, point_low = colatitude_tables(rows * lateral, MODES)
    coefficients, load = pl.pallas_call(
        spectrum_kernel,
        in_specs=[VMEM] * 6,
        out_specs=[VMEM, VMEM],
        out_shape=[f32((MODES, width)), f32((lateral * radial, rows, width))],
        compiler_params=params(16),
    )(orders, response, point_high.T.copy(), point_low.T.copy(), point_high, point_low)
    load = lax.all_to_all(load, both, split_axis=0, concat_axis=0, tiled=True)

    displacement = pl.pallas_call(
        second_kernel,
        in_specs=[ANY, ANY, ANY, ANY, ANY, VMEM, VMEM, VMEM, VMEM],
        out_specs=ANY,
        out_shape=f32(initial_displacement.shape),
        scratch_shapes=sweep_scratch,
        compiler_params=params(28),
        cost_estimate=cost,
    )(smoothed, force, eta, ring, ring_two, before, after, own_up, own_down)

    sea_load = pl.pallas_call(
        load_kernel,
        in_specs=[VMEM] * 4,
        out_specs=VMEM,
        out_shape=f32((rows, count)),
        compiler_params=params(20),
    )(load, ocean_mask, high.T.copy(), low.T.copy())
    return (displacement, coefficients, sea_load)


def solution(mesh):
    in_specs = (
        P("member", "radial", "lateral", None),
        P("member", "radial", "lateral", None),
        P("member"),
        P("radial", "lateral", None),
        P(None, "lateral"),
        P("lateral", None),
    )
    out_specs = (
        P("member", "radial", "lateral", None),
        P("member", ("lateral", "radial")),
        P("lateral", "member"),
    )
    return jax.shard_map(shards, mesh=mesh, in_specs=in_specs, out_specs=out_specs, check_vma=False)
```

```python
import functools
import math

import jax
import jax.numpy as jnp
import ml_dtypes
import numpy as np
from jax import lax
from jax.experimental import pallas as pl
from jax.experimental.pallas import tpu as pltpu
from jax.sharding import PartitionSpec as P

MODES = 512
RELAXATION = 0.8
TILE = 8
MIB = 1 << 20
ANY = pl.BlockSpec(memory_space=pl.ANY)
HBM = pl.BlockSpec(memory_space=pltpu.HBM)
SMEM = pl.BlockSpec(memory_space=pltpu.SMEM)
VMEM = pl.BlockSpec(memory_space=pltpu.VMEM)


def params(mib):
    return pltpu.CompilerParams(vmem_limit_bytes=mib * MIB)


def halves(table):
    high = table.astype(ml_dtypes.bfloat16)
    low = (table - high.astype(np.float64)).astype(ml_dtypes.bfloat16)
    return high, low


@functools.lru_cache
def longitude_tables(count, modes):
    points = np.arange(count // 2, dtype=np.int64)[:, None]
    orders = np.arange(modes, dtype=np.int64)[None, :]
    angle = (2.0 * math.pi / count) * (points * orders % count)
    table = np.concatenate([np.cos(angle), np.sin(angle)], axis=1) * math.sqrt(2.0 / count)
    return halves(table)


@functools.lru_cache
def colatitude_tables(count, modes):
    points = np.arange(count, dtype=np.int64)[:, None]
    waves = np.arange(modes, dtype=np.int64)[None, :]
    phase = waves * (2 * points + 1) % (4 * count)
    return halves(np.cos(math.pi / (2 * count) * phase) * math.sqrt(2.0 / count))


def split(values):
    high = values.astype(jnp.bfloat16)
    return high, (values - high.astype(jnp.float32)).astype(jnp.bfloat16)


def dot(a, b):
    return jnp.dot(a, b, preferred_element_type=jnp.float32)


def pack(block):
    rows, width = block.shape
    groups = max(1, 128 // width)
    rows //= groups
    return jnp.concatenate([block[k * rows : (k + 1) * rows] for k in range(groups)], axis=1)


def unpack(block, width):
    groups = max(1, 128 // width)
    return jnp.concatenate([block[:, k * width : (k + 1) * width] for k in range(groups)], axis=0)


def half_viscosity(index, viscosity_ref):
    values = [0.5 * viscosity_ref[k] for k in range(viscosity_ref.shape[0])]
    bit = 1
    while len(values) > 1:
        odd = (index & bit) != 0
        if len(values) % 2:
            values.append(values[-1])
        values = [jnp.where(odd, b, a) for a, b in zip(values[::2], values[1::2])]
        bit *= 2
    return values[0]


def row_number(shape):
    return lax.broadcasted_iota(jnp.int32, shape, 0)


def north_of(above, middle):
    return pltpu.roll(jnp.where(row_number(middle.shape) == TILE - 1, above, middle), 1, 0)


def south_of(below, middle):
    return pltpu.roll(jnp.where(row_number(middle.shape) == 0, below, middle), TILE - 1, 0)


def east_of(values):
    return pltpu.roll(values, values.shape[-1] - 1, values.ndim - 1)


def west_of(values):
    return pltpu.roll(values, 1, values.ndim - 1)


def relax_weights(middle, others):
    weights = [middle + other for other in others]
    diagonal = 1.0 + functools.reduce(jnp.add, weights)
    return weights, RELAXATION / diagonal


def relax(weights, factor, middle, others, force):
    total = force
    for weight, other in zip(weights, others):
        total = total + weight * other
    return (1.0 - RELAXATION) * middle + factor * total


def around(ref, lead, shell, start):
    rows = lambda first: pl.ds(pl.multiple_of(first, TILE), TILE)
    middle = ref[(*lead, shell, rows(start))]
    return middle, [
        ref[(*lead, shell + 1, rows(start))],
        ref[(*lead, shell - 1, rows(start))],
        south_of(ref[(*lead, shell, rows(start + TILE))], middle),
        north_of(ref[(*lead, shell, rows(start - TILE))], middle),
        west_of(middle),
        east_of(middle),
    ]


def surface_message_kernel(viscosity, d, f, index, up, down, fields, forces, layers, sems):
    shells, rows = index.shape[0], index.shape[1]
    top, pair = shells - 1, pl.ds(shells - 2, 2)
    copies = []
    for side, start in enumerate((0, rows - TILE)):
        part = pl.ds(start, TILE)
        copies += [
            pltpu.make_async_copy(d.at[0, pair, part], fields.at[side], sems.at[side, 0]),
            pltpu.make_async_copy(f.at[0, top, part], forces.at[side], sems.at[side, 1]),
            pltpu.make_async_copy(index.at[pair, part], layers.at[side], sems.at[side, 2]),
        ]
    for copy in copies:
        copy.start()
    for copy in copies:
        copy.wait()
    for side, message, near, far in ((0, down, 0, 1), (1, up, TILE - 1, TILE - 2)):
        below, surface = [half_viscosity(layers[side, k], viscosity) for k in range(2)]
        message[0] = fields[side, 1, far]
        message[1] = fields[side, 1, near]
        message[2] = fields[side, 0, near]
        message[3] = surface[far]
        message[4] = surface[near]
        message[5] = below[near]
        message[6] = forces[side, near]
        message[7] = jnp.zeros_like(below[near])


def main_message_kernel(viscosity, d, index_from, h, up, down, ring, tops, ends, index, sems):
    shells, rows = h.shape[0], h.shape[1]
    components = d.shape[0]
    shell = jnp.where(lax.axis_index("radial") == 0, shells - 1, 0)
    copies = [
        pltpu.make_async_copy(d.at[:, :, pl.ds(0, TILE)], tops, sems.at[0]),
        pltpu.make_async_copy(d.at[:, :, pl.ds(rows - TILE, TILE)], ends, sems.at[1]),
        pltpu.make_async_copy(d.at[:, shell], ring.at[pl.ds(0, components)], sems.at[2]),
    ]
    layers = [pltpu.make_async_copy(index_from.at[s], index.at[s], sems.at[4 + s]) for s in range(shells)]
    for copy in layers + copies:
        copy.start()
    for s in range(shells):
        layers[s].wait()

        def lookup(step, _):
            part = pl.ds(pl.multiple_of(step * TILE, TILE), TILE)
            h[s, part] = half_viscosity(index[s, part], viscosity)
            return 0

        lax.fori_loop(0, rows // TILE, lookup, 0)
    eta_copy = pltpu.make_async_copy(h.at[shell], ring.at[components], sems.at[3])
    eta_copy.start()
    for copy in copies[:2]:
        copy.wait()
    for message, row, place, a in ((down, 0, 0, tops), (up, rows - 1, TILE - 1, ends)):
        for s in range(shells):
            for c in range(components):
                message[c * shells + s] = a[c, s, place]
            message[components * shells + s] = h[s, row]
    copies[2].wait()
    eta_copy.wait()


def surface_kernel(d, f, h, before, after, high_from, low_from, out, field, force, eta, smoothed, high, low, sems):
    shells, rows, count = h.shape
    top = lax.axis_size("radial") - 1

    @pl.when(lax.axis_index("radial") == top)
    def _():
        inner = pl.ds(TILE, rows)
        copies = [
            pltpu.make_async_copy(d.at[0, pl.ds(shells - 3, 3)], field.at[pl.ds(0, 3), inner], sems.at[0]),
            pltpu.make_async_copy(h.at[pl.ds(shells - 3, 3)], eta.at[pl.ds(0, 3), inner], sems.at[1]),
            pltpu.make_async_copy(f.at[0, pl.ds(shells - 2, 2)], force, sems.at[2]),
        ]
        tables = [
            pltpu.make_async_copy(high_from, high, sems.at[3]),
            pltpu.make_async_copy(low_from, low, sems.at[4]),
        ]
        for copy in copies + tables:
            copy.start()
        zeros = jnp.zeros((rows, count), jnp.float32)
        field[3, inner] = zeros
        eta[3, inner] = zeros
        smoothed[2, inner] = zeros
        for message, place in ((before, TILE - 1), (after, rows + TILE)):
            field[2, place] = message[1]
            field[1, place] = message[2]
            eta[2, place] = message[4]
            eta[1, place] = message[5]
        for copy in copies:
            copy.wait()
        lateral = lax.axis_index("lateral")
        inside = (lateral > 0, lateral < lax.axis_size("lateral") - 1)
        for message, own, place, there in (
            (before, TILE, TILE - 1, inside[0]),
            (after, rows + TILE - 1, rows + TILE, inside[1]),
        ):
            row = lambda k: message[pl.ds(k, 1)]
            own_row = lambda ref: ref[2, pl.ds(own, 1)]
            none = jnp.zeros((1, count), jnp.float32)
            weights, factor = relax_weights(
                row(4), [none, row(5), row(3), own_row(eta), west_of(row(4)), east_of(row(4))]
            )
            edge = relax(
                weights,
                factor,
                row(1),
                [none, row(2), row(0), own_row(field), west_of(row(1)), east_of(row(1))],
                row(6),
            )
            smoothed[1, pl.ds(place, 1)] = jnp.where(there, edge, none)

        def first(step, _):
            start = pl.multiple_of(step * TILE, TILE)
            for s in (1, 2):
                weights, factor = relax_weights(*around(eta, (), s, start + TILE))
                middle, others = around(field, (), s, start + TILE)
                smoothed[s - 1, pl.ds(start + TILE, TILE)] = relax(
                    weights, factor, middle, others, force[s - 1, pl.ds(start, TILE)]
                )
            return 0

        lax.fori_loop(0, rows // TILE, first, 0)

        def second(step, _):
            start = pl.multiple_of(step * TILE, TILE)
            weights, factor = relax_weights(*around(eta, (), 2, start + TILE))
            middle, others = around(smoothed, (), 1, start + TILE)
            field[0, pl.ds(start, TILE)] = relax(weights, factor, middle, others, force[1, pl.ds(start, TILE)])
            return 0

        lax.fori_loop(0, rows // TILE, second, 0)
        half = count // 2
        left, right = field[0, pl.ds(0, rows), :half], field[0, pl.ds(0, rows), half:]
        near, far = split(jnp.concatenate([left + right, left - right], axis=0))
        for copy in tables:
            copy.wait()
        total = dot(jnp.concatenate([near, far], axis=0), high[...])
        total = total[: 2 * rows] + total[2 * rows :] + dot(near, low[...])
        odd = lax.broadcasted_iota(jnp.int32, (rows, total.shape[1]), 1) % 2 == 1
        fourier = jnp.where(odd, total[rows:], total[:rows])
        blocks = out.shape[0]
        width = fourier.shape[1] // blocks
        for block in range(blocks):
            out[block] = pack(fourier[:, block * width : (block + 1) * width])


def sweep_shells(d, f, h, ring_field, ring_eta, out, field, eta, force, result, sems, after_shell):
    components, shells, rows, count = d.shape
    inner = pl.ds(TILE, rows)
    lower = lax.axis_index("radial") == 0
    ring, nothing = jnp.where(lower, shells + 1, 0), jnp.where(lower, 0, shells + 1)
    halo = [
        pltpu.make_async_copy(source, field.at[c, ring, inner], sems.at[0, c])
        for c, source in enumerate(ring_field)
    ] + [pltpu.make_async_copy(ring_eta, eta.at[ring, inner], sems.at[0, components])]
    for copy in halo:
        copy.start()
    loads = []
    for s in range(shells):
        loads.append(
            [
                pltpu.make_async_copy(d.at[:, s], field.at[:, s + 1, inner], sems.at[s + 1, 0]),
                pltpu.make_async_copy(h.at[s], eta.at[s + 1, inner], sems.at[s + 1, 1]),
                pltpu.make_async_copy(f.at[:, s], force.at[:, s], sems.at[s + 1, 2]),
            ]
        )
        for copy in loads[s]:
            copy.start()
    zeros = jnp.zeros((rows, count), jnp.float32)
    for c in range(components):
        field[c, nothing, inner] = zeros
    eta[nothing, inner] = zeros
    for copy in halo + loads[0]:
        copy.wait()
    stores = []
    for s in range(shells):
        if s + 1 < shells:
            for copy in loads[s + 1]:
                copy.wait()

        def tile(step, _):
            start = pl.multiple_of(step * TILE, TILE)
            weights, factor = relax_weights(*around(eta, (), s + 1, start + TILE))
            for c in range(components):
                middle, others = around(field, (c,), s + 1, start + TILE)
                result[c, s, pl.ds(start, TILE)] = relax(
                    weights, factor, middle, others, force[c, s, pl.ds(start, TILE)]
                )
            return 0

        lax.fori_loop(0, rows // TILE, tile, 0)
        stores.append(pltpu.make_async_copy(result.at[:, s], out.at[:, s], sems.at[s + 1, 3]))
        stores[-1].start()
        after_shell(s)
    for copy in stores:
        copy.wait()


def set_edge(ref, lead, shells, rows, before, after):
    for s in range(shells):
        ref[(*lead, s + 1, TILE - 1)] = before(s)
        ref[(*lead, s + 1, rows + TILE)] = after(s)


def first_kernel(d, f, h, ring, before, after, *refs):
    components, shells, rows, _ = d.shape
    staged = (len(refs) - 11) // 2
    sources, refs = refs[:staged], refs[staged:]
    out, ring_out, up, down, *targets = refs[: 4 + staged]
    field, eta, force, result, sems, ring_sems, stage_sems = refs[4 + staged :]
    stages = [
        pltpu.make_async_copy(source, target, stage_sems.at[k]) for k, (source, target) in enumerate(zip(sources, targets))
    ]
    lower = lax.axis_index("radial") == 0
    row = lambda message, kind: lambda s: message[kind * shells + s]
    for c in range(components):
        set_edge(field, (c,), shells, rows, row(before, c), row(after, c))
    set_edge(eta, (), shells, rows, row(before, components), row(after, components))

    def ring_copies(s):
        return [pltpu.make_async_copy(result.at[:, s], ring_out, ring_sems.at[0])]

    def after_shell(s):
        if s == 0:
            for copy in stages:
                copy.start()
        for c in range(components):
            down[c * shells + s] = result[c, s, 0]
            up[c * shells + s] = result[c, s, rows - 1]
        if s in (0, shells - 1):

            @pl.when(lower if s else jnp.logical_not(lower))
            def _():
                for copy in ring_copies(s):
                    copy.start()

    sweep_shells(
        d, f, h, [ring.at[c] for c in range(components)], ring.at[components],
        out, field, eta, force, result, sems, after_shell,
    )
    for copy in ring_copies(0) + stages:
        copy.wait()


def second_kernel(
    d, f, h, ring, ring_two, eta_before, eta_after, before, after, out, field, eta, force, result, sems
):
    components, shells, rows, _ = d.shape
    row = lambda message, kind: lambda s: message[kind * shells + s]
    for c in range(components):
        set_edge(field, (c,), shells, rows, row(before, c), row(after, c))
    set_edge(eta, (), shells, rows, row(eta_before, components), row(eta_after, components))
    sweep_shells(
        d, f, h, [ring_two.at[c] for c in range(components)], ring.at[components],
        out, field, eta, force, result, sems, lambda s: None,
    )


def spectrum_kernel(orders, response, wave_high, wave_low, point_high, point_low, coefficients, out):
    radial = lax.axis_size("radial")
    width = coefficients.shape[0]
    bands, rows = orders.shape[0] // radial, point_high.shape[0] * radial // orders.shape[0]
    fourier = jnp.concatenate([unpack(orders[band * radial + radial - 1], width) for band in range(bands)], axis=0)
    high, low = split(fourier)
    spectrum = dot(wave_high[...], high) + dot(wave_high[...], low) + dot(wave_low[...], high)
    coefficients[...] = spectrum.T
    own = response[:, :width]
    for place in range(1, radial):
        own = jnp.where(
            lax.axis_index("radial") == place, response[:, place * width : (place + 1) * width], own
        )
    high, low = split(own * spectrum)
    load = dot(point_high[...], high) + dot(point_high[...], low) + dot(point_low[...], high)
    for band in range(bands):
        block = pack(load[band * rows : (band + 1) * rows])
        for place in range(radial):
            out[band * radial + place] = block


def load_kernel(load, mask, high, low, out):
    blocks, rows = load.shape[0], out.shape[0]
    half, width = out.shape[1] // 2, high.shape[0] // blocks
    values = jnp.concatenate([unpack(load[block], width) for block in range(blocks)], axis=1)
    odd = lax.broadcasted_iota(jnp.int32, values.shape, 1) % 2 == 1
    near, far = split(jnp.concatenate([values, jnp.where(odd, -values, values)], axis=0))
    total = dot(jnp.concatenate([near, far], axis=0), high[...])
    total = total[: 2 * rows] + total[2 * rows :] + dot(near, low[...])
    out[:, :half] = total[:rows] * mask[:, :half].astype(jnp.float32)
    out[:, half:] = total[rows:] * mask[:, half:].astype(jnp.float32)


def cost(microseconds):
    return pl.CostEstimate(flops=0, bytes_accessed=3_000_000 * microseconds, transcendentals=0)


def hbm(values):
    return pltpu.with_memory_space_constraint(values, pltpu.HBM)


def shards(initial_displacement, force, viscosity, layer_index, response, ocean_mask):
    components, shells, rows, count = initial_displacement.shape
    radial, lateral = lax.axis_size("radial"), lax.axis_size("lateral")
    f32 = functools.partial(jax.ShapeDtypeStruct, dtype=jnp.float32)
    scratch = lambda *shape: pltpu.VMEM(shape, jnp.float32)
    width = 2 * MODES // (lateral * radial)
    up = [(i, i + 1) for i in range(lateral - 1)]
    down = [(j, i) for i, j in up]
    top_only = lambda pairs: [(i * radial + radial - 1, j * radial + radial - 1) for i, j in pairs]

    tensors = [hbm(a) for a in (initial_displacement, force, layer_index)]
    surface_up, surface_down = pl.pallas_call(
        surface_message_kernel,
        in_specs=[SMEM, HBM, HBM, HBM],
        out_specs=[VMEM, VMEM],
        out_shape=[f32((TILE, count))] * 2,
        scratch_shapes=[
            scratch(2, 2, TILE, count),
            scratch(2, TILE, count),
            pltpu.VMEM((2, 2, TILE, count), jnp.int32),
            pltpu.SemaphoreType.DMA((2, 3)),
        ],
        compiler_params=params(8),
        cost_estimate=cost(2),
    )(viscosity, *tensors)
    both = ("lateral", "radial")
    surface_before = lax.ppermute(surface_up, both, top_only(up))
    surface_after = lax.ppermute(surface_down, both, top_only(down))

    fields = -(-(components + 1) * shells // TILE) * TILE
    message = f32((fields, count))
    edge_rows = scratch(components, shells, TILE, count)
    later, _ = lax.optimization_barrier((viscosity, surface_up))
    eta, own_up, own_down, ring = pl.pallas_call(
        main_message_kernel,
        in_specs=[SMEM, HBM, HBM],
        out_specs=[VMEM, VMEM, VMEM, ANY],
        out_shape=[f32((shells, rows, count)), message, message, f32((components + 1, rows, count))],
        scratch_shapes=[
            edge_rows,
            edge_rows,
            pltpu.VMEM(layer_index.shape, jnp.int32),
            pltpu.SemaphoreType.DMA((4 + shells,)),
        ],
        compiler_params=params(16),
        cost_estimate=cost(4),
    )(later, tensors[0], tensors[2])
    swap = [(i, radial - 1 - i) for i in range(radial)]
    ring = lax.ppermute(ring, "radial", swap)
    before = lax.ppermute(own_up, "lateral", up)
    after = lax.ppermute(own_down, "lateral", down)

    high, low = longitude_tables(count, MODES)
    table = pltpu.VMEM(high.shape, jnp.bfloat16)
    packed = (lateral * radial, rows * width // max(128, width), max(128, width))
    orders = pl.pallas_call(
        surface_kernel,
        in_specs=[HBM, HBM, ANY, VMEM, VMEM, HBM, HBM],
        out_specs=VMEM,
        out_shape=f32(packed),
        scratch_shapes=[
            scratch(4, rows + 2 * TILE, count),
            scratch(2, rows, count),
            scratch(4, rows + 2 * TILE, count),
            scratch(3, rows + 2 * TILE, count),
            table,
            table,
            pltpu.SemaphoreType.DMA((5,)),
        ],
        compiler_params=params(24),
        cost_estimate=cost(6),
    )(*tensors[:2], eta, surface_before, surface_after, hbm(jnp.asarray(high)), hbm(jnp.asarray(low)))
    later, _ = lax.optimization_barrier((eta, orders))
    orders = lax.all_to_all(orders, both, split_axis=0, concat_axis=0, tiled=True)

    sweep_scratch = [
        scratch(components, shells + 2, rows + 2 * TILE, count),
        scratch(shells + 2, rows + 2 * TILE, count),
        scratch(components, shells, rows, count),
        scratch(components, shells, rows, count),
        pltpu.SemaphoreType.DMA((shells + 1, 4)),
    ]
    point_high, point_low = colatitude_tables(rows * lateral, MODES)
    stages = [
        jnp.asarray(a)
        for a in (point_high.T.copy(), point_low.T.copy(), point_high, point_low, high.T.copy(), low.T.copy())
    ] + [response, ocean_mask]
    fields = -(-components * shells // TILE) * TILE
    message = f32((fields, count))
    smoothed, ring_two, next_up, next_down, *staged = pl.pallas_call(
        first_kernel,
        in_specs=[HBM, HBM, ANY, ANY, VMEM, VMEM] + [HBM] * len(stages),
        out_specs=[ANY, ANY, VMEM, VMEM] + [VMEM] * len(stages),
        out_shape=[f32(initial_displacement.shape), f32((components, rows, count)), message, message]
        + [jax.ShapeDtypeStruct(a.shape, a.dtype) for a in stages],
        scratch_shapes=sweep_scratch
        + [pltpu.SemaphoreType.DMA((1,)), pltpu.SemaphoreType.DMA((len(stages),))],
        compiler_params=params(28),
        cost_estimate=cost(10),
    )(*tensors[:2], later, ring, before, after, *(hbm(a) for a in stages))
    ring_two = lax.ppermute(ring_two, "radial", swap)
    next_before = lax.ppermute(next_up, "lateral", up)
    next_after = lax.ppermute(next_down, "lateral", down)

    *points, high, low, response, ocean_mask = staged
    coefficients, load = pl.pallas_call(
        spectrum_kernel,
        in_specs=[VMEM] * 6,
        out_specs=[VMEM, VMEM],
        out_shape=[f32((width, MODES)), f32(packed)],
        compiler_params=params(16),
        cost_estimate=cost(2),
    )(orders, response, *points)
    later, _ = lax.optimization_barrier((eta, load))
    load = lax.all_to_all(load, both, split_axis=0, concat_axis=0, tiled=True)

    displacement = pl.pallas_call(
        second_kernel,
        in_specs=[ANY, HBM, ANY, ANY, ANY, VMEM, VMEM, VMEM, VMEM],
        out_specs=HBM,
        out_shape=pltpu.HBM(initial_displacement.shape, jnp.float32),
        scratch_shapes=sweep_scratch,
        compiler_params=params(28),
        cost_estimate=cost(10),
    )(smoothed, tensors[1], later, ring, ring_two, before, after, next_before, next_after)

    sea_load = pl.pallas_call(
        load_kernel,
        in_specs=[VMEM] * 4,
        out_specs=VMEM,
        out_shape=f32((rows, count)),
        compiler_params=params(20),
        cost_estimate=cost(3),
    )(load, ocean_mask, high, low)
    return (displacement, coefficients.T, sea_load)


def solution(mesh):
    in_specs = (
        P("member", "radial", "lateral", None),
        P("member", "radial", "lateral", None),
        P("member"),
        P("radial", "lateral", None),
        P(None, "lateral"),
        P("lateral", None),
    )
    out_specs = (
        P("member", "radial", "lateral", None),
        P("member", ("lateral", "radial")),
        P("lateral", "member"),
    )
    return jax.shard_map(shards, mesh=mesh, in_specs=in_specs, out_specs=out_specs, check_vma=False)
```

```python
import functools
import math

import jax
import jax.numpy as jnp
import ml_dtypes
import numpy as np
from jax import lax
from jax.experimental import pallas as pl
from jax.experimental.pallas import tpu as pltpu
from jax.sharding import PartitionSpec as P

MODES = 512
RELAXATION = 0.8
TILE = 8
RADIX = 8
MIB = 1 << 20
ANY = pl.BlockSpec(memory_space=pl.ANY)
HBM = pl.BlockSpec(memory_space=pltpu.HBM)
SMEM = pl.BlockSpec(memory_space=pltpu.SMEM)
VMEM = pl.BlockSpec(memory_space=pltpu.VMEM)


def params(mib):
    return pltpu.CompilerParams(vmem_limit_bytes=mib * MIB)


def halves(table):
    high = table.astype(ml_dtypes.bfloat16)
    low = (table - high.astype(np.float64)).astype(ml_dtypes.bfloat16)
    return high, low


@functools.lru_cache
def longitude_tables(count, modes):
    points = np.arange(count // RADIX, dtype=np.int64)[:, None]
    orders = np.arange(modes, dtype=np.int64)[None, :]
    angle = (2.0 * math.pi / count) * (points * orders % count)
    table = np.concatenate([np.cos(angle), np.sin(angle)], axis=1) * math.sqrt(2.0 / count)
    return halves(table)


@functools.lru_cache
def colatitude_tables(count, modes):
    points = np.arange(count, dtype=np.int64)[:, None]
    waves = np.arange(modes, dtype=np.int64)[None, :]
    phase = waves * (2 * points + 1) % (4 * count)
    return halves(np.cos(math.pi / (2 * count) * phase) * math.sqrt(2.0 / count))


def split(values):
    high = values.astype(jnp.bfloat16)
    return high, (values - high.astype(jnp.float32)).astype(jnp.bfloat16)


def dot(a, b):
    return jnp.dot(a, b, preferred_element_type=jnp.float32)


def pack(block):
    rows, width = block.shape
    groups = max(1, 128 // width)
    rows //= groups
    return jnp.concatenate([block[k * rows : (k + 1) * rows] for k in range(groups)], axis=1)


def unpack(block, width):
    groups = max(1, 128 // width)
    return jnp.concatenate([block[:, k * width : (k + 1) * width] for k in range(groups)], axis=0)


def weighted_sum(terms):
    total = None
    for factor, values in terms:
        factor = round(factor, 15)
        if factor == 0.0:
            continue
        part = values if abs(factor) == 1.0 else abs(factor) * values
        if total is None:
            total = part if factor > 0 else -part
        else:
            total = total + part if factor > 0 else total - part
    return total


def turn(number):
    angle = 2.0 * math.pi * (number % RADIX) / RADIX
    return math.cos(angle), math.sin(angle)


def fold(values):
    step = values.shape[1] // RADIX
    parts = [values[:, m * step : (m + 1) * step] for m in range(RADIX)]
    cosines = [[(turn(k * m)[0], part) for m, part in enumerate(parts)] for k in range(RADIX // 2 + 1)]
    sines = [[(turn(k * m)[1], part) for m, part in enumerate(parts)] for k in range(1, RADIX // 2)]
    return [weighted_sum(terms) for terms in cosines + sines]


def unfold(blocks):
    cosines, sines = blocks[: RADIX // 2 + 1], blocks[RADIX // 2 + 1 :]
    return [
        weighted_sum(
            [(turn(k * m)[0], block) for k, block in enumerate(cosines)]
            + [(turn(k * m)[1], block) for k, block in enumerate(sines, 1)]
        )
        for m in range(RADIX)
    ]


def order_class(shape):
    order = lax.broadcasted_iota(jnp.int32, shape, len(shape) - 1) % RADIX
    mirrored = order > RADIX // 2
    return jnp.where(mirrored, RADIX - order, order), mirrored


def dot_nt(a, b):
    return lax.dot_general(a, b, (((1,), (1,)), ((), ())), preferred_element_type=jnp.float32)


def half_viscosity(index, viscosity_ref):
    values = [0.5 * viscosity_ref[k] for k in range(viscosity_ref.shape[0])]
    bit = 1
    while len(values) > 1:
        odd = (index & bit) != 0
        if len(values) % 2:
            values.append(values[-1])
        values = [jnp.where(odd, b, a) for a, b in zip(values[::2], values[1::2])]
        bit *= 2
    return values[0]


def row_number(shape):
    return lax.broadcasted_iota(jnp.int32, shape, 0)


def north_of(above, middle):
    return pltpu.roll(jnp.where(row_number(middle.shape) == TILE - 1, above, middle), 1, 0)


def south_of(below, middle):
    return pltpu.roll(jnp.where(row_number(middle.shape) == 0, below, middle), TILE - 1, 0)


def east_of(values):
    return pltpu.roll(values, values.shape[-1] - 1, values.ndim - 1)


def west_of(values):
    return pltpu.roll(values, 1, values.ndim - 1)


def relax_weights(middle, others):
    weights = [middle + other for other in others]
    diagonal = 1.0 + functools.reduce(jnp.add, weights)
    return weights, RELAXATION / diagonal


def relax(weights, factor, middle, others, force):
    total = force
    for weight, other in zip(weights, others):
        total = total + weight * other
    return (1.0 - RELAXATION) * middle + factor * total


def around(ref, lead, shell, start):
    rows = lambda first: pl.ds(pl.multiple_of(first, TILE), TILE)
    middle = ref[(*lead, shell, rows(start))]
    return middle, [
        ref[(*lead, shell + 1, rows(start))],
        ref[(*lead, shell - 1, rows(start))],
        south_of(ref[(*lead, shell, rows(start + TILE))], middle),
        north_of(ref[(*lead, shell, rows(start - TILE))], middle),
        west_of(middle),
        east_of(middle),
    ]


def odd_band():
    return lax.axis_index("lateral") % 2 == 1


def by_parity(one, two):
    one, two = one[...], two[...]
    return jnp.where(odd_band(), one, two), jnp.where(odd_band(), two, one)


def surface_message_kernel(viscosity_from, d, f, index, one, two, fields, forces, layers, viscosity, sems):
    shells, rows = index.shape[0], index.shape[1]
    top, pair = shells - 1, pl.ds(shells - 2, 2)
    copies = []
    for side, start in enumerate((0, rows - TILE)):
        part = pl.ds(start, TILE)
        copies += [
            pltpu.make_async_copy(d.at[0, pair, part], fields.at[side], sems.at[side, 0]),
            pltpu.make_async_copy(f.at[0, top, part], forces.at[side], sems.at[side, 1]),
            pltpu.make_async_copy(index.at[pair, part], layers.at[side], sems.at[side, 2]),
        ]
    copies.append(pltpu.make_async_copy(viscosity_from, viscosity, sems.at[2, 0]))
    for copy in copies:
        copy.start()
    for copy in copies:
        copy.wait()
    messages = []
    for side, near, far in ((0, 0, 1), (1, TILE - 1, TILE - 2)):
        below, surface = [half_viscosity(layers[side, k], viscosity) for k in range(2)]
        messages.append(
            (
                fields[side, 1, far],
                fields[side, 1, near],
                fields[side, 0, near],
                surface[far],
                surface[near],
                below[near],
                forces[side, near],
                jnp.zeros_like(below[near]),
            )
        )
    for place, (down, up) in enumerate(zip(*messages)):
        one[place] = jnp.where(odd_band(), down, up)
        two[place] = jnp.where(odd_band(), up, down)


def main_message_kernel(viscosity_from, d, index_from, token, h, one, two, ring, tops, ends, index, viscosity, sems):
    shells, rows = h.shape[0], h.shape[1]
    components = d.shape[0]
    del token
    shell = jnp.where(lax.axis_index("radial") == 0, shells - 1, 0)
    copies = [
        pltpu.make_async_copy(d.at[:, :, pl.ds(0, TILE)], tops, sems.at[0]),
        pltpu.make_async_copy(d.at[:, :, pl.ds(rows - TILE, TILE)], ends, sems.at[1]),
        pltpu.make_async_copy(d.at[:, shell], ring.at[pl.ds(0, components)], sems.at[2]),
    ]
    layers = [pltpu.make_async_copy(index_from.at[s], index.at[s], sems.at[4 + s]) for s in range(shells)]
    values = pltpu.make_async_copy(viscosity_from, viscosity, sems.at[4 + shells])
    for copy in [values] + layers + copies:
        copy.start()
    values.wait()
    for s in range(shells):
        layers[s].wait()

        def lookup(step, _):
            part = pl.ds(pl.multiple_of(step * TILE, TILE), TILE)
            h[s, part] = half_viscosity(index[s, part], viscosity)
            return 0

        lax.fori_loop(0, rows // TILE, lookup, 0)
    eta_copy = pltpu.make_async_copy(h.at[shell], ring.at[components], sems.at[3])
    eta_copy.start()
    for copy in copies[:2]:
        copy.wait()
    for s in range(shells):
        pairs = [(tops[c, s, 0], ends[c, s, TILE - 1]) for c in range(components)] + [(h[s, 0], h[s, rows - 1])]
        for c, (down, up) in enumerate(pairs):
            one[c * shells + s] = jnp.where(odd_band(), down, up)
            two[c * shells + s] = jnp.where(odd_band(), up, down)
    copies[2].wait()
    eta_copy.wait()


def surface_kernel(d, f, h, one, two, high_from, low_from, out, field, force, eta, smoothed, high, low, sems):
    shells, rows, count = h.shape
    top = lax.axis_size("radial") - 1

    @pl.when(lax.axis_index("radial") == top)
    def _():
        inner = pl.ds(TILE, rows)
        copies = [
            pltpu.make_async_copy(d.at[0, pl.ds(shells - 3, 3)], field.at[pl.ds(0, 3), inner], sems.at[0]),
            pltpu.make_async_copy(h.at[pl.ds(shells - 3, 3)], eta.at[pl.ds(0, 3), inner], sems.at[1]),
            pltpu.make_async_copy(f.at[0, pl.ds(shells - 2, 2)], force, sems.at[2]),
        ]
        tables = [
            pltpu.make_async_copy(high_from, high, sems.at[3]),
            pltpu.make_async_copy(low_from, low, sems.at[4]),
        ]
        for copy in copies + tables:
            copy.start()
        zeros = jnp.zeros((rows, count), jnp.float32)
        field[3, inner] = zeros
        eta[3, inner] = zeros
        smoothed[2, inner] = zeros
        before, after = by_parity(one, two)
        for message, place in ((before, TILE - 1), (after, rows + TILE)):
            field[2, place] = message[1]
            field[1, place] = message[2]
            eta[2, place] = message[4]
            eta[1, place] = message[5]
        for copy in copies:
            copy.wait()
        lateral = lax.axis_index("lateral")
        inside = (lateral > 0, lateral < lax.axis_size("lateral") - 1)
        for message, own, place, there in (
            (before, TILE, TILE - 1, inside[0]),
            (after, rows + TILE - 1, rows + TILE, inside[1]),
        ):
            row = lambda k: message[k : k + 1]
            own_row = lambda ref: ref[2, pl.ds(own, 1)]
            none = jnp.zeros((1, count), jnp.float32)
            weights, factor = relax_weights(
                row(4), [none, row(5), row(3), own_row(eta), west_of(row(4)), east_of(row(4))]
            )
            edge = relax(
                weights,
                factor,
                row(1),
                [none, row(2), row(0), own_row(field), west_of(row(1)), east_of(row(1))],
                row(6),
            )
            smoothed[1, pl.ds(place, 1)] = jnp.where(there, edge, none)

        def first(step, _):
            start = pl.multiple_of(step * TILE, TILE)
            for s in (1, 2):
                weights, factor = relax_weights(*around(eta, (), s, start + TILE))
                middle, others = around(field, (), s, start + TILE)
                smoothed[s - 1, pl.ds(start + TILE, TILE)] = relax(
                    weights, factor, middle, others, force[s - 1, pl.ds(start, TILE)]
                )
            return 0

        lax.fori_loop(0, rows // TILE, first, 0)

        def second(step, _):
            start = pl.multiple_of(step * TILE, TILE)
            weights, factor = relax_weights(*around(eta, (), 2, start + TILE))
            middle, others = around(smoothed, (), 1, start + TILE)
            field[0, pl.ds(start, TILE)] = relax(weights, factor, middle, others, force[1, pl.ds(start, TILE)])
            return 0

        lax.fori_loop(0, rows // TILE, second, 0)
        near, far = split(jnp.concatenate(fold(field[0, pl.ds(0, rows), :]), axis=0))
        for copy in tables:
            copy.wait()
        total = dot(near, high[...]) + dot(far, high[...]) + dot(near, low[...])
        blocks = [total[k * rows : (k + 1) * rows] for k in range(RADIX)]
        kind, mirrored = order_class((1, total.shape[1]))
        cosine, sine = blocks[0], jnp.zeros_like(blocks[0])
        for k in range(1, RADIX // 2 + 1):
            cosine = jnp.where(kind == k, blocks[k], cosine)
        for k in range(1, RADIX // 2):
            sine = jnp.where(kind == k, blocks[RADIX // 2 + k], sine)
        sine = jnp.where(mirrored, -sine, sine)
        modes = total.shape[1] // 2
        fourier = jnp.concatenate(
            [cosine[:, :modes] - sine[:, modes:], cosine[:, modes:] + sine[:, :modes]], axis=1
        )
        blocks = out.shape[0]
        width = fourier.shape[1] // blocks
        for block in range(blocks):
            out[block] = pack(fourier[:, block * width : (block + 1) * width])


def sweep_shells(d, f, h, ring_field, ring_eta, out, field, eta, force, result, sems, after_shell):
    components, shells, rows, count = d.shape
    inner = pl.ds(TILE, rows)
    lower = lax.axis_index("radial") == 0
    ring, nothing = jnp.where(lower, shells + 1, 0), jnp.where(lower, 0, shells + 1)
    halo = [
        pltpu.make_async_copy(source, field.at[c, ring, inner], sems.at[0, c])
        for c, source in enumerate(ring_field)
    ] + [pltpu.make_async_copy(ring_eta, eta.at[ring, inner], sems.at[0, components])]
    for copy in halo:
        copy.start()
    loads = []
    for s in range(shells):
        loads.append(
            [
                pltpu.make_async_copy(d.at[:, s], field.at[:, s + 1, inner], sems.at[s + 1, 0]),
                pltpu.make_async_copy(h.at[s], eta.at[s + 1, inner], sems.at[s + 1, 1]),
                pltpu.make_async_copy(f.at[:, s], force.at[:, s], sems.at[s + 1, 2]),
            ]
        )
        for copy in loads[s]:
            copy.start()
    zeros = jnp.zeros((rows, count), jnp.float32)
    for c in range(components):
        field[c, nothing, inner] = zeros
    eta[nothing, inner] = zeros
    for copy in halo + loads[0]:
        copy.wait()
    stores = []
    for s in range(shells):
        if s + 1 < shells:
            for copy in loads[s + 1]:
                copy.wait()

        def tile(step, _):
            start = pl.multiple_of(step * TILE, TILE)
            weights, factor = relax_weights(*around(eta, (), s + 1, start + TILE))
            for c in range(components):
                middle, others = around(field, (c,), s + 1, start + TILE)
                result[c, s, pl.ds(start, TILE)] = relax(
                    weights, factor, middle, others, force[c, s, pl.ds(start, TILE)]
                )
            return 0

        lax.fori_loop(0, rows // TILE, tile, 0)
        stores.append(pltpu.make_async_copy(result.at[:, s], out.at[:, s], sems.at[s + 1, 3]))
        stores[-1].start()
        after_shell(s)
    for copy in stores:
        copy.wait()


def set_edge(ref, lead, shells, rows, before, after):
    for s in range(shells):
        ref[(*lead, s + 1, TILE - 1)] = before(s)
        ref[(*lead, s + 1, rows + TILE)] = after(s)


def first_kernel(d, f, h, ring, one, two, *refs):
    components, shells, rows, _ = d.shape
    staged = (len(refs) - 11) // 2
    sources, refs = refs[:staged], refs[staged:]
    before, after = by_parity(one, two)
    out, ring_out, next_one, next_two, *targets = refs[: 4 + staged]
    field, eta, force, result, sems, ring_sems, stage_sems = refs[4 + staged :]
    stages = [
        pltpu.make_async_copy(source, target, stage_sems.at[k]) for k, (source, target) in enumerate(zip(sources, targets))
    ]
    lower = lax.axis_index("radial") == 0
    row = lambda message, kind: lambda s: message[kind * shells + s]
    for c in range(components):
        set_edge(field, (c,), shells, rows, row(before, c), row(after, c))
    set_edge(eta, (), shells, rows, row(before, components), row(after, components))

    def ring_copies(s):
        return [pltpu.make_async_copy(result.at[:, s], ring_out, ring_sems.at[0])]

    def after_shell(s):
        if s == 0:
            for copy in stages:
                copy.start()
        for c in range(components):
            down, up = result[c, s, 0], result[c, s, rows - 1]
            next_one[c * shells + s] = jnp.where(odd_band(), down, up)
            next_two[c * shells + s] = jnp.where(odd_band(), up, down)
        if s in (0, shells - 1):

            @pl.when(lower if s else jnp.logical_not(lower))
            def _():
                for copy in ring_copies(s):
                    copy.start()

    sweep_shells(
        d, f, h, [ring.at[c] for c in range(components)], ring.at[components],
        out, field, eta, force, result, sems, after_shell,
    )
    for copy in ring_copies(0) + stages:
        copy.wait()


def second_kernel(
    d, f, h, ring, ring_two, eta_one, eta_two, one, two, out, token, field, eta, force, result, sems
):
    components, shells, rows, _ = d.shape
    (eta_before, eta_after), (before, after) = by_parity(eta_one, eta_two), by_parity(one, two)
    token[...] = jnp.zeros_like(token)
    row = lambda message, kind: lambda s: message[kind * shells + s]
    for c in range(components):
        set_edge(field, (c,), shells, rows, row(before, c), row(after, c))
    set_edge(eta, (), shells, rows, row(eta_before, components), row(eta_after, components))
    sweep_shells(
        d, f, h, [ring_two.at[c] for c in range(components)], ring.at[components],
        out, field, eta, force, result, sems, lambda s: None,
    )


def spectrum_kernel(orders, response, wave_high, wave_low, point_high, point_low, coefficients, out):
    radial = lax.axis_size("radial")
    width = coefficients.shape[0]
    bands, rows = orders.shape[0] // radial, point_high.shape[0] * radial // orders.shape[0]
    fourier = jnp.concatenate([unpack(orders[band * radial + radial - 1], width) for band in range(bands)], axis=0)
    high, low = split(fourier)
    spectrum = dot(wave_high[...], high) + dot(wave_high[...], low) + dot(wave_low[...], high)
    coefficients[...] = spectrum.T
    own = response[:, :width]
    for place in range(1, radial):
        own = jnp.where(
            lax.axis_index("radial") == place, response[:, place * width : (place + 1) * width], own
        )
    high, low = split(own * spectrum)
    load = dot(point_high[...], high) + dot(point_high[...], low) + dot(point_low[...], high)
    for band in range(bands):
        block = pack(load[band * rows : (band + 1) * rows])
        for place in range(radial):
            out[band * radial + place] = block


def load_kernel(load, mask, high_from, low_from, token, out, high, low, sems):
    del token
    tables = [
        pltpu.make_async_copy(high_from, high, sems.at[0]),
        pltpu.make_async_copy(low_from, low, sems.at[1]),
    ]
    for copy in tables:
        copy.start()
    blocks, rows = load.shape[0], out.shape[0]
    step, width = out.shape[1] // RADIX, high.shape[1] // blocks
    values = jnp.concatenate([unpack(load[block], width) for block in range(blocks)], axis=1)
    modes = values.shape[1] // 2
    kind, mirrored = order_class((1, values.shape[1]))
    crossed = jnp.concatenate([values[:, modes:], -values[:, :modes]], axis=1)
    crossed = jnp.where(mirrored, -crossed, crossed)
    zero = jnp.zeros_like(values)
    stack = [jnp.where(kind == k, values, zero) for k in range(RADIX // 2 + 1)]
    stack += [jnp.where(kind == k, crossed, zero) for k in range(1, RADIX // 2)]
    near, far = split(jnp.concatenate(stack, axis=0))
    for copy in tables:
        copy.wait()
    total = dot_nt(near, high[...]) + dot_nt(far, high[...]) + dot_nt(near, low[...])
    for m, part in enumerate(unfold([total[k * rows : (k + 1) * rows] for k in range(RADIX)])):
        columns = slice(m * step, (m + 1) * step)
        out[:, columns] = part * mask[:, columns].astype(jnp.float32)


def cost(microseconds):
    return pl.CostEstimate(flops=0, bytes_accessed=3_000_000 * microseconds, transcendentals=0)


def hbm(values):
    return pltpu.with_memory_space_constraint(values, pltpu.HBM)


def shards(initial_displacement, force, viscosity, layer_index, response, ocean_mask):
    components, shells, rows, count = initial_displacement.shape
    radial, lateral = lax.axis_size("radial"), lax.axis_size("lateral")
    f32 = functools.partial(jax.ShapeDtypeStruct, dtype=jnp.float32)
    scratch = lambda *shape: pltpu.VMEM(shape, jnp.float32)
    width = 2 * MODES // (lateral * radial)
    first = [p for i in range(0, lateral - 1, 2) for p in ((i, i + 1), (i + 1, i))]
    second = [p for i in range(1, lateral - 1, 2) for p in ((i, i + 1), (i + 1, i))]
    top_only = lambda pairs: [(i * radial + radial - 1, j * radial + radial - 1) for i, j in pairs]

    tensors = [hbm(a) for a in (initial_displacement, force, layer_index)]
    viscosity = hbm(viscosity)
    surface_one, surface_two = pl.pallas_call(
        surface_message_kernel,
        in_specs=[HBM, HBM, HBM, HBM],
        out_specs=[VMEM, VMEM],
        out_shape=[f32((TILE, count))] * 2,
        scratch_shapes=[
            scratch(2, 2, TILE, count),
            scratch(2, TILE, count),
            pltpu.VMEM((2, 2, TILE, count), jnp.int32),
            pltpu.SMEM(viscosity.shape, jnp.float32),
            pltpu.SemaphoreType.DMA((3, 3)),
        ],
        compiler_params=params(8),
        cost_estimate=cost(2),
    )(viscosity, *tensors)
    token = surface_one
    both = ("lateral", "radial")
    surface_one = lax.ppermute(surface_one, both, top_only(first))
    surface_two = lax.ppermute(surface_two, both, top_only(second))

    fields = -(-(components + 1) * shells // TILE) * TILE
    message = f32((fields, count))
    edge_rows = scratch(components, shells, TILE, count)
    eta, one, two, ring = pl.pallas_call(
        main_message_kernel,
        in_specs=[HBM, HBM, HBM, ANY],
        out_specs=[VMEM, VMEM, VMEM, ANY],
        out_shape=[f32((shells, rows, count)), message, message, f32((components + 1, rows, count))],
        scratch_shapes=[
            edge_rows,
            edge_rows,
            pltpu.VMEM(layer_index.shape, jnp.int32),
            pltpu.SMEM(viscosity.shape, jnp.float32),
            pltpu.SemaphoreType.DMA((5 + shells,)),
        ],
        compiler_params=params(16),
        cost_estimate=cost(20),
    )(viscosity, tensors[0], tensors[2], token)
    swap = [(i, radial - 1 - i) for i in range(radial)]
    ring = lax.ppermute(ring, "radial", swap)
    one = lax.ppermute(one, "lateral", first)
    two = lax.ppermute(two, "lateral", second)

    high, low = longitude_tables(count, MODES)
    high, low = hbm(jnp.asarray(high)), hbm(jnp.asarray(low))
    table = pltpu.VMEM(high.shape, jnp.bfloat16)
    packed = (lateral * radial, rows * width // max(128, width), max(128, width))
    orders = pl.pallas_call(
        surface_kernel,
        in_specs=[HBM, HBM, ANY, VMEM, VMEM, HBM, HBM],
        out_specs=VMEM,
        out_shape=f32(packed),
        scratch_shapes=[
            scratch(4, rows + 2 * TILE, count),
            scratch(2, rows, count),
            scratch(4, rows + 2 * TILE, count),
            scratch(3, rows + 2 * TILE, count),
            table,
            table,
            pltpu.SemaphoreType.DMA((5,)),
        ],
        compiler_params=params(24),
        cost_estimate=cost(200),
    )(*tensors[:2], eta, surface_one, surface_two, high, low)
    later, _ = lax.optimization_barrier((eta, orders))
    orders = lax.all_to_all(orders, both, split_axis=0, concat_axis=0, tiled=True)

    sweep_scratch = [
        scratch(components, shells + 2, rows + 2 * TILE, count),
        scratch(shells + 2, rows + 2 * TILE, count),
        scratch(components, shells, rows, count),
        scratch(components, shells, rows, count),
        pltpu.SemaphoreType.DMA((shells + 1, 4)),
    ]
    point_high, point_low = colatitude_tables(rows * lateral, MODES)
    stages = [
        jnp.asarray(a)
        for a in (point_high.T.copy(), point_low.T.copy(), point_high, point_low)
    ] + [response]
    fields = -(-components * shells // TILE) * TILE
    message = f32((fields, count))
    smoothed, ring_two, next_one, next_two, *staged = pl.pallas_call(
        first_kernel,
        in_specs=[HBM, HBM, ANY, ANY, VMEM, VMEM] + [HBM] * len(stages),
        out_specs=[HBM, ANY, VMEM, VMEM] + [VMEM] * len(stages),
        out_shape=[pltpu.HBM(initial_displacement.shape, jnp.float32), f32((components, rows, count)), message, message]
        + [jax.ShapeDtypeStruct(a.shape, a.dtype) for a in stages],
        scratch_shapes=sweep_scratch
        + [pltpu.SemaphoreType.DMA((1,)), pltpu.SemaphoreType.DMA((len(stages),))],
        compiler_params=params(28),
        cost_estimate=cost(50),
    )(*tensors[:2], later, ring, one, two, *(hbm(a) for a in stages))
    ring_two = lax.ppermute(ring_two, "radial", swap)
    next_one = lax.ppermute(next_one, "lateral", first)
    next_two = lax.ppermute(next_two, "lateral", second)

    *points, response = staged
    coefficients, load = pl.pallas_call(
        spectrum_kernel,
        in_specs=[VMEM] * 6,
        out_specs=[VMEM, VMEM],
        out_shape=[f32((width, MODES)), f32(packed)],
        compiler_params=params(16),
        cost_estimate=cost(200),
    )(orders, response, *points)
    later, _ = lax.optimization_barrier((eta, load))
    load = lax.all_to_all(load, both, split_axis=0, concat_axis=0, tiled=True)

    displacement, token = pl.pallas_call(
        second_kernel,
        in_specs=[HBM, HBM, ANY, ANY, ANY, VMEM, VMEM, VMEM, VMEM],
        out_specs=[HBM, VMEM],
        out_shape=[pltpu.HBM(initial_displacement.shape, jnp.float32), f32((TILE, 128))],
        scratch_shapes=sweep_scratch,
        compiler_params=params(28),
        cost_estimate=cost(50),
    )(smoothed, tensors[1], later, ring, ring_two, one, two, next_one, next_two)

    sea_load = pl.pallas_call(
        load_kernel,
        in_specs=[VMEM, VMEM, HBM, HBM, ANY],
        out_specs=VMEM,
        out_shape=f32((rows, count)),
        scratch_shapes=[table, table, pltpu.SemaphoreType.DMA((2,))],
        compiler_params=params(20),
        cost_estimate=cost(3),
    )(load, ocean_mask, high, low, token)
    return (displacement, coefficients.T, sea_load)


def solution(mesh):
    in_specs = (
        P("member", "radial", "lateral", None),
        P("member", "radial", "lateral", None),
        P("member"),
        P("radial", "lateral", None),
        P(None, "lateral"),
        P("lateral", None),
    )
    out_specs = (
        P("member", "radial", "lateral", None),
        P("member", ("lateral", "radial")),
        P("lateral", "member"),
    )
    return jax.shard_map(shards, mesh=mesh, in_specs=in_specs, out_specs=out_specs, check_vma=False)
```

```python
import functools
import math

import jax
import jax.numpy as jnp
import ml_dtypes
import numpy as np
from jax import lax
from jax.experimental import pallas as pl
from jax.experimental.pallas import tpu as pltpu
from jax.sharding import PartitionSpec as P

MODES = 512
RELAXATION = 0.8
TILE = 8
RADIX = 8
MIB = 1 << 20
ANY = pl.BlockSpec(memory_space=pl.ANY)
HBM = pl.BlockSpec(memory_space=pltpu.HBM)
SMEM = pl.BlockSpec(memory_space=pltpu.SMEM)
VMEM = pl.BlockSpec(memory_space=pltpu.VMEM)


def params(mib):
    return pltpu.CompilerParams(vmem_limit_bytes=mib * MIB)


def halves(table):
    high = table.astype(ml_dtypes.bfloat16)
    low = (table - high.astype(np.float64)).astype(ml_dtypes.bfloat16)
    return high, low


@functools.lru_cache
def longitude_tables(count, modes):
    points = np.arange(count // RADIX, dtype=np.int64)[:, None]
    orders = np.arange(modes, dtype=np.int64)[None, :]
    angle = (2.0 * math.pi / count) * (points * orders % count)
    table = np.concatenate([np.cos(angle), np.sin(angle)], axis=1) * math.sqrt(2.0 / count)
    return halves(table)


@functools.lru_cache
def colatitude_tables(count, modes):
    points = np.arange(count, dtype=np.int64)[:, None]
    waves = np.arange(modes, dtype=np.int64)[None, :]
    phase = waves * (2 * points + 1) % (4 * count)
    return halves(np.cos(math.pi / (2 * count) * phase) * math.sqrt(2.0 / count))


def split(values):
    high = values.astype(jnp.bfloat16)
    return high, (values - high.astype(jnp.float32)).astype(jnp.bfloat16)


def dot(a, b):
    return jnp.dot(a, b, preferred_element_type=jnp.float32)


def pack(block):
    rows, width = block.shape
    groups = max(1, 128 // width)
    rows //= groups
    return jnp.concatenate([block[k * rows : (k + 1) * rows] for k in range(groups)], axis=1)


def unpack(block, width):
    groups = max(1, 128 // width)
    return jnp.concatenate([block[:, k * width : (k + 1) * width] for k in range(groups)], axis=0)


def weighted_sum(terms):
    total = None
    for factor, values in terms:
        factor = round(factor, 15)
        if factor == 0.0:
            continue
        part = values if abs(factor) == 1.0 else abs(factor) * values
        if total is None:
            total = part if factor > 0 else -part
        else:
            total = total + part if factor > 0 else total - part
    return total


def turn(number):
    angle = 2.0 * math.pi * (number % RADIX) / RADIX
    return math.cos(angle), math.sin(angle)


def fold(values):
    step = values.shape[1] // RADIX
    parts = [values[:, m * step : (m + 1) * step] for m in range(RADIX)]
    cosines = [[(turn(k * m)[0], part) for m, part in enumerate(parts)] for k in range(RADIX // 2 + 1)]
    sines = [[(turn(k * m)[1], part) for m, part in enumerate(parts)] for k in range(1, RADIX // 2)]
    return [weighted_sum(terms) for terms in cosines + sines]


def unfold(blocks):
    cosines, sines = blocks[: RADIX // 2 + 1], blocks[RADIX // 2 + 1 :]
    return [
        weighted_sum(
            [(turn(k * m)[0], block) for k, block in enumerate(cosines)]
            + [(turn(k * m)[1], block) for k, block in enumerate(sines, 1)]
        )
        for m in range(RADIX)
    ]


def order_class(shape):
    order = lax.broadcasted_iota(jnp.int32, shape, len(shape) - 1) % RADIX
    mirrored = order > RADIX // 2
    return jnp.where(mirrored, RADIX - order, order), mirrored


def dot_nt(a, b):
    return lax.dot_general(a, b, (((1,), (1,)), ((), ())), preferred_element_type=jnp.float32)


def half_viscosity(index, viscosity_ref):
    values = [0.5 * viscosity_ref[k] for k in range(viscosity_ref.shape[0])]
    bit = 1
    while len(values) > 1:
        odd = (index & bit) != 0
        if len(values) % 2:
            values.append(values[-1])
        values = [jnp.where(odd, b, a) for a, b in zip(values[::2], values[1::2])]
        bit *= 2
    return values[0]


def row_number(shape):
    return lax.broadcasted_iota(jnp.int32, shape, 0)


def north_of(above, middle):
    return pltpu.roll(jnp.where(row_number(middle.shape) == TILE - 1, above, middle), 1, 0)


def south_of(below, middle):
    return pltpu.roll(jnp.where(row_number(middle.shape) == 0, below, middle), TILE - 1, 0)


def east_of(values):
    return pltpu.roll(values, values.shape[-1] - 1, values.ndim - 1)


def west_of(values):
    return pltpu.roll(values, 1, values.ndim - 1)


def relax_weights(middle, others):
    weights = [middle + other for other in others]
    diagonal = 1.0 + functools.reduce(jnp.add, weights)
    return weights, RELAXATION / diagonal


def relax(weights, factor, middle, others, force):
    total = force
    for weight, other in zip(weights, others):
        total = total + weight * other
    return (1.0 - RELAXATION) * middle + factor * total


def around(ref, lead, shell, start):
    rows = lambda first: pl.ds(pl.multiple_of(first, TILE), TILE)
    middle = ref[(*lead, shell, rows(start))]
    return middle, [
        ref[(*lead, shell + 1, rows(start))],
        ref[(*lead, shell - 1, rows(start))],
        south_of(ref[(*lead, shell, rows(start + TILE))], middle),
        north_of(ref[(*lead, shell, rows(start - TILE))], middle),
        west_of(middle),
        east_of(middle),
    ]


def odd_band():
    return lax.axis_index("lateral") % 2 == 1


def by_parity(one, two):
    one, two = one[...], two[...]
    return jnp.where(odd_band(), one, two), jnp.where(odd_band(), two, one)


def surface_message_kernel(viscosity_from, d, f, index, one, two, fields, forces, layers, viscosity, sems):
    shells, rows = index.shape[0], index.shape[1]
    top, pair = shells - 1, pl.ds(shells - 2, 2)
    copies = []
    for side, start in enumerate((0, rows - TILE)):
        part = pl.ds(start, TILE)
        copies += [
            pltpu.make_async_copy(d.at[0, pair, part], fields.at[side], sems.at[side, 0]),
            pltpu.make_async_copy(f.at[0, top, part], forces.at[side], sems.at[side, 1]),
            pltpu.make_async_copy(index.at[pair, part], layers.at[side], sems.at[side, 2]),
        ]
    copies.append(pltpu.make_async_copy(viscosity_from, viscosity, sems.at[2, 0]))
    for copy in copies:
        copy.start()
    for copy in copies:
        copy.wait()
    messages = []
    for side, near, far in ((0, 0, 1), (1, TILE - 1, TILE - 2)):
        below, surface = [half_viscosity(layers[side, k], viscosity) for k in range(2)]
        messages.append(
            (
                fields[side, 1, far],
                fields[side, 1, near],
                fields[side, 0, near],
                surface[far],
                surface[near],
                below[near],
                forces[side, near],
                jnp.zeros_like(below[near]),
            )
        )
    for place, (down, up) in enumerate(zip(*messages)):
        one[place] = jnp.where(odd_band(), down, up)
        two[place] = jnp.where(odd_band(), up, down)


def main_message_kernel(
    viscosity_from, d, index_from, token, eta, one, two, ring, h, tops, ends, index, viscosity, sems, eta_sems
):
    shells, rows, _ = h.shape
    components = d.shape[0]
    del token
    shell = jnp.where(lax.axis_index("radial") == 0, shells - 1, 0)
    copies = [
        pltpu.make_async_copy(d.at[:, :, pl.ds(0, TILE)], tops, sems.at[0]),
        pltpu.make_async_copy(d.at[:, :, pl.ds(rows - TILE, TILE)], ends, sems.at[1]),
        pltpu.make_async_copy(d.at[:, shell], ring.at[pl.ds(0, components)], sems.at[2]),
    ]
    layers = [pltpu.make_async_copy(index_from.at[s], index.at[s], sems.at[4 + s]) for s in range(shells)]
    values = pltpu.make_async_copy(viscosity_from, viscosity, sems.at[4 + shells])
    for copy in [values] + layers + copies:
        copy.start()
    values.wait()
    stores = []
    for s in range(shells):
        layers[s].wait()

        def lookup(step, _):
            part = pl.ds(pl.multiple_of(step * TILE, TILE), TILE)
            h[s, part] = half_viscosity(index[s, part], viscosity)
            return 0

        lax.fori_loop(0, rows // TILE, lookup, 0)
        stores.append(pltpu.make_async_copy(h.at[s], eta.at[s], eta_sems.at[s]))
        stores[-1].start()
    stores.append(pltpu.make_async_copy(h.at[shell], ring.at[components], sems.at[3]))
    stores[-1].start()
    for copy in copies[:2]:
        copy.wait()
    for s in range(shells):
        pairs = [(tops[c, s, 0], ends[c, s, TILE - 1]) for c in range(components)] + [(h[s, 0], h[s, rows - 1])]
        for c, (down, up) in enumerate(pairs):
            one[c * shells + s] = jnp.where(odd_band(), down, up)
            two[c * shells + s] = jnp.where(odd_band(), up, down)
    for copy in copies[2:] + stores:
        copy.wait()


def surface_kernel(d, f, h, one, two, high_from, low_from, out, field, force, eta, smoothed, high, low, sems):
    shells, rows, count = h.shape
    top = lax.axis_size("radial") - 1

    @pl.when(lax.axis_index("radial") == top)
    def _():
        inner = pl.ds(TILE, rows)
        copies = [
            pltpu.make_async_copy(d.at[0, pl.ds(shells - 3, 3)], field.at[pl.ds(0, 3), inner], sems.at[0]),
            pltpu.make_async_copy(h.at[pl.ds(shells - 3, 3)], eta.at[pl.ds(0, 3), inner], sems.at[1]),
            pltpu.make_async_copy(f.at[0, pl.ds(shells - 2, 2)], force, sems.at[2]),
        ]
        tables = [
            pltpu.make_async_copy(high_from, high, sems.at[3]),
            pltpu.make_async_copy(low_from, low, sems.at[4]),
        ]
        for copy in copies + tables:
            copy.start()
        zeros = jnp.zeros((rows, count), jnp.float32)
        field[3, inner] = zeros
        eta[3, inner] = zeros
        smoothed[2, inner] = zeros
        before, after = by_parity(one, two)
        for message, place in ((before, TILE - 1), (after, rows + TILE)):
            field[2, place] = message[1]
            field[1, place] = message[2]
            eta[2, place] = message[4]
            eta[1, place] = message[5]
        for copy in copies:
            copy.wait()
        lateral = lax.axis_index("lateral")
        inside = (lateral > 0, lateral < lax.axis_size("lateral") - 1)
        for message, own, place, there in (
            (before, TILE, TILE - 1, inside[0]),
            (after, rows + TILE - 1, rows + TILE, inside[1]),
        ):
            row = lambda k: message[k : k + 1]
            own_row = lambda ref: ref[2, pl.ds(own, 1)]
            none = jnp.zeros((1, count), jnp.float32)
            weights, factor = relax_weights(
                row(4), [none, row(5), row(3), own_row(eta), west_of(row(4)), east_of(row(4))]
            )
            edge = relax(
                weights,
                factor,
                row(1),
                [none, row(2), row(0), own_row(field), west_of(row(1)), east_of(row(1))],
                row(6),
            )
            smoothed[1, pl.ds(place, 1)] = jnp.where(there, edge, none)

        def first(step, _):
            start = pl.multiple_of(step * TILE, TILE)
            for s in (1, 2):
                weights, factor = relax_weights(*around(eta, (), s, start + TILE))
                middle, others = around(field, (), s, start + TILE)
                smoothed[s - 1, pl.ds(start + TILE, TILE)] = relax(
                    weights, factor, middle, others, force[s - 1, pl.ds(start, TILE)]
                )
            return 0

        lax.fori_loop(0, rows // TILE, first, 0)

        def second(step, _):
            start = pl.multiple_of(step * TILE, TILE)
            weights, factor = relax_weights(*around(eta, (), 2, start + TILE))
            middle, others = around(smoothed, (), 1, start + TILE)
            field[0, pl.ds(start, TILE)] = relax(weights, factor, middle, others, force[1, pl.ds(start, TILE)])
            return 0

        lax.fori_loop(0, rows // TILE, second, 0)
        near, far = split(jnp.concatenate(fold(field[0, pl.ds(0, rows), :]), axis=0))
        for copy in tables:
            copy.wait()
        total = dot(near, high[...]) + dot(far, high[...]) + dot(near, low[...])
        blocks = [total[k * rows : (k + 1) * rows] for k in range(RADIX)]
        kind, mirrored = order_class((1, total.shape[1]))
        cosine, sine = blocks[0], jnp.zeros_like(blocks[0])
        for k in range(1, RADIX // 2 + 1):
            cosine = jnp.where(kind == k, blocks[k], cosine)
        for k in range(1, RADIX // 2):
            sine = jnp.where(kind == k, blocks[RADIX // 2 + k], sine)
        sine = jnp.where(mirrored, -sine, sine)
        modes = total.shape[1] // 2
        fourier = jnp.concatenate(
            [cosine[:, :modes] - sine[:, modes:], cosine[:, modes:] + sine[:, :modes]], axis=1
        )
        blocks = out.shape[0]
        width = fourier.shape[1] // blocks
        for block in range(blocks):
            out[block] = pack(fourier[:, block * width : (block + 1) * width])


def sweep_shells(d, f, h, ring_field, ring_eta, out, field, eta, force, result, sems, before_first, after_shell):
    components, shells, rows, count = d.shape
    inner = pl.ds(TILE, rows)
    lower = lax.axis_index("radial") == 0
    ring, nothing = jnp.where(lower, shells + 1, 0), jnp.where(lower, 0, shells + 1)
    halo = [
        pltpu.make_async_copy(source, field.at[c, ring, inner], sems.at[0, c])
        for c, source in enumerate(ring_field)
    ] + [pltpu.make_async_copy(ring_eta, eta.at[ring, inner], sems.at[0, components])]
    for copy in halo:
        copy.start()
    loads = []
    for s in range(shells):
        loads.append(
            [
                pltpu.make_async_copy(d.at[:, s], field.at[:, s + 1, inner], sems.at[s + 1, 0]),
                pltpu.make_async_copy(h.at[s], eta.at[s + 1, inner], sems.at[s + 1, 1]),
                pltpu.make_async_copy(f.at[:, s], force.at[:, s], sems.at[s + 1, 2]),
            ]
        )
        for copy in loads[s]:
            copy.start()
    zeros = jnp.zeros((rows, count), jnp.float32)
    for c in range(components):
        field[c, nothing, inner] = zeros
    eta[nothing, inner] = zeros
    before_first()
    for copy in halo + loads[0]:
        copy.wait()
    stores = []
    for s in range(shells):
        if s + 1 < shells:
            for copy in loads[s + 1]:
                copy.wait()

        def tile(step, _):
            start = pl.multiple_of(step * TILE, TILE)
            weights, factor = relax_weights(*around(eta, (), s + 1, start + TILE))
            for c in range(components):
                middle, others = around(field, (c,), s + 1, start + TILE)
                result[c, s, pl.ds(start, TILE)] = relax(
                    weights, factor, middle, others, force[c, s, pl.ds(start, TILE)]
                )
            return 0

        lax.fori_loop(0, rows // TILE, tile, 0)
        stores.append(pltpu.make_async_copy(result.at[:, s], out.at[:, s], sems.at[s + 1, 3]))
        stores[-1].start()
        after_shell(s)
    for copy in stores:
        copy.wait()


def set_edge(ref, lead, shells, rows, before, after):
    for s in range(shells):
        ref[(*lead, s + 1, TILE - 1)] = before(s)
        ref[(*lead, s + 1, rows + TILE)] = after(s)


def load_messages(sources, slots, sems):
    copies = [pltpu.make_async_copy(source, slots.at[k], sems.at[k]) for k, source in enumerate(sources)]
    for copy in copies:
        copy.start()
    return copies


def first_kernel(
    d, f, h, ring, one, two, out, ring_out, next_one, next_two, field, eta, force, result, messages, sems, more_sems
):
    components, shells, rows, _ = d.shape
    lower = lax.axis_index("radial") == 0
    arrivals = load_messages((one, two), messages, more_sems)

    def before_first():
        for copy in arrivals:
            copy.wait()
        before, after = by_parity(messages.at[0], messages.at[1])
        row = lambda message, kind: lambda s: message[kind * shells + s]
        for c in range(components):
            set_edge(field, (c,), shells, rows, row(before, c), row(after, c))
        set_edge(eta, (), shells, rows, row(before, components), row(after, components))

    def ring_copy(s):
        return pltpu.make_async_copy(result.at[:, s], ring_out, more_sems.at[2])

    def after_shell(s):
        for c in range(components):
            down, up = result[c, s, 0], result[c, s, rows - 1]
            next_one[c * shells + s] = jnp.where(odd_band(), down, up)
            next_two[c * shells + s] = jnp.where(odd_band(), up, down)
        if s in (0, shells - 1):

            @pl.when(lower if s else jnp.logical_not(lower))
            def _():
                ring_copy(s).start()

    sweep_shells(
        d, f, h, [ring.at[c] for c in range(components)], ring.at[components],
        out, field, eta, force, result, sems, before_first, after_shell,
    )
    ring_copy(0).wait()


def second_kernel(
    d, f, h, ring, ring_two, eta_one, eta_two, one, two, out, token, field, eta, force, result, messages, eta_messages,
    sems, more_sems
):
    components, shells, rows, _ = d.shape
    token[...] = jnp.zeros_like(token)
    arrivals = load_messages((one, two), messages, more_sems.at[0]) + load_messages(
        (eta_one, eta_two), eta_messages, more_sems.at[1]
    )

    def before_first():
        for copy in arrivals:
            copy.wait()
        before, after = by_parity(messages.at[0], messages.at[1])
        row = lambda message, kind: lambda s: message[kind * shells + s]
        for c in range(components):
            set_edge(field, (c,), shells, rows, row(before, c), row(after, c))
        before, after = by_parity(eta_messages.at[0], eta_messages.at[1])
        set_edge(eta, (), shells, rows, row(before, components), row(after, components))

    sweep_shells(
        d, f, h, [ring_two.at[c] for c in range(components)], ring.at[components],
        out, field, eta, force, result, sems, before_first, lambda s: None,
    )


def spectrum_kernel(orders, *refs):
    sources, (coefficients, out), refs = refs[:5], refs[5:7], refs[7:]
    copies = [pltpu.make_async_copy(source, refs[k], refs[5].at[k]) for k, source in enumerate(sources)]
    for copy in copies:
        copy.start()
    wave_high, wave_low, point_high, point_low, response = refs[:5]
    radial = lax.axis_size("radial")
    width = coefficients.shape[0]
    bands, rows = orders.shape[0] // radial, point_high.shape[0] * radial // orders.shape[0]
    fourier = jnp.concatenate([unpack(orders[band * radial + radial - 1], width) for band in range(bands)], axis=0)
    high, low = split(fourier)
    for copy in copies:
        copy.wait()
    spectrum = dot(wave_high[...], high) + dot(wave_high[...], low) + dot(wave_low[...], high)
    coefficients[...] = spectrum.T
    own = response[:, :width]
    for place in range(1, radial):
        own = jnp.where(
            lax.axis_index("radial") == place, response[:, place * width : (place + 1) * width], own
        )
    high, low = split(own * spectrum)
    load = dot(point_high[...], high) + dot(point_high[...], low) + dot(point_low[...], high)
    for band in range(bands):
        block = pack(load[band * rows : (band + 1) * rows])
        for place in range(radial):
            out[band * radial + place] = block


def load_kernel(load, mask, high_from, low_from, token, out, high, low, sems):
    del token
    tables = [
        pltpu.make_async_copy(high_from, high, sems.at[0]),
        pltpu.make_async_copy(low_from, low, sems.at[1]),
    ]
    for copy in tables:
        copy.start()
    blocks, rows = load.shape[0], out.shape[0]
    step, width = out.shape[1] // RADIX, high.shape[1] // blocks
    values = jnp.concatenate([unpack(load[block], width) for block in range(blocks)], axis=1)
    modes = values.shape[1] // 2
    kind, mirrored = order_class((1, values.shape[1]))
    crossed = jnp.concatenate([values[:, modes:], -values[:, :modes]], axis=1)
    crossed = jnp.where(mirrored, -crossed, crossed)
    zero = jnp.zeros_like(values)
    stack = [jnp.where(kind == k, values, zero) for k in range(RADIX // 2 + 1)]
    stack += [jnp.where(kind == k, crossed, zero) for k in range(1, RADIX // 2)]
    near, far = split(jnp.concatenate(stack, axis=0))
    for copy in tables:
        copy.wait()
    total = dot_nt(near, high[...]) + dot_nt(far, high[...]) + dot_nt(near, low[...])
    for m, part in enumerate(unfold([total[k * rows : (k + 1) * rows] for k in range(RADIX)])):
        columns = slice(m * step, (m + 1) * step)
        out[:, columns] = part * mask[:, columns].astype(jnp.float32)


def cost(microseconds):
    return pl.CostEstimate(flops=0, bytes_accessed=3_000_000 * microseconds, transcendentals=0)


def hbm(values):
    return pltpu.with_memory_space_constraint(values, pltpu.HBM)


def shards(initial_displacement, force, viscosity, layer_index, response, ocean_mask):
    components, shells, rows, count = initial_displacement.shape
    radial, lateral = lax.axis_size("radial"), lax.axis_size("lateral")
    f32 = functools.partial(jax.ShapeDtypeStruct, dtype=jnp.float32)
    scratch = lambda *shape: pltpu.VMEM(shape, jnp.float32)
    in_hbm = lambda *shape: pltpu.HBM(shape, jnp.float32)
    width = 2 * MODES // (lateral * radial)
    first = [p for i in range(0, lateral - 1, 2) for p in ((i, i + 1), (i + 1, i))]
    second = [p for i in range(1, lateral - 1, 2) for p in ((i, i + 1), (i + 1, i))]
    both = ("lateral", "radial")
    top_only = lambda pairs: [(i * radial + radial - 1, j * radial + radial - 1) for i, j in pairs]

    tensors = [hbm(a) for a in (initial_displacement, force, layer_index)]
    viscosity = hbm(viscosity)
    surface_one, surface_two = pl.pallas_call(
        surface_message_kernel,
        in_specs=[HBM, HBM, HBM, HBM],
        out_specs=[VMEM, VMEM],
        out_shape=[f32((TILE, count))] * 2,
        scratch_shapes=[
            scratch(2, 2, TILE, count),
            scratch(2, TILE, count),
            pltpu.VMEM((2, 2, TILE, count), jnp.int32),
            pltpu.SMEM(viscosity.shape, jnp.float32),
            pltpu.SemaphoreType.DMA((3, 3)),
        ],
        compiler_params=params(8),
        cost_estimate=cost(2),
    )(viscosity, *tensors)
    token = surface_one
    both = ("lateral", "radial")
    surface_two = lax.ppermute(surface_two, both, top_only(second))
    surface_one = lax.ppermute(surface_one, both, top_only(first))

    fields = -(-(components + 1) * shells // TILE) * TILE
    message = f32((fields, count))
    edge_rows = scratch(components, shells, TILE, count)
    eta, one, two, ring = pl.pallas_call(
        main_message_kernel,
        in_specs=[HBM, HBM, HBM, ANY],
        out_specs=[HBM, VMEM, VMEM, VMEM],
        out_shape=[in_hbm(shells, rows, count), message, message, f32((components + 1, rows, count))],
        scratch_shapes=[
            scratch(shells, rows, count),
            edge_rows,
            edge_rows,
            pltpu.VMEM(layer_index.shape, jnp.int32),
            pltpu.SMEM(viscosity.shape, jnp.float32),
            pltpu.SemaphoreType.DMA((5 + shells,)),
            pltpu.SemaphoreType.DMA((shells,)),
        ],
        compiler_params=params(16),
        cost_estimate=cost(20),
    )(viscosity, tensors[0], tensors[2], token)
    one, two, ring, surface_one, surface_two = lax.optimization_barrier((one, two, ring, surface_one, surface_two))
    swap = [(i, radial - 1 - i) for i in range(radial)]
    ring = lax.ppermute(ring, "radial", swap)
    one = lax.ppermute(one, "lateral", first)
    two = lax.ppermute(two, "lateral", second)

    high, low = longitude_tables(count, MODES)
    high, low = hbm(jnp.asarray(high)), hbm(jnp.asarray(low))
    table = pltpu.VMEM(high.shape, jnp.bfloat16)
    packed = (lateral * radial, rows * width // max(128, width), max(128, width))
    orders = pl.pallas_call(
        surface_kernel,
        in_specs=[HBM, HBM, HBM, VMEM, VMEM, HBM, HBM],
        out_specs=VMEM,
        out_shape=f32(packed),
        scratch_shapes=[
            scratch(4, rows + 2 * TILE, count),
            scratch(2, rows, count),
            scratch(4, rows + 2 * TILE, count),
            scratch(3, rows + 2 * TILE, count),
            table,
            table,
            pltpu.SemaphoreType.DMA((5,)),
        ],
        compiler_params=params(24),
        cost_estimate=cost(200),
    )(*tensors[:2], hbm(eta), surface_one, surface_two, high, low)
    orders, one, two, ring = lax.optimization_barrier((orders, one, two, ring))
    one, two, ring, eta = hbm(one), hbm(two), hbm(ring), hbm(eta)
    orders = lax.all_to_all(orders, both, split_axis=0, concat_axis=0, tiled=True)

    sweep_scratch = [
        scratch(components, shells + 2, rows + 2 * TILE, count),
        scratch(shells + 2, rows + 2 * TILE, count),
        scratch(components, shells, rows, count),
        scratch(components, shells, rows, count),
    ]
    sweep_sems = pltpu.SemaphoreType.DMA((shells + 1, 4))
    point_high, point_low = colatitude_tables(rows * lateral, MODES)
    stages = [
        jnp.asarray(a)
        for a in (point_high.T.copy(), point_low.T.copy(), point_high, point_low)
    ] + [response]
    message = f32((-(-components * shells // TILE) * TILE, count))
    smoothed, ring_two, next_one, next_two = pl.pallas_call(
        first_kernel,
        in_specs=[HBM] * 6,
        out_specs=[HBM, HBM, VMEM, VMEM],
        out_shape=[in_hbm(*initial_displacement.shape), in_hbm(components, rows, count), message, message],
        scratch_shapes=[*sweep_scratch, scratch(2, *one.shape), sweep_sems, pltpu.SemaphoreType.DMA((3,))],
        compiler_params=params(28),
        cost_estimate=cost(50),
    )(*tensors[:2], eta, ring, one, two)
    ring_two, next_one, next_two, orders = lax.optimization_barrier((ring_two, next_one, next_two, orders))
    ring_two = lax.ppermute(ring_two, "radial", swap)
    next_one = lax.ppermute(next_one, "lateral", first)
    next_two = lax.ppermute(next_two, "lateral", second)

    coefficients, load = pl.pallas_call(
        spectrum_kernel,
        in_specs=[VMEM] + [HBM] * 5,
        out_specs=[VMEM, VMEM],
        out_shape=[f32((width, MODES)), f32(packed)],
        scratch_shapes=[pltpu.VMEM(a.shape, a.dtype) for a in stages] + [pltpu.SemaphoreType.DMA((5,))],
        compiler_params=params(16),
        cost_estimate=cost(200),
    )(orders, *(hbm(a) for a in stages))
    load, ring_two, next_one, next_two = lax.optimization_barrier((load, ring_two, next_one, next_two))
    eta, load = lax.optimization_barrier((eta, load))
    load = lax.all_to_all(load, both, split_axis=0, concat_axis=0, tiled=True)

    displacement, token = pl.pallas_call(
        second_kernel,
        in_specs=[HBM] * 9,
        out_specs=[HBM, VMEM],
        out_shape=[in_hbm(*initial_displacement.shape), f32((TILE, 128))],
        scratch_shapes=[
            *sweep_scratch,
            scratch(2, *next_one.shape),
            scratch(2, *one.shape),
            sweep_sems,
            pltpu.SemaphoreType.DMA((2, 2)),
        ],
        compiler_params=params(28),
        cost_estimate=cost(50),
    )(hbm(smoothed), tensors[1], *(hbm(a) for a in (eta, ring, ring_two, one, two, next_one, next_two)))

    sea_load = pl.pallas_call(
        load_kernel,
        in_specs=[VMEM, VMEM, HBM, HBM, ANY],
        out_specs=VMEM,
        out_shape=f32((rows, count)),
        scratch_shapes=[table, table, pltpu.SemaphoreType.DMA((2,))],
        compiler_params=params(20),
        cost_estimate=cost(3),
    )(load, ocean_mask, high, low, token)
    return (displacement, coefficients.T, sea_load)


def solution(mesh):
    in_specs = (
        P("member", "radial", "lateral", None),
        P("member", "radial", "lateral", None),
        P("member"),
        P("radial", "lateral", None),
        P(None, "lateral"),
        P("lateral", None),
    )
    out_specs = (
        P("member", "radial", "lateral", None),
        P("member", ("lateral", "radial")),
        P("lateral", "member"),
    )
    return jax.shard_map(shards, mesh=mesh, in_specs=in_specs, out_specs=out_specs, check_vma=False)
```

```python
import functools
import math

import jax
import jax.numpy as jnp
import ml_dtypes
import numpy as np
from jax import lax
from jax.experimental import pallas as pl
from jax.experimental.pallas import tpu as pltpu
from jax.sharding import PartitionSpec as P

MODES = 512
RELAXATION = 0.8
TILE = 8
RADIX = 8
MIB = 1 << 20
ANY = pl.BlockSpec(memory_space=pl.ANY)
HBM = pl.BlockSpec(memory_space=pltpu.HBM)
SMEM = pl.BlockSpec(memory_space=pltpu.SMEM)
VMEM = pl.BlockSpec(memory_space=pltpu.VMEM)


def params(mib):
    return pltpu.CompilerParams(vmem_limit_bytes=mib * MIB)


def halves(table):
    high = table.astype(ml_dtypes.bfloat16)
    low = (table - high.astype(np.float64)).astype(ml_dtypes.bfloat16)
    return high, low


@functools.lru_cache
def longitude_tables(count, modes):
    points = np.arange(count // RADIX, dtype=np.int64)[:, None]
    orders = np.arange(modes, dtype=np.int64)[None, :]
    angle = (2.0 * math.pi / count) * (points * orders % count)
    table = np.concatenate([np.cos(angle), np.sin(angle)], axis=1) * math.sqrt(2.0 / count)
    return halves(table)


@functools.lru_cache
def colatitude_tables(count, modes):
    points = np.arange(count, dtype=np.int64)[:, None]
    waves = np.arange(modes, dtype=np.int64)[None, :]
    phase = waves * (2 * points + 1) % (4 * count)
    return halves(np.cos(math.pi / (2 * count) * phase) * math.sqrt(2.0 / count))


def split(values):
    high = values.astype(jnp.bfloat16)
    return high, (values - high.astype(jnp.float32)).astype(jnp.bfloat16)


def dot(a, b):
    return jnp.dot(a, b, preferred_element_type=jnp.float32)


def pack(block):
    rows, width = block.shape
    groups = max(1, 128 // width)
    rows //= groups
    return jnp.concatenate([block[k * rows : (k + 1) * rows] for k in range(groups)], axis=1)


def unpack(block, width):
    groups = max(1, 128 // width)
    return jnp.concatenate([block[:, k * width : (k + 1) * width] for k in range(groups)], axis=0)


def weighted_sum(terms):
    total = None
    for factor, values in terms:
        factor = round(factor, 15)
        if factor == 0.0:
            continue
        part = values if abs(factor) == 1.0 else abs(factor) * values
        if total is None:
            total = part if factor > 0 else -part
        else:
            total = total + part if factor > 0 else total - part
    return total


def turn(number):
    angle = 2.0 * math.pi * (number % RADIX) / RADIX
    return math.cos(angle), math.sin(angle)


def fold(values):
    step = values.shape[1] // RADIX
    parts = [values[:, m * step : (m + 1) * step] for m in range(RADIX)]
    cosines = [[(turn(k * m)[0], part) for m, part in enumerate(parts)] for k in range(RADIX // 2 + 1)]
    sines = [[(turn(k * m)[1], part) for m, part in enumerate(parts)] for k in range(1, RADIX // 2)]
    return [weighted_sum(terms) for terms in cosines + sines]


def unfold(blocks):
    cosines, sines = blocks[: RADIX // 2 + 1], blocks[RADIX // 2 + 1 :]
    return [
        weighted_sum(
            [(turn(k * m)[0], block) for k, block in enumerate(cosines)]
            + [(turn(k * m)[1], block) for k, block in enumerate(sines, 1)]
        )
        for m in range(RADIX)
    ]


def order_class(shape):
    order = lax.broadcasted_iota(jnp.int32, shape, len(shape) - 1) % RADIX
    mirrored = order > RADIX // 2
    return jnp.where(mirrored, RADIX - order, order), mirrored


def dot_nt(a, b):
    return lax.dot_general(a, b, (((1,), (1,)), ((), ())), preferred_element_type=jnp.float32)


def half_viscosity(index, viscosity_ref):
    values = [0.5 * viscosity_ref[k] for k in range(viscosity_ref.shape[0])]
    bit = 1
    while len(values) > 1:
        odd = (index & bit) != 0
        if len(values) % 2:
            values.append(values[-1])
        values = [jnp.where(odd, b, a) for a, b in zip(values[::2], values[1::2])]
        bit *= 2
    return values[0]


def row_number(shape):
    return lax.broadcasted_iota(jnp.int32, shape, 0)


def north_of(above, middle):
    return pltpu.roll(jnp.where(row_number(middle.shape) == TILE - 1, above, middle), 1, 0)


def south_of(below, middle):
    return pltpu.roll(jnp.where(row_number(middle.shape) == 0, below, middle), TILE - 1, 0)


def east_of(values):
    return pltpu.roll(values, values.shape[-1] - 1, values.ndim - 1)


def west_of(values):
    return pltpu.roll(values, 1, values.ndim - 1)


def relax_weights(middle, others):
    weights = [middle + other for other in others]
    diagonal = 1.0 + functools.reduce(jnp.add, weights)
    return weights, RELAXATION / diagonal


def relax(weights, factor, middle, others, force):
    total = force
    for weight, other in zip(weights, others):
        total = total + weight * other
    return (1.0 - RELAXATION) * middle + factor * total


def around(ref, lead, shell, start):
    rows = lambda first: pl.ds(pl.multiple_of(first, TILE), TILE)
    middle = ref[(*lead, shell, rows(start))]
    return middle, [
        ref[(*lead, shell + 1, rows(start))],
        ref[(*lead, shell - 1, rows(start))],
        south_of(ref[(*lead, shell, rows(start + TILE))], middle),
        north_of(ref[(*lead, shell, rows(start - TILE))], middle),
        west_of(middle),
        east_of(middle),
    ]


def odd_band():
    return lax.axis_index("lateral") % 2 == 1


def by_parity(one, two):
    one, two = one[...], two[...]
    return jnp.where(odd_band(), one, two), jnp.where(odd_band(), two, one)


def message_kernel(viscosity_from, d, f, index, one, two, fields, forces, layers, rows_of, viscosity, sems):
    components, shells, rows, count = d.shape
    copies = [pltpu.make_async_copy(viscosity_from, viscosity, sems.at[0])]
    for side, start in enumerate((0, rows - TILE)):
        part = pl.ds(start, TILE)
        copies += [
            pltpu.make_async_copy(index.at[:, part], layers.at[side], sems.at[1 + side]),
            pltpu.make_async_copy(d.at[:, :, part], fields.at[side], sems.at[3 + side]),
            pltpu.make_async_copy(f.at[:, :, part], forces.at[side], sems.at[5 + side]),
        ]
    for copy in copies:
        copy.start()
    for copy in copies[:2] + copies[4:5]:
        copy.wait()
    near_eta, far_eta = 2 * components, 2 * components + 1
    for side, near, far in ((0, 0, 1), (1, TILE - 1, TILE - 2)):
        for s in range(shells):
            eta = half_viscosity(layers[side, s], viscosity)
            rows_of[near_eta, side * shells + s] = eta[near]
            rows_of[far_eta, side * shells + s] = eta[far]
    for copy in copies[2:4] + copies[5:]:
        copy.wait()
    for side, near, far in ((0, 0, 1), (1, TILE - 1, TILE - 2)):
        for s in range(shells):
            for c in range(components):
                rows_of[c, side * shells + s] = fields[side, c, s, near]
                rows_of[components + c, side * shells + s] = fields[side, c, s, far]
                rows_of[far_eta + 1 + c, side * shells + s] = forces[side, c, s, near]
    radial = lax.axis_index("radial")
    place = row_number((2 * shells, count)) % shells
    highest, lowest = place == shells - 1, place == 0
    zero = jnp.zeros((2 * shells, count), jnp.float32)

    def beside(near, far):
        middle = rows_of[near]
        return middle, [
            jnp.where(highest, zero, pltpu.roll(middle, 2 * shells - 1, 0)),
            jnp.where(lowest, zero, pltpu.roll(middle, 1, 0)),
            rows_of[far],
            west_of(middle),
            east_of(middle),
        ]

    eta, others = beside(near_eta, far_eta)
    weights = [eta + other for other in others]
    inside = (radial < lax.axis_size("radial") - 1, radial > 0)
    weights[0] = jnp.where(jnp.logical_and(highest, inside[0]), zero, weights[0])
    weights[1] = jnp.where(jnp.logical_and(lowest, inside[1]), zero, weights[1])
    diagonal = 1.0 + functools.reduce(jnp.add, weights)
    values, sums = [], []
    for c in range(components):
        middle, others = beside(c, components + c)
        total = rows_of[far_eta + 1 + c]
        for weight, other in zip(weights, others):
            total = total + weight * other
        values.append(middle)
        sums.append(total)
    for place, field in enumerate(values + [eta] + sums + [diagonal]):
        both = jnp.where(odd_band(), field, pltpu.roll(field, shells, 0))
        one[pl.ds(place * shells, shells)] = both[:shells]
        two[pl.ds(place * shells, shells)] = both[shells:]


def viscosity_kernel(viscosity_from, d, index_from, token, eta, ring, h, index, viscosity, sems, eta_sems):
    del token
    shells, rows, _ = h.shape
    components = d.shape[0]
    shell = jnp.where(lax.axis_index("radial") == 0, shells - 1, 0)
    copies = [
        pltpu.make_async_copy(viscosity_from, viscosity, sems.at[shells]),
        pltpu.make_async_copy(d.at[:, shell], ring.at[pl.ds(0, components)], sems.at[shells + 1]),
    ]
    layers = [pltpu.make_async_copy(index_from.at[s], index.at[s], sems.at[s]) for s in range(shells)]
    for copy in copies[:1] + layers + copies[1:]:
        copy.start()
    copies[0].wait()
    stores = []
    for s in range(shells):
        layers[s].wait()

        def lookup(step, _):
            part = pl.ds(pl.multiple_of(step * TILE, TILE), TILE)
            h[s, part] = half_viscosity(index[s, part], viscosity)
            return 0

        lax.fori_loop(0, rows // TILE, lookup, 0)
        stores.append(pltpu.make_async_copy(h.at[s], eta.at[s], eta_sems.at[s]))
        stores[-1].start()
    stores.append(pltpu.make_async_copy(h.at[shell], ring.at[components], eta_sems.at[shells]))
    stores[-1].start()
    for copy in copies[1:] + stores:
        copy.wait()


def surface_kernel(d, f, h, one, two, high_from, low_from, out, field, force, eta, smoothed, high, low, sems):
    shells, rows, count = h.shape
    top = lax.axis_size("radial") - 1

    @pl.when(lax.axis_index("radial") == top)
    def _():
        block = pl.ds(TILE, rows)
        copies = [
            pltpu.make_async_copy(d.at[0, pl.ds(shells - 3, 3)], field.at[pl.ds(0, 3), block], sems.at[0]),
            pltpu.make_async_copy(h.at[pl.ds(shells - 3, 3)], eta.at[pl.ds(0, 3), block], sems.at[1]),
            pltpu.make_async_copy(f.at[0, pl.ds(shells - 2, 2)], force, sems.at[2]),
        ]
        tables = [
            pltpu.make_async_copy(high_from, high, sems.at[3]),
            pltpu.make_async_copy(low_from, low, sems.at[4]),
        ]
        for copy in copies + tables:
            copy.start()
        zeros = jnp.zeros((rows, count), jnp.float32)
        field[3, block] = zeros
        eta[3, block] = zeros
        smoothed[2, block] = zeros
        components = d.shape[0]
        before, after = by_parity(one, two)
        inner, weight, partial, diagonal = [
            k * shells for k in (0, components, components + 1, 2 * components + 1)
        ]
        for message, place in ((before, TILE - 1), (after, rows + TILE)):
            for k in (1, 2):
                field[k, place] = message[inner + shells - 3 + k]
                eta[k, place] = message[weight + shells - 3 + k]
        for copy in copies:
            copy.wait()
        lateral = lax.axis_index("lateral")
        inside = (lateral > 0, lateral < lax.axis_size("lateral") - 1)
        for message, own, place, there in (
            (before, TILE, TILE - 1, inside[0]),
            (after, rows + TILE - 1, rows + TILE, inside[1]),
        ):
            row = lambda start: message[start + shells - 1 : start + shells]
            last = row(weight) + eta[2, pl.ds(own, 1)]
            total = row(partial) + last * field[2, pl.ds(own, 1)]
            edge = (1.0 - RELAXATION) * row(inner) + RELAXATION / (row(diagonal) + last) * total
            smoothed[1, pl.ds(place, 1)] = jnp.where(there, edge, jnp.zeros_like(edge))

        def first(step, _):
            start = pl.multiple_of(step * TILE, TILE)
            for s in (1, 2):
                weights, factor = relax_weights(*around(eta, (), s, start + TILE))
                middle, others = around(field, (), s, start + TILE)
                smoothed[s - 1, pl.ds(start + TILE, TILE)] = relax(
                    weights, factor, middle, others, force[s - 1, pl.ds(start, TILE)]
                )
            return 0

        lax.fori_loop(0, rows // TILE, first, 0)

        def second(step, _):
            start = pl.multiple_of(step * TILE, TILE)
            weights, factor = relax_weights(*around(eta, (), 2, start + TILE))
            middle, others = around(smoothed, (), 1, start + TILE)
            field[0, pl.ds(start, TILE)] = relax(weights, factor, middle, others, force[1, pl.ds(start, TILE)])
            return 0

        lax.fori_loop(0, rows // TILE, second, 0)
        near, far = split(jnp.concatenate(fold(field[0, pl.ds(0, rows), :]), axis=0))
        for copy in tables:
            copy.wait()
        total = dot(near, high[...]) + dot(far, high[...]) + dot(near, low[...])
        blocks = [total[k * rows : (k + 1) * rows] for k in range(RADIX)]
        kind, mirrored = order_class((1, total.shape[1]))
        cosine, sine = blocks[0], jnp.zeros_like(blocks[0])
        for k in range(1, RADIX // 2 + 1):
            cosine = jnp.where(kind == k, blocks[k], cosine)
        for k in range(1, RADIX // 2):
            sine = jnp.where(kind == k, blocks[RADIX // 2 + k], sine)
        sine = jnp.where(mirrored, -sine, sine)
        modes = total.shape[1] // 2
        fourier = jnp.concatenate(
            [cosine[:, :modes] - sine[:, modes:], cosine[:, modes:] + sine[:, :modes]], axis=1
        )
        blocks = out.shape[0]
        width = fourier.shape[1] // blocks
        for block in range(blocks):
            out[block] = pack(fourier[:, block * width : (block + 1) * width])


def sweep_shells(d, f, h, ring_field, ring_eta, out, field, eta, force, result, sems, before_first, after_shell):
    components, shells, rows, count = d.shape
    inner = pl.ds(TILE, rows)
    lower = lax.axis_index("radial") == 0
    shell = lambda k: jnp.where(lower, k, shells - 1 - k)
    ring, nothing = jnp.where(lower, shells + 1, 0), jnp.where(lower, 0, shells + 1)

    def field_loads(k):
        if k == shells:
            return [
                pltpu.make_async_copy(ring_eta, eta.at[ring, inner], sems.at[k, components]),
                *(
                    pltpu.make_async_copy(source, field.at[c, ring, inner], sems.at[k, c])
                    for c, source in enumerate(ring_field)
                ),
            ]
        s = shell(k)
        return [
            pltpu.make_async_copy(d.at[:, s], field.at[:, s + 1, inner], sems.at[k, 0]),
            pltpu.make_async_copy(h.at[s], eta.at[s + 1, inner], sems.at[k, 1]),
        ]

    def force_load(k):
        return [pltpu.make_async_copy(f.at[:, shell(k)], force.at[:, shell(k)], sems.at[k, 2])]

    loads = [start_all(field_loads(0)), start_all(field_loads(1))]
    forces = [start_all(force_load(0))]
    loads.append(start_all(field_loads(2)))
    forces.append(start_all(force_load(1)))
    zeros = jnp.zeros((rows, count), jnp.float32)
    for c in range(components):
        field[c, nothing, inner] = zeros
    eta[nothing, inner] = zeros
    before_first()
    for copy in loads[0]:
        copy.wait()
    stores = []
    for k in range(shells):
        s = shell(k)
        if k + 3 <= shells:
            loads.append(start_all(field_loads(k + 3)))
        if k + 2 < shells:
            forces.append(start_all(force_load(k + 2)))
        for copy in loads[k + 1] + forces[k]:
            copy.wait()

        def tile(step, _):
            first = pl.multiple_of(step * TILE, TILE)
            weights, factor = relax_weights(*around(eta, (), s + 1, first + TILE))
            for c in range(components):
                middle, others = around(field, (c,), s + 1, first + TILE)
                result[c, s, pl.ds(first, TILE)] = relax(
                    weights, factor, middle, others, force[c, s, pl.ds(first, TILE)]
                )
            return 0

        lax.fori_loop(0, rows // TILE, tile, 0)
        stores += start_all([pltpu.make_async_copy(result.at[:, s], out.at[:, s], sems.at[k, 3])])
        after_shell(s, k)
    for copy in stores:
        copy.wait()


def set_edge(ref, lead, shells, rows, before, after):
    for s in range(shells):
        ref[(*lead, s + 1, TILE - 1)] = before(s)
        ref[(*lead, s + 1, rows + TILE)] = after(s)


def start_all(copies):
    for copy in copies:
        copy.start()
    return copies


def load_messages(sources, lower_sources, slots, sems):
    lower = lax.axis_index("radial") < lax.axis_size("radial") - 1
    part = pl.ds(0, slots.shape[1])
    copies = lambda refs: [pltpu.make_async_copy(ref.at[part], slots.at[k], sems.at[k]) for k, ref in enumerate(refs)]
    pl.when(lower)(lambda: [copy.start() for copy in copies(lower_sources)] and None)
    pl.when(jnp.logical_not(lower))(lambda: [copy.start() for copy in copies(sources)] and None)
    return copies(sources)


def first_kernel(d, f, h, ring, one, two, lower_one, lower_two, *refs):
    components, shells, rows, _ = d.shape
    staged = (len(refs) - 12) // 2
    sources, refs = refs[:staged], refs[staged:]
    out, ring_out, own_out, *targets = refs[: 3 + staged]
    field, eta, force, result, messages, edges, own, sems, more_sems = refs[3 + staged :]
    arrivals = load_messages((one, two), (lower_one, lower_two), messages, more_sems)
    lower = lax.axis_index("radial") == 0
    copies = []

    def before_first():
        for copy in arrivals:
            copy.wait()
        before, after = by_parity(messages.at[0], messages.at[1])
        row = lambda message, kind: lambda s: message[kind * shells + s]
        for c in range(components):
            set_edge(field, (c,), shells, rows, row(before, c), row(after, c))
        set_edge(eta, (), shells, rows, row(before, components), row(after, components))
        for side, message in enumerate((before, after)):
            for k in range(components + 1):
                edges[side * (components + 1) + k] = jnp.where(
                    lower, message[(k + 1) * shells - 1], message[k * shells]
                )
        tail = ring_out.at[pl.ds(components * rows, edges.shape[0])]
        copies.extend(start_all([pltpu.make_async_copy(edges, tail, more_sems.at[2])]))

    def after_shell(s, k):
        if k == 0:
            stages = [
                pltpu.make_async_copy(source, target, more_sems.at[4 + components + n])
                for n, (source, target) in enumerate(zip(sources, targets))
            ]
            copies.extend(start_all(stages))
        for side, place in enumerate((TILE, TILE + rows - 1)):
            for c in range(components):
                own[c, side * shells + s] = field[c, s + 1, place]
            own[components, side * shells + s] = eta[s + 1, place]
        if k == shells - 1:
            copies.extend(start_all([pltpu.make_async_copy(own, own_out, more_sems.at[3])]))
            copies.extend(
                start_all(
                    [
                        pltpu.make_async_copy(
                            result.at[c, s], ring_out.at[pl.ds(c * rows, rows)], more_sems.at[4 + c]
                        )
                        for c in range(components)
                    ]
                )
            )

    sweep_shells(
        d, f, h, [ring.at[c] for c in range(components)], ring.at[components],
        out, field, eta, force, result, sems, before_first, after_shell,
    )
    for copy in copies:
        copy.wait()


def second_kernel(d, f, h, ring, ring_two, one, two, lower_one, lower_two, own_from, *refs):
    components, shells, rows, count = d.shape
    staged = (len(refs) - 11) // 2
    sources, refs = refs[:staged], refs[staged:]
    out, token, *targets = refs[: 2 + staged]
    field, eta, force, result, messages, edges, own, sems, more_sems = refs[2 + staged :]
    token[...] = jnp.zeros_like(token)
    arrivals = load_messages((one, two), (lower_one, lower_two), messages, more_sems)
    tail = ring_two.at[pl.ds(components * rows, edges.shape[0])]
    arrivals += start_all(
        [
            pltpu.make_async_copy(tail, edges, more_sems.at[2]),
            pltpu.make_async_copy(own_from, own, more_sems.at[3]),
        ]
    )
    radial, lateral = lax.axis_index("radial"), lax.axis_index("lateral")
    copies = []

    def before_first():
        for copy in arrivals:
            copy.wait()
        before, after = by_parity(messages.at[0], messages.at[1])
        pair = lambda k: jnp.concatenate(
            [before[k * shells : (k + 1) * shells], after[k * shells : (k + 1) * shells]], axis=0
        )
        place = row_number((2 * shells, count))
        zero = jnp.zeros((2 * shells, count), jnp.float32)
        shared = place % shells == jnp.where(radial == 0, shells - 1, 0)
        beyond = lambda k: jnp.where(
            place < shells, edges[pl.ds(k, 1)], edges[pl.ds(components + 1 + k, 1)]
        )
        inside = jnp.where(place < shells, lateral, lax.axis_size("lateral") - 1 - lateral) > 0
        middle = pair(components)
        weight = middle + own[components]
        across = jnp.where(shared, middle + beyond(components), zero)
        factor = RELAXATION / (pair(2 * components + 1) + weight + across)
        for c in range(components):
            total = pair(components + 1 + c) + weight * own[c] + across * beyond(c)
            edge = jnp.where(inside, (1.0 - RELAXATION) * pair(c) + factor * total, zero)
            set_edge(field, (c,), shells, rows, lambda s: edge[s], lambda s: edge[shells + s])
        set_edge(eta, (), shells, rows, lambda s: middle[s], lambda s: middle[shells + s])

    def after_shell(s, k):
        if k == 0:
            stages = [
                pltpu.make_async_copy(source, target, more_sems.at[4 + n])
                for n, (source, target) in enumerate(zip(sources, targets))
            ]
            copies.extend(start_all(stages))

    sweep_shells(
        d, f, h, [ring_two.at[pl.ds(c * rows, rows)] for c in range(components)], ring.at[components],
        out, field, eta, force, result, sems, before_first, after_shell,
    )
    for copy in copies:
        copy.wait()


def spectrum_kernel(orders, wave_high, wave_low, point_high, point_low, response, coefficients, out):
    radial = lax.axis_size("radial")
    width = coefficients.shape[0]
    bands, rows = orders.shape[0] // radial, point_high.shape[0] * radial // orders.shape[0]
    fourier = jnp.concatenate([unpack(orders[band * radial + radial - 1], width) for band in range(bands)], axis=0)
    high, low = split(fourier)
    spectrum = dot(wave_high[...], high) + dot(wave_high[...], low) + dot(wave_low[...], high)
    coefficients[...] = spectrum.T
    own = response[:, :width]
    for place in range(1, radial):
        own = jnp.where(
            lax.axis_index("radial") == place, response[:, place * width : (place + 1) * width], own
        )
    high, low = split(own * spectrum)
    load = dot(point_high[...], high) + dot(point_high[...], low) + dot(point_low[...], high)
    for band in range(bands):
        block = pack(load[band * rows : (band + 1) * rows])
        for place in range(radial):
            out[band * radial + place] = block


def load_kernel(load, high, low, mask, out):
    blocks, rows = load.shape[0], out.shape[0]
    step, width = out.shape[1] // RADIX, high.shape[1] // blocks
    values = jnp.concatenate([unpack(load[block], width) for block in range(blocks)], axis=1)
    modes = values.shape[1] // 2
    kind, mirrored = order_class((1, values.shape[1]))
    crossed = jnp.concatenate([values[:, modes:], -values[:, :modes]], axis=1)
    crossed = jnp.where(mirrored, -crossed, crossed)
    zero = jnp.zeros_like(values)
    stack = [jnp.where(kind == k, values, zero) for k in range(RADIX // 2 + 1)]
    stack += [jnp.where(kind == k, crossed, zero) for k in range(1, RADIX // 2)]
    near, far = split(jnp.concatenate(stack, axis=0))
    total = dot_nt(near, high[...]) + dot_nt(far, high[...]) + dot_nt(near, low[...])
    for m, part in enumerate(unfold([total[k * rows : (k + 1) * rows] for k in range(RADIX)])):
        columns = slice(m * step, (m + 1) * step)
        out[:, columns] = part * mask[:, columns].astype(jnp.float32)


def cost(microseconds):
    return pl.CostEstimate(flops=0, bytes_accessed=3_000_000 * microseconds, transcendentals=0)


def hbm(values):
    return pltpu.with_memory_space_constraint(values, pltpu.HBM)


def shards(initial_displacement, force, viscosity, layer_index, response, ocean_mask):
    components, shells, rows, count = initial_displacement.shape
    radial, lateral = lax.axis_size("radial"), lax.axis_size("lateral")
    f32 = functools.partial(jax.ShapeDtypeStruct, dtype=jnp.float32)
    scratch = lambda *shape: pltpu.VMEM(shape, jnp.float32)
    in_hbm = lambda *shape: pltpu.HBM(shape, jnp.float32)
    width = 2 * MODES // (lateral * radial)
    first = [p for i in range(0, lateral - 1, 2) for p in ((i, i + 1), (i + 1, i))]
    second = [p for i in range(1, lateral - 1, 2) for p in ((i, i + 1), (i + 1, i))]
    both = ("lateral", "radial")
    top_only = lambda pairs: [(i * radial + radial - 1, j * radial + radial - 1) for i, j in pairs]

    lower_only = lambda pairs: [(i * radial + k, j * radial + k) for i, j in pairs for k in range(radial - 1)]
    tensors = [hbm(a) for a in (initial_displacement, force, layer_index)]
    viscosity = hbm(viscosity)
    message = f32((2 * (components + 1) * shells, count))
    sides = lambda *shape: scratch(2, *shape)
    mine = pl.pallas_call(
        message_kernel,
        in_specs=[HBM] * 4,
        out_specs=[VMEM] * 2,
        out_shape=[message] * 2,
        scratch_shapes=[
            sides(components, shells, TILE, count),
            sides(components, shells, TILE, count),
            pltpu.VMEM((2, shells, TILE, count), jnp.int32),
            scratch(3 * components + 2, 2 * shells, count),
            pltpu.SMEM(viscosity.shape, jnp.float32),
            pltpu.SemaphoreType.DMA((7,)),
        ],
        compiler_params=params(16),
        cost_estimate=cost(20),
    )(viscosity, *tensors)
    two = lax.ppermute(mine[1], both, top_only(second))
    one = lax.ppermute(mine[0], both, top_only(first))
    eta, ring = pl.pallas_call(
        viscosity_kernel,
        in_specs=[HBM, HBM, HBM, ANY],
        out_specs=[HBM, VMEM],
        out_shape=[in_hbm(shells, rows, count), f32((components + 1, rows, count))],
        scratch_shapes=[
            scratch(shells, rows, count),
            pltpu.VMEM(layer_index.shape, jnp.int32),
            pltpu.SMEM(viscosity.shape, jnp.float32),
            pltpu.SemaphoreType.DMA((2 + shells,)),
            pltpu.SemaphoreType.DMA((1 + shells,)),
        ],
        compiler_params=params(12),
        cost_estimate=cost(20),
    )(viscosity, tensors[0], tensors[2], mine[0])
    ring, lower_one, lower_two, one, two = lax.optimization_barrier((ring, *mine, one, two))
    swap = [(i, radial - 1 - i) for i in range(radial)]
    ring = lax.ppermute(ring, "radial", swap)
    lower_one = lax.ppermute(lower_one, both, lower_only(first))
    lower_two = lax.ppermute(lower_two, both, lower_only(second))

    high, low = longitude_tables(count, MODES)
    high, low = hbm(jnp.asarray(high)), hbm(jnp.asarray(low))
    table = pltpu.VMEM(high.shape, jnp.bfloat16)
    packed = (lateral * radial, rows * width // max(128, width), max(128, width))
    orders = pl.pallas_call(
        surface_kernel,
        in_specs=[HBM, HBM, HBM, VMEM, VMEM, HBM, HBM],
        out_specs=VMEM,
        out_shape=f32(packed),
        scratch_shapes=[
            scratch(4, rows + 2 * TILE, count),
            scratch(2, rows, count),
            scratch(4, rows + 2 * TILE, count),
            scratch(3, rows + 2 * TILE, count),
            table,
            table,
            pltpu.SemaphoreType.DMA((5,)),
        ],
        compiler_params=params(24),
        cost_estimate=cost(200),
    )(*tensors[:2], hbm(eta), one, two, high, low)
    orders, ring, lower_one, lower_two = lax.optimization_barrier((orders, ring, lower_one, lower_two))
    messages = [hbm(a) for a in (one, two, lower_one, lower_two)]
    ring, eta = hbm(ring), hbm(eta)
    orders = lax.all_to_all(orders, both, split_axis=0, concat_axis=0, tiled=True)

    sweep_scratch = [
        scratch(components, shells + 2, rows + 2 * TILE, count),
        scratch(shells + 2, rows + 2 * TILE, count),
        scratch(components, shells, rows, count),
        scratch(components, shells, rows, count),
    ]
    sweep_sems = pltpu.SemaphoreType.DMA((shells + 1, components + 1))
    point_high, point_low = colatitude_tables(rows * lateral, MODES)
    stages = [
        jnp.asarray(a)
        for a in (point_high.T.copy(), point_low.T.copy(), point_high, point_low)
    ] + [response]
    ring_rows = components * rows + 2 * (components + 1)
    own_rows = scratch(components + 1, 2 * shells, count)
    smoothed, ring_two, own, *staged = pl.pallas_call(
        first_kernel,
        in_specs=[HBM] * (8 + len(stages)),
        out_specs=[HBM] * 3 + [VMEM] * len(stages),
        out_shape=[
            in_hbm(*initial_displacement.shape),
            in_hbm(ring_rows, count),
            in_hbm(components + 1, 2 * shells, count),
            *(jax.ShapeDtypeStruct(a.shape, a.dtype) for a in stages),
        ],
        scratch_shapes=[
            *sweep_scratch,
            sides((components + 1) * shells, count),
            scratch(2 * (components + 1), count),
            own_rows,
            sweep_sems,
            pltpu.SemaphoreType.DMA((4 + components + len(stages),)),
        ],
        compiler_params=params(28),
        cost_estimate=cost(50),
    )(*tensors[:2], eta, ring, *messages, *(hbm(a) for a in stages))
    ring_two, orders = lax.optimization_barrier((ring_two, orders))
    ring_two = lax.ppermute(ring_two, "radial", swap)
    coefficients, load = pl.pallas_call(
        spectrum_kernel,
        in_specs=[VMEM] * 6,
        out_specs=[VMEM, VMEM],
        out_shape=[f32((width, MODES)), f32(packed)],
        compiler_params=params(16),
        cost_estimate=cost(200),
    )(orders, *staged)
    load, ring_two = lax.optimization_barrier((load, ring_two))
    eta, load = lax.optimization_barrier((eta, load))
    load = lax.all_to_all(load, both, split_axis=0, concat_axis=0, tiled=True)

    stages = [high, low, hbm(ocean_mask)]
    displacement, token, *staged = pl.pallas_call(
        second_kernel,
        in_specs=[HBM] * (10 + len(stages)),
        out_specs=[HBM, VMEM] + [VMEM] * len(stages),
        out_shape=[
            in_hbm(*initial_displacement.shape),
            f32((TILE, 128)),
            *(jax.ShapeDtypeStruct(a.shape, a.dtype) for a in stages),
        ],
        scratch_shapes=[
            *sweep_scratch,
            sides(message.shape[0], count),
            scratch(2 * (components + 1), count),
            own_rows,
            sweep_sems,
            pltpu.SemaphoreType.DMA((4 + len(stages),)),
        ],
        compiler_params=params(28),
        cost_estimate=cost(50),
    )(hbm(smoothed), tensors[1], hbm(eta), ring, hbm(ring_two), *messages, hbm(own), *stages)

    sea_load = pl.pallas_call(
        load_kernel,
        in_specs=[VMEM] * 4,
        out_specs=VMEM,
        out_shape=f32((rows, count)),
        compiler_params=params(20),
        cost_estimate=cost(3),
    )(load, *staged)
    return (displacement, coefficients.T, sea_load)


def solution(mesh):
    in_specs = (
        P("member", "radial", "lateral", None),
        P("member", "radial", "lateral", None),
        P("member"),
        P("radial", "lateral", None),
        P(None, "lateral"),
        P("lateral", None),
    )
    out_specs = (
        P("member", "radial", "lateral", None),
        P("member", ("lateral", "radial")),
        P("lateral", "member"),
    )
    return jax.shard_map(shards, mesh=mesh, in_specs=in_specs, out_specs=out_specs, check_vma=False)
```

```python
import functools
import math

import jax
import jax.numpy as jnp
import ml_dtypes
import numpy as np
from jax import lax
from jax.experimental import pallas as pl
from jax.experimental.pallas import tpu as pltpu
from jax.sharding import PartitionSpec as P

MODES = 512
RELAXATION = 0.8
TILE = 8
RADIX = 8
MIB = 1 << 20
ANY = pl.BlockSpec(memory_space=pl.ANY)
HBM = pl.BlockSpec(memory_space=pltpu.HBM)
SMEM = pl.BlockSpec(memory_space=pltpu.SMEM)
VMEM = pl.BlockSpec(memory_space=pltpu.VMEM)


def params(mib):
    return pltpu.CompilerParams(vmem_limit_bytes=mib * MIB)


def halves(table):
    high = table.astype(ml_dtypes.bfloat16)
    low = (table - high.astype(np.float64)).astype(ml_dtypes.bfloat16)
    return high, low


@functools.lru_cache
def longitude_tables(count, modes):
    points = np.arange(count // RADIX, dtype=np.int64)[:, None]
    orders = np.arange(modes, dtype=np.int64)[None, :]
    angle = (2.0 * math.pi / count) * (points * orders % count)
    table = np.concatenate([np.cos(angle), np.sin(angle)], axis=1) * math.sqrt(2.0 / count)
    return halves(table)


@functools.lru_cache
def colatitude_tables(count, modes):
    points = np.arange(count, dtype=np.int64)[:, None]
    waves = np.arange(modes, dtype=np.int64)[None, :]
    phase = waves * (2 * points + 1) % (4 * count)
    return halves(np.cos(math.pi / (2 * count) * phase) * math.sqrt(2.0 / count))


def split(values):
    high = values.astype(jnp.bfloat16)
    return high, (values - high.astype(jnp.float32)).astype(jnp.bfloat16)


def dot(a, b):
    return jnp.dot(a, b, preferred_element_type=jnp.float32)


def pack(block):
    rows, width = block.shape
    groups = max(1, 128 // width)
    rows //= groups
    return jnp.concatenate([block[k * rows : (k + 1) * rows] for k in range(groups)], axis=1)


def unpack(block, width):
    groups = max(1, 128 // width)
    return jnp.concatenate([block[:, k * width : (k + 1) * width] for k in range(groups)], axis=0)


def weighted_sum(terms):
    total = None
    for factor, values in terms:
        factor = round(factor, 15)
        if factor == 0.0:
            continue
        part = values if abs(factor) == 1.0 else abs(factor) * values
        if total is None:
            total = part if factor > 0 else -part
        else:
            total = total + part if factor > 0 else total - part
    return total


def turn(number):
    angle = 2.0 * math.pi * (number % RADIX) / RADIX
    return math.cos(angle), math.sin(angle)


def fold(values):
    step = values.shape[1] // RADIX
    parts = [values[:, m * step : (m + 1) * step] for m in range(RADIX)]
    cosines = [[(turn(k * m)[0], part) for m, part in enumerate(parts)] for k in range(RADIX // 2 + 1)]
    sines = [[(turn(k * m)[1], part) for m, part in enumerate(parts)] for k in range(1, RADIX // 2)]
    return [weighted_sum(terms) for terms in cosines + sines]


def unfold(blocks):
    cosines, sines = blocks[: RADIX // 2 + 1], blocks[RADIX // 2 + 1 :]
    return [
        weighted_sum(
            [(turn(k * m)[0], block) for k, block in enumerate(cosines)]
            + [(turn(k * m)[1], block) for k, block in enumerate(sines, 1)]
        )
        for m in range(RADIX)
    ]


def order_class(shape):
    order = lax.broadcasted_iota(jnp.int32, shape, len(shape) - 1) % RADIX
    mirrored = order > RADIX // 2
    return jnp.where(mirrored, RADIX - order, order), mirrored


def dot_nt(a, b):
    return lax.dot_general(a, b, (((1,), (1,)), ((), ())), preferred_element_type=jnp.float32)


def half_viscosity(index, viscosity_ref):
    values = [0.5 * viscosity_ref[k] for k in range(viscosity_ref.shape[0])]
    bit = 1
    while len(values) > 1:
        odd = (index & bit) != 0
        if len(values) % 2:
            values.append(values[-1])
        values = [jnp.where(odd, b, a) for a, b in zip(values[::2], values[1::2])]
        bit *= 2
    return values[0]


def row_number(shape):
    return lax.broadcasted_iota(jnp.int32, shape, 0)


def north_of(above, middle):
    return pltpu.roll(jnp.where(row_number(middle.shape) == TILE - 1, above, middle), 1, 0)


def south_of(below, middle):
    return pltpu.roll(jnp.where(row_number(middle.shape) == 0, below, middle), TILE - 1, 0)


def east_of(values):
    return pltpu.roll(values, values.shape[-1] - 1, values.ndim - 1)


def west_of(values):
    return pltpu.roll(values, 1, values.ndim - 1)


def relax_weights(middle, others):
    weights = [middle + other for other in others]
    diagonal = 1.0 + functools.reduce(jnp.add, weights)
    return weights, RELAXATION / diagonal


def relax(weights, factor, middle, others, force):
    total = force
    for weight, other in zip(weights, others):
        total = total + weight * other
    return (1.0 - RELAXATION) * middle + factor * total


def around(ref, lead, shell, start):
    rows = lambda first: pl.ds(pl.multiple_of(first, TILE), TILE)
    middle = ref[(*lead, shell, rows(start))]
    return middle, [
        ref[(*lead, shell + 1, rows(start))],
        ref[(*lead, shell - 1, rows(start))],
        south_of(ref[(*lead, shell, rows(start + TILE))], middle),
        north_of(ref[(*lead, shell, rows(start - TILE))], middle),
        west_of(middle),
        east_of(middle),
    ]


def odd_band():
    return lax.axis_index("lateral") % 2 == 1


def by_parity(one, two):
    one, two = one[...], two[...]
    return jnp.where(odd_band(), one, two), jnp.where(odd_band(), two, one)


def message_kernel(viscosity_from, d, f, index, one, two, fields, forces, layers, rows_of, viscosity, sems):
    components, shells, rows, count = d.shape
    copies = [pltpu.make_async_copy(viscosity_from, viscosity, sems.at[0])]
    for side, start in enumerate((0, rows - TILE)):
        part = pl.ds(start, TILE)
        copies += [
            pltpu.make_async_copy(index.at[:, part], layers.at[side], sems.at[1 + side]),
            pltpu.make_async_copy(d.at[:, :, part], fields.at[side], sems.at[3 + side]),
            pltpu.make_async_copy(f.at[:, :, part], forces.at[side], sems.at[5 + side]),
        ]
    for copy in copies:
        copy.start()
    for copy in copies[:2] + copies[4:5]:
        copy.wait()
    near_eta, far_eta = 2 * components, 2 * components + 1
    for side, near, far in ((0, 0, 1), (1, TILE - 1, TILE - 2)):
        for s in range(shells):
            eta = half_viscosity(layers[side, s], viscosity)
            rows_of[near_eta, side * shells + s] = eta[near]
            rows_of[far_eta, side * shells + s] = eta[far]
    for copy in copies[2:4] + copies[5:]:
        copy.wait()
    for side, near, far in ((0, 0, 1), (1, TILE - 1, TILE - 2)):
        for s in range(shells):
            for c in range(components):
                rows_of[c, side * shells + s] = fields[side, c, s, near]
                rows_of[components + c, side * shells + s] = fields[side, c, s, far]
                rows_of[far_eta + 1 + c, side * shells + s] = forces[side, c, s, near]
    radial = lax.axis_index("radial")
    place = row_number((2 * shells, count)) % shells
    highest, lowest = place == shells - 1, place == 0
    zero = jnp.zeros((2 * shells, count), jnp.float32)

    def beside(near, far):
        middle = rows_of[near]
        return middle, [
            jnp.where(highest, zero, pltpu.roll(middle, 2 * shells - 1, 0)),
            jnp.where(lowest, zero, pltpu.roll(middle, 1, 0)),
            rows_of[far],
            west_of(middle),
            east_of(middle),
        ]

    eta, others = beside(near_eta, far_eta)
    weights = [eta + other for other in others]
    inside = (radial < lax.axis_size("radial") - 1, radial > 0)
    weights[0] = jnp.where(jnp.logical_and(highest, inside[0]), zero, weights[0])
    weights[1] = jnp.where(jnp.logical_and(lowest, inside[1]), zero, weights[1])
    diagonal = 1.0 + functools.reduce(jnp.add, weights)
    values, sums = [], []
    for c in range(components):
        middle, others = beside(c, components + c)
        total = rows_of[far_eta + 1 + c]
        for weight, other in zip(weights, others):
            total = total + weight * other
        values.append(middle)
        sums.append(total)
    for place, field in enumerate(values + [eta] + sums + [diagonal]):
        both = jnp.where(odd_band(), field, pltpu.roll(field, shells, 0))
        one[pl.ds(place * shells, shells)] = both[:shells]
        two[pl.ds(place * shells, shells)] = both[shells:]


def viscosity_kernel(
    viscosity_from, d, f, index_from, token, eta_out, surface_swept, surface_eta, surface_force,
    index, eta, field, force, viscosity, sems, eta_sems,
):
    del token
    _, shells, rows, count = d.shape
    block = pl.ds(TILE, rows)
    value_copy = pltpu.make_async_copy(viscosity_from, viscosity, sems.at[shells])
    layers = [pltpu.make_async_copy(index_from.at[s], index.at[s], sems.at[s]) for s in range(shells)]
    surface_copies = [
        pltpu.make_async_copy(d.at[0, pl.ds(shells - 3, 3)], field.at[pl.ds(0, 3), block], sems.at[shells + 1]),
        pltpu.make_async_copy(f.at[0, pl.ds(shells - 2, 2)], force, sems.at[shells + 2]),
    ]
    start_all([value_copy, *layers, *surface_copies])
    zeros = jnp.zeros((rows, count), jnp.float32)
    field[3, block] = zeros
    eta[shells, block] = zeros
    value_copy.wait()
    stores = []
    for s in range(shells):
        layers[s].wait()

        def lookup(step, _):
            start = pl.multiple_of(step * TILE, TILE)
            eta[s, pl.ds(start + TILE, TILE)] = half_viscosity(index[s, pl.ds(start, TILE)], viscosity)
            return 0

        lax.fori_loop(0, rows // TILE, lookup, 0)
        stores += start_all([pltpu.make_async_copy(eta.at[s, block], eta_out.at[s], eta_sems.at[s])])
    for copy in surface_copies:
        copy.wait()

    def sweep(step, _):
        start = pl.multiple_of(step * TILE, TILE)
        part = pl.ds(start, TILE)
        for k in range(2):
            weights, factor = relax_weights(*around(eta, (), shells - 2 + k, start + TILE))
            middle, others = around(field, (), k + 1, start + TILE)
            surface_swept[k, part] = relax(weights, factor, middle, others, force[k, part])
            surface_eta[k, part] = eta[shells - 2 + k, pl.ds(start + TILE, TILE)]
        surface_force[part] = force[1, part]
        return 0

    lax.fori_loop(0, rows // TILE, sweep, 0)
    for copy in stores:
        copy.wait()


def surface_kernel(
    surface_swept, surface_eta, force, own_one, own_two, one, two, high_from, low_from, out,
    swept, eta, surface, high, low, sems, components,
):
    rows, count = force.shape

    @pl.when(lax.axis_index("radial") == lax.axis_size("radial") - 1)
    def _():
        tables = start_all(
            [
                pltpu.make_async_copy(high_from, high, sems.at[0]),
                pltpu.make_async_copy(low_from, low, sems.at[1]),
            ]
        )
        block = pl.ds(TILE, rows)
        for k in range(2):
            swept[k, block] = surface_swept[k]
            eta[k, block] = surface_eta[k]
        swept[2, block] = jnp.zeros((rows, count), jnp.float32)
        eta[2, block] = jnp.zeros((rows, count), jnp.float32)
        fields = one.shape[0]
        shells = fields // (2 * (components + 1))
        lateral = lax.axis_index("lateral")
        inside = (lateral > 0, lateral < lax.axis_size("lateral") - 1)
        for beside, own, place, own_place, there in zip(
            by_parity(one, two), by_parity(own_one, own_two), (TILE - 1, rows + TILE), (TILE, rows + TILE - 1), inside
        ):
            for k in range(2):
                row = lambda message, kind: message[kind * shells + shells - 2 + k : kind * shells + shells - 1 + k]
                weight = row(beside, components) + row(own, components)

                def finish(message, other):
                    total = row(message, components + 1) + weight * row(other, 0)
                    factor = RELAXATION / (row(message, 2 * components + 1) + weight)
                    return (1.0 - RELAXATION) * row(message, 0) + factor * total

                swept[k, pl.ds(own_place, 1)] = finish(own, beside)
                if k == 1:
                    edge = finish(beside, own)
                    swept[k, pl.ds(place, 1)] = jnp.where(there, edge, jnp.zeros_like(edge))
                    eta[k, pl.ds(place, 1)] = row(beside, components)

        def second(step, _):
            start = pl.multiple_of(step * TILE, TILE)
            weights, factor = relax_weights(*around(eta, (), 1, start + TILE))
            middle, others = around(swept, (), 1, start + TILE)
            surface[pl.ds(start, TILE)] = relax(weights, factor, middle, others, force[pl.ds(start, TILE)])
            return 0

        lax.fori_loop(0, rows // TILE, second, 0)
        near, far = split(jnp.concatenate(fold(surface[...]), axis=0))
        for copy in tables:
            copy.wait()
        total = dot(near, high[...]) + dot(far, high[...]) + dot(near, low[...])
        blocks = [total[k * rows : (k + 1) * rows] for k in range(RADIX)]
        kind, mirrored = order_class((1, total.shape[1]))
        cosine, sine = blocks[0], jnp.zeros_like(blocks[0])
        for k in range(1, RADIX // 2 + 1):
            cosine = jnp.where(kind == k, blocks[k], cosine)
        for k in range(1, RADIX // 2):
            sine = jnp.where(kind == k, blocks[RADIX // 2 + k], sine)
        sine = jnp.where(mirrored, -sine, sine)
        modes = total.shape[1] // 2
        fourier = jnp.concatenate(
            [cosine[:, :modes] - sine[:, modes:], cosine[:, modes:] + sine[:, :modes]], axis=1
        )
        blocks = out.shape[0]
        width = fourier.shape[1] // blocks
        for block in range(blocks):
            out[block] = pack(fourier[:, block * width : (block + 1) * width])


def sweep_shells(d, f, h, out, field, eta, force, result, sems, before_first, last_loads, arrived, finish, after_shell):
    components, shells, rows, count = d.shape
    inner = pl.ds(TILE, rows)
    lower = lax.axis_index("radial") == 0
    shell = lambda k: jnp.where(lower, k, shells - 1 - k)
    nothing = jnp.where(lower, 0, shells + 1)

    def field_loads(k):
        s = shell(k)
        return [
            pltpu.make_async_copy(d.at[:, s], field.at[:, s + 1, inner], sems.at[k, 0]),
            pltpu.make_async_copy(h.at[s], eta.at[s + 1, inner], sems.at[k, 1]),
            *(last_loads if k == shells - 1 else []),
        ]

    def force_load(k):
        return [pltpu.make_async_copy(f.at[:, shell(k)], force.at[:, shell(k)], sems.at[k, 2])]

    loads = [start_all(field_loads(0)), start_all(field_loads(1))]
    forces = [start_all(force_load(0))]
    zeros = jnp.zeros((rows, count), jnp.float32)
    for c in range(components):
        field[c, nothing, inner] = zeros
    eta[nothing, inner] = zeros
    before_first()
    loads.append(start_all(field_loads(2)))
    forces.append(start_all(force_load(1)))
    for copy in loads[0]:
        copy.wait()
    stores = []
    for k in range(shells):
        s = shell(k)
        if k + 3 < shells:
            loads.append(start_all(field_loads(k + 3)))
        if k + 2 < shells:
            forces.append(start_all(force_load(k + 2)))
        for copy in (loads[k + 1] if k + 1 < shells else []) + forces[k]:
            copy.wait()
        if k == shells - 2:
            arrived()

        def tile(step, _):
            first = pl.multiple_of(step * TILE, TILE)
            part = pl.ds(first, TILE)
            if k == shells - 1:
                finish(s, first)
            else:
                weights, factor = relax_weights(*around(eta, (), s + 1, first + TILE))
                for c in range(components):
                    middle, others = around(field, (c,), s + 1, first + TILE)
                    result[c, s, part] = relax(weights, factor, middle, others, force[c, s, part])
            pltpu.make_async_copy(result.at[:, s, part], out.at[:, s, part], sems.at[k, 3]).start()
            return 0

        lax.fori_loop(0, rows // TILE, tile, 0)
        stores.append(pltpu.make_async_copy(result.at[:, s], out.at[:, s], sems.at[k, 3]))
        after_shell(s, k)
    for copy in stores:
        copy.wait()


def set_edge(ref, lead, shells, rows, before, after):
    for s in range(shells):
        ref[(*lead, s + 1, TILE - 1)] = before(s)
        ref[(*lead, s + 1, rows + TILE)] = after(s)


def start_all(copies):
    for copy in copies:
        copy.start()
    return copies


def load_messages(sources, lower_sources, slots, sems):
    lower = lax.axis_index("radial") < lax.axis_size("radial") - 1
    copies = lambda refs: [pltpu.make_async_copy(ref, slots.at[k], sems.at[k]) for k, ref in enumerate(refs)]
    pl.when(lower)(lambda: [copy.start() for copy in copies(lower_sources)] and None)
    pl.when(jnp.logical_not(lower))(lambda: [copy.start() for copy in copies(sources)] and None)
    return copies(sources)


def first_kernel(d, f, h, one, two, lower_one, lower_two, *refs):
    components, shells, rows, count = d.shape
    staged = (len(refs) - 14) // 2
    sources, refs = refs[:staged], refs[staged:]
    out, diagonal_out, ring_out, own_out, beside_out, *targets = refs[: 5 + staged]
    field, eta, force, result, messages, edges, own, diagonal, sems, more_sems = refs[5 + staged :]
    arrivals = load_messages((one, two), (lower_one, lower_two), messages, more_sems)
    lower = lax.axis_index("radial") == 0
    last = jnp.where(lower, shells - 1, 0)
    copies = []

    def before_first():
        for copy in arrivals:
            copy.wait()
        before, after = by_parity(messages.at[0], messages.at[1])
        row = lambda message, kind: lambda s: message[kind * shells + s]
        for c in range(components):
            set_edge(field, (c,), shells, rows, row(before, c), row(after, c))
        set_edge(eta, (), shells, rows, row(before, components), row(after, components))
        for side, message in enumerate((before, after)):
            for k in range(components + 1):
                edges[side * (components + 1) + k] = jnp.where(
                    lower, message[(k + 1) * shells - 1], message[k * shells]
                )
        tail = ring_out.at[pl.ds(2 * (components + 1) * rows, edges.shape[0])]
        copies.extend(
            start_all(
                [
                    pltpu.make_async_copy(edges, tail, more_sems.at[2]),
                    pltpu.make_async_copy(messages, beside_out, more_sems.at[3]),
                ]
            )
        )

    def arrived():
        block = pl.ds(TILE, rows)
        zeros = jnp.zeros((rows, count), jnp.float32)
        beyond = jnp.where(lower, shells + 1, 0)
        for c in range(components):
            field[c, beyond, block] = zeros
        eta[beyond, block] = zeros
        sources = [field.at[c, last + 1, block] for c in range(components)] + [eta.at[last + 1, block]]
        copies.extend(
            start_all(
                [
                    pltpu.make_async_copy(source, ring_out.at[pl.ds(k * rows, rows)], more_sems.at[4 + k])
                    for k, source in enumerate(sources)
                ]
            )
        )

    def finish(s, first):
        part = pl.ds(first, TILE)
        middle, others = around(eta, (), s + 1, first + TILE)
        weights = [middle + other for other in others]
        zero = jnp.zeros_like(middle)
        weights[0] = jnp.where(lower, zero, weights[0])
        weights[1] = jnp.where(lower, weights[1], zero)
        diagonal[part] = 1.0 + functools.reduce(jnp.add, weights)
        for c in range(components):
            total = force[c, s, part]
            for weight, other in zip(weights, around(field, (c,), s + 1, first + TILE)[1]):
                total = total + weight * other
            result[c, s, part] = total

    def after_shell(s, k):
        if k == 0:
            copies.extend(
                start_all(
                    [
                        pltpu.make_async_copy(source, target, more_sems.at[7 + 2 * components + n])
                        for n, (source, target) in enumerate(zip(sources, targets))
                    ]
                )
            )
        for side, place in enumerate((TILE, TILE + rows - 1)):
            for c in range(components):
                own[c, side * shells + s] = field[c, s + 1, place]
            own[components, side * shells + s] = eta[s + 1, place]
        if k == shells - 1:
            sums = [result.at[c, s] for c in range(components)] + [diagonal]
            copies.extend(
                start_all(
                    [
                        pltpu.make_async_copy(
                            source,
                            ring_out.at[pl.ds((components + 1 + n) * rows, rows)],
                            more_sems.at[5 + components + n],
                        )
                        for n, source in enumerate(sums)
                    ]
                    + [
                        pltpu.make_async_copy(diagonal, diagonal_out, more_sems.at[6 + 2 * components]),
                        pltpu.make_async_copy(own, own_out, more_sems.at[0]),
                    ]
                )
            )

    sweep_shells(
        d, f, h, out, field, eta, force, result, sems, before_first, [], arrived, finish, after_shell
    )
    for copy in copies:
        copy.wait()


def second_kernel(d, f, h, start, diagonal_from, ring, beside, own_from, *refs):
    components, shells, rows, count = d.shape
    staged = (len(refs) - 14) // 2
    sources, refs = refs[:staged], refs[staged:]
    out, token, *targets = refs[: 2 + staged]
    field, eta, force, result, messages, edges, own, diagonal, raw, ring_diagonal, sems, more_sems = refs[2 + staged :]
    token[...] = jnp.zeros_like(token)
    tail = ring.at[pl.ds(2 * (components + 1) * rows, edges.shape[0])]
    arrivals = start_all(
        [
            pltpu.make_async_copy(beside, messages, more_sems.at[0]),
            pltpu.make_async_copy(tail, edges, more_sems.at[1]),
            pltpu.make_async_copy(own_from, own, more_sems.at[2]),
        ]
    )
    radial, lateral = lax.axis_index("radial"), lax.axis_index("lateral")
    lower = radial == 0
    last, beyond = jnp.where(lower, shells - 1, 0), jnp.where(lower, shells + 1, 0)
    block = pl.ds(TILE, rows)
    from_ring = lambda k, target, sem: pltpu.make_async_copy(
        ring.at[pl.ds(k * rows, rows)], target, more_sems.at[sem]
    )
    last_loads = [
        pltpu.make_async_copy(start.at[:, last], raw.at[pl.ds(0, components)], more_sems.at[3]),
        pltpu.make_async_copy(diagonal_from, diagonal, more_sems.at[4]),
        *(from_ring(c, raw.at[components + c], 5 + c) for c in range(components)),
        from_ring(components, eta.at[beyond, block], 5 + components),
        *(
            from_ring(components + 1 + c, field.at[c, beyond, block], 6 + components + c)
            for c in range(components)
        ),
        from_ring(2 * components + 1, ring_diagonal, 6 + 2 * components),
    ]
    copies = []

    def before_first():
        for copy in arrivals:
            copy.wait()
        before, after = by_parity(messages.at[0], messages.at[1])
        pair = lambda k: jnp.concatenate(
            [before[k * shells : (k + 1) * shells], after[k * shells : (k + 1) * shells]], axis=0
        )
        place = row_number((2 * shells, count))
        zero = jnp.zeros((2 * shells, count), jnp.float32)
        shared = place % shells == last
        across_of = lambda k: jnp.where(
            place < shells, edges[pl.ds(k, 1)], edges[pl.ds(components + 1 + k, 1)]
        )
        inside = jnp.where(place < shells, lateral, lax.axis_size("lateral") - 1 - lateral) > 0
        middle = pair(components)
        weight = middle + own[components]
        across = jnp.where(shared, middle + across_of(components), zero)
        factor = RELAXATION / (pair(2 * components + 1) + weight + across)
        for c in range(components):
            total = pair(components + 1 + c) + weight * own[c] + across * across_of(c)
            edge = jnp.where(inside, (1.0 - RELAXATION) * pair(c) + factor * total, zero)
            set_edge(field, (c,), shells, rows, lambda s: edge[s], lambda s: edge[shells + s])
        set_edge(eta, (), shells, rows, lambda s: middle[s], lambda s: middle[shells + s])

    def arrived():
        def tile(step, _):
            first = pl.multiple_of(step * TILE, TILE)
            part, place = pl.ds(first, TILE), pl.ds(first + TILE, TILE)
            weight = eta[last + 1, place] + eta[beyond, place]
            here, there = RELAXATION / (diagonal[part] + weight), RELAXATION / (ring_diagonal[part] + weight)
            for c in range(components):
                mine, other = raw[c, part], raw[components + c, part]
                field[c, last + 1, place] = (1.0 - RELAXATION) * mine + here * (
                    field[c, last + 1, place] + weight * other
                )
                field[c, beyond, place] = (1.0 - RELAXATION) * other + there * (
                    field[c, beyond, place] + weight * mine
                )
            return 0

        lax.fori_loop(0, rows // TILE, tile, 0)

    def finish(s, first):
        part = pl.ds(first, TILE)
        weights, factor = relax_weights(*around(eta, (), s + 1, first + TILE))
        for c in range(components):
            middle, others = around(field, (c,), s + 1, first + TILE)
            result[c, s, part] = relax(weights, factor, middle, others, force[c, s, part])

    def after_shell(s, k):
        if k == 0:
            copies.extend(
                start_all(
                    [
                        pltpu.make_async_copy(source, target, more_sems.at[7 + 2 * components + n])
                        for n, (source, target) in enumerate(zip(sources, targets))
                    ]
                )
            )

    sweep_shells(
        d, f, h, out, field, eta, force, result, sems, before_first, last_loads, arrived, finish, after_shell
    )
    for copy in copies:
        copy.wait()


def spectrum_kernel(
    orders, wave_high, wave_low, point_high, point_low, response_from, coefficients, out, response, sem
):
    copy = pltpu.make_async_copy(response_from, response, sem)
    copy.start()
    radial = lax.axis_size("radial")
    width = coefficients.shape[0]
    bands, rows = orders.shape[0] // radial, point_high.shape[0] * radial // orders.shape[0]
    fourier = jnp.concatenate([unpack(orders[band * radial + radial - 1], width) for band in range(bands)], axis=0)
    high, low = split(fourier)
    spectrum = dot(wave_high[...], high) + dot(wave_high[...], low) + dot(wave_low[...], high)
    coefficients[...] = spectrum.T
    copy.wait()
    own = response[:, :width]
    for place in range(1, radial):
        own = jnp.where(
            lax.axis_index("radial") == place, response[:, place * width : (place + 1) * width], own
        )
    high, low = split(own * spectrum)
    load = dot(point_high[...], high) + dot(point_high[...], low) + dot(point_low[...], high)
    for band in range(bands):
        block = pack(load[band * rows : (band + 1) * rows])
        for place in range(radial):
            out[band * radial + place] = block


def load_kernel(load, high, low, mask_from, out, mask, sem):
    copy = pltpu.make_async_copy(mask_from, mask, sem)
    copy.start()
    blocks, rows = load.shape[0], out.shape[0]
    step, width = out.shape[1] // RADIX, high.shape[1] // blocks
    values = jnp.concatenate([unpack(load[block], width) for block in range(blocks)], axis=1)
    modes = values.shape[1] // 2
    kind, mirrored = order_class((1, values.shape[1]))
    crossed = jnp.concatenate([values[:, modes:], -values[:, :modes]], axis=1)
    crossed = jnp.where(mirrored, -crossed, crossed)
    zero = jnp.zeros_like(values)
    stack = [jnp.where(kind == k, values, zero) for k in range(RADIX // 2 + 1)]
    stack += [jnp.where(kind == k, crossed, zero) for k in range(1, RADIX // 2)]
    near, far = split(jnp.concatenate(stack, axis=0))
    total = dot_nt(near, high[...]) + dot_nt(far, high[...]) + dot_nt(near, low[...])
    copy.wait()
    for m, part in enumerate(unfold([total[k * rows : (k + 1) * rows] for k in range(RADIX)])):
        columns = slice(m * step, (m + 1) * step)
        out[:, columns] = part * mask[:, columns].astype(jnp.float32)


def cost(microseconds):
    return pl.CostEstimate(flops=0, bytes_accessed=3_000_000 * microseconds, transcendentals=0)


def hbm(values):
    return pltpu.with_memory_space_constraint(values, pltpu.HBM)


def shards(initial_displacement, force, viscosity, layer_index, response, ocean_mask):
    components, shells, rows, count = initial_displacement.shape
    radial, lateral = lax.axis_size("radial"), lax.axis_size("lateral")
    f32 = functools.partial(jax.ShapeDtypeStruct, dtype=jnp.float32)
    scratch = lambda *shape: pltpu.VMEM(shape, jnp.float32)
    in_hbm = lambda *shape: pltpu.HBM(shape, jnp.float32)
    width = 2 * MODES // (lateral * radial)
    first = [p for i in range(0, lateral - 1, 2) for p in ((i, i + 1), (i + 1, i))]
    second = [p for i in range(1, lateral - 1, 2) for p in ((i, i + 1), (i + 1, i))]
    both = ("lateral", "radial")
    top_only = lambda pairs: [(i * radial + radial - 1, j * radial + radial - 1) for i, j in pairs]

    lower_only = lambda pairs: [(i * radial + k, j * radial + k) for i, j in pairs for k in range(radial - 1)]
    swap = [(i, radial - 1 - i) for i in range(radial)]
    tensors = [hbm(a) for a in (initial_displacement, force, layer_index)]
    viscosity = hbm(viscosity)
    message = f32((2 * (components + 1) * shells, count))
    sides = lambda *shape: scratch(2, *shape)
    mine = pl.pallas_call(
        message_kernel,
        in_specs=[HBM] * 4,
        out_specs=[VMEM] * 2,
        out_shape=[message] * 2,
        scratch_shapes=[
            sides(components, shells, TILE, count),
            sides(components, shells, TILE, count),
            pltpu.VMEM((2, shells, TILE, count), jnp.int32),
            scratch(3 * components + 2, 2 * shells, count),
            pltpu.SMEM(viscosity.shape, jnp.float32),
            pltpu.SemaphoreType.DMA((7,)),
        ],
        compiler_params=params(16),
        cost_estimate=cost(20),
    )(viscosity, *tensors)
    two = lax.ppermute(mine[1], both, top_only(second))
    one = lax.ppermute(mine[0], both, top_only(first))
    eta, *surface = pl.pallas_call(
        viscosity_kernel,
        in_specs=[HBM] * 4 + [ANY],
        out_specs=[HBM, VMEM, VMEM, VMEM],
        out_shape=[
            in_hbm(shells, rows, count),
            f32((2, rows, count)),
            f32((2, rows, count)),
            f32((rows, count)),
        ],
        scratch_shapes=[
            pltpu.VMEM(layer_index.shape, jnp.int32),
            scratch(shells + 1, rows + 2 * TILE, count),
            scratch(4, rows + 2 * TILE, count),
            scratch(2, rows, count),
            pltpu.SMEM(viscosity.shape, jnp.float32),
            pltpu.SemaphoreType.DMA((3 + shells,)),
            pltpu.SemaphoreType.DMA((shells,)),
        ],
        compiler_params=params(16),
        cost_estimate=cost(20),
    )(viscosity, *tensors, mine[0])
    lower_one, lower_two, eta = lax.optimization_barrier((*mine, eta))
    lower_one = lax.ppermute(lower_one, both, lower_only(first))
    lower_two = lax.ppermute(lower_two, both, lower_only(second))

    high, low = longitude_tables(count, MODES)
    high, low = hbm(jnp.asarray(high)), hbm(jnp.asarray(low))
    table = pltpu.VMEM(high.shape, jnp.bfloat16)
    packed = (lateral * radial, rows * width // max(128, width), max(128, width))
    orders = pl.pallas_call(
        functools.partial(surface_kernel, components=components),
        in_specs=[VMEM] * 7 + [HBM, HBM],
        out_specs=VMEM,
        out_shape=f32(packed),
        scratch_shapes=[
            scratch(3, rows + 2 * TILE, count),
            scratch(3, rows + 2 * TILE, count),
            scratch(rows, count),
            table,
            table,
            pltpu.SemaphoreType.DMA((2,)),
        ],
        compiler_params=params(16),
        cost_estimate=cost(200),
    )(*surface, *mine, one, two, high, low)
    eta, _ = lax.optimization_barrier((eta, orders))
    orders = lax.all_to_all(orders, both, split_axis=0, concat_axis=0, tiled=True)
    eta = hbm(eta)

    sweep_scratch = [
        scratch(components, shells + 2, rows + 2 * TILE, count),
        scratch(shells + 2, rows + 2 * TILE, count),
        scratch(components, shells, rows, count),
        scratch(components, shells, rows, count),
    ]
    sweep_sems = pltpu.SemaphoreType.DMA((shells, 4))
    point_high, point_low = colatitude_tables(rows * lateral, MODES)
    stages = [
        jnp.asarray(a)
        for a in (point_high.T.copy(), point_low.T.copy(), point_high, point_low)
    ]
    ring_rows = 2 * (components + 1) * (rows + 1)
    sweep_scratch += [
        sides(*message.shape),
        scratch(2 * (components + 1), count),
        scratch(components + 1, 2 * shells, count),
        scratch(rows, count),
    ]
    smoothed, diagonal, ring, own, beside, *staged = pl.pallas_call(
        first_kernel,
        in_specs=[HBM] * 3 + [ANY] * 4 + [HBM] * len(stages),
        out_specs=[HBM] * 5 + [VMEM] * len(stages),
        out_shape=[
            in_hbm(*initial_displacement.shape),
            in_hbm(rows, count),
            in_hbm(ring_rows, count),
            in_hbm(components + 1, 2 * shells, count),
            in_hbm(2, *message.shape),
            *(jax.ShapeDtypeStruct(a.shape, a.dtype) for a in stages),
        ],
        scratch_shapes=[
            *sweep_scratch,
            sweep_sems,
            pltpu.SemaphoreType.DMA((7 + 2 * components + len(stages),)),
        ],
        compiler_params=params(28),
        cost_estimate=cost(50),
    )(*tensors[:2], eta, one, two, lower_one, lower_two, *(hbm(a) for a in stages))
    ring, orders = lax.optimization_barrier((ring, orders))
    ring = lax.ppermute(ring, "radial", swap)
    coefficients, load = pl.pallas_call(
        spectrum_kernel,
        in_specs=[VMEM] * 5 + [HBM],
        out_specs=[VMEM, VMEM],
        out_shape=[f32((width, MODES)), f32(packed)],
        scratch_shapes=[pltpu.VMEM(response.shape, jnp.float32), pltpu.SemaphoreType.DMA],
        compiler_params=params(16),
        cost_estimate=cost(200),
    )(orders, *staged, hbm(response))
    eta, load = lax.optimization_barrier((eta, load))
    load = lax.all_to_all(load, both, split_axis=0, concat_axis=0, tiled=True)

    stages = [high, low]
    displacement, token, *staged = pl.pallas_call(
        second_kernel,
        in_specs=[HBM] * 5 + [ANY] + [HBM] * (2 + len(stages)),
        out_specs=[HBM, VMEM] + [VMEM] * len(stages),
        out_shape=[
            in_hbm(*initial_displacement.shape),
            f32((TILE, 128)),
            *(jax.ShapeDtypeStruct(a.shape, a.dtype) for a in stages),
        ],
        scratch_shapes=[
            *sweep_scratch,
            scratch(2 * components, rows, count),
            scratch(rows, count),
            sweep_sems,
            pltpu.SemaphoreType.DMA((7 + 2 * components + len(stages),)),
        ],
        compiler_params=params(28),
        cost_estimate=cost(50),
    )(
        *(hbm(a) for a in (smoothed, tensors[1], eta, tensors[0], diagonal)),
        ring,
        *(hbm(a) for a in (beside, own)),
        *stages,
    )

    sea_load = pl.pallas_call(
        load_kernel,
        in_specs=[VMEM] * 3 + [HBM],
        out_specs=VMEM,
        out_shape=f32((rows, count)),
        scratch_shapes=[pltpu.VMEM(ocean_mask.shape, ocean_mask.dtype), pltpu.SemaphoreType.DMA],
        compiler_params=params(20),
        cost_estimate=cost(3),
    )(load, *staged, hbm(ocean_mask))
    return (displacement, coefficients.T, sea_load)


def solution(mesh):
    in_specs = (
        P("member", "radial", "lateral", None),
        P("member", "radial", "lateral", None),
        P("member"),
        P("radial", "lateral", None),
        P(None, "lateral"),
        P("lateral", None),
    )
    out_specs = (
        P("member", "radial", "lateral", None),
        P("member", ("lateral", "radial")),
        P("lateral", "member"),
    )
    return jax.shard_map(shards, mesh=mesh, in_specs=in_specs, out_specs=out_specs, check_vma=False)
```

```python
import functools
import math

import jax
import jax.numpy as jnp
import ml_dtypes
import numpy as np
from jax import lax
from jax.experimental import pallas as pl
from jax.experimental.pallas import tpu as pltpu
from jax.sharding import PartitionSpec as P

MODES = 512
RELAXATION = 0.8
TILE = 8
RADIX = 8
MIB = 1 << 20
ANY = pl.BlockSpec(memory_space=pl.ANY)
HBM = pl.BlockSpec(memory_space=pltpu.HBM)
SMEM = pl.BlockSpec(memory_space=pltpu.SMEM)
VMEM = pl.BlockSpec(memory_space=pltpu.VMEM)


def params(mib):
    return pltpu.CompilerParams(vmem_limit_bytes=mib * MIB)


def halves(table):
    high = table.astype(ml_dtypes.bfloat16)
    low = (table - high.astype(np.float64)).astype(ml_dtypes.bfloat16)
    return high, low


@functools.lru_cache
def longitude_tables(count, modes):
    points = np.arange(count // RADIX, dtype=np.int64)[:, None]
    orders = np.arange(modes, dtype=np.int64)[None, :]
    angle = (2.0 * math.pi / count) * (points * orders % count)
    table = np.concatenate([np.cos(angle), np.sin(angle)], axis=1) * math.sqrt(2.0 / count)
    return halves(table)


@functools.lru_cache
def colatitude_tables(count, modes):
    points = np.arange(count, dtype=np.int64)[:, None]
    waves = np.arange(modes, dtype=np.int64)[None, :]
    phase = waves * (2 * points + 1) % (4 * count)
    return halves(np.cos(math.pi / (2 * count) * phase) * math.sqrt(2.0 / count))


def split(values):
    high = values.astype(jnp.bfloat16)
    return high, (values - high.astype(jnp.float32)).astype(jnp.bfloat16)


def dot(a, b):
    return jnp.dot(a, b, preferred_element_type=jnp.float32)


def pack(block):
    rows, width = block.shape
    groups = max(1, 128 // width)
    rows //= groups
    return jnp.concatenate([block[k * rows : (k + 1) * rows] for k in range(groups)], axis=1)


def unpack(block, width):
    groups = max(1, 128 // width)
    return jnp.concatenate([block[:, k * width : (k + 1) * width] for k in range(groups)], axis=0)


def weighted_sum(terms):
    total = None
    for factor, values in terms:
        factor = round(factor, 15)
        if factor == 0.0:
            continue
        part = values if abs(factor) == 1.0 else abs(factor) * values
        if total is None:
            total = part if factor > 0 else -part
        else:
            total = total + part if factor > 0 else total - part
    return total


def turn(number):
    angle = 2.0 * math.pi * (number % RADIX) / RADIX
    return math.cos(angle), math.sin(angle)


def fold(values):
    step = values.shape[1] // RADIX
    parts = [values[:, m * step : (m + 1) * step] for m in range(RADIX)]
    cosines = [[(turn(k * m)[0], part) for m, part in enumerate(parts)] for k in range(RADIX // 2 + 1)]
    sines = [[(turn(k * m)[1], part) for m, part in enumerate(parts)] for k in range(1, RADIX // 2)]
    return [weighted_sum(terms) for terms in cosines + sines]


def unfold(blocks):
    cosines, sines = blocks[: RADIX // 2 + 1], blocks[RADIX // 2 + 1 :]
    return [
        weighted_sum(
            [(turn(k * m)[0], block) for k, block in enumerate(cosines)]
            + [(turn(k * m)[1], block) for k, block in enumerate(sines, 1)]
        )
        for m in range(RADIX)
    ]


def order_class(shape):
    order = lax.broadcasted_iota(jnp.int32, shape, len(shape) - 1) % RADIX
    mirrored = order > RADIX // 2
    return jnp.where(mirrored, RADIX - order, order), mirrored


def dot_nt(a, b):
    return lax.dot_general(a, b, (((1,), (1,)), ((), ())), preferred_element_type=jnp.float32)


def half_viscosity(index, viscosity_ref):
    values = [0.5 * viscosity_ref[k] for k in range(viscosity_ref.shape[0])]
    bit = 1
    while len(values) > 1:
        odd = (index & bit) != 0
        if len(values) % 2:
            values.append(values[-1])
        values = [jnp.where(odd, b, a) for a, b in zip(values[::2], values[1::2])]
        bit *= 2
    return values[0]


def row_number(shape):
    return lax.broadcasted_iota(jnp.int32, shape, 0)


def north_of(above, middle):
    return pltpu.roll(jnp.where(row_number(middle.shape) == TILE - 1, above, middle), 1, 0)


def south_of(below, middle):
    return pltpu.roll(jnp.where(row_number(middle.shape) == 0, below, middle), TILE - 1, 0)


def east_of(values):
    return pltpu.roll(values, values.shape[-1] - 1, values.ndim - 1)


def west_of(values):
    return pltpu.roll(values, 1, values.ndim - 1)


def relax_weights(middle, others):
    weights = [middle + other for other in others]
    diagonal = 1.0 + functools.reduce(jnp.add, weights)
    return weights, RELAXATION / diagonal


def relax(weights, factor, middle, others, force):
    total = force
    for weight, other in zip(weights, others):
        total = total + weight * other
    return (1.0 - RELAXATION) * middle + factor * total


def around(ref, lead, shell, start):
    rows = lambda first: pl.ds(pl.multiple_of(first, TILE), TILE)
    middle = ref[(*lead, shell, rows(start))]
    return middle, [
        ref[(*lead, shell + 1, rows(start))],
        ref[(*lead, shell - 1, rows(start))],
        south_of(ref[(*lead, shell, rows(start + TILE))], middle),
        north_of(ref[(*lead, shell, rows(start - TILE))], middle),
        west_of(middle),
        east_of(middle),
    ]


def odd_band():
    return lax.axis_index("lateral") % 2 == 1


def by_parity(one, two):
    one, two = one[...], two[...]
    return jnp.where(odd_band(), one, two), jnp.where(odd_band(), two, one)


def message_kernel(viscosity_from, d, f, index, one, two, fields, forces, layers, rows_of, viscosity, sems):
    components, shells, rows, count = d.shape
    copies = [pltpu.make_async_copy(viscosity_from, viscosity, sems.at[0])]
    for side, start in enumerate((0, rows - TILE)):
        part = pl.ds(start, TILE)
        copies += [
            pltpu.make_async_copy(index.at[:, part], layers.at[side], sems.at[1 + side]),
            pltpu.make_async_copy(d.at[:, :, part], fields.at[side], sems.at[3 + side]),
            pltpu.make_async_copy(f.at[:, :, part], forces.at[side], sems.at[5 + side]),
        ]
    for copy in copies:
        copy.start()
    for copy in copies[:2] + copies[4:5]:
        copy.wait()
    near_eta, far_eta = 2 * components, 2 * components + 1
    for side, near, far in ((0, 0, 1), (1, TILE - 1, TILE - 2)):
        for s in range(shells):
            eta = half_viscosity(layers[side, s], viscosity)
            rows_of[near_eta, side * shells + s] = eta[near]
            rows_of[far_eta, side * shells + s] = eta[far]
    for copy in copies[2:4] + copies[5:]:
        copy.wait()
    for side, near, far in ((0, 0, 1), (1, TILE - 1, TILE - 2)):
        for s in range(shells):
            for c in range(components):
                rows_of[c, side * shells + s] = fields[side, c, s, near]
                rows_of[components + c, side * shells + s] = fields[side, c, s, far]
                rows_of[far_eta + 1 + c, side * shells + s] = forces[side, c, s, near]
    radial = lax.axis_index("radial")
    place = row_number((2 * shells, count)) % shells
    highest, lowest = place == shells - 1, place == 0
    zero = jnp.zeros((2 * shells, count), jnp.float32)

    def beside(near, far):
        middle = rows_of[near]
        return middle, [
            jnp.where(highest, zero, pltpu.roll(middle, 2 * shells - 1, 0)),
            jnp.where(lowest, zero, pltpu.roll(middle, 1, 0)),
            rows_of[far],
            west_of(middle),
            east_of(middle),
        ]

    eta, others = beside(near_eta, far_eta)
    weights = [eta + other for other in others]
    inside = (radial < lax.axis_size("radial") - 1, radial > 0)
    weights[0] = jnp.where(jnp.logical_and(highest, inside[0]), zero, weights[0])
    weights[1] = jnp.where(jnp.logical_and(lowest, inside[1]), zero, weights[1])
    diagonal = 1.0 + functools.reduce(jnp.add, weights)
    values, sums = [], []
    for c in range(components):
        middle, others = beside(c, components + c)
        total = rows_of[far_eta + 1 + c]
        for weight, other in zip(weights, others):
            total = total + weight * other
        values.append(middle)
        sums.append(total)
    for place, field in enumerate(values + [eta] + sums + [diagonal]):
        both = jnp.where(odd_band(), field, pltpu.roll(field, shells, 0))
        one[pl.ds(place * shells, shells)] = both[:shells]
        two[pl.ds(place * shells, shells)] = both[shells:]


def viscosity_kernel(
    viscosity_from, d, f, index_from, token, eta_out, surface_swept, surface_eta, surface_force,
    index, eta, field, force, viscosity, sems, eta_sems,
):
    del token
    _, shells, rows, count = d.shape
    block = pl.ds(TILE, rows)
    value_copy = pltpu.make_async_copy(viscosity_from, viscosity, sems.at[shells])
    layers = [pltpu.make_async_copy(index_from.at[s], index.at[s], sems.at[s]) for s in range(shells)]
    surface_copies = [
        pltpu.make_async_copy(d.at[0, pl.ds(shells - 3, 3)], field.at[pl.ds(0, 3), block], sems.at[shells + 1]),
        pltpu.make_async_copy(f.at[0, pl.ds(shells - 2, 2)], force, sems.at[shells + 2]),
    ]
    start_all([value_copy, *layers, *surface_copies])
    zeros = jnp.zeros((rows, count), jnp.float32)
    field[3, block] = zeros
    eta[shells, block] = zeros
    value_copy.wait()
    stores = []
    for s in range(shells):
        layers[s].wait()

        def lookup(step, _):
            start = pl.multiple_of(step * TILE, TILE)
            eta[s, pl.ds(start + TILE, TILE)] = half_viscosity(index[s, pl.ds(start, TILE)], viscosity)
            return 0

        lax.fori_loop(0, rows // TILE, lookup, 0)
        stores += start_all([pltpu.make_async_copy(eta.at[s, block], eta_out.at[s], eta_sems.at[s])])
    for copy in surface_copies:
        copy.wait()

    def sweep(step, _):
        start = pl.multiple_of(step * TILE, TILE)
        part = pl.ds(start, TILE)
        for k in range(2):
            weights, factor = relax_weights(*around(eta, (), shells - 2 + k, start + TILE))
            middle, others = around(field, (), k + 1, start + TILE)
            surface_swept[k, part] = relax(weights, factor, middle, others, force[k, part])
            surface_eta[k, part] = eta[shells - 2 + k, pl.ds(start + TILE, TILE)]
        surface_force[part] = force[1, part]
        return 0

    lax.fori_loop(0, rows // TILE, sweep, 0)
    for copy in stores:
        copy.wait()


def surface_kernel(
    surface_swept, surface_eta, force, own_one, own_two, one, two, high_from, low_from, out,
    swept, eta, surface, high, low, sems, components,
):
    rows, count = force.shape

    @pl.when(lax.axis_index("radial") == lax.axis_size("radial") - 1)
    def _():
        tables = start_all(
            [
                pltpu.make_async_copy(high_from, high, sems.at[0]),
                pltpu.make_async_copy(low_from, low, sems.at[1]),
            ]
        )
        block = pl.ds(TILE, rows)
        for k in range(2):
            swept[k, block] = surface_swept[k]
            eta[k, block] = surface_eta[k]
        swept[2, block] = jnp.zeros((rows, count), jnp.float32)
        eta[2, block] = jnp.zeros((rows, count), jnp.float32)
        fields = one.shape[0]
        shells = fields // (2 * (components + 1))
        lateral = lax.axis_index("lateral")
        inside = (lateral > 0, lateral < lax.axis_size("lateral") - 1)
        for beside, own, place, own_place, there in zip(
            by_parity(one, two), by_parity(own_one, own_two), (TILE - 1, rows + TILE), (TILE, rows + TILE - 1), inside
        ):
            for k in range(2):
                row = lambda message, kind: message[kind * shells + shells - 2 + k : kind * shells + shells - 1 + k]
                weight = row(beside, components) + row(own, components)

                def finish(message, other):
                    total = row(message, components + 1) + weight * row(other, 0)
                    factor = RELAXATION / (row(message, 2 * components + 1) + weight)
                    return (1.0 - RELAXATION) * row(message, 0) + factor * total

                swept[k, pl.ds(own_place, 1)] = finish(own, beside)
                if k == 1:
                    edge = finish(beside, own)
                    swept[k, pl.ds(place, 1)] = jnp.where(there, edge, jnp.zeros_like(edge))
                    eta[k, pl.ds(place, 1)] = row(beside, components)

        def second(step, _):
            start = pl.multiple_of(step * TILE, TILE)
            weights, factor = relax_weights(*around(eta, (), 1, start + TILE))
            middle, others = around(swept, (), 1, start + TILE)
            surface[pl.ds(start, TILE)] = relax(weights, factor, middle, others, force[pl.ds(start, TILE)])
            return 0

        lax.fori_loop(0, rows // TILE, second, 0)
        near, far = split(jnp.concatenate(fold(surface[...]), axis=0))
        for copy in tables:
            copy.wait()
        total = dot(near, high[...]) + dot(far, high[...]) + dot(near, low[...])
        blocks = [total[k * rows : (k + 1) * rows] for k in range(RADIX)]
        kind, mirrored = order_class((1, total.shape[1]))
        cosine, sine = blocks[0], jnp.zeros_like(blocks[0])
        for k in range(1, RADIX // 2 + 1):
            cosine = jnp.where(kind == k, blocks[k], cosine)
        for k in range(1, RADIX // 2):
            sine = jnp.where(kind == k, blocks[RADIX // 2 + k], sine)
        sine = jnp.where(mirrored, -sine, sine)
        modes = total.shape[1] // 2
        fourier = jnp.concatenate(
            [cosine[:, :modes] - sine[:, modes:], cosine[:, modes:] + sine[:, :modes]], axis=1
        )
        blocks = out.shape[0]
        width = fourier.shape[1] // blocks
        for block in range(blocks):
            out[block] = pack(fourier[:, block * width : (block + 1) * width])


def sweep_shells(d, f, h, out, field, eta, force, result, sems, before_first, last_loads, arrived, finish, after_shell):
    components, shells, rows, count = d.shape
    inner = pl.ds(TILE, rows)
    lower = lax.axis_index("radial") == 0
    shell = lambda k: jnp.where(lower, k, shells - 1 - k)
    nothing = jnp.where(lower, 0, shells + 1)

    def field_loads(k):
        s = shell(k)
        return [
            pltpu.make_async_copy(d.at[:, s], field.at[:, s + 1, inner], sems.at[k, 0]),
            pltpu.make_async_copy(h.at[s], eta.at[s + 1, inner], sems.at[k, 1]),
            *(last_loads if k == shells - 1 else []),
        ]

    def force_load(k):
        return [pltpu.make_async_copy(f.at[:, shell(k)], force.at[:, shell(k)], sems.at[k, 2])]

    loads = [start_all(field_loads(0)), start_all(field_loads(1))]
    forces = [start_all(force_load(0))]
    zeros = jnp.zeros((rows, count), jnp.float32)
    for c in range(components):
        field[c, nothing, inner] = zeros
    eta[nothing, inner] = zeros
    before_first()
    loads.append(start_all(field_loads(2)))
    forces.append(start_all(force_load(1)))
    for copy in loads[0]:
        copy.wait()
    stores = []
    for k in range(shells):
        s = shell(k)
        if k + 3 < shells:
            loads.append(start_all(field_loads(k + 3)))
        if k + 2 < shells:
            forces.append(start_all(force_load(k + 2)))
        for copy in (loads[k + 1] if k + 1 < shells else []) + forces[k]:
            copy.wait()
        if k == shells - 2:
            arrived()

        def tile(step, _):
            first = pl.multiple_of(step * TILE, TILE)
            part = pl.ds(first, TILE)
            if k == shells - 1:
                finish(s, first)
            else:
                weights, factor = relax_weights(*around(eta, (), s + 1, first + TILE))
                for c in range(components):
                    middle, others = around(field, (c,), s + 1, first + TILE)
                    result[c, s, part] = relax(weights, factor, middle, others, force[c, s, part])
            pltpu.make_async_copy(result.at[:, s, part], out.at[:, s, part], sems.at[k, 3]).start()
            return 0

        lax.fori_loop(0, rows // TILE, tile, 0, unroll=2)
        stores.append(pltpu.make_async_copy(result.at[:, s], out.at[:, s], sems.at[k, 3]))
        after_shell(s, k)
    for copy in stores:
        copy.wait()


def set_edge(ref, lead, shells, rows, before, after):
    for s in range(shells):
        ref[(*lead, s + 1, TILE - 1)] = before(s)
        ref[(*lead, s + 1, rows + TILE)] = after(s)


def start_all(copies):
    for copy in copies:
        copy.start()
    return copies


def load_messages(sources, lower_sources, slots, sems):
    lower = lax.axis_index("radial") < lax.axis_size("radial") - 1
    copies = lambda refs: [pltpu.make_async_copy(ref, slots.at[k], sems.at[k]) for k, ref in enumerate(refs)]
    pl.when(lower)(lambda: [copy.start() for copy in copies(lower_sources)] and None)
    pl.when(jnp.logical_not(lower))(lambda: [copy.start() for copy in copies(sources)] and None)
    return copies(sources)


def first_kernel(d, f, h, one, two, lower_one, lower_two, *refs):
    components, shells, rows, count = d.shape
    staged = (len(refs) - 14) // 2
    sources, refs = refs[:staged], refs[staged:]
    out, diagonal_out, ring_out, own_out, beside_out, *targets = refs[: 5 + staged]
    field, eta, force, result, messages, edges, own, diagonal, sems, more_sems = refs[5 + staged :]
    arrivals = load_messages((one, two), (lower_one, lower_two), messages, more_sems)
    lower = lax.axis_index("radial") == 0
    last = jnp.where(lower, shells - 1, 0)
    copies = []

    def before_first():
        for copy in arrivals:
            copy.wait()
        before, after = by_parity(messages.at[0], messages.at[1])
        row = lambda message, kind: lambda s: message[kind * shells + s]
        for c in range(components):
            set_edge(field, (c,), shells, rows, row(before, c), row(after, c))
        set_edge(eta, (), shells, rows, row(before, components), row(after, components))
        for side, message in enumerate((before, after)):
            for k in range(components + 1):
                edges[side * (components + 1) + k] = jnp.where(
                    lower, message[(k + 1) * shells - 1], message[k * shells]
                )
        tail = ring_out.at[pl.ds(2 * (components + 1) * rows, edges.shape[0])]
        copies.extend(
            start_all(
                [
                    pltpu.make_async_copy(edges, tail, more_sems.at[2]),
                    pltpu.make_async_copy(messages, beside_out, more_sems.at[3]),
                ]
            )
        )

    def arrived():
        block = pl.ds(TILE, rows)
        zeros = jnp.zeros((rows, count), jnp.float32)
        beyond = jnp.where(lower, shells + 1, 0)
        for c in range(components):
            field[c, beyond, block] = zeros
        eta[beyond, block] = zeros
        sources = [field.at[c, last + 1, block] for c in range(components)] + [eta.at[last + 1, block]]
        copies.extend(
            start_all(
                [
                    pltpu.make_async_copy(source, ring_out.at[pl.ds(k * rows, rows)], more_sems.at[4 + k])
                    for k, source in enumerate(sources)
                ]
            )
        )

    def finish(s, first):
        part = pl.ds(first, TILE)
        middle, others = around(eta, (), s + 1, first + TILE)
        weights = [middle + other for other in others]
        zero = jnp.zeros_like(middle)
        weights[0] = jnp.where(lower, zero, weights[0])
        weights[1] = jnp.where(lower, weights[1], zero)
        diagonal[part] = 1.0 + functools.reduce(jnp.add, weights)
        for c in range(components):
            total = force[c, s, part]
            for weight, other in zip(weights, around(field, (c,), s + 1, first + TILE)[1]):
                total = total + weight * other
            result[c, s, part] = total

    def after_shell(s, k):
        if k == 0:
            copies.extend(
                start_all(
                    [
                        pltpu.make_async_copy(source, target, more_sems.at[7 + 2 * components + n])
                        for n, (source, target) in enumerate(zip(sources, targets))
                    ]
                )
            )
        for side, place in enumerate((TILE, TILE + rows - 1)):
            for c in range(components):
                own[c, side * shells + s] = field[c, s + 1, place]
            own[components, side * shells + s] = eta[s + 1, place]
        if k == shells - 1:
            sums = [result.at[c, s] for c in range(components)] + [diagonal]
            copies.extend(
                start_all(
                    [
                        pltpu.make_async_copy(
                            source,
                            ring_out.at[pl.ds((components + 1 + n) * rows, rows)],
                            more_sems.at[5 + components + n],
                        )
                        for n, source in enumerate(sums)
                    ]
                    + [
                        pltpu.make_async_copy(diagonal, diagonal_out, more_sems.at[6 + 2 * components]),
                        pltpu.make_async_copy(own, own_out, more_sems.at[0]),
                    ]
                )
            )

    sweep_shells(
        d, f, h, out, field, eta, force, result, sems, before_first, [], arrived, finish, after_shell
    )
    for copy in copies:
        copy.wait()


def second_kernel(d, f, h, start, diagonal_from, ring, beside, own_from, *refs):
    components, shells, rows, count = d.shape
    staged = (len(refs) - 17) // 2
    mask_from, *sources = refs[: 1 + staged]
    out, token, mask_out, *targets = refs[1 + staged : 4 + 2 * staged]
    (
        field, eta, force, result, messages, edges, own, diagonal, raw, ring_diagonal, mask, sems, more_sems
    ) = refs[4 + 2 * staged :]
    token[...] = jnp.zeros_like(token)
    tail = ring.at[pl.ds(2 * (components + 1) * rows, edges.shape[0])]
    arrivals = start_all(
        [
            pltpu.make_async_copy(beside, messages, more_sems.at[0]),
            pltpu.make_async_copy(tail, edges, more_sems.at[1]),
            pltpu.make_async_copy(own_from, own, more_sems.at[2]),
        ]
    )
    radial, lateral = lax.axis_index("radial"), lax.axis_index("lateral")
    lower = radial == 0
    last, beyond = jnp.where(lower, shells - 1, 0), jnp.where(lower, shells + 1, 0)
    block = pl.ds(TILE, rows)
    from_ring = lambda k, target, sem: pltpu.make_async_copy(
        ring.at[pl.ds(k * rows, rows)], target, more_sems.at[sem]
    )
    last_loads = [
        pltpu.make_async_copy(start.at[:, last], raw.at[pl.ds(0, components)], more_sems.at[3]),
        pltpu.make_async_copy(diagonal_from, diagonal, more_sems.at[4]),
        *(from_ring(c, raw.at[components + c], 5 + c) for c in range(components)),
        from_ring(components, eta.at[beyond, block], 5 + components),
        *(
            from_ring(components + 1 + c, field.at[c, beyond, block], 6 + components + c)
            for c in range(components)
        ),
        from_ring(2 * components + 1, ring_diagonal, 6 + 2 * components),
    ]
    copies = []
    mask_copy = pltpu.make_async_copy(mask_from, mask, more_sems.at[7 + 2 * components])

    def before_first():
        for copy in arrivals:
            copy.wait()
        before, after = by_parity(messages.at[0], messages.at[1])
        pair = lambda k: jnp.concatenate(
            [before[k * shells : (k + 1) * shells], after[k * shells : (k + 1) * shells]], axis=0
        )
        place = row_number((2 * shells, count))
        zero = jnp.zeros((2 * shells, count), jnp.float32)
        shared = place % shells == last
        across_of = lambda k: jnp.where(
            place < shells, edges[pl.ds(k, 1)], edges[pl.ds(components + 1 + k, 1)]
        )
        inside = jnp.where(place < shells, lateral, lax.axis_size("lateral") - 1 - lateral) > 0
        middle = pair(components)
        weight = middle + own[components]
        across = jnp.where(shared, middle + across_of(components), zero)
        factor = RELAXATION / (pair(2 * components + 1) + weight + across)
        for c in range(components):
            total = pair(components + 1 + c) + weight * own[c] + across * across_of(c)
            edge = jnp.where(inside, (1.0 - RELAXATION) * pair(c) + factor * total, zero)
            set_edge(field, (c,), shells, rows, lambda s: edge[s], lambda s: edge[shells + s])
        set_edge(eta, (), shells, rows, lambda s: middle[s], lambda s: middle[shells + s])

    def arrived():
        def tile(step, _):
            first = pl.multiple_of(step * TILE, TILE)
            part, place = pl.ds(first, TILE), pl.ds(first + TILE, TILE)
            weight = eta[last + 1, place] + eta[beyond, place]
            here, there = RELAXATION / (diagonal[part] + weight), RELAXATION / (ring_diagonal[part] + weight)
            for c in range(components):
                mine, other = raw[c, part], raw[components + c, part]
                field[c, last + 1, place] = (1.0 - RELAXATION) * mine + here * (
                    field[c, last + 1, place] + weight * other
                )
                field[c, beyond, place] = (1.0 - RELAXATION) * other + there * (
                    field[c, beyond, place] + weight * mine
                )
            return 0

        lax.fori_loop(0, rows // TILE, tile, 0)

    def finish(s, first):
        part = pl.ds(first, TILE)
        weights, factor = relax_weights(*around(eta, (), s + 1, first + TILE))
        for c in range(components):
            middle, others = around(field, (c,), s + 1, first + TILE)
            result[c, s, part] = relax(weights, factor, middle, others, force[c, s, part])

    def after_shell(s, k):
        if k == 0:
            copies.extend(
                start_all(
                    [
                        pltpu.make_async_copy(source, target, more_sems.at[8 + 2 * components + n])
                        for n, (source, target) in enumerate(zip(sources, targets))
                    ]
                )
            )
            mask_copy.start()
        if k == shells - 2:
            mask_copy.wait()
            mask_out[...] = mask[...].astype(jnp.float32).astype(jnp.bfloat16)

    sweep_shells(
        d, f, h, out, field, eta, force, result, sems, before_first, last_loads, arrived, finish, after_shell
    )
    for copy in copies:
        copy.wait()


def spectrum_kernel(orders, high, low, response, coefficients, out):
    radial = lax.axis_size("radial")
    width = coefficients.shape[0]
    bands, rows = orders.shape[0] // radial, high.shape[0] * radial // orders.shape[0]
    fourier = jnp.concatenate([unpack(orders[band * radial + radial - 1], width) for band in range(bands)], axis=0)
    near, far = split(fourier.T)
    spectrum = dot(near, high[...]) + dot(far, high[...]) + dot(near, low[...])
    coefficients[...] = spectrum
    own = response[:, :width]
    for place in range(1, radial):
        own = jnp.where(
            lax.axis_index("radial") == place, response[:, place * width : (place + 1) * width], own
        )
    near, far = split(own.T * spectrum)
    load = (dot_nt(near, high[...]) + dot_nt(far, high[...]) + dot_nt(near, low[...])).T
    for band in range(bands):
        block = pack(load[band * rows : (band + 1) * rows])
        for place in range(radial):
            out[band * radial + place] = block


def load_kernel(load, high, low, mask, out):
    blocks, rows = load.shape[0], out.shape[0]
    step, width = out.shape[1] // RADIX, high.shape[1] // blocks
    values = jnp.concatenate([unpack(load[block], width) for block in range(blocks)], axis=1)
    modes = values.shape[1] // 2
    kind, mirrored = order_class((1, values.shape[1]))
    crossed = jnp.concatenate([values[:, modes:], -values[:, :modes]], axis=1)
    crossed = jnp.where(mirrored, -crossed, crossed)
    zero = jnp.zeros_like(values)
    stack = [jnp.where(kind == k, values, zero) for k in range(RADIX // 2 + 1)]
    stack += [jnp.where(kind == k, crossed, zero) for k in range(1, RADIX // 2)]
    near, far = split(jnp.concatenate(stack, axis=0))
    total = dot_nt(near, high[...]) + dot_nt(far, high[...]) + dot_nt(near, low[...])
    for m, part in enumerate(unfold([total[k * rows : (k + 1) * rows] for k in range(RADIX)])):
        columns = slice(m * step, (m + 1) * step)
        out[:, columns] = part * mask[:, columns].astype(jnp.float32)


def cost(microseconds):
    return pl.CostEstimate(flops=0, bytes_accessed=3_000_000 * microseconds, transcendentals=0)


def hbm(values):
    return pltpu.with_memory_space_constraint(values, pltpu.HBM)


def shards(initial_displacement, force, viscosity, layer_index, response, ocean_mask):
    components, shells, rows, count = initial_displacement.shape
    radial, lateral = lax.axis_size("radial"), lax.axis_size("lateral")
    f32 = functools.partial(jax.ShapeDtypeStruct, dtype=jnp.float32)
    scratch = lambda *shape: pltpu.VMEM(shape, jnp.float32)
    in_hbm = lambda *shape: pltpu.HBM(shape, jnp.float32)
    width = 2 * MODES // (lateral * radial)
    first = [p for i in range(0, lateral - 1, 2) for p in ((i, i + 1), (i + 1, i))]
    second = [p for i in range(1, lateral - 1, 2) for p in ((i, i + 1), (i + 1, i))]
    both = ("lateral", "radial")
    top_only = lambda pairs: [(i * radial + radial - 1, j * radial + radial - 1) for i, j in pairs]

    lower_only = lambda pairs: [(i * radial + k, j * radial + k) for i, j in pairs for k in range(radial - 1)]
    swap = [(i, radial - 1 - i) for i in range(radial)]
    tensors = [hbm(a) for a in (initial_displacement, force, layer_index)]
    viscosity = hbm(viscosity)
    message = f32((2 * (components + 1) * shells, count))
    sides = lambda *shape: scratch(2, *shape)
    mine = pl.pallas_call(
        message_kernel,
        in_specs=[HBM] * 4,
        out_specs=[VMEM] * 2,
        out_shape=[message] * 2,
        scratch_shapes=[
            sides(components, shells, TILE, count),
            sides(components, shells, TILE, count),
            pltpu.VMEM((2, shells, TILE, count), jnp.int32),
            scratch(3 * components + 2, 2 * shells, count),
            pltpu.SMEM(viscosity.shape, jnp.float32),
            pltpu.SemaphoreType.DMA((7,)),
        ],
        compiler_params=params(16),
        cost_estimate=cost(20),
    )(viscosity, *tensors)
    two = lax.ppermute(mine[1], both, top_only(second))
    one = lax.ppermute(mine[0], both, top_only(first))
    eta, *surface = pl.pallas_call(
        viscosity_kernel,
        in_specs=[HBM] * 4 + [ANY],
        out_specs=[HBM, VMEM, VMEM, VMEM],
        out_shape=[
            in_hbm(shells, rows, count),
            f32((2, rows, count)),
            f32((2, rows, count)),
            f32((rows, count)),
        ],
        scratch_shapes=[
            pltpu.VMEM(layer_index.shape, jnp.int32),
            scratch(shells + 1, rows + 2 * TILE, count),
            scratch(4, rows + 2 * TILE, count),
            scratch(2, rows, count),
            pltpu.SMEM(viscosity.shape, jnp.float32),
            pltpu.SemaphoreType.DMA((3 + shells,)),
            pltpu.SemaphoreType.DMA((shells,)),
        ],
        compiler_params=params(16),
        cost_estimate=cost(20),
    )(viscosity, *tensors, mine[0])
    lower_one, lower_two, eta = lax.optimization_barrier((*mine, eta))
    lower_one = lax.ppermute(lower_one, both, lower_only(first))
    lower_two = lax.ppermute(lower_two, both, lower_only(second))

    high, low = longitude_tables(count, MODES)
    high, low = hbm(jnp.asarray(high)), hbm(jnp.asarray(low))
    table = pltpu.VMEM(high.shape, jnp.bfloat16)
    packed = (lateral * radial, rows * width // max(128, width), max(128, width))
    orders = pl.pallas_call(
        functools.partial(surface_kernel, components=components),
        in_specs=[VMEM] * 7 + [HBM, HBM],
        out_specs=VMEM,
        out_shape=f32(packed),
        scratch_shapes=[
            scratch(3, rows + 2 * TILE, count),
            scratch(3, rows + 2 * TILE, count),
            scratch(rows, count),
            table,
            table,
            pltpu.SemaphoreType.DMA((2,)),
        ],
        compiler_params=params(16),
        cost_estimate=cost(200),
    )(*surface, *mine, one, two, high, low)
    eta, _ = lax.optimization_barrier((eta, orders))
    orders = lax.all_to_all(orders, both, split_axis=0, concat_axis=0, tiled=True)
    eta = hbm(eta)

    sweep_scratch = [
        scratch(components, shells + 2, rows + 2 * TILE, count),
        scratch(shells + 2, rows + 2 * TILE, count),
        scratch(components, shells, rows, count),
        scratch(components, shells, rows, count),
    ]
    sweep_sems = pltpu.SemaphoreType.DMA((shells, 4))
    point_high, point_low = colatitude_tables(rows * lateral, MODES)
    stages = [jnp.asarray(point_high), jnp.asarray(point_low)] + [response]
    ring_rows = 2 * (components + 1) * (rows + 1)
    sweep_scratch += [
        sides(*message.shape),
        scratch(2 * (components + 1), count),
        scratch(components + 1, 2 * shells, count),
        scratch(rows, count),
    ]
    smoothed, diagonal, ring, own, beside, *staged = pl.pallas_call(
        first_kernel,
        in_specs=[HBM] * 3 + [ANY] * 4 + [HBM] * len(stages),
        out_specs=[HBM] * 5 + [VMEM] * len(stages),
        out_shape=[
            in_hbm(*initial_displacement.shape),
            in_hbm(rows, count),
            in_hbm(ring_rows, count),
            in_hbm(components + 1, 2 * shells, count),
            in_hbm(2, *message.shape),
            *(jax.ShapeDtypeStruct(a.shape, a.dtype) for a in stages),
        ],
        scratch_shapes=[
            *sweep_scratch,
            sweep_sems,
            pltpu.SemaphoreType.DMA((7 + 2 * components + len(stages),)),
        ],
        compiler_params=params(28),
        cost_estimate=cost(50),
    )(*tensors[:2], eta, one, two, lower_one, lower_two, *(hbm(a) for a in stages))
    ring, orders = lax.optimization_barrier((ring, orders))
    ring = lax.ppermute(ring, "radial", swap)
    coefficients, load = pl.pallas_call(
        spectrum_kernel,
        in_specs=[VMEM] * 4,
        out_specs=[VMEM, VMEM],
        out_shape=[f32((width, MODES)), f32(packed)],
        compiler_params=params(16),
        cost_estimate=cost(200),
    )(orders, *staged)
    eta, load = lax.optimization_barrier((eta, load))
    load = lax.all_to_all(load, both, split_axis=0, concat_axis=0, tiled=True)

    stages = [high, low]
    displacement, token, mask, *staged = pl.pallas_call(
        second_kernel,
        in_specs=[HBM] * 5 + [ANY] + [HBM] * (3 + len(stages)),
        out_specs=[HBM, VMEM, VMEM] + [VMEM] * len(stages),
        out_shape=[
            in_hbm(*initial_displacement.shape),
            f32((TILE, 128)),
            jax.ShapeDtypeStruct(ocean_mask.shape, jnp.bfloat16),
            *(jax.ShapeDtypeStruct(a.shape, a.dtype) for a in stages),
        ],
        scratch_shapes=[
            *sweep_scratch,
            scratch(2 * components, rows, count),
            scratch(rows, count),
            pltpu.VMEM(ocean_mask.shape, ocean_mask.dtype),
            sweep_sems,
            pltpu.SemaphoreType.DMA((8 + 2 * components + len(stages),)),
        ],
        compiler_params=params(28),
        cost_estimate=cost(50),
    )(
        *(hbm(a) for a in (smoothed, tensors[1], eta, tensors[0], diagonal)),
        ring,
        *(hbm(a) for a in (beside, own, ocean_mask)),
        *stages,
    )

    sea_load = pl.pallas_call(
        load_kernel,
        in_specs=[VMEM] * 4,
        out_specs=VMEM,
        out_shape=f32((rows, count)),
        compiler_params=params(20),
        cost_estimate=cost(3),
    )(load, *staged, mask)
    return (displacement, coefficients.T, sea_load)


def solution(mesh):
    in_specs = (
        P("member", "radial", "lateral", None),
        P("member", "radial", "lateral", None),
        P("member"),
        P("radial", "lateral", None),
        P(None, "lateral"),
        P("lateral", None),
    )
    out_specs = (
        P("member", "radial", "lateral", None),
        P("member", ("lateral", "radial")),
        P("lateral", "member"),
    )
    return jax.shard_map(shards, mesh=mesh, in_specs=in_specs, out_specs=out_specs, check_vma=False)
```

```python
import functools
import math

import jax
import jax.numpy as jnp
import ml_dtypes
import numpy as np
from jax import lax
from jax.experimental import pallas as pl
from jax.experimental.pallas import tpu as pltpu
from jax.sharding import PartitionSpec as P

MODES = 512
RELAXATION = 0.8
TILE = 8
RADIX = 8
EARLY = 2
MIB = 1 << 20
ANY = pl.BlockSpec(memory_space=pl.ANY)
HBM = pl.BlockSpec(memory_space=pltpu.HBM)
SMEM = pl.BlockSpec(memory_space=pltpu.SMEM)
VMEM = pl.BlockSpec(memory_space=pltpu.VMEM)


def params(mib):
    return pltpu.CompilerParams(vmem_limit_bytes=mib * MIB)


def halves(table):
    high = table.astype(ml_dtypes.bfloat16)
    low = (table - high.astype(np.float64)).astype(ml_dtypes.bfloat16)
    return high, low


@functools.lru_cache
def longitude_tables(count, modes):
    points = np.arange(count // RADIX, dtype=np.int64)[:, None]
    orders = np.arange(modes, dtype=np.int64)[None, :]
    angle = (2.0 * math.pi / count) * (points * orders % count)
    table = np.concatenate([np.cos(angle), np.sin(angle)], axis=1) * math.sqrt(2.0 / count)
    return halves(table)


@functools.lru_cache
def colatitude_tables(count, modes):
    points = np.arange(count, dtype=np.int64)[:, None]
    waves = np.arange(modes, dtype=np.int64)[None, :]
    phase = waves * (2 * points + 1) % (4 * count)
    return halves(np.cos(math.pi / (2 * count) * phase) * math.sqrt(2.0 / count))


def split(values):
    high = values.astype(jnp.bfloat16)
    return high, (values - high.astype(jnp.float32)).astype(jnp.bfloat16)


def dot(a, b):
    return jnp.dot(a, b, preferred_element_type=jnp.float32)


def pack(block):
    rows, width = block.shape
    groups = max(1, 128 // width)
    rows //= groups
    return jnp.concatenate([block[k * rows : (k + 1) * rows] for k in range(groups)], axis=1)


def unpack(block, width):
    groups = max(1, 128 // width)
    return jnp.concatenate([block[:, k * width : (k + 1) * width] for k in range(groups)], axis=0)


def weighted_sum(terms):
    total = None
    for factor, values in terms:
        factor = round(factor, 15)
        if factor == 0.0:
            continue
        part = values if abs(factor) == 1.0 else abs(factor) * values
        if total is None:
            total = part if factor > 0 else -part
        else:
            total = total + part if factor > 0 else total - part
    return total


def turn(number):
    angle = 2.0 * math.pi * (number % RADIX) / RADIX
    return math.cos(angle), math.sin(angle)


def fold(values):
    step = values.shape[1] // RADIX
    parts = [values[:, m * step : (m + 1) * step] for m in range(RADIX)]
    cosines = [[(turn(k * m)[0], part) for m, part in enumerate(parts)] for k in range(RADIX // 2 + 1)]
    sines = [[(turn(k * m)[1], part) for m, part in enumerate(parts)] for k in range(1, RADIX // 2)]
    return [weighted_sum(terms) for terms in cosines + sines]


def unfold(blocks):
    cosines, sines = blocks[: RADIX // 2 + 1], blocks[RADIX // 2 + 1 :]
    return [
        weighted_sum(
            [(turn(k * m)[0], block) for k, block in enumerate(cosines)]
            + [(turn(k * m)[1], block) for k, block in enumerate(sines, 1)]
        )
        for m in range(RADIX)
    ]


def order_class(shape):
    order = lax.broadcasted_iota(jnp.int32, shape, len(shape) - 1) % RADIX
    mirrored = order > RADIX // 2
    return jnp.where(mirrored, RADIX - order, order), mirrored


def dot_nt(a, b):
    return lax.dot_general(a, b, (((1,), (1,)), ((), ())), preferred_element_type=jnp.float32)


def half_viscosity(index, viscosity_ref):
    values = [0.5 * viscosity_ref[k] for k in range(viscosity_ref.shape[0])]
    bit = 1
    while len(values) > 1:
        odd = (index & bit) != 0
        if len(values) % 2:
            values.append(values[-1])
        values = [jnp.where(odd, b, a) for a, b in zip(values[::2], values[1::2])]
        bit *= 2
    return values[0]


def row_number(shape):
    return lax.broadcasted_iota(jnp.int32, shape, 0)


def north_of(above, middle):
    return pltpu.roll(jnp.where(row_number(middle.shape) == TILE - 1, above, middle), 1, 0)


def south_of(below, middle):
    return pltpu.roll(jnp.where(row_number(middle.shape) == 0, below, middle), TILE - 1, 0)


def east_of(values):
    return pltpu.roll(values, values.shape[-1] - 1, values.ndim - 1)


def west_of(values):
    return pltpu.roll(values, 1, values.ndim - 1)


def relax_weights(middle, others):
    weights = [middle + other for other in others]
    diagonal = 1.0 + functools.reduce(jnp.add, weights)
    return weights, RELAXATION / diagonal


def relax(weights, factor, middle, others, force):
    total = force
    for weight, other in zip(weights, others):
        total = total + weight * other
    return (1.0 - RELAXATION) * middle + factor * total


def around(ref, lead, shell, start):
    rows = lambda first: pl.ds(pl.multiple_of(first, TILE), TILE)
    middle = ref[(*lead, shell, rows(start))]
    return middle, [
        ref[(*lead, shell + 1, rows(start))],
        ref[(*lead, shell - 1, rows(start))],
        south_of(ref[(*lead, shell, rows(start + TILE))], middle),
        north_of(ref[(*lead, shell, rows(start - TILE))], middle),
        west_of(middle),
        east_of(middle),
    ]


def odd_band():
    return lax.axis_index("lateral") % 2 == 1


def by_parity(one, two):
    one, two = one[...], two[...]
    return jnp.where(odd_band(), one, two), jnp.where(odd_band(), two, one)


def message_kernel(viscosity_from, d, f, index, one, two, fields, forces, layers, rows_of, viscosity, sems):
    components, shells, rows, count = d.shape
    copies = [pltpu.make_async_copy(viscosity_from, viscosity, sems.at[0])]
    for side, start in enumerate((0, rows - TILE)):
        part = pl.ds(start, TILE)
        copies += [
            pltpu.make_async_copy(index.at[:, part], layers.at[side], sems.at[1 + side]),
            pltpu.make_async_copy(d.at[:, :, part], fields.at[side], sems.at[3 + side]),
            pltpu.make_async_copy(f.at[:, :, part], forces.at[side], sems.at[5 + side]),
        ]
    for copy in copies:
        copy.start()
    for copy in copies[:2] + copies[4:5]:
        copy.wait()
    near_eta, far_eta = 2 * components, 2 * components + 1
    for side, near, far in ((0, 0, 1), (1, TILE - 1, TILE - 2)):
        for s in range(shells):
            eta = half_viscosity(layers[side, s], viscosity)
            rows_of[near_eta, side * shells + s] = eta[near]
            rows_of[far_eta, side * shells + s] = eta[far]
    for copy in copies[2:4] + copies[5:]:
        copy.wait()
    for side, near, far in ((0, 0, 1), (1, TILE - 1, TILE - 2)):
        for s in range(shells):
            for c in range(components):
                rows_of[c, side * shells + s] = fields[side, c, s, near]
                rows_of[components + c, side * shells + s] = fields[side, c, s, far]
                rows_of[far_eta + 1 + c, side * shells + s] = forces[side, c, s, near]
    radial = lax.axis_index("radial")
    place = row_number((2 * shells, count)) % shells
    highest, lowest = place == shells - 1, place == 0
    zero = jnp.zeros((2 * shells, count), jnp.float32)

    def beside(near, far):
        middle = rows_of[near]
        return middle, [
            jnp.where(highest, zero, pltpu.roll(middle, 2 * shells - 1, 0)),
            jnp.where(lowest, zero, pltpu.roll(middle, 1, 0)),
            rows_of[far],
            west_of(middle),
            east_of(middle),
        ]

    eta, others = beside(near_eta, far_eta)
    weights = [eta + other for other in others]
    inside = (radial < lax.axis_size("radial") - 1, radial > 0)
    weights[0] = jnp.where(jnp.logical_and(highest, inside[0]), zero, weights[0])
    weights[1] = jnp.where(jnp.logical_and(lowest, inside[1]), zero, weights[1])
    diagonal = 1.0 + functools.reduce(jnp.add, weights)
    values, sums = [], []
    for c in range(components):
        middle, others = beside(c, components + c)
        total = rows_of[far_eta + 1 + c]
        for weight, other in zip(weights, others):
            total = total + weight * other
        values.append(middle)
        sums.append(total)
    for place, field in enumerate(values + [eta] + sums + [diagonal]):
        both = jnp.where(odd_band(), field, pltpu.roll(field, shells, 0))
        one[pl.ds(place * shells, shells)] = both[:shells]
        two[pl.ds(place * shells, shells)] = both[shells:]


def shell_order(shells):
    lower = lax.axis_index("radial") == 0
    return lambda k: jnp.where(lower, k, shells - 1 - k)


def viscosity_kernel(
    viscosity_from, d, f, index_from, token, eta_out, out, surface_swept, surface_eta, surface_force,
    index, eta, field, force, result, viscosity, sems, more_sems,
):
    del token
    _, shells, rows, count = d.shape
    components = d.shape[0]
    block = pl.ds(TILE, rows)
    shell = shell_order(shells)
    value_copy = pltpu.make_async_copy(viscosity_from, viscosity, sems.at[shells])
    layers = [pltpu.make_async_copy(index_from.at[shell(k)], index.at[k], sems.at[k]) for k in range(shells)]
    fields = [
        pltpu.make_async_copy(d.at[:, shell(k)], field.at[:, k + 1, block], more_sems.at[k]) for k in range(EARLY + 1)
    ]
    forces = [
        pltpu.make_async_copy(f.at[:, shell(k)], force.at[:, k], more_sems.at[EARLY + 1 + k]) for k in range(EARLY)
    ]
    start_all([value_copy, *layers, *fields, *forces])
    zeros = jnp.zeros((rows, count), jnp.float32)
    for c in range(components):
        field[c, 0, block] = zeros
    eta[0, block] = zeros
    value_copy.wait()
    stores = []
    for k in range(shells):
        layers[k].wait()

        def lookup(step, _):
            start = pl.multiple_of(step * TILE, TILE)
            eta[k + 1, pl.ds(start + TILE, TILE)] = half_viscosity(index[k, pl.ds(start, TILE)], viscosity)
            return 0

        lax.fori_loop(0, rows // TILE, lookup, 0)
        stores += start_all(
            [pltpu.make_async_copy(eta.at[k + 1, block], eta_out.at[shell(k)], more_sems.at[2 * EARLY + 1 + k])]
        )
    for k in range(EARLY):
        for copy in (fields[: EARLY + 1] if k == 0 else []) + forces[k : k + 1]:
            copy.wait()

        def sweep(step, _):
            start = pl.multiple_of(step * TILE, TILE)
            part = pl.ds(start, TILE)
            weights, factor = relax_weights(*around(eta, (), k + 1, start + TILE))
            for c in range(components):
                middle, others = around(field, (c,), k + 1, start + TILE)
                result[c, k, part] = relax(weights, factor, middle, others, force[c, k, part])
            surface_swept[1 - k, part] = result[0, k, part]
            surface_eta[1 - k, part] = eta[k + 1, pl.ds(start + TILE, TILE)]
            if k == 0:
                surface_force[part] = force[0, 0, part]
            return 0

        lax.fori_loop(0, rows // TILE, sweep, 0, unroll=2)
        stores += start_all(
            [pltpu.make_async_copy(result.at[:, k], out.at[:, k], more_sems.at[2 * EARLY + 1 + shells + k])]
        )
    for copy in stores:
        copy.wait()


def surface_kernel(
    surface_swept, surface_eta, force, own_one, own_two, one, two, high_from, low_from, out,
    swept, eta, surface, high, low, sems, components,
):
    rows, count = force.shape

    @pl.when(lax.axis_index("radial") == lax.axis_size("radial") - 1)
    def _():
        tables = start_all(
            [
                pltpu.make_async_copy(high_from, high, sems.at[0]),
                pltpu.make_async_copy(low_from, low, sems.at[1]),
            ]
        )
        block = pl.ds(TILE, rows)
        for k in range(2):
            swept[k, block] = surface_swept[k]
            eta[k, block] = surface_eta[k]
        swept[2, block] = jnp.zeros((rows, count), jnp.float32)
        eta[2, block] = jnp.zeros((rows, count), jnp.float32)
        fields = one.shape[0]
        shells = fields // (2 * (components + 1))
        lateral = lax.axis_index("lateral")
        inside = (lateral > 0, lateral < lax.axis_size("lateral") - 1)
        for beside, own, place, own_place, there in zip(
            by_parity(one, two), by_parity(own_one, own_two), (TILE - 1, rows + TILE), (TILE, rows + TILE - 1), inside
        ):
            for k in range(2):
                row = lambda message, kind: message[kind * shells + shells - 2 + k : kind * shells + shells - 1 + k]
                weight = row(beside, components) + row(own, components)

                def finish(message, other):
                    total = row(message, components + 1) + weight * row(other, 0)
                    factor = RELAXATION / (row(message, 2 * components + 1) + weight)
                    return (1.0 - RELAXATION) * row(message, 0) + factor * total

                swept[k, pl.ds(own_place, 1)] = finish(own, beside)
                if k == 1:
                    edge = finish(beside, own)
                    swept[k, pl.ds(place, 1)] = jnp.where(there, edge, jnp.zeros_like(edge))
                    eta[k, pl.ds(place, 1)] = row(beside, components)

        def second(step, _):
            start = pl.multiple_of(step * TILE, TILE)
            weights, factor = relax_weights(*around(eta, (), 1, start + TILE))
            middle, others = around(swept, (), 1, start + TILE)
            surface[pl.ds(start, TILE)] = relax(weights, factor, middle, others, force[pl.ds(start, TILE)])
            return 0

        lax.fori_loop(0, rows // TILE, second, 0)
        near, far = split(jnp.concatenate(fold(surface[...]), axis=0))
        for copy in tables:
            copy.wait()
        total = dot(near, high[...]) + dot(far, high[...]) + dot(near, low[...])
        blocks = [total[k * rows : (k + 1) * rows] for k in range(RADIX)]
        kind, mirrored = order_class((1, total.shape[1]))
        cosine, sine = blocks[0], jnp.zeros_like(blocks[0])
        for k in range(1, RADIX // 2 + 1):
            cosine = jnp.where(kind == k, blocks[k], cosine)
        for k in range(1, RADIX // 2):
            sine = jnp.where(kind == k, blocks[RADIX // 2 + k], sine)
        sine = jnp.where(mirrored, -sine, sine)
        modes = total.shape[1] // 2
        fourier = jnp.concatenate(
            [cosine[:, :modes] - sine[:, modes:], cosine[:, modes:] + sine[:, :modes]], axis=1
        )
        blocks = out.shape[0]
        width = fourier.shape[1] // blocks
        for block in range(blocks):
            out[block] = pack(fourier[:, block * width : (block + 1) * width])


def sweep_shells(
    begin, source, f, h, store, field, eta, force, result, sems, before_first, last_loads, arrived, finish, after_shell
):
    components, shells, rows, count = f.shape
    inner = pl.ds(TILE, rows)
    shell = shell_order(shells)

    def field_loads(k):
        s = shell(k)
        return [
            pltpu.make_async_copy(source(k), field.at[:, s + 1, inner], sems.at[k, 0]),
            pltpu.make_async_copy(h.at[s], eta.at[s + 1, inner], sems.at[k, 1]),
            *(last_loads if k == shells - 1 else []),
        ]

    def force_load(k):
        return [pltpu.make_async_copy(f.at[:, shell(k)], force.at[:, shell(k)], sems.at[k, 2])]

    loads = {k: start_all(field_loads(k)) for k in range(max(begin - 1, 0), begin + 2)}
    forces = {begin: start_all(force_load(begin))}
    if begin == 0:
        nothing = jnp.where(lax.axis_index("radial") == 0, 0, shells + 1)
        zeros = jnp.zeros((rows, count), jnp.float32)
        for c in range(components):
            field[c, nothing, inner] = zeros
        eta[nothing, inner] = zeros
    before_first()

    def start_until(k):
        for ahead in range(begin, shells):
            if ahead <= k and ahead not in loads:
                loads[ahead] = start_all(field_loads(ahead))
            if ahead < k and ahead not in forces:
                forces[ahead] = start_all(force_load(ahead))

    start_until(begin + 2)
    stores, there = [], set()
    for k in range(begin, shells):
        s = shell(k)
        start_until(k + 3)
        for near in range(max(k - 1, 0), min(k + 2, shells)):
            if near not in there:
                there.add(near)
                for copy in loads[near]:
                    copy.wait()
                arrived(near)
        for copy in forces[k]:
            copy.wait()

        def tile(step, _):
            first = pl.multiple_of(step * TILE, TILE)
            part = pl.ds(first, TILE)
            if k == shells - 1:
                finish(s, first)
            else:
                weights, factor = relax_weights(*around(eta, (), s + 1, first + TILE))
                for c in range(components):
                    middle, others = around(field, (c,), s + 1, first + TILE)
                    result[c, s, part] = relax(weights, factor, middle, others, force[c, s, part])
            pltpu.make_async_copy(result.at[:, s, part], store(k).at[:, part], sems.at[k, 3]).start()
            return 0

        lax.fori_loop(0, rows // TILE, tile, 0, unroll=2)
        stores.append(pltpu.make_async_copy(result.at[:, s], store(k), sems.at[k, 3]))
        after_shell(s, k)
    for copy in stores:
        copy.wait()


def set_edge(ref, lead, shells, rows, before, after):
    for s in range(shells):
        ref[(*lead, s + 1, TILE - 1)] = before(s)
        ref[(*lead, s + 1, rows + TILE)] = after(s)


def start_all(copies):
    for copy in copies:
        copy.start()
    return copies


def load_messages(sources, lower_sources, slots, sems):
    lower = lax.axis_index("radial") < lax.axis_size("radial") - 1
    copies = lambda refs: [pltpu.make_async_copy(ref, slots.at[k], sems.at[k]) for k, ref in enumerate(refs)]
    pl.when(lower)(lambda: [copy.start() for copy in copies(lower_sources)] and None)
    pl.when(jnp.logical_not(lower))(lambda: [copy.start() for copy in copies(sources)] and None)
    return copies(sources)


def first_kernel(d, f, h, one, two, lower_one, lower_two, mine_one, mine_two, *refs):
    components, shells, rows, count = d.shape
    staged = (len(refs) - 13) // 2
    sources, refs = refs[:staged], refs[staged:]
    out, diagonal_out, ring_out, own_out, beside_out, *targets = refs[: 5 + staged]
    field, eta, force, result, messages, edges, diagonal, sems, more_sems = refs[5 + staged :]
    arrivals = load_messages((one, two), (lower_one, lower_two), messages, more_sems)
    lower = lax.axis_index("radial") == 0
    last, beyond = jnp.where(lower, shells - 1, 0), jnp.where(lower, shells + 1, 0)
    values = pl.ds(0, own_out.shape[1])
    copies = start_all(
        [
            pltpu.make_async_copy(mine.at[values], own_out.at[k], more_sems.at[4 + components + k])
            for k, mine in enumerate((mine_one, mine_two))
        ]
    )

    def before_first():
        block = pl.ds(TILE, rows)
        zeros = jnp.zeros((rows, count), jnp.float32)
        for c in range(components):
            field[c, beyond, block] = zeros
        eta[beyond, block] = zeros
        for copy in arrivals:
            copy.wait()
        before, after = by_parity(messages.at[0], messages.at[1])
        row = lambda message, kind: lambda s: message[kind * shells + s]
        for c in range(components):
            set_edge(field, (c,), shells, rows, row(before, c), row(after, c))
        set_edge(eta, (), shells, rows, row(before, components), row(after, components))
        for side, message in enumerate((before, after)):
            for k in range(components + 1):
                edges[side * (components + 1) + k] = jnp.where(
                    lower, message[(k + 1) * shells - 1], message[k * shells]
                )
        tail = ring_out.at[pl.ds(2 * (components + 1) * rows, edges.shape[0])]
        copies.extend(
            start_all(
                [
                    pltpu.make_async_copy(edges, tail, more_sems.at[2]),
                    pltpu.make_async_copy(messages, beside_out, more_sems.at[3]),
                ]
            )
        )

    def arrived(k):
        if k < shells - 1:
            return
        block = pl.ds(TILE, rows)
        sources = [field.at[c, last + 1, block] for c in range(components)] + [eta.at[last + 1, block]]
        copies.extend(
            start_all(
                [
                    pltpu.make_async_copy(source, ring_out.at[pl.ds(k * rows, rows)], more_sems.at[6 + components + k])
                    for k, source in enumerate(sources)
                ]
            )
        )

    def finish(s, first):
        part = pl.ds(first, TILE)
        middle, others = around(eta, (), s + 1, first + TILE)
        weights = [middle + other for other in others]
        zero = jnp.zeros_like(middle)
        weights[0] = jnp.where(lower, zero, weights[0])
        weights[1] = jnp.where(lower, weights[1], zero)
        diagonal[part] = 1.0 + functools.reduce(jnp.add, weights)
        for c in range(components):
            total = force[c, s, part]
            for weight, other in zip(weights, around(field, (c,), s + 1, first + TILE)[1]):
                total = total + weight * other
            result[c, s, part] = total

    def after_shell(s, k):
        if k == EARLY:
            copies.extend(
                start_all(
                    [
                        pltpu.make_async_copy(source, target, more_sems.at[8 + 3 * components + n])
                        for n, (source, target) in enumerate(zip(sources, targets))
                    ]
                )
            )
        if k == shells - 1:
            sums = [result.at[c, s] for c in range(components)] + [diagonal]
            copies.extend(
                start_all(
                    [
                        pltpu.make_async_copy(
                            source,
                            ring_out.at[pl.ds((components + 1 + n) * rows, rows)],
                            more_sems.at[7 + 2 * components + n],
                        )
                        for n, source in enumerate(sums)
                    ]
                    + [pltpu.make_async_copy(diagonal, diagonal_out, more_sems.at[0])]
                )
            )

    shell = shell_order(shells)
    sweep_shells(
        EARLY, lambda k: d.at[:, shell(k)], f, h, lambda k: out.at[:, k - EARLY],
        field, eta, force, result, sems, before_first, [], arrived, finish, after_shell,
    )
    for copy in copies:
        copy.wait()


def second_kernel(early, late, f, h, start, diagonal_from, ring, beside, own_from, *refs):
    components, shells, rows, count = f.shape
    staged = (len(refs) - 18) // 2
    mask_from, *sources = refs[: 1 + staged]
    out, token, mask_out, *targets = refs[1 + staged : 4 + 2 * staged]
    (
        field, eta, force, result, messages, edges, own, diagonal, raw, ring_diagonal, mask, ends, sems, more_sems
    ) = refs[4 + 2 * staged :]
    token[...] = jnp.zeros_like(token)
    tail = ring.at[pl.ds(2 * (components + 1) * rows, edges.shape[0])]
    arrivals = start_all(
        [
            pltpu.make_async_copy(beside, messages, more_sems.at[0]),
            pltpu.make_async_copy(tail, edges, more_sems.at[1]),
            pltpu.make_async_copy(own_from, own, more_sems.at[2]),
        ]
    )
    radial, lateral = lax.axis_index("radial"), lax.axis_index("lateral")
    lower = radial == 0
    last, beyond = jnp.where(lower, shells - 1, 0), jnp.where(lower, shells + 1, 0)
    block = pl.ds(TILE, rows)
    shell = shell_order(shells)
    from_ring = lambda k, target, sem: pltpu.make_async_copy(
        ring.at[pl.ds(k * rows, rows)], target, more_sems.at[sem]
    )
    last_loads = [
        pltpu.make_async_copy(start.at[:, last], raw.at[pl.ds(0, components)], more_sems.at[3]),
        pltpu.make_async_copy(diagonal_from, diagonal, more_sems.at[4]),
        *(from_ring(c, raw.at[components + c], 5 + c) for c in range(components)),
        from_ring(components, eta.at[beyond, block], 5 + components),
        *(
            from_ring(components + 1 + c, field.at[c, beyond, block], 6 + components + c)
            for c in range(components)
        ),
        from_ring(2 * components + 1, ring_diagonal, 6 + 2 * components),
    ]
    copies = []
    mask_copy = pltpu.make_async_copy(mask_from, mask, more_sems.at[7 + 2 * components])

    def before_first():
        for copy in arrivals:
            copy.wait()
        before, after = by_parity(messages.at[0], messages.at[1])
        pair = lambda k: jnp.concatenate(
            [before[k * shells : (k + 1) * shells], after[k * shells : (k + 1) * shells]], axis=0
        )
        place = row_number((2 * shells, count))
        zero = jnp.zeros((2 * shells, count), jnp.float32)
        shared = place % shells == last
        across_of = lambda k: jnp.where(
            place < shells, edges[pl.ds(k, 1)], edges[pl.ds(components + 1 + k, 1)]
        )
        inside = jnp.where(place < shells, lateral, lax.axis_size("lateral") - 1 - lateral) > 0
        mine = by_parity(own.at[0], own.at[1])
        own_row = lambda k: jnp.concatenate([part[k * shells : (k + 1) * shells] for part in mine], axis=0)
        middle = pair(components)
        weight = middle + own_row(components)
        across = jnp.where(shared, middle + across_of(components), zero)
        factor = RELAXATION / (pair(2 * components + 1) + weight + across)
        own_factor = RELAXATION / (own_row(2 * components + 1) + weight)
        for c in range(components):
            total = pair(components + 1 + c) + weight * own_row(c) + across * across_of(c)
            edge = jnp.where(inside, (1.0 - RELAXATION) * pair(c) + factor * total, zero)
            total = own_row(components + 1 + c) + weight * pair(c)
            ends[c] = (1.0 - RELAXATION) * own_row(c) + own_factor * total
            set_edge(field, (c,), shells, rows, lambda s: edge[s], lambda s: edge[shells + s])
        set_edge(eta, (), shells, rows, lambda s: middle[s], lambda s: middle[shells + s])

    def arrived(k):
        if k < EARLY:
            s = shell(k)
            for side, place in enumerate((TILE, TILE + rows - 1)):
                for c in range(components):
                    field[c, s + 1, pl.ds(place, 1)] = ends[c, pl.ds(side * shells + s, 1)]
        if k < shells - 1:
            return

        def tile(step, _):
            first = pl.multiple_of(step * TILE, TILE)
            part, place = pl.ds(first, TILE), pl.ds(first + TILE, TILE)
            weight = eta[last + 1, place] + eta[beyond, place]
            here, there = RELAXATION / (diagonal[part] + weight), RELAXATION / (ring_diagonal[part] + weight)
            for c in range(components):
                mine, other = raw[c, part], raw[components + c, part]
                field[c, last + 1, place] = (1.0 - RELAXATION) * mine + here * (
                    field[c, last + 1, place] + weight * other
                )
                field[c, beyond, place] = (1.0 - RELAXATION) * other + there * (
                    field[c, beyond, place] + weight * mine
                )
            return 0

        lax.fori_loop(0, rows // TILE, tile, 0)

    def finish(s, first):
        part = pl.ds(first, TILE)
        weights, factor = relax_weights(*around(eta, (), s + 1, first + TILE))
        for c in range(components):
            middle, others = around(field, (c,), s + 1, first + TILE)
            result[c, s, part] = relax(weights, factor, middle, others, force[c, s, part])

    def after_shell(s, k):
        if k == 0:
            copies.extend(
                start_all(
                    [
                        pltpu.make_async_copy(source, target, more_sems.at[8 + 2 * components + n])
                        for n, (source, target) in enumerate(zip(sources, targets))
                    ]
                )
            )
            mask_copy.start()
        if k == shells - 2:
            mask_copy.wait()
            mask_out[...] = mask[...].astype(jnp.float32).astype(jnp.bfloat16)

    sweep_shells(
        0, lambda k: early.at[:, k] if k < EARLY else late.at[:, k - EARLY], f, h, lambda k: out.at[:, shell(k)],
        field, eta, force, result, sems, before_first, last_loads, arrived, finish, after_shell,
    )
    for copy in copies:
        copy.wait()


def spectrum_kernel(orders, high, low, response, coefficients, out):
    radial = lax.axis_size("radial")
    width = coefficients.shape[0]
    bands, rows = orders.shape[0] // radial, high.shape[0] * radial // orders.shape[0]
    fourier = jnp.concatenate([unpack(orders[band * radial + radial - 1], width) for band in range(bands)], axis=0)
    near, far = split(fourier.T)
    spectrum = dot(near, high[...]) + dot(far, high[...]) + dot(near, low[...])
    coefficients[...] = spectrum
    own = response[:, :width]
    for place in range(1, radial):
        own = jnp.where(
            lax.axis_index("radial") == place, response[:, place * width : (place + 1) * width], own
        )
    near, far = split(own.T * spectrum)
    load = (dot_nt(near, high[...]) + dot_nt(far, high[...]) + dot_nt(near, low[...])).T
    for band in range(bands):
        block = pack(load[band * rows : (band + 1) * rows])
        for place in range(radial):
            out[band * radial + place] = block


def load_kernel(load, high, low, mask, out):
    blocks, rows = load.shape[0], out.shape[0]
    step, width = out.shape[1] // RADIX, high.shape[1] // blocks
    values = jnp.concatenate([unpack(load[block], width) for block in range(blocks)], axis=1)
    modes = values.shape[1] // 2
    kind, mirrored = order_class((1, values.shape[1]))
    crossed = jnp.concatenate([values[:, modes:], -values[:, :modes]], axis=1)
    crossed = jnp.where(mirrored, -crossed, crossed)
    zero = jnp.zeros_like(values)
    stack = [jnp.where(kind == k, values, zero) for k in range(RADIX // 2 + 1)]
    stack += [jnp.where(kind == k, crossed, zero) for k in range(1, RADIX // 2)]
    near, far = split(jnp.concatenate(stack, axis=0))
    total = dot_nt(near, high[...]) + dot_nt(far, high[...]) + dot_nt(near, low[...])
    for m, part in enumerate(unfold([total[k * rows : (k + 1) * rows] for k in range(RADIX)])):
        columns = slice(m * step, (m + 1) * step)
        out[:, columns] = part * mask[:, columns].astype(jnp.float32)


def cost(microseconds):
    return pl.CostEstimate(flops=0, bytes_accessed=3_000_000 * microseconds, transcendentals=0)


def hbm(values):
    return pltpu.with_memory_space_constraint(values, pltpu.HBM)


def shards(initial_displacement, force, viscosity, layer_index, response, ocean_mask):
    components, shells, rows, count = initial_displacement.shape
    radial, lateral = lax.axis_size("radial"), lax.axis_size("lateral")
    f32 = functools.partial(jax.ShapeDtypeStruct, dtype=jnp.float32)
    scratch = lambda *shape: pltpu.VMEM(shape, jnp.float32)
    in_hbm = lambda *shape: pltpu.HBM(shape, jnp.float32)
    width = 2 * MODES // (lateral * radial)
    first = [p for i in range(0, lateral - 1, 2) for p in ((i, i + 1), (i + 1, i))]
    second = [p for i in range(1, lateral - 1, 2) for p in ((i, i + 1), (i + 1, i))]
    both = ("lateral", "radial")
    top_only = lambda pairs: [(i * radial + radial - 1, j * radial + radial - 1) for i, j in pairs]

    lower_only = lambda pairs: [(i * radial + k, j * radial + k) for i, j in pairs for k in range(radial - 1)]
    swap = [(i, radial - 1 - i) for i in range(radial)]
    tensors = [hbm(a) for a in (initial_displacement, force, layer_index)]
    viscosity = hbm(viscosity)
    message = f32((2 * (components + 1) * shells, count))
    sides = lambda *shape: scratch(2, *shape)
    mine = pl.pallas_call(
        message_kernel,
        in_specs=[HBM] * 4,
        out_specs=[VMEM] * 2,
        out_shape=[message] * 2,
        scratch_shapes=[
            sides(components, shells, TILE, count),
            sides(components, shells, TILE, count),
            pltpu.VMEM((2, shells, TILE, count), jnp.int32),
            scratch(3 * components + 2, 2 * shells, count),
            pltpu.SMEM(viscosity.shape, jnp.float32),
            pltpu.SemaphoreType.DMA((7,)),
        ],
        compiler_params=params(16),
        cost_estimate=cost(20),
    )(viscosity, *tensors)
    two = lax.ppermute(mine[1], both, top_only(second))
    one = lax.ppermute(mine[0], both, top_only(first))
    eta, early, *surface = pl.pallas_call(
        viscosity_kernel,
        in_specs=[HBM] * 4 + [ANY],
        out_specs=[HBM, HBM, VMEM, VMEM, VMEM],
        out_shape=[
            in_hbm(shells, rows, count),
            in_hbm(components, EARLY, rows, count),
            f32((2, rows, count)),
            f32((2, rows, count)),
            f32((rows, count)),
        ],
        scratch_shapes=[
            pltpu.VMEM(layer_index.shape, jnp.int32),
            scratch(shells + 1, rows + 2 * TILE, count),
            scratch(components, EARLY + 2, rows + 2 * TILE, count),
            scratch(components, EARLY, rows, count),
            scratch(components, EARLY, rows, count),
            pltpu.SMEM(viscosity.shape, jnp.float32),
            pltpu.SemaphoreType.DMA((1 + shells,)),
            pltpu.SemaphoreType.DMA((3 * EARLY + 1 + shells,)),
        ],
        compiler_params=params(24),
        cost_estimate=cost(20),
    )(viscosity, *tensors, mine[0])
    lower_one, lower_two, eta = lax.optimization_barrier((*mine, eta))
    lower_one = lax.ppermute(lower_one, both, lower_only(first))
    lower_two = lax.ppermute(lower_two, both, lower_only(second))

    high, low = longitude_tables(count, MODES)
    high, low = hbm(jnp.asarray(high)), hbm(jnp.asarray(low))
    table = pltpu.VMEM(high.shape, jnp.bfloat16)
    packed = (lateral * radial, rows * width // max(128, width), max(128, width))
    orders = pl.pallas_call(
        functools.partial(surface_kernel, components=components),
        in_specs=[VMEM] * 7 + [HBM, HBM],
        out_specs=VMEM,
        out_shape=f32(packed),
        scratch_shapes=[
            scratch(3, rows + 2 * TILE, count),
            scratch(3, rows + 2 * TILE, count),
            scratch(rows, count),
            table,
            table,
            pltpu.SemaphoreType.DMA((2,)),
        ],
        compiler_params=params(16),
        cost_estimate=cost(200),
    )(*surface, *mine, one, two, high, low)
    eta, _ = lax.optimization_barrier((eta, orders))
    orders = lax.all_to_all(orders, both, split_axis=0, concat_axis=0, tiled=True)
    eta = hbm(eta)

    sweep_scratch = [
        scratch(components, shells + 2, rows + 2 * TILE, count),
        scratch(shells + 2, rows + 2 * TILE, count),
        scratch(components, shells, rows, count),
        scratch(components, shells, rows, count),
    ]
    sweep_sems = pltpu.SemaphoreType.DMA((shells, 4))
    point_high, point_low = colatitude_tables(rows * lateral, MODES)
    stages = [jnp.asarray(point_high), jnp.asarray(point_low)] + [response]
    ring_rows = 2 * (components + 1) * (rows + 1)
    sweep_scratch += [
        sides(*message.shape),
        scratch(2 * (components + 1), count),
    ]
    own_shape = (2, *message.shape)
    late, diagonal, ring, own, beside, *staged = pl.pallas_call(
        first_kernel,
        in_specs=[HBM] * 3 + [ANY] * 6 + [HBM] * len(stages),
        out_specs=[HBM] * 5 + [VMEM] * len(stages),
        out_shape=[
            in_hbm(components, shells - EARLY, rows, count),
            in_hbm(rows, count),
            in_hbm(ring_rows, count),
            in_hbm(*own_shape),
            in_hbm(2, *message.shape),
            *(jax.ShapeDtypeStruct(a.shape, a.dtype) for a in stages),
        ],
        scratch_shapes=[
            *sweep_scratch,
            scratch(rows, count),
            sweep_sems,
            pltpu.SemaphoreType.DMA((8 + 3 * components + len(stages),)),
        ],
        compiler_params=params(28),
        cost_estimate=cost(50),
    )(*tensors[:2], hbm(eta), one, two, lower_one, lower_two, *mine, *(hbm(a) for a in stages))
    ring, orders = lax.optimization_barrier((ring, orders))
    ring = lax.ppermute(ring, "radial", swap)
    coefficients, load = pl.pallas_call(
        spectrum_kernel,
        in_specs=[VMEM] * 4,
        out_specs=[VMEM, VMEM],
        out_shape=[f32((width, MODES)), f32(packed)],
        compiler_params=params(16),
        cost_estimate=cost(200),
    )(orders, *staged)
    eta, load = lax.optimization_barrier((eta, load))
    load = lax.all_to_all(load, both, split_axis=0, concat_axis=0, tiled=True)

    stages = [high, low]
    displacement, token, mask, *staged = pl.pallas_call(
        second_kernel,
        in_specs=[HBM] * 6 + [ANY] + [HBM] * (3 + len(stages)),
        out_specs=[HBM, VMEM, VMEM] + [VMEM] * len(stages),
        out_shape=[
            in_hbm(*initial_displacement.shape),
            f32((TILE, 128)),
            jax.ShapeDtypeStruct(ocean_mask.shape, jnp.bfloat16),
            *(jax.ShapeDtypeStruct(a.shape, a.dtype) for a in stages),
        ],
        scratch_shapes=[
            *sweep_scratch,
            scratch(*own_shape),
            scratch(rows, count),
            scratch(2 * components, rows, count),
            scratch(rows, count),
            pltpu.VMEM(ocean_mask.shape, ocean_mask.dtype),
            scratch(components, 2 * shells, count),
            sweep_sems,
            pltpu.SemaphoreType.DMA((8 + 2 * components + len(stages),)),
        ],
        compiler_params=params(28),
        cost_estimate=cost(50),
    )(
        *(hbm(a) for a in (early, late, tensors[1], eta, tensors[0], diagonal)),
        ring,
        *(hbm(a) for a in (beside, own, ocean_mask)),
        *stages,
    )

    sea_load = pl.pallas_call(
        load_kernel,
        in_specs=[VMEM] * 4,
        out_specs=VMEM,
        out_shape=f32((rows, count)),
        compiler_params=params(20),
        cost_estimate=cost(3),
    )(load, *staged, mask)
    return (displacement, coefficients.T, sea_load)


def solution(mesh):
    in_specs = (
        P("member", "radial", "lateral", None),
        P("member", "radial", "lateral", None),
        P("member"),
        P("radial", "lateral", None),
        P(None, "lateral"),
        P("lateral", None),
    )
    out_specs = (
        P("member", "radial", "lateral", None),
        P("member", ("lateral", "radial")),
        P("lateral", "member"),
    )
    return jax.shard_map(shards, mesh=mesh, in_specs=in_specs, out_specs=out_specs, check_vma=False)
```

```python
import functools
import math

import jax
import jax.numpy as jnp
import ml_dtypes
import numpy as np
from jax import lax
from jax.experimental import pallas as pl
from jax.experimental.pallas import tpu as pltpu
from jax.sharding import PartitionSpec as P

MODES = 512
RELAXATION = 0.8
TILE = 8
RADIX = 8
EARLY = 2
MIB = 1 << 20
ANY = pl.BlockSpec(memory_space=pl.ANY)
HBM = pl.BlockSpec(memory_space=pltpu.HBM)
SMEM = pl.BlockSpec(memory_space=pltpu.SMEM)
VMEM = pl.BlockSpec(memory_space=pltpu.VMEM)


def params(mib):
    return pltpu.CompilerParams(vmem_limit_bytes=mib * MIB)


def halves(table):
    high = table.astype(ml_dtypes.bfloat16)
    low = (table - high.astype(np.float64)).astype(ml_dtypes.bfloat16)
    return high, low


@functools.lru_cache
def longitude_tables(count, modes):
    points = np.arange(count // RADIX, dtype=np.int64)[:, None]
    orders = np.arange(modes, dtype=np.int64)[None, :]
    angle = (2.0 * math.pi / count) * (points * orders % count)
    table = np.concatenate([np.cos(angle), np.sin(angle)], axis=1) * math.sqrt(2.0 / count)
    return halves(table)


@functools.lru_cache
def colatitude_tables(count, modes):
    points = np.arange(count, dtype=np.int64)[:, None]
    waves = np.arange(modes, dtype=np.int64)[None, :]
    phase = waves * (2 * points + 1) % (4 * count)
    return halves(np.cos(math.pi / (2 * count) * phase) * math.sqrt(2.0 / count))


def split(values):
    high = values.astype(jnp.bfloat16)
    return high, (values - high.astype(jnp.float32)).astype(jnp.bfloat16)


def dot(a, b):
    return jnp.dot(a, b, preferred_element_type=jnp.float32)


def pack(block):
    rows, width = block.shape
    groups = max(1, 128 // width)
    rows //= groups
    return jnp.concatenate([block[k * rows : (k + 1) * rows] for k in range(groups)], axis=1)


def unpack(block, width):
    groups = max(1, 128 // width)
    return jnp.concatenate([block[:, k * width : (k + 1) * width] for k in range(groups)], axis=0)


def weighted_sum(terms):
    total = None
    for factor, values in terms:
        factor = round(factor, 15)
        if factor == 0.0:
            continue
        part = values if abs(factor) == 1.0 else abs(factor) * values
        if total is None:
            total = part if factor > 0 else -part
        else:
            total = total + part if factor > 0 else total - part
    return total


def turn(number):
    angle = 2.0 * math.pi * (number % RADIX) / RADIX
    return math.cos(angle), math.sin(angle)


def fold(values):
    step = values.shape[1] // RADIX
    parts = [values[:, m * step : (m + 1) * step] for m in range(RADIX)]
    cosines = [[(turn(k * m)[0], part) for m, part in enumerate(parts)] for k in range(RADIX // 2 + 1)]
    sines = [[(turn(k * m)[1], part) for m, part in enumerate(parts)] for k in range(1, RADIX // 2)]
    return [weighted_sum(terms) for terms in cosines + sines]


def unfold(blocks):
    cosines, sines = blocks[: RADIX // 2 + 1], blocks[RADIX // 2 + 1 :]
    return [
        weighted_sum(
            [(turn(k * m)[0], block) for k, block in enumerate(cosines)]
            + [(turn(k * m)[1], block) for k, block in enumerate(sines, 1)]
        )
        for m in range(RADIX)
    ]


def order_class(shape):
    order = lax.broadcasted_iota(jnp.int32, shape, len(shape) - 1) % RADIX
    mirrored = order > RADIX // 2
    return jnp.where(mirrored, RADIX - order, order), mirrored


def dot_nt(a, b):
    return lax.dot_general(a, b, (((1,), (1,)), ((), ())), preferred_element_type=jnp.float32)


def half_viscosity(index, viscosity_ref):
    values = [0.5 * viscosity_ref[k] for k in range(viscosity_ref.shape[0])]
    bit = 1
    while len(values) > 1:
        odd = (index & bit) != 0
        if len(values) % 2:
            values.append(values[-1])
        values = [jnp.where(odd, b, a) for a, b in zip(values[::2], values[1::2])]
        bit *= 2
    return values[0]


def row_number(shape):
    return lax.broadcasted_iota(jnp.int32, shape, 0)


def north_of(above, middle):
    return pltpu.roll(jnp.where(row_number(middle.shape) == TILE - 1, above, middle), 1, 0)


def south_of(below, middle):
    return pltpu.roll(jnp.where(row_number(middle.shape) == 0, below, middle), TILE - 1, 0)


def east_of(values):
    return pltpu.roll(values, values.shape[-1] - 1, values.ndim - 1)


def west_of(values):
    return pltpu.roll(values, 1, values.ndim - 1)


def relax_weights(middle, others):
    weights = [middle + other for other in others]
    diagonal = 1.0 + functools.reduce(jnp.add, weights)
    return weights, RELAXATION / diagonal


def relax(weights, factor, middle, others, force):
    total = force
    for weight, other in zip(weights, others):
        total = total + weight * other
    return (1.0 - RELAXATION) * middle + factor * total


def around(ref, lead, shell, start):
    rows = lambda first: pl.ds(pl.multiple_of(first, TILE), TILE)
    middle = ref[(*lead, shell, rows(start))]
    return middle, [
        ref[(*lead, shell + 1, rows(start))],
        ref[(*lead, shell - 1, rows(start))],
        south_of(ref[(*lead, shell, rows(start + TILE))], middle),
        north_of(ref[(*lead, shell, rows(start - TILE))], middle),
        west_of(middle),
        east_of(middle),
    ]


def message_kernel(viscosity_from, d, f, index, one, two, fields, forces, layers, rows_of, viscosity, sems):
    components, shells, rows, count = d.shape
    copies = [pltpu.make_async_copy(viscosity_from, viscosity, sems.at[0])]
    for side, start in enumerate((0, rows - TILE)):
        part = pl.ds(start, TILE)
        copies += [
            pltpu.make_async_copy(index.at[:, part], layers.at[side], sems.at[1 + side]),
            pltpu.make_async_copy(d.at[:, :, part], fields.at[side], sems.at[3 + side]),
            pltpu.make_async_copy(f.at[:, :, part], forces.at[side], sems.at[5 + side]),
        ]
    for copy in copies:
        copy.start()
    for copy in copies[:2] + copies[4:5]:
        copy.wait()
    near_eta, far_eta = 2 * components, 2 * components + 1
    for side, near, far in ((0, 0, 1), (1, TILE - 1, TILE - 2)):
        for s in range(shells):
            eta = half_viscosity(layers[side, s], viscosity)
            rows_of[near_eta, side * shells + s] = eta[near]
            rows_of[far_eta, side * shells + s] = eta[far]
    for copy in copies[2:4] + copies[5:]:
        copy.wait()
    for side, near, far in ((0, 0, 1), (1, TILE - 1, TILE - 2)):
        for s in range(shells):
            for c in range(components):
                rows_of[c, side * shells + s] = fields[side, c, s, near]
                rows_of[components + c, side * shells + s] = fields[side, c, s, far]
                rows_of[far_eta + 1 + c, side * shells + s] = forces[side, c, s, near]
    radial = lax.axis_index("radial")
    place = row_number((2 * shells, count)) % shells
    highest, lowest = place == shells - 1, place == 0
    zero = jnp.zeros((2 * shells, count), jnp.float32)

    def beside(near, far):
        middle = rows_of[near]
        return middle, [
            jnp.where(highest, zero, pltpu.roll(middle, 2 * shells - 1, 0)),
            jnp.where(lowest, zero, pltpu.roll(middle, 1, 0)),
            rows_of[far],
            west_of(middle),
            east_of(middle),
        ]

    eta, others = beside(near_eta, far_eta)
    weights = [eta + other for other in others]
    inside = (radial < lax.axis_size("radial") - 1, radial > 0)
    weights[0] = jnp.where(jnp.logical_and(highest, inside[0]), zero, weights[0])
    weights[1] = jnp.where(jnp.logical_and(lowest, inside[1]), zero, weights[1])
    diagonal = 1.0 + functools.reduce(jnp.add, weights)
    values, sums = [], []
    for c in range(components):
        middle, others = beside(c, components + c)
        total = rows_of[far_eta + 1 + c]
        for weight, other in zip(weights, others):
            total = total + weight * other
        values.append(middle)
        sums.append(total)
    for place, field in enumerate(values + [eta] + sums + [diagonal]):
        both = pltpu.roll(field, shells, 0)
        one[pl.ds(place * shells, shells)] = both[:shells]
        two[pl.ds(place * shells, shells)] = both[shells:]


def shell_order(shells):
    lower = lax.axis_index("radial") == 0
    return lambda k: jnp.where(lower, k, shells - 1 - k)


def viscosity_kernel(
    viscosity_from, d, f, index_from, token, eta_out, out, surface_swept, surface_eta, surface_force,
    index, eta, field, force, result, viscosity, sems, more_sems,
):
    del token
    _, shells, rows, count = d.shape
    components = d.shape[0]
    block = pl.ds(TILE, rows)
    shell = shell_order(shells)
    value_copy = pltpu.make_async_copy(viscosity_from, viscosity, sems.at[shells])
    layers = [pltpu.make_async_copy(index_from.at[shell(k)], index.at[k], sems.at[k]) for k in range(shells)]
    fields = [
        pltpu.make_async_copy(d.at[:, shell(k)], field.at[:, k + 1, block], more_sems.at[k]) for k in range(EARLY + 1)
    ]
    forces = [
        pltpu.make_async_copy(f.at[:, shell(k)], force.at[:, k], more_sems.at[EARLY + 1 + k]) for k in range(EARLY)
    ]
    start_all([value_copy, *layers, *fields, *forces])
    zeros = jnp.zeros((rows, count), jnp.float32)
    for c in range(components):
        field[c, 0, block] = zeros
    eta[0, block] = zeros
    value_copy.wait()
    stores = []
    for k in range(shells):
        layers[k].wait()

        def lookup(step, _):
            start = pl.multiple_of(step * TILE, TILE)
            eta[k + 1, pl.ds(start + TILE, TILE)] = half_viscosity(index[k, pl.ds(start, TILE)], viscosity)
            return 0

        lax.fori_loop(0, rows // TILE, lookup, 0)
        stores += start_all(
            [pltpu.make_async_copy(eta.at[k + 1, block], eta_out.at[shell(k)], more_sems.at[2 * EARLY + 1 + k])]
        )
    for k in range(EARLY):
        for copy in (fields[: EARLY + 1] if k == 0 else []) + forces[k : k + 1]:
            copy.wait()

        def sweep(step, _):
            start = pl.multiple_of(step * TILE, TILE)
            part = pl.ds(start, TILE)
            weights, factor = relax_weights(*around(eta, (), k + 1, start + TILE))
            for c in range(components):
                middle, others = around(field, (c,), k + 1, start + TILE)
                result[c, k, part] = relax(weights, factor, middle, others, force[c, k, part])
            surface_swept[1 - k, part] = result[0, k, part]
            surface_eta[1 - k, part] = eta[k + 1, pl.ds(start + TILE, TILE)]
            if k == 0:
                surface_force[part] = force[0, 0, part]
            sem = more_sems.at[2 * EARLY + 1 + shells + k]
            pltpu.make_async_copy(result.at[:, k, part], out.at[:, k, part], sem).start()
            return 0

        lax.fori_loop(0, rows // TILE, sweep, 0, unroll=2)
        stores.append(pltpu.make_async_copy(result.at[:, k], out.at[:, k], more_sems.at[2 * EARLY + 1 + shells + k]))
    for copy in stores:
        copy.wait()


def surface_kernel(
    surface_swept, surface_eta, force, own_one, own_two, one, two, high_from, low_from, out,
    swept, eta, surface, high, low, sems, components,
):
    rows, count = force.shape

    @pl.when(lax.axis_index("radial") == lax.axis_size("radial") - 1)
    def _():
        tables = start_all(
            [
                pltpu.make_async_copy(high_from, high, sems.at[0]),
                pltpu.make_async_copy(low_from, low, sems.at[1]),
            ]
        )
        block = pl.ds(TILE, rows)
        for k in range(2):
            swept[k, block] = surface_swept[k]
            eta[k, block] = surface_eta[k]
        swept[2, block] = jnp.zeros((rows, count), jnp.float32)
        eta[2, block] = jnp.zeros((rows, count), jnp.float32)
        fields = one.shape[0]
        shells = fields // (2 * (components + 1))
        lateral = lax.axis_index("lateral")
        inside = (lateral > 0, lateral < lax.axis_size("lateral") - 1)
        for beside, own, place, own_place, there in zip(
            (one[...], two[...]), (own_two[...], own_one[...]), (TILE - 1, rows + TILE), (TILE, rows + TILE - 1), inside
        ):
            for k in range(2):
                row = lambda message, kind: message[kind * shells + shells - 2 + k : kind * shells + shells - 1 + k]
                weight = row(beside, components) + row(own, components)

                def finish(message, other):
                    total = row(message, components + 1) + weight * row(other, 0)
                    factor = RELAXATION / (row(message, 2 * components + 1) + weight)
                    return (1.0 - RELAXATION) * row(message, 0) + factor * total

                swept[k, pl.ds(own_place, 1)] = finish(own, beside)
                if k == 1:
                    edge = finish(beside, own)
                    swept[k, pl.ds(place, 1)] = jnp.where(there, edge, jnp.zeros_like(edge))
                    eta[k, pl.ds(place, 1)] = row(beside, components)

        def second(step, _):
            start = pl.multiple_of(step * TILE, TILE)
            weights, factor = relax_weights(*around(eta, (), 1, start + TILE))
            middle, others = around(swept, (), 1, start + TILE)
            surface[pl.ds(start, TILE)] = relax(weights, factor, middle, others, force[pl.ds(start, TILE)])
            return 0

        lax.fori_loop(0, rows // TILE, second, 0, unroll=2)
        near, far = split(jnp.concatenate(fold(surface[...]), axis=0))
        for copy in tables:
            copy.wait()
        total = dot(near, high[...]) + dot(far, high[...]) + dot(near, low[...])
        blocks = [total[k * rows : (k + 1) * rows] for k in range(RADIX)]
        kind, mirrored = order_class((1, total.shape[1]))
        cosine, sine = blocks[0], jnp.zeros_like(blocks[0])
        for k in range(1, RADIX // 2 + 1):
            cosine = jnp.where(kind == k, blocks[k], cosine)
        for k in range(1, RADIX // 2):
            sine = jnp.where(kind == k, blocks[RADIX // 2 + k], sine)
        sine = jnp.where(mirrored, -sine, sine)
        modes = total.shape[1] // 2
        fourier = jnp.concatenate(
            [cosine[:, :modes] - sine[:, modes:], cosine[:, modes:] + sine[:, :modes]], axis=1
        )
        blocks = out.shape[0]
        width = fourier.shape[1] // blocks
        for block in range(blocks):
            out[block] = pack(fourier[:, block * width : (block + 1) * width])


def sweep_shells(
    begin, source, f, h, store, field, eta, force, result, sems, before_first, last_loads, arrived, finish, after_shell
):
    components, shells, rows, count = f.shape
    inner = pl.ds(TILE, rows)
    shell = shell_order(shells)

    def field_loads(k):
        s = shell(k)
        return [
            pltpu.make_async_copy(source(k), field.at[:, s + 1, inner], sems.at[k, 0]),
            pltpu.make_async_copy(h.at[s], eta.at[s + 1, inner], sems.at[k, 1]),
            *(last_loads if k == shells - 1 else []),
        ]

    def force_load(k):
        return [pltpu.make_async_copy(f.at[:, shell(k)], force.at[:, shell(k)], sems.at[k, 2])]

    loads = {k: start_all(field_loads(k)) for k in range(max(begin - 1, 0), begin + 2)}
    forces = {begin: start_all(force_load(begin))}
    if begin == 0:
        nothing = jnp.where(lax.axis_index("radial") == 0, 0, shells + 1)
        zeros = jnp.zeros((rows, count), jnp.float32)
        for c in range(components):
            field[c, nothing, inner] = zeros
        eta[nothing, inner] = zeros
    before_first()

    def start_until(k):
        for ahead in range(begin, shells):
            if ahead <= k and ahead not in loads:
                loads[ahead] = start_all(field_loads(ahead))
            if ahead < k and ahead not in forces:
                forces[ahead] = start_all(force_load(ahead))

    start_until(begin + 2)
    stores, there = [], set()
    for k in range(begin, shells):
        s = shell(k)
        start_until(k + 3)
        for near in range(max(k - 1, 0), min(k + 2, shells)):
            if near not in there:
                there.add(near)
                for copy in loads[near]:
                    copy.wait()
                arrived(near)
        for copy in forces[k]:
            copy.wait()

        def tile(step, _):
            first = pl.multiple_of(step * TILE, TILE)
            part = pl.ds(first, TILE)
            if k == shells - 1:
                finish(s, first)
            else:
                weights, factor = relax_weights(*around(eta, (), s + 1, first + TILE))
                for c in range(components):
                    middle, others = around(field, (c,), s + 1, first + TILE)
                    result[c, s, part] = relax(weights, factor, middle, others, force[c, s, part])
            pltpu.make_async_copy(result.at[:, s, part], store(k).at[:, part], sems.at[k, 3]).start()
            return 0

        lax.fori_loop(0, rows // TILE, tile, 0, unroll=2)
        stores.append(pltpu.make_async_copy(result.at[:, s], store(k), sems.at[k, 3]))
        after_shell(s, k)
    for copy in stores:
        copy.wait()


def set_edge(ref, lead, shells, rows, before, after):
    for s in range(shells):
        ref[(*lead, s + 1, TILE - 1)] = before(s)
        ref[(*lead, s + 1, rows + TILE)] = after(s)


def start_all(copies):
    for copy in copies:
        copy.start()
    return copies


def load_messages(sources, lower_sources, slots, sems):
    lower = lax.axis_index("radial") < lax.axis_size("radial") - 1
    copies = lambda refs: [pltpu.make_async_copy(ref, slots.at[k], sems.at[k]) for k, ref in enumerate(refs)]
    pl.when(lower)(lambda: [copy.start() for copy in copies(lower_sources)] and None)
    pl.when(jnp.logical_not(lower))(lambda: [copy.start() for copy in copies(sources)] and None)
    return copies(sources)


def first_kernel(d, f, h, one, two, lower_one, lower_two, mine_one, mine_two, *refs):
    components, shells, rows, count = d.shape
    staged = (len(refs) - 13) // 2
    sources, refs = refs[:staged], refs[staged:]
    out, diagonal_out, ring_out, own_out, beside_out, *targets = refs[: 5 + staged]
    field, eta, force, result, messages, edges, diagonal, sems, more_sems = refs[5 + staged :]
    arrivals = load_messages((one, two), (lower_one, lower_two), messages, more_sems)
    lower = lax.axis_index("radial") == 0
    last, beyond = jnp.where(lower, shells - 1, 0), jnp.where(lower, shells + 1, 0)
    values = pl.ds(0, own_out.shape[1])
    copies = start_all(
        [
            pltpu.make_async_copy(mine.at[values], own_out.at[k], more_sems.at[4 + components + k])
            for k, mine in enumerate((mine_one, mine_two))
        ]
    )

    def before_first():
        block = pl.ds(TILE, rows)
        zeros = jnp.zeros((rows, count), jnp.float32)
        for c in range(components):
            field[c, beyond, block] = zeros
        eta[beyond, block] = zeros
        for copy in arrivals:
            copy.wait()
        before, after = messages[0], messages[1]
        row = lambda message, kind: lambda s: message[kind * shells + s]
        for c in range(components):
            set_edge(field, (c,), shells, rows, row(before, c), row(after, c))
        set_edge(eta, (), shells, rows, row(before, components), row(after, components))
        for side, message in enumerate((before, after)):
            for k in range(components + 1):
                edges[side * (components + 1) + k] = jnp.where(
                    lower, message[(k + 1) * shells - 1], message[k * shells]
                )
        tail = ring_out.at[pl.ds(2 * (components + 1) * rows, edges.shape[0])]
        copies.extend(
            start_all(
                [
                    pltpu.make_async_copy(edges, tail, more_sems.at[2]),
                    pltpu.make_async_copy(messages, beside_out, more_sems.at[3]),
                ]
            )
        )

    def arrived(k):
        if k < shells - 1:
            return
        block = pl.ds(TILE, rows)
        sources = [field.at[c, last + 1, block] for c in range(components)] + [eta.at[last + 1, block]]
        copies.extend(
            start_all(
                [
                    pltpu.make_async_copy(source, ring_out.at[pl.ds(k * rows, rows)], more_sems.at[6 + components + k])
                    for k, source in enumerate(sources)
                ]
            )
        )

    def finish(s, first):
        part = pl.ds(first, TILE)
        middle, others = around(eta, (), s + 1, first + TILE)
        weights = [middle + other for other in others]
        zero = jnp.zeros_like(middle)
        weights[0] = jnp.where(lower, zero, weights[0])
        weights[1] = jnp.where(lower, weights[1], zero)
        diagonal[part] = 1.0 + functools.reduce(jnp.add, weights)
        for c in range(components):
            total = force[c, s, part]
            for weight, other in zip(weights, around(field, (c,), s + 1, first + TILE)[1]):
                total = total + weight * other
            result[c, s, part] = total

    def after_shell(s, k):
        if k == EARLY:
            copies.extend(
                start_all(
                    [
                        pltpu.make_async_copy(source, target, more_sems.at[8 + 3 * components + n])
                        for n, (source, target) in enumerate(zip(sources, targets))
                    ]
                )
            )
        if k == shells - 1:
            sums = [result.at[c, s] for c in range(components)] + [diagonal]
            copies.extend(
                start_all(
                    [
                        pltpu.make_async_copy(
                            source,
                            ring_out.at[pl.ds((components + 1 + n) * rows, rows)],
                            more_sems.at[7 + 2 * components + n],
                        )
                        for n, source in enumerate(sums)
                    ]
                    + [pltpu.make_async_copy(diagonal, diagonal_out, more_sems.at[0])]
                )
            )

    shell = shell_order(shells)
    sweep_shells(
        EARLY, lambda k: d.at[:, shell(k)], f, h, lambda k: out.at[:, k - EARLY],
        field, eta, force, result, sems, before_first, [], arrived, finish, after_shell,
    )
    for copy in copies:
        copy.wait()


def second_kernel(early, late, f, h, start, diagonal_from, ring, beside, own_from, *refs):
    components, shells, rows, count = f.shape
    staged = (len(refs) - 18) // 2
    mask_from, *sources = refs[: 1 + staged]
    out, token, mask_out, *targets = refs[1 + staged : 4 + 2 * staged]
    (
        field, eta, force, result, messages, edges, own, diagonal, raw, ring_diagonal, mask, ends, sems, more_sems
    ) = refs[4 + 2 * staged :]
    token[...] = jnp.zeros_like(token)
    tail = ring.at[pl.ds(2 * (components + 1) * rows, edges.shape[0])]
    arrivals = start_all(
        [
            pltpu.make_async_copy(beside, messages, more_sems.at[0]),
            pltpu.make_async_copy(tail, edges, more_sems.at[1]),
            pltpu.make_async_copy(own_from, own, more_sems.at[2]),
        ]
    )
    radial, lateral = lax.axis_index("radial"), lax.axis_index("lateral")
    lower = radial == 0
    last, beyond = jnp.where(lower, shells - 1, 0), jnp.where(lower, shells + 1, 0)
    block = pl.ds(TILE, rows)
    shell = shell_order(shells)
    from_ring = lambda k, target, sem: pltpu.make_async_copy(
        ring.at[pl.ds(k * rows, rows)], target, more_sems.at[sem]
    )
    last_loads = [
        pltpu.make_async_copy(start.at[:, last], raw.at[pl.ds(0, components)], more_sems.at[3]),
        pltpu.make_async_copy(diagonal_from, diagonal, more_sems.at[4]),
        *(from_ring(c, raw.at[components + c], 5 + c) for c in range(components)),
        from_ring(components, eta.at[beyond, block], 5 + components),
        *(
            from_ring(components + 1 + c, field.at[c, beyond, block], 6 + components + c)
            for c in range(components)
        ),
        from_ring(2 * components + 1, ring_diagonal, 6 + 2 * components),
    ]
    copies = []
    mask_copy = pltpu.make_async_copy(mask_from, mask, more_sems.at[7 + 2 * components])

    def before_first():
        for copy in arrivals:
            copy.wait()
        before, after = messages[0], messages[1]
        pair = lambda k: jnp.concatenate(
            [before[k * shells : (k + 1) * shells], after[k * shells : (k + 1) * shells]], axis=0
        )
        place = row_number((2 * shells, count))
        zero = jnp.zeros((2 * shells, count), jnp.float32)
        shared = place % shells == last
        across_of = lambda k: jnp.where(
            place < shells, edges[pl.ds(k, 1)], edges[pl.ds(components + 1 + k, 1)]
        )
        inside = jnp.where(place < shells, lateral, lax.axis_size("lateral") - 1 - lateral) > 0
        mine = (own[1], own[0])
        own_row = lambda k: jnp.concatenate([part[k * shells : (k + 1) * shells] for part in mine], axis=0)
        middle = pair(components)
        weight = middle + own_row(components)
        across = jnp.where(shared, middle + across_of(components), zero)
        factor = RELAXATION / (pair(2 * components + 1) + weight + across)
        own_factor = RELAXATION / (own_row(2 * components + 1) + weight)
        for c in range(components):
            total = pair(components + 1 + c) + weight * own_row(c) + across * across_of(c)
            edge = jnp.where(inside, (1.0 - RELAXATION) * pair(c) + factor * total, zero)
            total = own_row(components + 1 + c) + weight * pair(c)
            ends[c] = (1.0 - RELAXATION) * own_row(c) + own_factor * total
            set_edge(field, (c,), shells, rows, lambda s: edge[s], lambda s: edge[shells + s])
        set_edge(eta, (), shells, rows, lambda s: middle[s], lambda s: middle[shells + s])

    def arrived(k):
        if k < EARLY:
            s = shell(k)
            for side, place in enumerate((TILE, TILE + rows - 1)):
                for c in range(components):
                    field[c, s + 1, pl.ds(place, 1)] = ends[c, pl.ds(side * shells + s, 1)]
        if k < shells - 1:
            return

        def tile(step, _):
            first = pl.multiple_of(step * TILE, TILE)
            part, place = pl.ds(first, TILE), pl.ds(first + TILE, TILE)
            weight = eta[last + 1, place] + eta[beyond, place]
            here, there = RELAXATION / (diagonal[part] + weight), RELAXATION / (ring_diagonal[part] + weight)
            for c in range(components):
                mine, other = raw[c, part], raw[components + c, part]
                field[c, last + 1, place] = (1.0 - RELAXATION) * mine + here * (
                    field[c, last + 1, place] + weight * other
                )
                field[c, beyond, place] = (1.0 - RELAXATION) * other + there * (
                    field[c, beyond, place] + weight * mine
                )
            return 0

        lax.fori_loop(0, rows // TILE, tile, 0)

    def finish(s, first):
        part = pl.ds(first, TILE)
        weights, factor = relax_weights(*around(eta, (), s + 1, first + TILE))
        for c in range(components):
            middle, others = around(field, (c,), s + 1, first + TILE)
            result[c, s, part] = relax(weights, factor, middle, others, force[c, s, part])

    def after_shell(s, k):
        if k == 0:
            copies.extend(
                start_all(
                    [
                        pltpu.make_async_copy(source, target, more_sems.at[8 + 2 * components + n])
                        for n, (source, target) in enumerate(zip(sources, targets))
                    ]
                )
            )
            mask_copy.start()
        if k == shells - 2:
            mask_copy.wait()
            mask_out[...] = mask[...].astype(jnp.float32).astype(jnp.bfloat16)

    sweep_shells(
        0, lambda k: early.at[:, k] if k < EARLY else late.at[:, k - EARLY], f, h, lambda k: out.at[:, shell(k)],
        field, eta, force, result, sems, before_first, last_loads, arrived, finish, after_shell,
    )
    for copy in copies:
        copy.wait()


def spectrum_kernel(orders, high, low, response, coefficients, out):
    radial = lax.axis_size("radial")
    width = coefficients.shape[0]
    bands, rows = orders.shape[0] // radial, high.shape[0] * radial // orders.shape[0]
    fourier = jnp.concatenate([unpack(orders[band * radial + radial - 1], width) for band in range(bands)], axis=0)
    near, far = split(fourier.T)
    spectrum = dot(near, high[...]) + dot(far, high[...]) + dot(near, low[...])
    coefficients[...] = spectrum
    own = response[:, :width]
    for place in range(1, radial):
        own = jnp.where(
            lax.axis_index("radial") == place, response[:, place * width : (place + 1) * width], own
        )
    near, far = split(own.T * spectrum)
    load = (dot_nt(near, high[...]) + dot_nt(far, high[...]) + dot_nt(near, low[...])).T
    for band in range(bands):
        block = pack(load[band * rows : (band + 1) * rows])
        for place in range(radial):
            out[band * radial + place] = block


def load_kernel(load, high, low, mask, out):
    blocks, rows = load.shape[0], out.shape[0]
    step, width = out.shape[1] // RADIX, high.shape[1] // blocks
    values = jnp.concatenate([unpack(load[block], width) for block in range(blocks)], axis=1)
    modes = values.shape[1] // 2
    kind, mirrored = order_class((1, values.shape[1]))
    crossed = jnp.concatenate([values[:, modes:], -values[:, :modes]], axis=1)
    crossed = jnp.where(mirrored, -crossed, crossed)
    zero = jnp.zeros_like(values)
    stack = [jnp.where(kind == k, values, zero) for k in range(RADIX // 2 + 1)]
    stack += [jnp.where(kind == k, crossed, zero) for k in range(1, RADIX // 2)]
    near, far = split(jnp.concatenate(stack, axis=0))
    total = dot_nt(near, high[...]) + dot_nt(far, high[...]) + dot_nt(near, low[...])
    for m, part in enumerate(unfold([total[k * rows : (k + 1) * rows] for k in range(RADIX)])):
        columns = slice(m * step, (m + 1) * step)
        out[:, columns] = part * mask[:, columns].astype(jnp.float32)


def cost(microseconds):
    return pl.CostEstimate(flops=0, bytes_accessed=3_000_000 * microseconds, transcendentals=0)


def hbm(values):
    return pltpu.with_memory_space_constraint(values, pltpu.HBM)


def shards(initial_displacement, force, viscosity, layer_index, response, ocean_mask):
    components, shells, rows, count = initial_displacement.shape
    radial, lateral = lax.axis_size("radial"), lax.axis_size("lateral")
    f32 = functools.partial(jax.ShapeDtypeStruct, dtype=jnp.float32)
    scratch = lambda *shape: pltpu.VMEM(shape, jnp.float32)
    in_hbm = lambda *shape: pltpu.HBM(shape, jnp.float32)
    width = 2 * MODES // (lateral * radial)
    first = [(i, i + 1) for i in range(lateral - 1)]
    second = [(i + 1, i) for i in range(lateral - 1)]
    both = ("lateral", "radial")
    top_only = lambda pairs: [(i * radial + radial - 1, j * radial + radial - 1) for i, j in pairs]

    lower_only = lambda pairs: [(i * radial + k, j * radial + k) for i, j in pairs for k in range(radial - 1)]
    swap = [(i, radial - 1 - i) for i in range(radial)]
    tensors = [hbm(a) for a in (initial_displacement, force, layer_index)]
    viscosity = hbm(viscosity)
    message = f32((2 * (components + 1) * shells, count))
    sides = lambda *shape: scratch(2, *shape)
    mine = pl.pallas_call(
        message_kernel,
        in_specs=[HBM] * 4,
        out_specs=[VMEM] * 2,
        out_shape=[message] * 2,
        scratch_shapes=[
            sides(components, shells, TILE, count),
            sides(components, shells, TILE, count),
            pltpu.VMEM((2, shells, TILE, count), jnp.int32),
            scratch(3 * components + 2, 2 * shells, count),
            pltpu.SMEM(viscosity.shape, jnp.float32),
            pltpu.SemaphoreType.DMA((7,)),
        ],
        compiler_params=params(16),
        cost_estimate=cost(20),
    )(viscosity, *tensors)
    two = lax.ppermute(mine[1], both, top_only(second))
    one = lax.ppermute(mine[0], both, top_only(first))
    eta, early, *surface = pl.pallas_call(
        viscosity_kernel,
        in_specs=[HBM] * 4 + [ANY],
        out_specs=[HBM, HBM, VMEM, VMEM, VMEM],
        out_shape=[
            in_hbm(shells, rows, count),
            in_hbm(components, EARLY, rows, count),
            f32((2, rows, count)),
            f32((2, rows, count)),
            f32((rows, count)),
        ],
        scratch_shapes=[
            pltpu.VMEM(layer_index.shape, jnp.int32),
            scratch(shells + 1, rows + 2 * TILE, count),
            scratch(components, EARLY + 2, rows + 2 * TILE, count),
            scratch(components, EARLY, rows, count),
            scratch(components, EARLY, rows, count),
            pltpu.SMEM(viscosity.shape, jnp.float32),
            pltpu.SemaphoreType.DMA((1 + shells,)),
            pltpu.SemaphoreType.DMA((3 * EARLY + 1 + shells,)),
        ],
        compiler_params=params(24),
        cost_estimate=cost(20),
    )(viscosity, *tensors, mine[0])
    lower_one, lower_two, eta = lax.optimization_barrier((*mine, eta))
    lower_one = lax.ppermute(lower_one, both, lower_only(first))
    lower_two = lax.ppermute(lower_two, both, lower_only(second))

    high, low = longitude_tables(count, MODES)
    high, low = hbm(jnp.asarray(high)), hbm(jnp.asarray(low))
    table = pltpu.VMEM(high.shape, jnp.bfloat16)
    packed = (lateral * radial, rows * width // max(128, width), max(128, width))
    orders = pl.pallas_call(
        functools.partial(surface_kernel, components=components),
        in_specs=[VMEM] * 7 + [HBM, HBM],
        out_specs=VMEM,
        out_shape=f32(packed),
        scratch_shapes=[
            scratch(3, rows + 2 * TILE, count),
            scratch(3, rows + 2 * TILE, count),
            scratch(rows, count),
            table,
            table,
            pltpu.SemaphoreType.DMA((2,)),
        ],
        compiler_params=params(16),
        cost_estimate=cost(200),
    )(*surface, *mine, one, two, high, low)
    eta, _ = lax.optimization_barrier((eta, orders))
    orders = lax.all_to_all(orders, both, split_axis=0, concat_axis=0, tiled=True)
    eta = hbm(eta)

    sweep_scratch = [
        scratch(components, shells + 2, rows + 2 * TILE, count),
        scratch(shells + 2, rows + 2 * TILE, count),
        scratch(components, shells, rows, count),
        scratch(components, shells, rows, count),
    ]
    sweep_sems = pltpu.SemaphoreType.DMA((shells, 4))
    point_high, point_low = colatitude_tables(rows * lateral, MODES)
    stages = [jnp.asarray(point_high), jnp.asarray(point_low)] + [response]
    ring_rows = 2 * (components + 1) * (rows + 1)
    sweep_scratch += [
        sides(*message.shape),
        scratch(2 * (components + 1), count),
    ]
    own_shape = (2, *message.shape)
    late, diagonal, ring, own, beside, *staged = pl.pallas_call(
        first_kernel,
        in_specs=[HBM] * 3 + [ANY] * 6 + [HBM] * len(stages),
        out_specs=[HBM] * 5 + [VMEM] * len(stages),
        out_shape=[
            in_hbm(components, shells - EARLY, rows, count),
            in_hbm(rows, count),
            in_hbm(ring_rows, count),
            in_hbm(*own_shape),
            in_hbm(2, *message.shape),
            *(jax.ShapeDtypeStruct(a.shape, a.dtype) for a in stages),
        ],
        scratch_shapes=[
            *sweep_scratch,
            scratch(rows, count),
            sweep_sems,
            pltpu.SemaphoreType.DMA((8 + 3 * components + len(stages),)),
        ],
        compiler_params=params(28),
        cost_estimate=cost(50),
    )(*tensors[:2], hbm(eta), one, two, lower_one, lower_two, *mine, *(hbm(a) for a in stages))
    ring, orders = lax.optimization_barrier((ring, orders))
    ring = lax.ppermute(ring, "radial", swap)
    coefficients, load = pl.pallas_call(
        spectrum_kernel,
        in_specs=[VMEM] * 4,
        out_specs=[VMEM, VMEM],
        out_shape=[f32((width, MODES)), f32(packed)],
        compiler_params=params(16),
        cost_estimate=cost(200),
    )(orders, *staged)
    eta, load = lax.optimization_barrier((eta, load))
    load = lax.all_to_all(load, both, split_axis=0, concat_axis=0, tiled=True)

    stages = [high, low]
    displacement, token, mask, *staged = pl.pallas_call(
        second_kernel,
        in_specs=[HBM] * 6 + [ANY] + [HBM] * (3 + len(stages)),
        out_specs=[HBM, VMEM, VMEM] + [VMEM] * len(stages),
        out_shape=[
            in_hbm(*initial_displacement.shape),
            f32((TILE, 128)),
            jax.ShapeDtypeStruct(ocean_mask.shape, jnp.bfloat16),
            *(jax.ShapeDtypeStruct(a.shape, a.dtype) for a in stages),
        ],
        scratch_shapes=[
            *sweep_scratch,
            scratch(*own_shape),
            scratch(rows, count),
            scratch(2 * components, rows, count),
            scratch(rows, count),
            pltpu.VMEM(ocean_mask.shape, ocean_mask.dtype),
            scratch(components, 2 * shells, count),
            sweep_sems,
            pltpu.SemaphoreType.DMA((8 + 2 * components + len(stages),)),
        ],
        compiler_params=params(28),
        cost_estimate=cost(50),
    )(
        *(hbm(a) for a in (early, late, tensors[1], eta, tensors[0], diagonal)),
        ring,
        *(hbm(a) for a in (beside, own, ocean_mask)),
        *stages,
    )

    sea_load = pl.pallas_call(
        load_kernel,
        in_specs=[VMEM] * 4,
        out_specs=VMEM,
        out_shape=f32((rows, count)),
        compiler_params=params(20),
        cost_estimate=cost(3),
    )(load, *staged, mask)
    return (displacement, coefficients.T, sea_load)


def solution(mesh):
    in_specs = (
        P("member", "radial", "lateral", None),
        P("member", "radial", "lateral", None),
        P("member"),
        P("radial", "lateral", None),
        P(None, "lateral"),
        P("lateral", None),
    )
    out_specs = (
        P("member", "radial", "lateral", None),
        P("member", ("lateral", "radial")),
        P("lateral", "member"),
    )
    return jax.shard_map(shards, mesh=mesh, in_specs=in_specs, out_specs=out_specs, check_vma=False)
```

```python
import functools
import math

import jax
import jax.numpy as jnp
import ml_dtypes
import numpy as np
from jax import lax
from jax.experimental import pallas as pl
from jax.experimental.pallas import tpu as pltpu
from jax.sharding import PartitionSpec as P

MODES = 512
RELAXATION = 0.8
TILE = 8
RADIX = 8
EARLY = 2
MIB = 1 << 20
ANY = pl.BlockSpec(memory_space=pl.ANY)
HBM = pl.BlockSpec(memory_space=pltpu.HBM)
SMEM = pl.BlockSpec(memory_space=pltpu.SMEM)
VMEM = pl.BlockSpec(memory_space=pltpu.VMEM)


def params(mib):
    return pltpu.CompilerParams(vmem_limit_bytes=mib * MIB)


def halves(table):
    high = table.astype(ml_dtypes.bfloat16)
    low = (table - high.astype(np.float64)).astype(ml_dtypes.bfloat16)
    return high, low


@functools.lru_cache
def longitude_tables(count, modes):
    points = np.arange(count // RADIX, dtype=np.int64)[:, None]
    orders = np.arange(modes, dtype=np.int64)[None, :]
    angle = (2.0 * math.pi / count) * (points * orders % count)
    table = np.concatenate([np.cos(angle), np.sin(angle)], axis=1) * math.sqrt(2.0 / count)
    return halves(table)


@functools.lru_cache
def colatitude_tables(count, modes):
    points = np.arange(count, dtype=np.int64)[:, None]
    waves = np.arange(modes, dtype=np.int64)[None, :]
    phase = waves * (2 * points + 1) % (4 * count)
    return halves(np.cos(math.pi / (2 * count) * phase) * math.sqrt(2.0 / count))


def split(values):
    high = values.astype(jnp.bfloat16)
    return high, (values - high.astype(jnp.float32)).astype(jnp.bfloat16)


def dot(a, b):
    return jnp.dot(a, b, preferred_element_type=jnp.float32)


def pack(block):
    rows, width = block.shape
    groups = max(1, 128 // width)
    rows //= groups
    return jnp.concatenate([block[k * rows : (k + 1) * rows] for k in range(groups)], axis=1)


def unpack(block, width):
    groups = max(1, 128 // width)
    return jnp.concatenate([block[:, k * width : (k + 1) * width] for k in range(groups)], axis=0)


def weighted_sum(terms):
    total = None
    for factor, values in terms:
        factor = round(factor, 15)
        if factor == 0.0:
            continue
        part = values if abs(factor) == 1.0 else abs(factor) * values
        if total is None:
            total = part if factor > 0 else -part
        else:
            total = total + part if factor > 0 else total - part
    return total


def turn(number):
    angle = 2.0 * math.pi * (number % RADIX) / RADIX
    return math.cos(angle), math.sin(angle)


def fold(values):
    step = values.shape[1] // RADIX
    parts = [values[:, m * step : (m + 1) * step] for m in range(RADIX)]
    cosines = [[(turn(k * m)[0], part) for m, part in enumerate(parts)] for k in range(RADIX // 2 + 1)]
    sines = [[(turn(k * m)[1], part) for m, part in enumerate(parts)] for k in range(1, RADIX // 2)]
    return [weighted_sum(terms) for terms in cosines + sines]


def unfold(blocks):
    cosines, sines = blocks[: RADIX // 2 + 1], blocks[RADIX // 2 + 1 :]
    return [
        weighted_sum(
            [(turn(k * m)[0], block) for k, block in enumerate(cosines)]
            + [(turn(k * m)[1], block) for k, block in enumerate(sines, 1)]
        )
        for m in range(RADIX)
    ]


def order_class(shape):
    order = lax.broadcasted_iota(jnp.int32, shape, len(shape) - 1) % RADIX
    mirrored = order > RADIX // 2
    return jnp.where(mirrored, RADIX - order, order), mirrored


def dot_nt(a, b):
    return lax.dot_general(a, b, (((1,), (1,)), ((), ())), preferred_element_type=jnp.float32)


def half_viscosity(index, viscosity_ref):
    values = [0.5 * viscosity_ref[k] for k in range(viscosity_ref.shape[0])]
    bit = 1
    while len(values) > 1:
        odd = (index & bit) != 0
        if len(values) % 2:
            values.append(values[-1])
        values = [jnp.where(odd, b, a) for a, b in zip(values[::2], values[1::2])]
        bit *= 2
    return values[0]


def row_number(shape):
    return lax.broadcasted_iota(jnp.int32, shape, 0)


def north_of(above, middle):
    return pltpu.roll(jnp.where(row_number(middle.shape) == TILE - 1, above, middle), 1, 0)


def south_of(below, middle):
    return pltpu.roll(jnp.where(row_number(middle.shape) == 0, below, middle), TILE - 1, 0)


def east_of(values):
    return pltpu.roll(values, values.shape[-1] - 1, values.ndim - 1)


def west_of(values):
    return pltpu.roll(values, 1, values.ndim - 1)


def relax_weights(middle, others):
    weights = [middle + other for other in others]
    diagonal = 1.0 + functools.reduce(jnp.add, weights)
    return weights, RELAXATION / diagonal


def relax(weights, factor, middle, others, force):
    total = force
    for weight, other in zip(weights, others):
        total = total + weight * other
    return (1.0 - RELAXATION) * middle + factor * total


def around(ref, lead, shell, start):
    rows = lambda first: pl.ds(pl.multiple_of(first, TILE), TILE)
    middle = ref[(*lead, shell, rows(start))]
    return middle, [
        ref[(*lead, shell + 1, rows(start))],
        ref[(*lead, shell - 1, rows(start))],
        south_of(ref[(*lead, shell, rows(start + TILE))], middle),
        north_of(ref[(*lead, shell, rows(start - TILE))], middle),
        west_of(middle),
        east_of(middle),
    ]


def message_kernel(viscosity_from, d, f, index, one, two, fields, forces, layers, rows_of, viscosity, sems):
    components, shells, rows, count = d.shape
    copies = [pltpu.make_async_copy(viscosity_from, viscosity, sems.at[0])]
    for side, start in enumerate((0, rows - TILE)):
        part = pl.ds(start, TILE)
        copies += [
            pltpu.make_async_copy(index.at[:, part], layers.at[side], sems.at[1 + side]),
            pltpu.make_async_copy(d.at[:, :, part], fields.at[side], sems.at[3 + side]),
            pltpu.make_async_copy(f.at[:, :, part], forces.at[side], sems.at[5 + side]),
        ]
    for copy in copies:
        copy.start()
    for copy in copies[:2] + copies[4:5]:
        copy.wait()
    near_eta, far_eta = 2 * components, 2 * components + 1
    for side, near, far in ((0, 0, 1), (1, TILE - 1, TILE - 2)):
        for s in range(shells):
            eta = half_viscosity(layers[side, s], viscosity)
            rows_of[near_eta, side * shells + s] = eta[near]
            rows_of[far_eta, side * shells + s] = eta[far]
    for copy in copies[2:4] + copies[5:]:
        copy.wait()
    for side, near, far in ((0, 0, 1), (1, TILE - 1, TILE - 2)):
        for s in range(shells):
            for c in range(components):
                rows_of[c, side * shells + s] = fields[side, c, s, near]
                rows_of[components + c, side * shells + s] = fields[side, c, s, far]
                rows_of[far_eta + 1 + c, side * shells + s] = forces[side, c, s, near]
    radial = lax.axis_index("radial")
    place = row_number((2 * shells, count)) % shells
    highest, lowest = place == shells - 1, place == 0
    zero = jnp.zeros((2 * shells, count), jnp.float32)

    def beside(near, far):
        middle = rows_of[near]
        return middle, [
            jnp.where(highest, zero, pltpu.roll(middle, 2 * shells - 1, 0)),
            jnp.where(lowest, zero, pltpu.roll(middle, 1, 0)),
            rows_of[far],
            west_of(middle),
            east_of(middle),
        ]

    eta, others = beside(near_eta, far_eta)
    weights = [eta + other for other in others]
    inside = (radial < lax.axis_size("radial") - 1, radial > 0)
    weights[0] = jnp.where(jnp.logical_and(highest, inside[0]), zero, weights[0])
    weights[1] = jnp.where(jnp.logical_and(lowest, inside[1]), zero, weights[1])
    diagonal = 1.0 + functools.reduce(jnp.add, weights)
    values, sums = [], []
    for c in range(components):
        middle, others = beside(c, components + c)
        total = rows_of[far_eta + 1 + c]
        for weight, other in zip(weights, others):
            total = total + weight * other
        values.append(middle)
        sums.append(total)
    for place, field in enumerate(values + [eta] + sums + [diagonal]):
        both = pltpu.roll(field, shells, 0)
        one[pl.ds(place * shells, shells)] = both[:shells]
        two[pl.ds(place * shells, shells)] = both[shells:]


def shell_order(shells):
    lower = lax.axis_index("radial") == 0
    return lambda k: jnp.where(lower, k, shells - 1 - k)


def viscosity_kernel(
    viscosity_from, d, f, index_from, token, table_from, eta_out, out, surface_swept, surface_eta, surface_force, table,
    index, eta, field, force, result, viscosity, sems, more_sems,
):
    del token
    _, shells, rows, count = d.shape
    components = d.shape[0]
    block = pl.ds(TILE, rows)
    shell = shell_order(shells)
    value_copy = pltpu.make_async_copy(viscosity_from, viscosity, sems.at[shells])
    layers = [pltpu.make_async_copy(index_from.at[shell(k)], index.at[k], sems.at[k]) for k in range(shells)]
    fields = [
        pltpu.make_async_copy(d.at[:, shell(k)], field.at[:, k + 1, block], more_sems.at[k]) for k in range(EARLY + 1)
    ]
    forces = [
        pltpu.make_async_copy(f.at[:, shell(k)], force.at[:, k], more_sems.at[EARLY + 1 + k]) for k in range(EARLY)
    ]
    table_copy = pltpu.make_async_copy(table_from, table, sems.at[shells + 1])
    start_all([value_copy, *layers, *fields, *forces])
    zeros = jnp.zeros((rows, count), jnp.float32)
    for c in range(components):
        field[c, 0, block] = zeros
    eta[0, block] = zeros
    value_copy.wait()
    stores = start_all([table_copy])
    for k in range(shells):
        layers[k].wait()

        def lookup(step, _):
            start = pl.multiple_of(step * TILE, TILE)
            eta[k + 1, pl.ds(start + TILE, TILE)] = half_viscosity(index[k, pl.ds(start, TILE)], viscosity)
            return 0

        lax.fori_loop(0, rows // TILE, lookup, 0)
        stores += start_all(
            [pltpu.make_async_copy(eta.at[k + 1, block], eta_out.at[shell(k)], more_sems.at[2 * EARLY + 1 + k])]
        )
    for k in range(EARLY):
        for copy in (fields[: EARLY + 1] if k == 0 else []) + forces[k : k + 1]:
            copy.wait()

        def sweep(step, _):
            start = pl.multiple_of(step * TILE, TILE)
            part = pl.ds(start, TILE)
            weights, factor = relax_weights(*around(eta, (), k + 1, start + TILE))
            for c in range(components):
                middle, others = around(field, (c,), k + 1, start + TILE)
                result[c, k, part] = relax(weights, factor, middle, others, force[c, k, part])
            surface_swept[1 - k, part] = result[0, k, part]
            surface_eta[1 - k, part] = eta[k + 1, pl.ds(start + TILE, TILE)]
            if k == 0:
                surface_force[part] = force[0, 0, part]
            sem = more_sems.at[2 * EARLY + 1 + shells + k]
            pltpu.make_async_copy(result.at[:, k, part], out.at[:, k, part], sem).start()
            return 0

        lax.fori_loop(0, rows // TILE, sweep, 0, unroll=2)
        stores.append(pltpu.make_async_copy(result.at[:, k], out.at[:, k], more_sems.at[2 * EARLY + 1 + shells + k]))
    for copy in stores:
        copy.wait()


def surface_kernel(
    surface_swept, surface_eta, force, own_one, own_two, one, two, high, low_from, out,
    swept, eta, surface, low, sem, components,
):
    rows, count = force.shape

    @pl.when(lax.axis_index("radial") == lax.axis_size("radial") - 1)
    def _():
        low_copy = pltpu.make_async_copy(low_from, low, sem)
        low_copy.start()
        block = pl.ds(TILE, rows)
        for k in range(2):
            swept[k, block] = surface_swept[k]
            eta[k, block] = surface_eta[k]
        swept[2, block] = jnp.zeros((rows, count), jnp.float32)
        eta[2, block] = jnp.zeros((rows, count), jnp.float32)
        fields = one.shape[0]
        shells = fields // (2 * (components + 1))
        lateral = lax.axis_index("lateral")
        inside = (lateral > 0, lateral < lax.axis_size("lateral") - 1)
        for beside, own, place, own_place, there in zip(
            (one[...], two[...]), (own_two[...], own_one[...]), (TILE - 1, rows + TILE), (TILE, rows + TILE - 1), inside
        ):
            for k in range(2):
                row = lambda message, kind: message[kind * shells + shells - 2 + k : kind * shells + shells - 1 + k]
                weight = row(beside, components) + row(own, components)

                def finish(message, other):
                    total = row(message, components + 1) + weight * row(other, 0)
                    factor = RELAXATION / (row(message, 2 * components + 1) + weight)
                    return (1.0 - RELAXATION) * row(message, 0) + factor * total

                swept[k, pl.ds(own_place, 1)] = finish(own, beside)
                if k == 1:
                    edge = finish(beside, own)
                    swept[k, pl.ds(place, 1)] = jnp.where(there, edge, jnp.zeros_like(edge))
                    eta[k, pl.ds(place, 1)] = row(beside, components)

        def second(step, _):
            start = pl.multiple_of(step * TILE, TILE)
            weights, factor = relax_weights(*around(eta, (), 1, start + TILE))
            middle, others = around(swept, (), 1, start + TILE)
            surface[pl.ds(start, TILE)] = relax(weights, factor, middle, others, force[pl.ds(start, TILE)])
            return 0

        lax.fori_loop(0, rows // TILE, second, 0, unroll=2)
        near, far = split(jnp.concatenate(fold(surface[...]), axis=0))
        total = dot(near, high[...]) + dot(far, high[...])
        low_copy.wait()
        total = total + dot(near, low[...])
        blocks = [total[k * rows : (k + 1) * rows] for k in range(RADIX)]
        kind, mirrored = order_class((1, total.shape[1]))
        cosine, sine = blocks[0], jnp.zeros_like(blocks[0])
        for k in range(1, RADIX // 2 + 1):
            cosine = jnp.where(kind == k, blocks[k], cosine)
        for k in range(1, RADIX // 2):
            sine = jnp.where(kind == k, blocks[RADIX // 2 + k], sine)
        sine = jnp.where(mirrored, -sine, sine)
        modes = total.shape[1] // 2
        fourier = jnp.concatenate(
            [cosine[:, :modes] - sine[:, modes:], cosine[:, modes:] + sine[:, :modes]], axis=1
        )
        blocks = out.shape[0]
        width = fourier.shape[1] // blocks
        for block in range(blocks):
            out[block] = pack(fourier[:, block * width : (block + 1) * width])


def sweep_shells(
    begin, source, f, h, store, field, eta, force, result, sems, before_first, last_loads, arrived, finish, after_shell
):
    components, shells, rows, count = f.shape
    inner = pl.ds(TILE, rows)
    shell = shell_order(shells)

    def field_loads(k):
        s = shell(k)
        return [
            pltpu.make_async_copy(source(k), field.at[:, s + 1, inner], sems.at[k, 0]),
            pltpu.make_async_copy(h.at[s], eta.at[s + 1, inner], sems.at[k, 1]),
            *(last_loads if k == shells - 1 else []),
        ]

    def force_load(k):
        return [pltpu.make_async_copy(f.at[:, shell(k)], force.at[:, shell(k)], sems.at[k, 2])]

    loads = {k: start_all(field_loads(k)) for k in range(max(begin - 1, 0), begin + 2)}
    forces = {begin: start_all(force_load(begin))}
    if begin == 0:
        nothing = jnp.where(lax.axis_index("radial") == 0, 0, shells + 1)
        zeros = jnp.zeros((rows, count), jnp.float32)
        for c in range(components):
            field[c, nothing, inner] = zeros
        eta[nothing, inner] = zeros
    before_first()

    def start_until(k):
        for ahead in range(begin, shells):
            if ahead <= k and ahead not in loads:
                loads[ahead] = start_all(field_loads(ahead))
            if ahead < k and ahead not in forces:
                forces[ahead] = start_all(force_load(ahead))

    start_until(begin + 2)
    stores, there = [], set()
    for k in range(begin, shells):
        s = shell(k)
        start_until(k + 3)
        for near in range(max(k - 1, 0), min(k + 2, shells)):
            if near not in there:
                there.add(near)
                for copy in loads[near]:
                    copy.wait()
                arrived(near)
        for copy in forces[k]:
            copy.wait()

        def tile(step, _):
            first = pl.multiple_of(step * TILE, TILE)
            part = pl.ds(first, TILE)
            if k == shells - 1:
                finish(s, first)
            else:
                weights, factor = relax_weights(*around(eta, (), s + 1, first + TILE))
                for c in range(components):
                    middle, others = around(field, (c,), s + 1, first + TILE)
                    result[c, s, part] = relax(weights, factor, middle, others, force[c, s, part])
            pltpu.make_async_copy(result.at[:, s, part], store(k).at[:, part], sems.at[k, 3]).start()
            return 0

        lax.fori_loop(0, rows // TILE, tile, 0, unroll=2)
        stores.append(pltpu.make_async_copy(result.at[:, s], store(k), sems.at[k, 3]))
        after_shell(s, k)
    for copy in stores:
        copy.wait()


def set_edge(ref, lead, shells, rows, before, after):
    for s in range(shells):
        ref[(*lead, s + 1, TILE - 1)] = before(s)
        ref[(*lead, s + 1, rows + TILE)] = after(s)


def start_all(copies):
    for copy in copies:
        copy.start()
    return copies


def load_messages(sources, lower_sources, slots, sems):
    lower = lax.axis_index("radial") < lax.axis_size("radial") - 1
    copies = lambda refs: [pltpu.make_async_copy(ref, slots.at[k], sems.at[k]) for k, ref in enumerate(refs)]
    pl.when(lower)(lambda: [copy.start() for copy in copies(lower_sources)] and None)
    pl.when(jnp.logical_not(lower))(lambda: [copy.start() for copy in copies(sources)] and None)
    return copies(sources)


def first_kernel(d, f, h, one, two, lower_one, lower_two, mine_one, mine_two, *refs):
    components, shells, rows, count = d.shape
    staged = (len(refs) - 13) // 2
    sources, refs = refs[:staged], refs[staged:]
    out, diagonal_out, ring_out, own_out, beside_out, *targets = refs[: 5 + staged]
    field, eta, force, result, messages, edges, diagonal, sems, more_sems = refs[5 + staged :]
    arrivals = load_messages((one, two), (lower_one, lower_two), messages, more_sems)
    lower = lax.axis_index("radial") == 0
    last, beyond = jnp.where(lower, shells - 1, 0), jnp.where(lower, shells + 1, 0)
    values = pl.ds(0, own_out.shape[1])
    copies = start_all(
        [
            pltpu.make_async_copy(mine.at[values], own_out.at[k], more_sems.at[4 + components + k])
            for k, mine in enumerate((mine_one, mine_two))
        ]
    )

    def before_first():
        block = pl.ds(TILE, rows)
        zeros = jnp.zeros((rows, count), jnp.float32)
        for c in range(components):
            field[c, beyond, block] = zeros
        eta[beyond, block] = zeros
        for copy in arrivals:
            copy.wait()
        before, after = messages[0], messages[1]
        row = lambda message, kind: lambda s: message[kind * shells + s]
        for c in range(components):
            set_edge(field, (c,), shells, rows, row(before, c), row(after, c))
        set_edge(eta, (), shells, rows, row(before, components), row(after, components))
        for side, message in enumerate((before, after)):
            for k in range(components + 1):
                edges[side * (components + 1) + k] = jnp.where(
                    lower, message[(k + 1) * shells - 1], message[k * shells]
                )
        tail = ring_out.at[pl.ds(2 * (components + 1) * rows, edges.shape[0])]
        copies.extend(
            start_all(
                [
                    pltpu.make_async_copy(edges, tail, more_sems.at[2]),
                    pltpu.make_async_copy(messages, beside_out, more_sems.at[3]),
                ]
            )
        )

    def arrived(k):
        if k < shells - 1:
            return
        block = pl.ds(TILE, rows)
        sources = [field.at[c, last + 1, block] for c in range(components)] + [eta.at[last + 1, block]]
        copies.extend(
            start_all(
                [
                    pltpu.make_async_copy(source, ring_out.at[pl.ds(k * rows, rows)], more_sems.at[6 + components + k])
                    for k, source in enumerate(sources)
                ]
            )
        )

    def finish(s, first):
        part = pl.ds(first, TILE)
        middle, others = around(eta, (), s + 1, first + TILE)
        weights = [middle + other for other in others]
        zero = jnp.zeros_like(middle)
        weights[0] = jnp.where(lower, zero, weights[0])
        weights[1] = jnp.where(lower, weights[1], zero)
        diagonal[part] = 1.0 + functools.reduce(jnp.add, weights)
        for c in range(components):
            total = force[c, s, part]
            for weight, other in zip(weights, around(field, (c,), s + 1, first + TILE)[1]):
                total = total + weight * other
            result[c, s, part] = total

    def after_shell(s, k):
        if k == EARLY:
            copies.extend(
                start_all(
                    [
                        pltpu.make_async_copy(source, target, more_sems.at[8 + 3 * components + n])
                        for n, (source, target) in enumerate(zip(sources, targets))
                    ]
                )
            )
        if k == shells - 1:
            sums = [result.at[c, s] for c in range(components)] + [diagonal]
            copies.extend(
                start_all(
                    [
                        pltpu.make_async_copy(
                            source,
                            ring_out.at[pl.ds((components + 1 + n) * rows, rows)],
                            more_sems.at[7 + 2 * components + n],
                        )
                        for n, source in enumerate(sums)
                    ]
                    + [pltpu.make_async_copy(diagonal, diagonal_out, more_sems.at[0])]
                )
            )

    shell = shell_order(shells)
    sweep_shells(
        EARLY, lambda k: d.at[:, shell(k)], f, h, lambda k: out.at[:, k - EARLY],
        field, eta, force, result, sems, before_first, [], arrived, finish, after_shell,
    )
    for copy in copies:
        copy.wait()


def second_kernel(early, late, f, h, start, diagonal_from, ring, beside, own_from, *refs):
    components, shells, rows, count = f.shape
    staged = (len(refs) - 18) // 2
    mask_from, *sources = refs[: 1 + staged]
    out, token, mask_out, *targets = refs[1 + staged : 4 + 2 * staged]
    (
        field, eta, force, result, messages, edges, own, diagonal, raw, ring_diagonal, mask, ends, sems, more_sems
    ) = refs[4 + 2 * staged :]
    token[...] = jnp.zeros_like(token)
    tail = ring.at[pl.ds(2 * (components + 1) * rows, edges.shape[0])]
    arrivals = start_all(
        [
            pltpu.make_async_copy(beside, messages, more_sems.at[0]),
            pltpu.make_async_copy(tail, edges, more_sems.at[1]),
            pltpu.make_async_copy(own_from, own, more_sems.at[2]),
        ]
    )
    radial, lateral = lax.axis_index("radial"), lax.axis_index("lateral")
    lower = radial == 0
    last, beyond = jnp.where(lower, shells - 1, 0), jnp.where(lower, shells + 1, 0)
    block = pl.ds(TILE, rows)
    shell = shell_order(shells)
    from_ring = lambda k, target, sem: pltpu.make_async_copy(
        ring.at[pl.ds(k * rows, rows)], target, more_sems.at[sem]
    )
    last_loads = [
        pltpu.make_async_copy(start.at[:, last], raw.at[pl.ds(0, components)], more_sems.at[3]),
        pltpu.make_async_copy(diagonal_from, diagonal, more_sems.at[4]),
        *(from_ring(c, raw.at[components + c], 5 + c) for c in range(components)),
        from_ring(components, eta.at[beyond, block], 5 + components),
        *(
            from_ring(components + 1 + c, field.at[c, beyond, block], 6 + components + c)
            for c in range(components)
        ),
        from_ring(2 * components + 1, ring_diagonal, 6 + 2 * components),
    ]
    copies = []
    mask_copy = pltpu.make_async_copy(mask_from, mask, more_sems.at[7 + 2 * components])

    def before_first():
        for copy in arrivals:
            copy.wait()
        before, after = messages[0], messages[1]
        pair = lambda k: jnp.concatenate(
            [before[k * shells : (k + 1) * shells], after[k * shells : (k + 1) * shells]], axis=0
        )
        place = row_number((2 * shells, count))
        zero = jnp.zeros((2 * shells, count), jnp.float32)
        shared = place % shells == last
        across_of = lambda k: jnp.where(
            place < shells, edges[pl.ds(k, 1)], edges[pl.ds(components + 1 + k, 1)]
        )
        inside = jnp.where(place < shells, lateral, lax.axis_size("lateral") - 1 - lateral) > 0
        mine = (own[1], own[0])
        own_row = lambda k: jnp.concatenate([part[k * shells : (k + 1) * shells] for part in mine], axis=0)
        middle = pair(components)
        weight = middle + own_row(components)
        across = jnp.where(shared, middle + across_of(components), zero)
        factor = RELAXATION / (pair(2 * components + 1) + weight + across)
        own_factor = RELAXATION / (own_row(2 * components + 1) + weight)
        for c in range(components):
            total = pair(components + 1 + c) + weight * own_row(c) + across * across_of(c)
            edge = jnp.where(inside, (1.0 - RELAXATION) * pair(c) + factor * total, zero)
            total = own_row(components + 1 + c) + weight * pair(c)
            ends[c] = (1.0 - RELAXATION) * own_row(c) + own_factor * total
            set_edge(field, (c,), shells, rows, lambda s: edge[s], lambda s: edge[shells + s])
        set_edge(eta, (), shells, rows, lambda s: middle[s], lambda s: middle[shells + s])

    def arrived(k):
        if k < EARLY:
            s = shell(k)
            for side, place in enumerate((TILE, TILE + rows - 1)):
                for c in range(components):
                    field[c, s + 1, pl.ds(place, 1)] = ends[c, pl.ds(side * shells + s, 1)]
        if k < shells - 1:
            return

        def tile(step, _):
            first = pl.multiple_of(step * TILE, TILE)
            part, place = pl.ds(first, TILE), pl.ds(first + TILE, TILE)
            weight = eta[last + 1, place] + eta[beyond, place]
            here, there = RELAXATION / (diagonal[part] + weight), RELAXATION / (ring_diagonal[part] + weight)
            for c in range(components):
                mine, other = raw[c, part], raw[components + c, part]
                field[c, last + 1, place] = (1.0 - RELAXATION) * mine + here * (
                    field[c, last + 1, place] + weight * other
                )
                field[c, beyond, place] = (1.0 - RELAXATION) * other + there * (
                    field[c, beyond, place] + weight * mine
                )
            return 0

        lax.fori_loop(0, rows // TILE, tile, 0)

    def finish(s, first):
        part = pl.ds(first, TILE)
        weights, factor = relax_weights(*around(eta, (), s + 1, first + TILE))
        for c in range(components):
            middle, others = around(field, (c,), s + 1, first + TILE)
            result[c, s, part] = relax(weights, factor, middle, others, force[c, s, part])

    def after_shell(s, k):
        if k == 0:
            copies.extend(
                start_all(
                    [
                        pltpu.make_async_copy(source, target, more_sems.at[8 + 2 * components + n])
                        for n, (source, target) in enumerate(zip(sources, targets))
                    ]
                )
            )
            mask_copy.start()
        if k == shells - 2:
            mask_copy.wait()
            mask_out[...] = mask[...].astype(jnp.float32).astype(jnp.bfloat16)

    sweep_shells(
        0, lambda k: early.at[:, k] if k < EARLY else late.at[:, k - EARLY], f, h, lambda k: out.at[:, shell(k)],
        field, eta, force, result, sems, before_first, last_loads, arrived, finish, after_shell,
    )
    for copy in copies:
        copy.wait()


def spectrum_kernel(orders, high, low, response, coefficients, out):
    radial = lax.axis_size("radial")
    width = coefficients.shape[0]
    bands, rows = orders.shape[0] // radial, high.shape[0] * radial // orders.shape[0]
    fourier = jnp.concatenate([unpack(orders[band * radial + radial - 1], width) for band in range(bands)], axis=0)
    near, far = split(fourier.T)
    spectrum = dot(near, high[...]) + dot(far, high[...]) + dot(near, low[...])
    coefficients[...] = spectrum
    own = response[:, :width]
    for place in range(1, radial):
        own = jnp.where(
            lax.axis_index("radial") == place, response[:, place * width : (place + 1) * width], own
        )
    near, far = split(own.T * spectrum)
    load = (dot_nt(near, high[...]) + dot_nt(far, high[...]) + dot_nt(near, low[...])).T
    for band in range(bands):
        block = pack(load[band * rows : (band + 1) * rows])
        for place in range(radial):
            out[band * radial + place] = block


def load_kernel(load, high, low, mask, out):
    blocks, rows = load.shape[0], out.shape[0]
    step, width = out.shape[1] // RADIX, high.shape[1] // blocks
    values = jnp.concatenate([unpack(load[block], width) for block in range(blocks)], axis=1)
    modes = values.shape[1] // 2
    kind, mirrored = order_class((1, values.shape[1]))
    crossed = jnp.concatenate([values[:, modes:], -values[:, :modes]], axis=1)
    crossed = jnp.where(mirrored, -crossed, crossed)
    zero = jnp.zeros_like(values)
    stack = [jnp.where(kind == k, values, zero) for k in range(RADIX // 2 + 1)]
    stack += [jnp.where(kind == k, crossed, zero) for k in range(1, RADIX // 2)]
    near, far = split(jnp.concatenate(stack, axis=0))
    total = dot_nt(near, high[...]) + dot_nt(far, high[...]) + dot_nt(near, low[...])
    for m, part in enumerate(unfold([total[k * rows : (k + 1) * rows] for k in range(RADIX)])):
        columns = slice(m * step, (m + 1) * step)
        out[:, columns] = part * mask[:, columns].astype(jnp.float32)


def cost(microseconds):
    return pl.CostEstimate(flops=0, bytes_accessed=3_000_000 * microseconds, transcendentals=0)


def hbm(values):
    return pltpu.with_memory_space_constraint(values, pltpu.HBM)


def shards(initial_displacement, force, viscosity, layer_index, response, ocean_mask):
    components, shells, rows, count = initial_displacement.shape
    radial, lateral = lax.axis_size("radial"), lax.axis_size("lateral")
    f32 = functools.partial(jax.ShapeDtypeStruct, dtype=jnp.float32)
    scratch = lambda *shape: pltpu.VMEM(shape, jnp.float32)
    in_hbm = lambda *shape: pltpu.HBM(shape, jnp.float32)
    width = 2 * MODES // (lateral * radial)
    first = [(i, i + 1) for i in range(lateral - 1)]
    second = [(i + 1, i) for i in range(lateral - 1)]
    both = ("lateral", "radial")
    top_only = lambda pairs: [(i * radial + radial - 1, j * radial + radial - 1) for i, j in pairs]

    lower_only = lambda pairs: [(i * radial + k, j * radial + k) for i, j in pairs for k in range(radial - 1)]
    swap = [(i, radial - 1 - i) for i in range(radial)]
    tensors = [hbm(a) for a in (initial_displacement, force, layer_index)]
    viscosity = hbm(viscosity)
    message = f32((2 * (components + 1) * shells, count))
    sides = lambda *shape: scratch(2, *shape)
    mine = pl.pallas_call(
        message_kernel,
        in_specs=[HBM] * 4,
        out_specs=[VMEM] * 2,
        out_shape=[message] * 2,
        scratch_shapes=[
            sides(components, shells, TILE, count),
            sides(components, shells, TILE, count),
            pltpu.VMEM((2, shells, TILE, count), jnp.int32),
            scratch(3 * components + 2, 2 * shells, count),
            pltpu.SMEM(viscosity.shape, jnp.float32),
            pltpu.SemaphoreType.DMA((7,)),
        ],
        compiler_params=params(16),
        cost_estimate=cost(20),
    )(viscosity, *tensors)
    two = lax.ppermute(mine[1], both, top_only(second))
    one = lax.ppermute(mine[0], both, top_only(first))
    high, low = longitude_tables(count, MODES)
    high, low = hbm(jnp.asarray(high)), hbm(jnp.asarray(low))
    eta, early, *surface, table = pl.pallas_call(
        viscosity_kernel,
        in_specs=[HBM] * 4 + [ANY, HBM],
        out_specs=[HBM, HBM, VMEM, VMEM, VMEM, VMEM],
        out_shape=[
            in_hbm(shells, rows, count),
            in_hbm(components, EARLY, rows, count),
            f32((2, rows, count)),
            f32((2, rows, count)),
            f32((rows, count)),
            jax.ShapeDtypeStruct(high.shape, high.dtype),
        ],
        scratch_shapes=[
            pltpu.VMEM(layer_index.shape, jnp.int32),
            scratch(shells + 1, rows + 2 * TILE, count),
            scratch(components, EARLY + 2, rows + 2 * TILE, count),
            scratch(components, EARLY, rows, count),
            scratch(components, EARLY, rows, count),
            pltpu.SMEM(viscosity.shape, jnp.float32),
            pltpu.SemaphoreType.DMA((2 + shells,)),
            pltpu.SemaphoreType.DMA((3 * EARLY + 1 + shells,)),
        ],
        compiler_params=params(24),
        cost_estimate=cost(20),
    )(viscosity, *tensors, mine[0], high)
    lower_one, lower_two, eta = lax.optimization_barrier((*mine, eta))
    lower_one = lax.ppermute(lower_one, both, lower_only(first))
    lower_two = lax.ppermute(lower_two, both, lower_only(second))

    packed = (lateral * radial, rows * width // max(128, width), max(128, width))
    orders = pl.pallas_call(
        functools.partial(surface_kernel, components=components),
        in_specs=[VMEM] * 8 + [HBM],
        out_specs=VMEM,
        out_shape=f32(packed),
        scratch_shapes=[
            scratch(3, rows + 2 * TILE, count),
            scratch(3, rows + 2 * TILE, count),
            scratch(rows, count),
            pltpu.VMEM(low.shape, low.dtype),
            pltpu.SemaphoreType.DMA,
        ],
        compiler_params=params(16),
        cost_estimate=cost(200),
    )(*surface, *mine, one, two, table, low)
    eta, _ = lax.optimization_barrier((eta, orders))
    orders = lax.all_to_all(orders, both, split_axis=0, concat_axis=0, tiled=True)
    eta = hbm(eta)

    sweep_scratch = [
        scratch(components, shells + 2, rows + 2 * TILE, count),
        scratch(shells + 2, rows + 2 * TILE, count),
        scratch(components, shells, rows, count),
        scratch(components, shells, rows, count),
    ]
    sweep_sems = pltpu.SemaphoreType.DMA((shells, 4))
    point_high, point_low = colatitude_tables(rows * lateral, MODES)
    stages = [jnp.asarray(point_high), jnp.asarray(point_low)] + [response]
    ring_rows = 2 * (components + 1) * (rows + 1)
    sweep_scratch += [
        sides(*message.shape),
        scratch(2 * (components + 1), count),
    ]
    own_shape = (2, *message.shape)
    late, diagonal, ring, own, beside, *staged = pl.pallas_call(
        first_kernel,
        in_specs=[HBM] * 3 + [ANY] * 6 + [HBM] * len(stages),
        out_specs=[HBM] * 5 + [VMEM] * len(stages),
        out_shape=[
            in_hbm(components, shells - EARLY, rows, count),
            in_hbm(rows, count),
            in_hbm(ring_rows, count),
            in_hbm(*own_shape),
            in_hbm(2, *message.shape),
            *(jax.ShapeDtypeStruct(a.shape, a.dtype) for a in stages),
        ],
        scratch_shapes=[
            *sweep_scratch,
            scratch(rows, count),
            sweep_sems,
            pltpu.SemaphoreType.DMA((8 + 3 * components + len(stages),)),
        ],
        compiler_params=params(28),
        cost_estimate=cost(50),
    )(*tensors[:2], hbm(eta), one, two, lower_one, lower_two, *mine, *(hbm(a) for a in stages))
    ring, orders = lax.optimization_barrier((ring, orders))
    ring = lax.ppermute(ring, "radial", swap)
    coefficients, load = pl.pallas_call(
        spectrum_kernel,
        in_specs=[VMEM] * 4,
        out_specs=[VMEM, VMEM],
        out_shape=[f32((width, MODES)), f32(packed)],
        compiler_params=params(16),
        cost_estimate=cost(200),
    )(orders, *staged)
    eta, load = lax.optimization_barrier((eta, load))
    load = lax.all_to_all(load, both, split_axis=0, concat_axis=0, tiled=True)

    stages = [high, low]
    displacement, token, mask, *staged = pl.pallas_call(
        second_kernel,
        in_specs=[HBM] * 6 + [ANY] + [HBM] * (3 + len(stages)),
        out_specs=[HBM, VMEM, VMEM] + [VMEM] * len(stages),
        out_shape=[
            in_hbm(*initial_displacement.shape),
            f32((TILE, 128)),
            jax.ShapeDtypeStruct(ocean_mask.shape, jnp.bfloat16),
            *(jax.ShapeDtypeStruct(a.shape, a.dtype) for a in stages),
        ],
        scratch_shapes=[
            *sweep_scratch,
            scratch(*own_shape),
            scratch(rows, count),
            scratch(2 * components, rows, count),
            scratch(rows, count),
            pltpu.VMEM(ocean_mask.shape, ocean_mask.dtype),
            scratch(components, 2 * shells, count),
            sweep_sems,
            pltpu.SemaphoreType.DMA((8 + 2 * components + len(stages),)),
        ],
        compiler_params=params(28),
        cost_estimate=cost(50),
    )(
        *(hbm(a) for a in (early, late, tensors[1], eta, tensors[0], diagonal)),
        ring,
        *(hbm(a) for a in (beside, own, ocean_mask)),
        *stages,
    )

    sea_load = pl.pallas_call(
        load_kernel,
        in_specs=[VMEM] * 4,
        out_specs=VMEM,
        out_shape=f32((rows, count)),
        compiler_params=params(20),
        cost_estimate=cost(3),
    )(load, *staged, mask)
    return (displacement, coefficients.T, sea_load)


def solution(mesh):
    in_specs = (
        P("member", "radial", "lateral", None),
        P("member", "radial", "lateral", None),
        P("member"),
        P("radial", "lateral", None),
        P(None, "lateral"),
        P("lateral", None),
    )
    out_specs = (
        P("member", "radial", "lateral", None),
        P("member", ("lateral", "radial")),
        P("lateral", "member"),
    )
    return jax.shard_map(shards, mesh=mesh, in_specs=in_specs, out_specs=out_specs, check_vma=False)
```

```python
import functools
import math

import jax
import jax.numpy as jnp
import ml_dtypes
import numpy as np
from jax import lax
from jax.experimental import pallas as pl
from jax.experimental.pallas import tpu as pltpu
from jax.sharding import PartitionSpec as P

MODES = 512
RELAXATION = 0.8
TILE = 8
RADIX = 8
EARLY = 2
MIB = 1 << 20
ANY = pl.BlockSpec(memory_space=pl.ANY)
HBM = pl.BlockSpec(memory_space=pltpu.HBM)
SMEM = pl.BlockSpec(memory_space=pltpu.SMEM)
VMEM = pl.BlockSpec(memory_space=pltpu.VMEM)


def params(mib):
    return pltpu.CompilerParams(vmem_limit_bytes=mib * MIB)


def halves(table):
    high = table.astype(ml_dtypes.bfloat16)
    low = (table - high.astype(np.float64)).astype(ml_dtypes.bfloat16)
    return high, low


@functools.lru_cache
def longitude_tables(count, modes):
    points = np.arange(count // RADIX, dtype=np.int64)[:, None]
    orders = np.arange(modes, dtype=np.int64)[None, :]
    angle = (2.0 * math.pi / count) * (points * orders % count)
    table = np.concatenate([np.cos(angle), np.sin(angle)], axis=1) * math.sqrt(2.0 / count)
    return halves(table)


@functools.lru_cache
def colatitude_tables(count, modes):
    points = np.arange(count, dtype=np.int64)[:, None]
    waves = np.arange(modes, dtype=np.int64)[None, :]
    phase = waves * (2 * points + 1) % (4 * count)
    return halves(np.cos(math.pi / (2 * count) * phase) * math.sqrt(2.0 / count))


def split(values):
    high = values.astype(jnp.bfloat16)
    return high, (values - high.astype(jnp.float32)).astype(jnp.bfloat16)


def dot(a, b):
    return jnp.dot(a, b, preferred_element_type=jnp.float32)


def pack(block):
    rows, width = block.shape
    groups = max(1, 128 // width)
    rows //= groups
    return jnp.concatenate([block[k * rows : (k + 1) * rows] for k in range(groups)], axis=1)


def unpack(block, width):
    groups = max(1, 128 // width)
    return jnp.concatenate([block[:, k * width : (k + 1) * width] for k in range(groups)], axis=0)


def weighted_sum(terms):
    total = None
    for factor, values in terms:
        factor = round(factor, 15)
        if factor == 0.0:
            continue
        part = values if abs(factor) == 1.0 else abs(factor) * values
        if total is None:
            total = part if factor > 0 else -part
        else:
            total = total + part if factor > 0 else total - part
    return total


def turn(number):
    angle = 2.0 * math.pi * (number % RADIX) / RADIX
    return math.cos(angle), math.sin(angle)


def fold(values):
    step = values.shape[1] // RADIX
    parts = [values[:, m * step : (m + 1) * step] for m in range(RADIX)]
    cosines = [[(turn(k * m)[0], part) for m, part in enumerate(parts)] for k in range(RADIX // 2 + 1)]
    sines = [[(turn(k * m)[1], part) for m, part in enumerate(parts)] for k in range(1, RADIX // 2)]
    return [weighted_sum(terms) for terms in cosines + sines]


def unfold(blocks):
    cosines, sines = blocks[: RADIX // 2 + 1], blocks[RADIX // 2 + 1 :]
    return [
        weighted_sum(
            [(turn(k * m)[0], block) for k, block in enumerate(cosines)]
            + [(turn(k * m)[1], block) for k, block in enumerate(sines, 1)]
        )
        for m in range(RADIX)
    ]


def order_class(shape):
    order = lax.broadcasted_iota(jnp.int32, shape, len(shape) - 1) % RADIX
    mirrored = order > RADIX // 2
    return jnp.where(mirrored, RADIX - order, order), mirrored


def three_pass(product, near, far, high, low):
    both = product(jnp.concatenate([near, far], axis=0), high[...])
    return both[: near.shape[0]] + both[near.shape[0] :] + product(near, low[...])


def dot_nt(a, b):
    return lax.dot_general(a, b, (((1,), (1,)), ((), ())), preferred_element_type=jnp.float32)


def half_viscosity(index, viscosity_ref):
    values = [0.5 * viscosity_ref[k] for k in range(viscosity_ref.shape[0])]
    bit = 1
    while len(values) > 1:
        odd = (index & bit) != 0
        if len(values) % 2:
            values.append(values[-1])
        values = [jnp.where(odd, b, a) for a, b in zip(values[::2], values[1::2])]
        bit *= 2
    return values[0]


def row_number(shape):
    return lax.broadcasted_iota(jnp.int32, shape, 0)


def north_of(above, middle):
    return pltpu.roll(jnp.where(row_number(middle.shape) == TILE - 1, above, middle), 1, 0)


def south_of(below, middle):
    return pltpu.roll(jnp.where(row_number(middle.shape) == 0, below, middle), TILE - 1, 0)


def east_of(values):
    return pltpu.roll(values, values.shape[-1] - 1, values.ndim - 1)


def west_of(values):
    return pltpu.roll(values, 1, values.ndim - 1)


def relax_weights(middle, others):
    weights = [middle + other for other in others]
    diagonal = 1.0 + functools.reduce(jnp.add, weights)
    return weights, RELAXATION / diagonal


def relax(weights, factor, middle, others, force):
    total = force
    for weight, other in zip(weights, others):
        total = total + weight * other
    return (1.0 - RELAXATION) * middle + factor * total


def around(ref, lead, shell, start):
    rows = lambda first: pl.ds(pl.multiple_of(first, TILE), TILE)
    middle = ref[(*lead, shell, rows(start))]
    return middle, [
        ref[(*lead, shell + 1, rows(start))],
        ref[(*lead, shell - 1, rows(start))],
        south_of(ref[(*lead, shell, rows(start + TILE))], middle),
        north_of(ref[(*lead, shell, rows(start - TILE))], middle),
        west_of(middle),
        east_of(middle),
    ]


def message_kernel(viscosity_from, d, f, index, one, two, fields, forces, layers, rows_of, viscosity, sems):
    components, shells, rows, count = d.shape
    copies = [pltpu.make_async_copy(viscosity_from, viscosity, sems.at[0])]
    for side, start in enumerate((0, rows - TILE)):
        part = pl.ds(start, TILE)
        copies += [
            pltpu.make_async_copy(index.at[:, part], layers.at[side], sems.at[1 + side]),
            pltpu.make_async_copy(d.at[:, :, part], fields.at[side], sems.at[3 + side]),
            pltpu.make_async_copy(f.at[:, :, part], forces.at[side], sems.at[5 + side]),
        ]
    for copy in copies:
        copy.start()
    for copy in copies[:2] + copies[4:5]:
        copy.wait()
    near_eta, far_eta = 2 * components, 2 * components + 1
    for side, near, far in ((0, 0, 1), (1, TILE - 1, TILE - 2)):
        for s in range(shells):
            eta = half_viscosity(layers[side, s], viscosity)
            rows_of[near_eta, side * shells + s] = eta[near]
            rows_of[far_eta, side * shells + s] = eta[far]
    for copy in copies[2:4] + copies[5:]:
        copy.wait()
    for side, near, far in ((0, 0, 1), (1, TILE - 1, TILE - 2)):
        for s in range(shells):
            for c in range(components):
                rows_of[c, side * shells + s] = fields[side, c, s, near]
                rows_of[components + c, side * shells + s] = fields[side, c, s, far]
                rows_of[far_eta + 1 + c, side * shells + s] = forces[side, c, s, near]
    radial = lax.axis_index("radial")
    place = row_number((2 * shells, count)) % shells
    highest, lowest = place == shells - 1, place == 0
    zero = jnp.zeros((2 * shells, count), jnp.float32)

    def beside(near, far):
        middle = rows_of[near]
        return middle, [
            jnp.where(highest, zero, pltpu.roll(middle, 2 * shells - 1, 0)),
            jnp.where(lowest, zero, pltpu.roll(middle, 1, 0)),
            rows_of[far],
            west_of(middle),
            east_of(middle),
        ]

    eta, others = beside(near_eta, far_eta)
    weights = [eta + other for other in others]
    inside = (radial < lax.axis_size("radial") - 1, radial > 0)
    weights[0] = jnp.where(jnp.logical_and(highest, inside[0]), zero, weights[0])
    weights[1] = jnp.where(jnp.logical_and(lowest, inside[1]), zero, weights[1])
    diagonal = 1.0 + functools.reduce(jnp.add, weights)
    values, sums = [], []
    for c in range(components):
        middle, others = beside(c, components + c)
        total = rows_of[far_eta + 1 + c]
        for weight, other in zip(weights, others):
            total = total + weight * other
        values.append(middle)
        sums.append(total)
    for place, field in enumerate(values + [eta] + sums + [diagonal]):
        both = pltpu.roll(field, shells, 0)
        one[pl.ds(place * shells, shells)] = both[:shells]
        two[pl.ds(place * shells, shells)] = both[shells:]


def shell_order(shells):
    lower = lax.axis_index("radial") == 0
    return lambda k: jnp.where(lower, k, shells - 1 - k)


def viscosity_kernel(
    viscosity_from, d, f, index_from, token, table_from, eta_out, out, surface_swept, surface_eta, surface_force, table,
    index, eta, field, force, result, viscosity, sems, more_sems,
):
    del token
    _, shells, rows, count = d.shape
    components = d.shape[0]
    block = pl.ds(TILE, rows)
    shell = shell_order(shells)
    value_copy = pltpu.make_async_copy(viscosity_from, viscosity, sems.at[shells])
    layers = [pltpu.make_async_copy(index_from.at[shell(k)], index.at[k], sems.at[k]) for k in range(shells)]
    fields = [
        pltpu.make_async_copy(d.at[:, shell(k)], field.at[:, k + 1, block], more_sems.at[k]) for k in range(EARLY + 1)
    ]
    forces = [
        pltpu.make_async_copy(f.at[:, shell(k)], force.at[:, k], more_sems.at[EARLY + 1 + k]) for k in range(EARLY)
    ]
    table_copy = pltpu.make_async_copy(table_from, table, sems.at[shells + 1])
    start_all([value_copy, *layers, *fields, *forces])
    zeros = jnp.zeros((rows, count), jnp.float32)
    for c in range(components):
        field[c, 0, block] = zeros
    eta[0, block] = zeros
    value_copy.wait()
    stores = start_all([table_copy])
    for k in range(shells):
        layers[k].wait()

        def lookup(step, _):
            start = pl.multiple_of(step * TILE, TILE)
            eta[k + 1, pl.ds(start + TILE, TILE)] = half_viscosity(index[k, pl.ds(start, TILE)], viscosity)
            return 0

        lax.fori_loop(0, rows // TILE, lookup, 0, unroll=2)
        stores += start_all(
            [pltpu.make_async_copy(eta.at[k + 1, block], eta_out.at[shell(k)], more_sems.at[2 * EARLY + 1 + k])]
        )
    for k in range(EARLY):
        for copy in (fields[: EARLY + 1] if k == 0 else []) + forces[k : k + 1]:
            copy.wait()

        def sweep(step, _):
            start = pl.multiple_of(step * TILE, TILE)
            part = pl.ds(start, TILE)
            weights, factor = relax_weights(*around(eta, (), k + 1, start + TILE))
            for c in range(components):
                middle, others = around(field, (c,), k + 1, start + TILE)
                result[c, k, part] = relax(weights, factor, middle, others, force[c, k, part])
            surface_swept[1 - k, part] = result[0, k, part]
            surface_eta[1 - k, part] = eta[k + 1, pl.ds(start + TILE, TILE)]
            if k == 0:
                surface_force[part] = force[0, 0, part]
            sem = more_sems.at[2 * EARLY + 1 + shells + k]
            pltpu.make_async_copy(result.at[:, k, part], out.at[:, k, part], sem).start()
            return 0

        lax.fori_loop(0, rows // TILE, sweep, 0, unroll=2)
        stores.append(pltpu.make_async_copy(result.at[:, k], out.at[:, k], more_sems.at[2 * EARLY + 1 + shells + k]))
    for copy in stores:
        copy.wait()


def surface_kernel(
    surface_swept, surface_eta, force, own_one, own_two, one, two, high, low_from, out,
    swept, eta, surface, low, sem, components,
):
    rows, count = force.shape

    @pl.when(lax.axis_index("radial") == lax.axis_size("radial") - 1)
    def _():
        low_copy = pltpu.make_async_copy(low_from, low, sem)
        low_copy.start()
        block = pl.ds(TILE, rows)
        for k in range(2):
            swept[k, block] = surface_swept[k]
            eta[k, block] = surface_eta[k]
        swept[2, block] = jnp.zeros((rows, count), jnp.float32)
        eta[2, block] = jnp.zeros((rows, count), jnp.float32)
        fields = one.shape[0]
        shells = fields // (2 * (components + 1))
        lateral = lax.axis_index("lateral")
        inside = (lateral > 0, lateral < lax.axis_size("lateral") - 1)
        for beside, own, place, own_place, there in zip(
            (one[...], two[...]), (own_two[...], own_one[...]), (TILE - 1, rows + TILE), (TILE, rows + TILE - 1), inside
        ):
            for k in range(2):
                row = lambda message, kind: message[kind * shells + shells - 2 + k : kind * shells + shells - 1 + k]
                weight = row(beside, components) + row(own, components)

                def finish(message, other):
                    total = row(message, components + 1) + weight * row(other, 0)
                    factor = RELAXATION / (row(message, 2 * components + 1) + weight)
                    return (1.0 - RELAXATION) * row(message, 0) + factor * total

                swept[k, pl.ds(own_place, 1)] = finish(own, beside)
                if k == 1:
                    edge = finish(beside, own)
                    swept[k, pl.ds(place, 1)] = jnp.where(there, edge, jnp.zeros_like(edge))
                    eta[k, pl.ds(place, 1)] = row(beside, components)

        def second(step, _):
            start = pl.multiple_of(step * TILE, TILE)
            weights, factor = relax_weights(*around(eta, (), 1, start + TILE))
            middle, others = around(swept, (), 1, start + TILE)
            surface[pl.ds(start, TILE)] = relax(weights, factor, middle, others, force[pl.ds(start, TILE)])
            return 0

        lax.fori_loop(0, rows // TILE, second, 0, unroll=2)
        near, far = split(jnp.concatenate(fold(surface[...]), axis=0))
        total = dot(near, high[...]) + dot(far, high[...])
        low_copy.wait()
        total = total + dot(near, low[...])
        blocks = [total[k * rows : (k + 1) * rows] for k in range(RADIX)]
        kind, mirrored = order_class((1, total.shape[1]))
        cosine, sine = blocks[0], jnp.zeros_like(blocks[0])
        for k in range(1, RADIX // 2 + 1):
            cosine = jnp.where(kind == k, blocks[k], cosine)
        for k in range(1, RADIX // 2):
            sine = jnp.where(kind == k, blocks[RADIX // 2 + k], sine)
        sine = jnp.where(mirrored, -sine, sine)
        modes = total.shape[1] // 2
        fourier = jnp.concatenate(
            [cosine[:, :modes] - sine[:, modes:], cosine[:, modes:] + sine[:, :modes]], axis=1
        )
        blocks = out.shape[0]
        width = fourier.shape[1] // blocks
        for block in range(blocks):
            out[block] = pack(fourier[:, block * width : (block + 1) * width])


def sweep_shells(
    begin, source, f, h, store, field, eta, force, result, sems, before_first, last_loads, arrived, finish, after_shell
):
    components, shells, rows, count = f.shape
    inner = pl.ds(TILE, rows)
    shell = shell_order(shells)

    def field_loads(k):
        s = shell(k)
        return [
            pltpu.make_async_copy(source(k), field.at[:, s + 1, inner], sems.at[k, 0]),
            pltpu.make_async_copy(h.at[s], eta.at[s + 1, inner], sems.at[k, 1]),
            *(last_loads if k == shells - 1 else []),
        ]

    def force_load(k):
        return [pltpu.make_async_copy(f.at[:, shell(k)], force.at[:, shell(k)], sems.at[k, 2])]

    loads = {k: start_all(field_loads(k)) for k in range(max(begin - 1, 0), begin + 2)}
    forces = {begin: start_all(force_load(begin))}
    if begin == 0:
        nothing = jnp.where(lax.axis_index("radial") == 0, 0, shells + 1)
        zeros = jnp.zeros((rows, count), jnp.float32)
        for c in range(components):
            field[c, nothing, inner] = zeros
        eta[nothing, inner] = zeros

    def start_until(k):
        for ahead in range(begin, shells):
            if ahead <= k and ahead not in loads:
                loads[ahead] = start_all(field_loads(ahead))
            if ahead < k and ahead not in forces:
                forces[ahead] = start_all(force_load(ahead))

    start_until(begin + 2)
    before_first()
    stores, there = [], set()
    for k in range(begin, shells):
        s = shell(k)
        start_until(k + 3)
        for near in range(max(k - 1, 0), min(k + 2, shells)):
            if near not in there:
                there.add(near)
                for copy in loads[near]:
                    copy.wait()
                arrived(near)
        for copy in forces[k]:
            copy.wait()

        def tile(step, _):
            first = pl.multiple_of(step * TILE, TILE)
            part = pl.ds(first, TILE)
            if k == shells - 1:
                finish(s, first)
            else:
                weights, factor = relax_weights(*around(eta, (), s + 1, first + TILE))
                for c in range(components):
                    middle, others = around(field, (c,), s + 1, first + TILE)
                    result[c, s, part] = relax(weights, factor, middle, others, force[c, s, part])
            pltpu.make_async_copy(result.at[:, s, part], store(k).at[:, part], sems.at[k, 3]).start()
            return 0

        lax.fori_loop(0, rows // TILE, tile, 0, unroll=2)
        stores.append(pltpu.make_async_copy(result.at[:, s], store(k), sems.at[k, 3]))
        after_shell(s, k)
    for copy in stores:
        copy.wait()


def set_edge(ref, lead, shells, rows, before, after):
    for s in range(shells):
        ref[(*lead, s + 1, TILE - 1)] = before(s)
        ref[(*lead, s + 1, rows + TILE)] = after(s)


def start_all(copies):
    for copy in copies:
        copy.start()
    return copies


def load_messages(sources, lower_sources, slots, sems):
    lower = lax.axis_index("radial") < lax.axis_size("radial") - 1
    copies = lambda refs: [pltpu.make_async_copy(ref, slots.at[k], sems.at[k]) for k, ref in enumerate(refs)]
    pl.when(lower)(lambda: [copy.start() for copy in copies(lower_sources)] and None)
    pl.when(jnp.logical_not(lower))(lambda: [copy.start() for copy in copies(sources)] and None)
    return copies(sources)


def first_kernel(d, f, h, one, two, lower_one, lower_two, mine_one, mine_two, *refs):
    components, shells, rows, count = d.shape
    staged = (len(refs) - 13) // 2
    sources, refs = refs[:staged], refs[staged:]
    out, diagonal_out, ring_out, own_out, beside_out, *targets = refs[: 5 + staged]
    field, eta, force, result, messages, edges, diagonal, sems, more_sems = refs[5 + staged :]
    arrivals = load_messages((one, two), (lower_one, lower_two), messages, more_sems)
    lower = lax.axis_index("radial") == 0
    last, beyond = jnp.where(lower, shells - 1, 0), jnp.where(lower, shells + 1, 0)
    values = pl.ds(0, own_out.shape[1])
    copies = start_all(
        [
            pltpu.make_async_copy(mine.at[values], own_out.at[k], more_sems.at[4 + components + k])
            for k, mine in enumerate((mine_one, mine_two))
        ]
    )

    def before_first():
        block = pl.ds(TILE, rows)
        zeros = jnp.zeros((rows, count), jnp.float32)
        for c in range(components):
            field[c, beyond, block] = zeros
        eta[beyond, block] = zeros
        for copy in arrivals:
            copy.wait()
        before, after = messages[0], messages[1]
        row = lambda message, kind: lambda s: message[kind * shells + s]
        for c in range(components):
            set_edge(field, (c,), shells, rows, row(before, c), row(after, c))
        set_edge(eta, (), shells, rows, row(before, components), row(after, components))
        for side, message in enumerate((before, after)):
            for k in range(components + 1):
                edges[side * (components + 1) + k] = jnp.where(
                    lower, message[(k + 1) * shells - 1], message[k * shells]
                )
        tail = ring_out.at[pl.ds(2 * (components + 1) * rows, edges.shape[0])]
        copies.extend(
            start_all(
                [
                    pltpu.make_async_copy(edges, tail, more_sems.at[2]),
                    pltpu.make_async_copy(messages, beside_out, more_sems.at[3]),
                ]
            )
        )

    def arrived(k):
        if k < shells - 1:
            return
        block = pl.ds(TILE, rows)
        sources = [field.at[c, last + 1, block] for c in range(components)] + [eta.at[last + 1, block]]
        copies.extend(
            start_all(
                [
                    pltpu.make_async_copy(source, ring_out.at[pl.ds(k * rows, rows)], more_sems.at[6 + components + k])
                    for k, source in enumerate(sources)
                ]
            )
        )

    def finish(s, first):
        part = pl.ds(first, TILE)
        middle, others = around(eta, (), s + 1, first + TILE)
        weights = [middle + other for other in others]
        zero = jnp.zeros_like(middle)
        weights[0] = jnp.where(lower, zero, weights[0])
        weights[1] = jnp.where(lower, weights[1], zero)
        diagonal[part] = 1.0 + functools.reduce(jnp.add, weights)
        for c in range(components):
            total = force[c, s, part]
            for weight, other in zip(weights, around(field, (c,), s + 1, first + TILE)[1]):
                total = total + weight * other
            result[c, s, part] = total

    def after_shell(s, k):
        if k == EARLY:
            copies.extend(
                start_all(
                    [
                        pltpu.make_async_copy(source, target, more_sems.at[8 + 3 * components + n])
                        for n, (source, target) in enumerate(zip(sources, targets))
                    ]
                )
            )
        if k == shells - 1:
            sums = [result.at[c, s] for c in range(components)] + [diagonal]
            copies.extend(
                start_all(
                    [
                        pltpu.make_async_copy(
                            source,
                            ring_out.at[pl.ds((components + 1 + n) * rows, rows)],
                            more_sems.at[7 + 2 * components + n],
                        )
                        for n, source in enumerate(sums)
                    ]
                    + [pltpu.make_async_copy(diagonal, diagonal_out, more_sems.at[0])]
                )
            )

    shell = shell_order(shells)
    sweep_shells(
        EARLY, lambda k: d.at[:, shell(k)], f, h, lambda k: out.at[:, k - EARLY],
        field, eta, force, result, sems, before_first, [], arrived, finish, after_shell,
    )
    for copy in copies:
        copy.wait()


def second_kernel(early, late, f, h, start, diagonal_from, ring, beside, own_from, *refs):
    components, shells, rows, count = f.shape
    staged = (len(refs) - 18) // 2
    mask_from, *sources = refs[: 1 + staged]
    out, token, mask_out, *targets = refs[1 + staged : 4 + 2 * staged]
    (
        field, eta, force, result, messages, edges, own, diagonal, raw, ring_diagonal, mask, ends, sems, more_sems
    ) = refs[4 + 2 * staged :]
    token[...] = jnp.zeros_like(token)
    tail = ring.at[pl.ds(2 * (components + 1) * rows, edges.shape[0])]
    arrivals = start_all(
        [
            pltpu.make_async_copy(beside, messages, more_sems.at[0]),
            pltpu.make_async_copy(tail, edges, more_sems.at[1]),
            pltpu.make_async_copy(own_from, own, more_sems.at[2]),
        ]
    )
    radial, lateral = lax.axis_index("radial"), lax.axis_index("lateral")
    lower = radial == 0
    last, beyond = jnp.where(lower, shells - 1, 0), jnp.where(lower, shells + 1, 0)
    block = pl.ds(TILE, rows)
    shell = shell_order(shells)
    from_ring = lambda k, target, sem: pltpu.make_async_copy(
        ring.at[pl.ds(k * rows, rows)], target, more_sems.at[sem]
    )
    last_loads = [
        pltpu.make_async_copy(start.at[:, last], raw.at[pl.ds(0, components)], more_sems.at[3]),
        pltpu.make_async_copy(diagonal_from, diagonal, more_sems.at[4]),
        *(from_ring(c, raw.at[components + c], 5 + c) for c in range(components)),
        from_ring(components, eta.at[beyond, block], 5 + components),
        *(
            from_ring(components + 1 + c, field.at[c, beyond, block], 6 + components + c)
            for c in range(components)
        ),
        from_ring(2 * components + 1, ring_diagonal, 6 + 2 * components),
    ]
    copies = []
    mask_copy = pltpu.make_async_copy(mask_from, mask, more_sems.at[7 + 2 * components])

    def before_first():
        for copy in arrivals:
            copy.wait()
        before, after = messages[0], messages[1]
        pair = lambda k: jnp.concatenate(
            [before[k * shells : (k + 1) * shells], after[k * shells : (k + 1) * shells]], axis=0
        )
        place = row_number((2 * shells, count))
        zero = jnp.zeros((2 * shells, count), jnp.float32)
        shared = place % shells == last
        across_of = lambda k: jnp.where(
            place < shells, edges[pl.ds(k, 1)], edges[pl.ds(components + 1 + k, 1)]
        )
        inside = jnp.where(place < shells, lateral, lax.axis_size("lateral") - 1 - lateral) > 0
        mine = (own[1], own[0])
        own_row = lambda k: jnp.concatenate([part[k * shells : (k + 1) * shells] for part in mine], axis=0)
        middle = pair(components)
        weight = middle + own_row(components)
        across = jnp.where(shared, middle + across_of(components), zero)
        factor = RELAXATION / (pair(2 * components + 1) + weight + across)
        own_factor = RELAXATION / (own_row(2 * components + 1) + weight)
        for c in range(components):
            total = pair(components + 1 + c) + weight * own_row(c) + across * across_of(c)
            edge = jnp.where(inside, (1.0 - RELAXATION) * pair(c) + factor * total, zero)
            total = own_row(components + 1 + c) + weight * pair(c)
            ends[c] = (1.0 - RELAXATION) * own_row(c) + own_factor * total
            set_edge(field, (c,), shells, rows, lambda s: edge[s], lambda s: edge[shells + s])
        set_edge(eta, (), shells, rows, lambda s: middle[s], lambda s: middle[shells + s])

    def arrived(k):
        if k < EARLY:
            s = shell(k)
            for side, place in enumerate((TILE, TILE + rows - 1)):
                for c in range(components):
                    field[c, s + 1, pl.ds(place, 1)] = ends[c, pl.ds(side * shells + s, 1)]
        if k < shells - 1:
            return

        def tile(step, _):
            first = pl.multiple_of(step * TILE, TILE)
            part, place = pl.ds(first, TILE), pl.ds(first + TILE, TILE)
            weight = eta[last + 1, place] + eta[beyond, place]
            here, there = RELAXATION / (diagonal[part] + weight), RELAXATION / (ring_diagonal[part] + weight)
            for c in range(components):
                mine, other = raw[c, part], raw[components + c, part]
                field[c, last + 1, place] = (1.0 - RELAXATION) * mine + here * (
                    field[c, last + 1, place] + weight * other
                )
                field[c, beyond, place] = (1.0 - RELAXATION) * other + there * (
                    field[c, beyond, place] + weight * mine
                )
            return 0

        lax.fori_loop(0, rows // TILE, tile, 0)

    def finish(s, first):
        part = pl.ds(first, TILE)
        weights, factor = relax_weights(*around(eta, (), s + 1, first + TILE))
        for c in range(components):
            middle, others = around(field, (c,), s + 1, first + TILE)
            result[c, s, part] = relax(weights, factor, middle, others, force[c, s, part])

    def after_shell(s, k):
        if k == shells - 2:
            copies.extend(
                start_all(
                    [
                        pltpu.make_async_copy(source, target, more_sems.at[8 + 2 * components + n])
                        for n, (source, target) in enumerate(zip(sources, targets))
                    ]
                )
            )
            mask_copy.start()
        if k == shells - 1:
            mask_copy.wait()
            mask_out[...] = mask[...].astype(jnp.float32).astype(jnp.bfloat16)

    sweep_shells(
        0, lambda k: early.at[:, k] if k < EARLY else late.at[:, k - EARLY], f, h, lambda k: out.at[:, shell(k)],
        field, eta, force, result, sems, before_first, last_loads, arrived, finish, after_shell,
    )
    for copy in copies:
        copy.wait()


def spectrum_kernel(orders, high, low, response, coefficients, out):
    radial = lax.axis_size("radial")
    width = coefficients.shape[0]
    bands, rows = orders.shape[0] // radial, high.shape[0] * radial // orders.shape[0]
    fourier = jnp.concatenate([unpack(orders[band * radial + radial - 1], width) for band in range(bands)], axis=0)
    near, far = split(fourier.T)
    spectrum = three_pass(dot, near, far, high, low)
    coefficients[...] = spectrum
    own = response[:, :width]
    for place in range(1, radial):
        own = jnp.where(
            lax.axis_index("radial") == place, response[:, place * width : (place + 1) * width], own
        )
    near, far = split(own.T * spectrum)
    load = three_pass(dot_nt, near, far, high, low).T
    for band in range(bands):
        block = pack(load[band * rows : (band + 1) * rows])
        for place in range(radial):
            out[band * radial + place] = block


def load_kernel(load, high, low, mask, out):
    blocks, rows = load.shape[0], out.shape[0]
    step, width = out.shape[1] // RADIX, high.shape[1] // blocks
    values = jnp.concatenate([unpack(load[block], width) for block in range(blocks)], axis=1)
    modes = values.shape[1] // 2
    kind, mirrored = order_class((1, values.shape[1]))
    crossed = jnp.concatenate([values[:, modes:], -values[:, :modes]], axis=1)
    crossed = jnp.where(mirrored, -crossed, crossed)
    zero = jnp.zeros_like(values)
    stack = [jnp.where(kind == k, values, zero) for k in range(RADIX // 2 + 1)]
    stack += [jnp.where(kind == k, crossed, zero) for k in range(1, RADIX // 2)]
    near, far = split(jnp.concatenate(stack, axis=0))
    total = dot_nt(near, high[...]) + dot_nt(far, high[...]) + dot_nt(near, low[...])
    for m, part in enumerate(unfold([total[k * rows : (k + 1) * rows] for k in range(RADIX)])):
        columns = slice(m * step, (m + 1) * step)
        out[:, columns] = part * mask[:, columns].astype(jnp.float32)


def cost(microseconds):
    return pl.CostEstimate(flops=0, bytes_accessed=3_000_000 * microseconds, transcendentals=0)


def hbm(values):
    return pltpu.with_memory_space_constraint(values, pltpu.HBM)


def shards(initial_displacement, force, viscosity, layer_index, response, ocean_mask):
    components, shells, rows, count = initial_displacement.shape
    radial, lateral = lax.axis_size("radial"), lax.axis_size("lateral")
    f32 = functools.partial(jax.ShapeDtypeStruct, dtype=jnp.float32)
    scratch = lambda *shape: pltpu.VMEM(shape, jnp.float32)
    in_hbm = lambda *shape: pltpu.HBM(shape, jnp.float32)
    width = 2 * MODES // (lateral * radial)
    first = [(i, i + 1) for i in range(lateral - 1)]
    second = [(i + 1, i) for i in range(lateral - 1)]
    both = ("lateral", "radial")
    top_only = lambda pairs: [(i * radial + radial - 1, j * radial + radial - 1) for i, j in pairs]

    lower_only = lambda pairs: [(i * radial + k, j * radial + k) for i, j in pairs for k in range(radial - 1)]
    swap = [(i, radial - 1 - i) for i in range(radial)]
    tensors = [hbm(a) for a in (initial_displacement, force, layer_index)]
    viscosity = hbm(viscosity)
    message = f32((2 * (components + 1) * shells, count))
    sides = lambda *shape: scratch(2, *shape)
    mine = pl.pallas_call(
        message_kernel,
        in_specs=[HBM] * 4,
        out_specs=[VMEM] * 2,
        out_shape=[message] * 2,
        scratch_shapes=[
            sides(components, shells, TILE, count),
            sides(components, shells, TILE, count),
            pltpu.VMEM((2, shells, TILE, count), jnp.int32),
            scratch(3 * components + 2, 2 * shells, count),
            pltpu.SMEM(viscosity.shape, jnp.float32),
            pltpu.SemaphoreType.DMA((7,)),
        ],
        compiler_params=params(16),
        cost_estimate=cost(20),
    )(viscosity, *tensors)
    two = lax.ppermute(mine[1], both, top_only(second))
    one = lax.ppermute(mine[0], both, top_only(first))
    high, low = longitude_tables(count, MODES)
    high, low = hbm(jnp.asarray(high)), hbm(jnp.asarray(low))
    eta, early, *surface, table = pl.pallas_call(
        viscosity_kernel,
        in_specs=[HBM] * 4 + [ANY, HBM],
        out_specs=[HBM, HBM, VMEM, VMEM, VMEM, VMEM],
        out_shape=[
            in_hbm(shells, rows, count),
            in_hbm(components, EARLY, rows, count),
            f32((2, rows, count)),
            f32((2, rows, count)),
            f32((rows, count)),
            jax.ShapeDtypeStruct(high.shape, high.dtype),
        ],
        scratch_shapes=[
            pltpu.VMEM(layer_index.shape, jnp.int32),
            scratch(shells + 1, rows + 2 * TILE, count),
            scratch(components, EARLY + 2, rows + 2 * TILE, count),
            scratch(components, EARLY, rows, count),
            scratch(components, EARLY, rows, count),
            pltpu.SMEM(viscosity.shape, jnp.float32),
            pltpu.SemaphoreType.DMA((2 + shells,)),
            pltpu.SemaphoreType.DMA((3 * EARLY + 1 + shells,)),
        ],
        compiler_params=params(24),
        cost_estimate=cost(20),
    )(viscosity, *tensors, mine[0], high)
    lower_one, lower_two, eta = lax.optimization_barrier((*mine, eta))
    lower_one = lax.ppermute(lower_one, both, lower_only(first))
    lower_two = lax.ppermute(lower_two, both, lower_only(second))

    packed = (lateral * radial, rows * width // max(128, width), max(128, width))
    orders = pl.pallas_call(
        functools.partial(surface_kernel, components=components),
        in_specs=[VMEM] * 8 + [HBM],
        out_specs=VMEM,
        out_shape=f32(packed),
        scratch_shapes=[
            scratch(3, rows + 2 * TILE, count),
            scratch(3, rows + 2 * TILE, count),
            scratch(rows, count),
            pltpu.VMEM(low.shape, low.dtype),
            pltpu.SemaphoreType.DMA,
        ],
        compiler_params=params(16),
        cost_estimate=cost(200),
    )(*surface, *mine, one, two, table, low)
    eta, _ = lax.optimization_barrier((eta, orders))
    orders = lax.all_to_all(orders, both, split_axis=0, concat_axis=0, tiled=True)
    eta = hbm(eta)

    sweep_scratch = [
        scratch(components, shells + 2, rows + 2 * TILE, count),
        scratch(shells + 2, rows + 2 * TILE, count),
        scratch(components, shells, rows, count),
        scratch(components, shells, rows, count),
    ]
    sweep_sems = pltpu.SemaphoreType.DMA((shells, 4))
    point_high, point_low = colatitude_tables(rows * lateral, MODES)
    stages = [jnp.asarray(point_high), jnp.asarray(point_low)] + [response]
    ring_rows = 2 * (components + 1) * (rows + 1)
    sweep_scratch += [
        sides(*message.shape),
        scratch(2 * (components + 1), count),
    ]
    own_shape = (2, *message.shape)
    late, diagonal, ring, own, beside, *staged = pl.pallas_call(
        first_kernel,
        in_specs=[HBM] * 3 + [ANY] * 6 + [HBM] * len(stages),
        out_specs=[HBM] * 5 + [VMEM] * len(stages),
        out_shape=[
            in_hbm(components, shells - EARLY, rows, count),
            in_hbm(rows, count),
            in_hbm(ring_rows, count),
            in_hbm(*own_shape),
            in_hbm(2, *message.shape),
            *(jax.ShapeDtypeStruct(a.shape, a.dtype) for a in stages),
        ],
        scratch_shapes=[
            *sweep_scratch,
            scratch(rows, count),
            sweep_sems,
            pltpu.SemaphoreType.DMA((8 + 3 * components + len(stages),)),
        ],
        compiler_params=params(28),
        cost_estimate=cost(50),
    )(*tensors[:2], hbm(eta), one, two, lower_one, lower_two, *mine, *(hbm(a) for a in stages))
    ring, orders = lax.optimization_barrier((ring, orders))
    ring = lax.ppermute(ring, "radial", swap)
    coefficients, load = pl.pallas_call(
        spectrum_kernel,
        in_specs=[VMEM] * 4,
        out_specs=[VMEM, VMEM],
        out_shape=[f32((width, MODES)), f32(packed)],
        compiler_params=params(16),
        cost_estimate=cost(200),
    )(orders, *staged)
    eta, load = lax.optimization_barrier((eta, load))
    load = lax.all_to_all(load, both, split_axis=0, concat_axis=0, tiled=True)

    stages = [high, low]
    displacement, token, mask, *staged = pl.pallas_call(
        second_kernel,
        in_specs=[HBM] * 6 + [ANY] + [HBM] * (3 + len(stages)),
        out_specs=[HBM, VMEM, VMEM] + [VMEM] * len(stages),
        out_shape=[
            in_hbm(*initial_displacement.shape),
            f32((TILE, 128)),
            jax.ShapeDtypeStruct(ocean_mask.shape, jnp.bfloat16),
            *(jax.ShapeDtypeStruct(a.shape, a.dtype) for a in stages),
        ],
        scratch_shapes=[
            *sweep_scratch,
            scratch(*own_shape),
            scratch(rows, count),
            scratch(2 * components, rows, count),
            scratch(rows, count),
            pltpu.VMEM(ocean_mask.shape, ocean_mask.dtype),
            scratch(components, 2 * shells, count),
            sweep_sems,
            pltpu.SemaphoreType.DMA((8 + 2 * components + len(stages),)),
        ],
        compiler_params=params(28),
        cost_estimate=cost(50),
    )(
        *(hbm(a) for a in (early, late, tensors[1], eta, tensors[0], diagonal)),
        ring,
        *(hbm(a) for a in (beside, own, ocean_mask)),
        *stages,
    )

    sea_load = pl.pallas_call(
        load_kernel,
        in_specs=[VMEM] * 4,
        out_specs=VMEM,
        out_shape=f32((rows, count)),
        compiler_params=params(20),
        cost_estimate=cost(3),
    )(load, *staged, mask)
    return (displacement, coefficients.T, sea_load)


def solution(mesh):
    in_specs = (
        P("member", "radial", "lateral", None),
        P("member", "radial", "lateral", None),
        P("member"),
        P("radial", "lateral", None),
        P(None, "lateral"),
        P("lateral", None),
    )
    out_specs = (
        P("member", "radial", "lateral", None),
        P("member", ("lateral", "radial")),
        P("lateral", "member"),
    )
    return jax.shard_map(shards, mesh=mesh, in_specs=in_specs, out_specs=out_specs, check_vma=False)
```

```python
import functools
import math

import jax
import jax.numpy as jnp
import ml_dtypes
import numpy as np
from jax import lax
from jax.experimental import pallas as pl
from jax.experimental.pallas import tpu as pltpu
from jax.sharding import PartitionSpec as P

MODES = 512
RELAXATION = 0.8
TILE = 8
RADIX = 8
EARLY = 2
MIB = 1 << 20
ANY = pl.BlockSpec(memory_space=pl.ANY)
HBM = pl.BlockSpec(memory_space=pltpu.HBM)
SMEM = pl.BlockSpec(memory_space=pltpu.SMEM)
VMEM = pl.BlockSpec(memory_space=pltpu.VMEM)


def params(mib):
    return pltpu.CompilerParams(vmem_limit_bytes=mib * MIB)


def halves(table):
    high = table.astype(ml_dtypes.bfloat16)
    low = (table - high.astype(np.float64)).astype(ml_dtypes.bfloat16)
    return high, low


@functools.lru_cache
def longitude_tables(count, modes):
    points = np.arange(count // RADIX, dtype=np.int64)[:, None]
    orders = np.arange(modes, dtype=np.int64)[None, :]
    angle = (2.0 * math.pi / count) * (points * orders % count)
    table = np.concatenate([np.cos(angle), np.sin(angle)], axis=1) * math.sqrt(2.0 / count)
    return halves(table)


@functools.lru_cache
def colatitude_tables(count, modes):
    points = np.arange(count, dtype=np.int64)[:, None]
    waves = np.arange(modes, dtype=np.int64)[None, :]
    phase = waves * (2 * points + 1) % (4 * count)
    return halves(np.cos(math.pi / (2 * count) * phase) * math.sqrt(2.0 / count))


def split(values):
    high = values.astype(jnp.bfloat16)
    return high, (values - high.astype(jnp.float32)).astype(jnp.bfloat16)


def dot(a, b):
    return jnp.dot(a, b, preferred_element_type=jnp.float32)


def pack(block):
    rows, width = block.shape
    groups = max(1, 128 // width)
    rows //= groups
    return jnp.concatenate([block[k * rows : (k + 1) * rows] for k in range(groups)], axis=1)


def unpack(block, width):
    groups = max(1, 128 // width)
    return jnp.concatenate([block[:, k * width : (k + 1) * width] for k in range(groups)], axis=0)


def weighted_sum(terms):
    total = None
    for factor, values in terms:
        factor = round(factor, 15)
        if factor == 0.0:
            continue
        part = values if abs(factor) == 1.0 else abs(factor) * values
        if total is None:
            total = part if factor > 0 else -part
        else:
            total = total + part if factor > 0 else total - part
    return total


def turn(number):
    angle = 2.0 * math.pi * (number % RADIX) / RADIX
    return math.cos(angle), math.sin(angle)


def fold(values):
    step = values.shape[1] // RADIX
    parts = [values[:, m * step : (m + 1) * step] for m in range(RADIX)]
    cosines = [[(turn(k * m)[0], part) for m, part in enumerate(parts)] for k in range(RADIX // 2 + 1)]
    sines = [[(turn(k * m)[1], part) for m, part in enumerate(parts)] for k in range(1, RADIX // 2)]
    return [weighted_sum(terms) for terms in cosines + sines]


def unfold(blocks):
    cosines, sines = blocks[: RADIX // 2 + 1], blocks[RADIX // 2 + 1 :]
    return [
        weighted_sum(
            [(turn(k * m)[0], block) for k, block in enumerate(cosines)]
            + [(turn(k * m)[1], block) for k, block in enumerate(sines, 1)]
        )
        for m in range(RADIX)
    ]


def order_class(shape):
    order = lax.broadcasted_iota(jnp.int32, shape, len(shape) - 1) % RADIX
    mirrored = order > RADIX // 2
    return jnp.where(mirrored, RADIX - order, order), mirrored


def three_pass(product, near, far, high, low):
    both = product(jnp.concatenate([near, far], axis=0), high[...])
    return both[: near.shape[0]] + both[near.shape[0] :] + product(near, low[...])


def dot_nt(a, b):
    return lax.dot_general(a, b, (((1,), (1,)), ((), ())), preferred_element_type=jnp.float32)


def half_viscosity(index, viscosity_ref):
    values = [0.5 * viscosity_ref[k] for k in range(viscosity_ref.shape[0])]
    bit = 1
    while len(values) > 1:
        odd = (index & bit) != 0
        if len(values) % 2:
            values.append(values[-1])
        values = [jnp.where(odd, b, a) for a, b in zip(values[::2], values[1::2])]
        bit *= 2
    return values[0]


def row_number(shape):
    return lax.broadcasted_iota(jnp.int32, shape, 0)


def north_of(above, middle):
    return pltpu.roll(jnp.where(row_number(middle.shape) == TILE - 1, above, middle), 1, 0)


def south_of(below, middle):
    return pltpu.roll(jnp.where(row_number(middle.shape) == 0, below, middle), TILE - 1, 0)


def east_of(values):
    return pltpu.roll(values, values.shape[-1] - 1, values.ndim - 1)


def west_of(values):
    return pltpu.roll(values, 1, values.ndim - 1)


def relax_weights(middle, others):
    weights = [middle + other for other in others]
    diagonal = 1.0 + functools.reduce(jnp.add, weights)
    return weights, RELAXATION / diagonal


def relax(weights, factor, middle, others, force):
    total = force
    for weight, other in zip(weights, others):
        total = total + weight * other
    return (1.0 - RELAXATION) * middle + factor * total


def around(ref, lead, shell, start):
    rows = lambda first: pl.ds(pl.multiple_of(first, TILE), TILE)
    middle = ref[(*lead, shell, rows(start))]
    return middle, [
        ref[(*lead, shell + 1, rows(start))],
        ref[(*lead, shell - 1, rows(start))],
        south_of(ref[(*lead, shell, rows(start + TILE))], middle),
        north_of(ref[(*lead, shell, rows(start - TILE))], middle),
        west_of(middle),
        east_of(middle),
    ]


def message_kernel(viscosity_from, d, f, index, one, two, fields, forces, layers, rows_of, viscosity, sems):
    components, shells, rows, count = d.shape
    copies = [pltpu.make_async_copy(viscosity_from, viscosity, sems.at[0])]
    for side, start in enumerate((0, rows - TILE)):
        part = pl.ds(start, TILE)
        copies += [
            pltpu.make_async_copy(index.at[:, part], layers.at[side], sems.at[1 + side]),
            pltpu.make_async_copy(d.at[:, :, part], fields.at[side], sems.at[3 + side]),
            pltpu.make_async_copy(f.at[:, :, part], forces.at[side], sems.at[5 + side]),
        ]
    for copy in copies:
        copy.start()
    for copy in copies[:2] + copies[4:5]:
        copy.wait()
    near_eta, far_eta = 2 * components, 2 * components + 1
    for side, near, far in ((0, 0, 1), (1, TILE - 1, TILE - 2)):
        for s in range(shells):
            eta = half_viscosity(layers[side, s], viscosity)
            rows_of[near_eta, side * shells + s] = eta[near]
            rows_of[far_eta, side * shells + s] = eta[far]
    for copy in copies[2:4] + copies[5:]:
        copy.wait()
    for side, near, far in ((0, 0, 1), (1, TILE - 1, TILE - 2)):
        for s in range(shells):
            for c in range(components):
                rows_of[c, side * shells + s] = fields[side, c, s, near]
                rows_of[components + c, side * shells + s] = fields[side, c, s, far]
                rows_of[far_eta + 1 + c, side * shells + s] = forces[side, c, s, near]
    radial = lax.axis_index("radial")
    place = row_number((2 * shells, count)) % shells
    highest, lowest = place == shells - 1, place == 0
    zero = jnp.zeros((2 * shells, count), jnp.float32)

    def beside(near, far):
        middle = rows_of[near]
        return middle, [
            jnp.where(highest, zero, pltpu.roll(middle, 2 * shells - 1, 0)),
            jnp.where(lowest, zero, pltpu.roll(middle, 1, 0)),
            rows_of[far],
            west_of(middle),
            east_of(middle),
        ]

    eta, others = beside(near_eta, far_eta)
    weights = [eta + other for other in others]
    inside = (radial < lax.axis_size("radial") - 1, radial > 0)
    weights[0] = jnp.where(jnp.logical_and(highest, inside[0]), zero, weights[0])
    weights[1] = jnp.where(jnp.logical_and(lowest, inside[1]), zero, weights[1])
    diagonal = 1.0 + functools.reduce(jnp.add, weights)
    values, sums = [], []
    for c in range(components):
        middle, others = beside(c, components + c)
        total = rows_of[far_eta + 1 + c]
        for weight, other in zip(weights, others):
            total = total + weight * other
        values.append(middle)
        sums.append(total)
    for place, field in enumerate(values + [eta] + sums + [diagonal]):
        both = pltpu.roll(field, shells, 0)
        one[pl.ds(place * shells, shells)] = both[:shells]
        two[pl.ds(place * shells, shells)] = both[shells:]


def shell_order(shells):
    lower = lax.axis_index("radial") == 0
    return lambda k: jnp.where(lower, k, shells - 1 - k)


def viscosity_kernel(
    viscosity_from, d, f, index_from, token, table_from, eta_out, out, surface_swept, surface_eta, surface_force, table,
    index, eta, field, force, result, viscosity, sems, more_sems,
):
    del token
    _, shells, rows, count = d.shape
    components = d.shape[0]
    block = pl.ds(TILE, rows)
    shell = shell_order(shells)
    value_copy = pltpu.make_async_copy(viscosity_from, viscosity, sems.at[shells])
    layers = [pltpu.make_async_copy(index_from.at[shell(k)], index.at[k], sems.at[k]) for k in range(shells)]
    fields = [
        pltpu.make_async_copy(d.at[:, shell(k)], field.at[:, k + 1, block], more_sems.at[k]) for k in range(EARLY + 1)
    ]
    forces = [
        pltpu.make_async_copy(f.at[:, shell(k)], force.at[:, k], more_sems.at[EARLY + 1 + k]) for k in range(EARLY)
    ]
    table_copy = pltpu.make_async_copy(table_from, table, sems.at[shells + 1])
    start_all([value_copy, *layers, *fields, *forces])
    zeros = jnp.zeros((rows, count), jnp.float32)
    for c in range(components):
        field[c, 0, block] = zeros
    eta[0, block] = zeros
    value_copy.wait()
    stores = start_all([table_copy])
    for k in range(shells):
        layers[k].wait()

        def lookup(step, _):
            start = pl.multiple_of(step * TILE, TILE)
            eta[k + 1, pl.ds(start + TILE, TILE)] = half_viscosity(index[k, pl.ds(start, TILE)], viscosity)
            return 0

        lax.fori_loop(0, rows // TILE, lookup, 0, unroll=2)
        stores += start_all(
            [pltpu.make_async_copy(eta.at[k + 1, block], eta_out.at[shell(k)], more_sems.at[2 * EARLY + 1 + k])]
        )
    for k in range(EARLY):
        for copy in (fields[: EARLY + 1] if k == 0 else []) + forces[k : k + 1]:
            copy.wait()

        def sweep(step, _):
            start = pl.multiple_of(step * TILE, TILE)
            part = pl.ds(start, TILE)
            weights, factor = relax_weights(*around(eta, (), k + 1, start + TILE))
            for c in range(components):
                middle, others = around(field, (c,), k + 1, start + TILE)
                result[c, k, part] = relax(weights, factor, middle, others, force[c, k, part])
            surface_swept[1 - k, part] = result[0, k, part]
            surface_eta[1 - k, part] = eta[k + 1, pl.ds(start + TILE, TILE)]
            if k == 0:
                surface_force[part] = force[0, 0, part]
            sem = more_sems.at[2 * EARLY + 1 + shells + k]
            pltpu.make_async_copy(result.at[:, k, part], out.at[:, k, part], sem).start()
            return 0

        lax.fori_loop(0, rows // TILE, sweep, 0, unroll=2)
        stores.append(pltpu.make_async_copy(result.at[:, k], out.at[:, k], more_sems.at[2 * EARLY + 1 + shells + k]))
    for copy in stores:
        copy.wait()


def surface_kernel(
    surface_swept, surface_eta, force, own_one, own_two, one, two, high, low_from, out,
    swept, eta, surface, low, sem, components,
):
    rows, count = force.shape

    @pl.when(lax.axis_index("radial") == lax.axis_size("radial") - 1)
    def _():
        low_copy = pltpu.make_async_copy(low_from, low, sem)
        low_copy.start()
        block = pl.ds(TILE, rows)
        for k in range(2):
            swept[k, block] = surface_swept[k]
            eta[k, block] = surface_eta[k]
        swept[2, block] = jnp.zeros((rows, count), jnp.float32)
        eta[2, block] = jnp.zeros((rows, count), jnp.float32)
        fields = one.shape[0]
        shells = fields // (2 * (components + 1))
        lateral = lax.axis_index("lateral")
        inside = (lateral > 0, lateral < lax.axis_size("lateral") - 1)
        for beside, own, place, own_place, there in zip(
            (one[...], two[...]), (own_two[...], own_one[...]), (TILE - 1, rows + TILE), (TILE, rows + TILE - 1), inside
        ):
            for k in range(2):
                row = lambda message, kind: message[kind * shells + shells - 2 + k : kind * shells + shells - 1 + k]
                weight = row(beside, components) + row(own, components)

                def finish(message, other):
                    total = row(message, components + 1) + weight * row(other, 0)
                    factor = RELAXATION / (row(message, 2 * components + 1) + weight)
                    return (1.0 - RELAXATION) * row(message, 0) + factor * total

                swept[k, pl.ds(own_place, 1)] = finish(own, beside)
                if k == 1:
                    edge = finish(beside, own)
                    swept[k, pl.ds(place, 1)] = jnp.where(there, edge, jnp.zeros_like(edge))
                    eta[k, pl.ds(place, 1)] = row(beside, components)

        def second(step, _):
            start = pl.multiple_of(step * TILE, TILE)
            weights, factor = relax_weights(*around(eta, (), 1, start + TILE))
            middle, others = around(swept, (), 1, start + TILE)
            surface[pl.ds(start, TILE)] = relax(weights, factor, middle, others, force[pl.ds(start, TILE)])
            return 0

        lax.fori_loop(0, rows // TILE, second, 0, unroll=2)
        near, far = split(jnp.concatenate(fold(surface[...]), axis=0))
        total = dot(near, high[...]) + dot(far, high[...])
        low_copy.wait()
        total = total + dot(near, low[...])
        blocks = [total[k * rows : (k + 1) * rows] for k in range(RADIX)]
        kind, mirrored = order_class((1, total.shape[1]))
        cosine, sine = blocks[0], jnp.zeros_like(blocks[0])
        for k in range(1, RADIX // 2 + 1):
            cosine = jnp.where(kind == k, blocks[k], cosine)
        for k in range(1, RADIX // 2):
            sine = jnp.where(kind == k, blocks[RADIX // 2 + k], sine)
        sine = jnp.where(mirrored, -sine, sine)
        modes = total.shape[1] // 2
        fourier = jnp.concatenate(
            [cosine[:, :modes] - sine[:, modes:], cosine[:, modes:] + sine[:, :modes]], axis=1
        )
        blocks = out.shape[0]
        width = fourier.shape[1] // blocks
        for block in range(blocks):
            out[block] = pack(fourier[:, block * width : (block + 1) * width])


def sweep_shells(
    begin, source, f, h, store, field, eta, force, result, sems, before_first, last_loads, arrived, finish, after_shell
):
    components, shells, rows, count = f.shape
    inner = pl.ds(TILE, rows)
    shell = shell_order(shells)

    def field_loads(k):
        s = shell(k)
        return [
            pltpu.make_async_copy(source(k), field.at[:, s + 1, inner], sems.at[k, 0]),
            pltpu.make_async_copy(h.at[s], eta.at[s + 1, inner], sems.at[k, 1]),
            *(last_loads if k == shells - 1 else []),
        ]

    def force_load(k):
        return [pltpu.make_async_copy(f.at[:, shell(k)], force.at[:, shell(k)], sems.at[k, 2])]

    loads = {k: start_all(field_loads(k)) for k in range(max(begin - 1, 0), begin + 2)}
    forces = {begin: start_all(force_load(begin))}
    if begin == 0:
        nothing = jnp.where(lax.axis_index("radial") == 0, 0, shells + 1)
        zeros = jnp.zeros((rows, count), jnp.float32)
        for c in range(components):
            field[c, nothing, inner] = zeros
        eta[nothing, inner] = zeros

    def start_until(k):
        for ahead in range(begin, shells):
            if ahead <= k and ahead not in loads:
                loads[ahead] = start_all(field_loads(ahead))
            if ahead < k and ahead not in forces:
                forces[ahead] = start_all(force_load(ahead))

    start_until(begin + 2)
    before_first()
    stores, there = [], set()
    for k in range(begin, shells):
        s = shell(k)
        start_until(k + 3)
        for near in range(max(k - 1, 0), min(k + 2, shells)):
            if near not in there:
                there.add(near)
                for copy in loads[near]:
                    copy.wait()
                arrived(near)
        for copy in forces[k]:
            copy.wait()

        def tile(step, _):
            first = pl.multiple_of(step * TILE, TILE)
            part = pl.ds(first, TILE)
            if k == shells - 1:
                finish(s, first)
            else:
                weights, factor = relax_weights(*around(eta, (), s + 1, first + TILE))
                for c in range(components):
                    middle, others = around(field, (c,), s + 1, first + TILE)
                    result[c, s, part] = relax(weights, factor, middle, others, force[c, s, part])
            pltpu.make_async_copy(result.at[:, s, part], store(k).at[:, part], sems.at[k, 3]).start()
            return 0

        lax.fori_loop(0, rows // TILE, tile, 0, unroll=2)
        stores.append(pltpu.make_async_copy(result.at[:, s], store(k), sems.at[k, 3]))
        after_shell(s, k)
    for copy in stores:
        copy.wait()


def set_edge(ref, lead, shells, rows, before, after):
    for s in range(shells):
        ref[(*lead, s + 1, TILE - 1)] = before(s)
        ref[(*lead, s + 1, rows + TILE)] = after(s)


def start_all(copies):
    for copy in copies:
        copy.start()
    return copies


def load_messages(sources, lower_sources, slots, sems):
    lower = lax.axis_index("radial") < lax.axis_size("radial") - 1
    copies = lambda refs: [pltpu.make_async_copy(ref, slots.at[k], sems.at[k]) for k, ref in enumerate(refs)]
    pl.when(lower)(lambda: [copy.start() for copy in copies(lower_sources)] and None)
    pl.when(jnp.logical_not(lower))(lambda: [copy.start() for copy in copies(sources)] and None)
    return copies(sources)


def first_kernel(d, f, h, one, two, lower_one, lower_two, mine_one, mine_two, *refs):
    components, shells, rows, count = d.shape
    staged = (len(refs) - 13) // 2
    sources, refs = refs[:staged], refs[staged:]
    out, diagonal_out, ring_out, own_out, beside_out, *targets = refs[: 5 + staged]
    field, eta, force, result, messages, edges, diagonal, sems, more_sems = refs[5 + staged :]
    arrivals = load_messages((one, two), (lower_one, lower_two), messages, more_sems)
    lower = lax.axis_index("radial") == 0
    last, beyond = jnp.where(lower, shells - 1, 0), jnp.where(lower, shells + 1, 0)
    values = pl.ds(0, own_out.shape[1])
    copies = []
    own_copies = lambda: start_all(
        [
            pltpu.make_async_copy(mine.at[values], own_out.at[k], more_sems.at[4 + components + k])
            for k, mine in enumerate((mine_one, mine_two))
        ]
    )

    def before_first():
        block = pl.ds(TILE, rows)
        zeros = jnp.zeros((rows, count), jnp.float32)
        for c in range(components):
            field[c, beyond, block] = zeros
        eta[beyond, block] = zeros
        for copy in arrivals:
            copy.wait()
        before, after = messages[0], messages[1]
        row = lambda message, kind: lambda s: message[kind * shells + s]
        for c in range(components):
            set_edge(field, (c,), shells, rows, row(before, c), row(after, c))
        set_edge(eta, (), shells, rows, row(before, components), row(after, components))
        for side, message in enumerate((before, after)):
            for k in range(components + 1):
                edges[side * (components + 1) + k] = jnp.where(
                    lower, message[(k + 1) * shells - 1], message[k * shells]
                )
        tail = ring_out.at[pl.ds(2 * (components + 1) * rows, edges.shape[0])]
        copies.extend(
            start_all(
                [
                    pltpu.make_async_copy(edges, tail, more_sems.at[2]),
                ]
            )
        )

    def arrived(k):
        if k < shells - 1:
            return
        block = pl.ds(TILE, rows)
        sources = [field.at[c, last + 1, block] for c in range(components)] + [eta.at[last + 1, block]]
        copies.extend(
            start_all(
                [
                    pltpu.make_async_copy(source, ring_out.at[pl.ds(k * rows, rows)], more_sems.at[6 + components + k])
                    for k, source in enumerate(sources)
                ]
            )
        )

    def finish(s, first):
        part = pl.ds(first, TILE)
        middle, others = around(eta, (), s + 1, first + TILE)
        weights = [middle + other for other in others]
        zero = jnp.zeros_like(middle)
        weights[0] = jnp.where(lower, zero, weights[0])
        weights[1] = jnp.where(lower, weights[1], zero)
        diagonal[part] = 1.0 + functools.reduce(jnp.add, weights)
        for c in range(components):
            total = force[c, s, part]
            for weight, other in zip(weights, around(field, (c,), s + 1, first + TILE)[1]):
                total = total + weight * other
            result[c, s, part] = total

    def after_shell(s, k):
        if k == EARLY:
            copies.extend(own_copies())
            copies.extend(start_all([pltpu.make_async_copy(messages, beside_out, more_sems.at[3])]))
            copies.extend(
                start_all(
                    [
                        pltpu.make_async_copy(source, target, more_sems.at[8 + 3 * components + n])
                        for n, (source, target) in enumerate(zip(sources, targets))
                    ]
                )
            )
        if k == shells - 1:
            sums = [result.at[c, s] for c in range(components)] + [diagonal]
            copies.extend(
                start_all(
                    [
                        pltpu.make_async_copy(
                            source,
                            ring_out.at[pl.ds((components + 1 + n) * rows, rows)],
                            more_sems.at[7 + 2 * components + n],
                        )
                        for n, source in enumerate(sums)
                    ]
                    + [pltpu.make_async_copy(diagonal, diagonal_out, more_sems.at[0])]
                )
            )

    shell = shell_order(shells)
    sweep_shells(
        EARLY, lambda k: d.at[:, shell(k)], f, h, lambda k: out.at[:, k - EARLY],
        field, eta, force, result, sems, before_first, [], arrived, finish, after_shell,
    )
    for copy in copies:
        copy.wait()


def second_kernel(early, late, f, h, start, diagonal_from, ring, beside, own_from, *refs):
    components, shells, rows, count = f.shape
    staged = (len(refs) - 18) // 2
    mask_from, *sources = refs[: 1 + staged]
    out, token, mask_out, *targets = refs[1 + staged : 4 + 2 * staged]
    (
        field, eta, force, result, messages, edges, own, diagonal, raw, ring_diagonal, mask, ends, sems, more_sems
    ) = refs[4 + 2 * staged :]
    token[...] = jnp.zeros_like(token)
    tail = ring.at[pl.ds(2 * (components + 1) * rows, edges.shape[0])]
    arrivals = start_all(
        [
            pltpu.make_async_copy(beside, messages, more_sems.at[0]),
            pltpu.make_async_copy(tail, edges, more_sems.at[1]),
            pltpu.make_async_copy(own_from, own, more_sems.at[2]),
        ]
    )
    radial, lateral = lax.axis_index("radial"), lax.axis_index("lateral")
    lower = radial == 0
    last, beyond = jnp.where(lower, shells - 1, 0), jnp.where(lower, shells + 1, 0)
    block = pl.ds(TILE, rows)
    shell = shell_order(shells)
    from_ring = lambda k, target, sem: pltpu.make_async_copy(
        ring.at[pl.ds(k * rows, rows)], target, more_sems.at[sem]
    )
    last_loads = [
        pltpu.make_async_copy(start.at[:, last], raw.at[pl.ds(0, components)], more_sems.at[3]),
        pltpu.make_async_copy(diagonal_from, diagonal, more_sems.at[4]),
        *(from_ring(c, raw.at[components + c], 5 + c) for c in range(components)),
        from_ring(components, eta.at[beyond, block], 5 + components),
        *(
            from_ring(components + 1 + c, field.at[c, beyond, block], 6 + components + c)
            for c in range(components)
        ),
        from_ring(2 * components + 1, ring_diagonal, 6 + 2 * components),
    ]
    copies = []
    mask_copy = pltpu.make_async_copy(mask_from, mask, more_sems.at[7 + 2 * components])

    def before_first():
        for copy in arrivals:
            copy.wait()
        before, after = messages[0], messages[1]
        pair = lambda k: jnp.concatenate(
            [before[k * shells : (k + 1) * shells], after[k * shells : (k + 1) * shells]], axis=0
        )
        place = row_number((2 * shells, count))
        zero = jnp.zeros((2 * shells, count), jnp.float32)
        shared = place % shells == last
        across_of = lambda k: jnp.where(
            place < shells, edges[pl.ds(k, 1)], edges[pl.ds(components + 1 + k, 1)]
        )
        inside = jnp.where(place < shells, lateral, lax.axis_size("lateral") - 1 - lateral) > 0
        mine = (own[1], own[0])
        own_row = lambda k: jnp.concatenate([part[k * shells : (k + 1) * shells] for part in mine], axis=0)
        middle = pair(components)
        weight = middle + own_row(components)
        across = jnp.where(shared, middle + across_of(components), zero)
        factor = RELAXATION / (pair(2 * components + 1) + weight + across)
        own_factor = RELAXATION / (own_row(2 * components + 1) + weight)
        for c in range(components):
            total = pair(components + 1 + c) + weight * own_row(c) + across * across_of(c)
            edge = jnp.where(inside, (1.0 - RELAXATION) * pair(c) + factor * total, zero)
            total = own_row(components + 1 + c) + weight * pair(c)
            ends[c] = (1.0 - RELAXATION) * own_row(c) + own_factor * total
            set_edge(field, (c,), shells, rows, lambda s: edge[s], lambda s: edge[shells + s])
        set_edge(eta, (), shells, rows, lambda s: middle[s], lambda s: middle[shells + s])

    def arrived(k):
        if k < EARLY:
            s = shell(k)
            for side, place in enumerate((TILE, TILE + rows - 1)):
                for c in range(components):
                    field[c, s + 1, pl.ds(place, 1)] = ends[c, pl.ds(side * shells + s, 1)]
        if k < shells - 1:
            return

        def tile(step, _):
            first = pl.multiple_of(step * TILE, TILE)
            part, place = pl.ds(first, TILE), pl.ds(first + TILE, TILE)
            weight = eta[last + 1, place] + eta[beyond, place]
            here, there = RELAXATION / (diagonal[part] + weight), RELAXATION / (ring_diagonal[part] + weight)
            for c in range(components):
                mine, other = raw[c, part], raw[components + c, part]
                field[c, last + 1, place] = (1.0 - RELAXATION) * mine + here * (
                    field[c, last + 1, place] + weight * other
                )
                field[c, beyond, place] = (1.0 - RELAXATION) * other + there * (
                    field[c, beyond, place] + weight * mine
                )
            return 0

        lax.fori_loop(0, rows // TILE, tile, 0)

    def finish(s, first):
        part = pl.ds(first, TILE)
        weights, factor = relax_weights(*around(eta, (), s + 1, first + TILE))
        for c in range(components):
            middle, others = around(field, (c,), s + 1, first + TILE)
            result[c, s, part] = relax(weights, factor, middle, others, force[c, s, part])

    def after_shell(s, k):
        if k == shells - 2:
            copies.extend(
                start_all(
                    [
                        pltpu.make_async_copy(source, target, more_sems.at[8 + 2 * components + n])
                        for n, (source, target) in enumerate(zip(sources, targets))
                    ]
                )
            )
            mask_copy.start()
        if k == shells - 1:
            mask_copy.wait()
            mask_out[...] = mask[...].astype(jnp.float32).astype(jnp.bfloat16)

    sweep_shells(
        0, lambda k: early.at[:, k] if k < EARLY else late.at[:, k - EARLY], f, h, lambda k: out.at[:, shell(k)],
        field, eta, force, result, sems, before_first, last_loads, arrived, finish, after_shell,
    )
    for copy in copies:
        copy.wait()


def spectrum_kernel(orders, high, low, response, coefficients, out):
    radial = lax.axis_size("radial")
    width = coefficients.shape[0]
    bands, rows = orders.shape[0] // radial, high.shape[0] * radial // orders.shape[0]
    fourier = jnp.concatenate([unpack(orders[band * radial + radial - 1], width) for band in range(bands)], axis=0)
    near, far = split(fourier.T)
    spectrum = three_pass(dot, near, far, high, low)
    coefficients[...] = spectrum
    own = response[:, :width]
    for place in range(1, radial):
        own = jnp.where(
            lax.axis_index("radial") == place, response[:, place * width : (place + 1) * width], own
        )
    near, far = split(own.T * spectrum)
    load = three_pass(dot_nt, near, far, high, low).T
    for band in range(bands):
        block = pack(load[band * rows : (band + 1) * rows])
        for place in range(radial):
            out[band * radial + place] = block


def load_kernel(load, high, low, mask, out):
    blocks, rows = load.shape[0], out.shape[0]
    step, width = out.shape[1] // RADIX, high.shape[1] // blocks
    values = jnp.concatenate([unpack(load[block], width) for block in range(blocks)], axis=1)
    modes = values.shape[1] // 2
    kind, mirrored = order_class((1, values.shape[1]))
    crossed = jnp.concatenate([values[:, modes:], -values[:, :modes]], axis=1)
    crossed = jnp.where(mirrored, -crossed, crossed)
    zero = jnp.zeros_like(values)
    stack = [jnp.where(kind == k, values, zero) for k in range(RADIX // 2 + 1)]
    stack += [jnp.where(kind == k, crossed, zero) for k in range(1, RADIX // 2)]
    near, far = split(jnp.concatenate(stack, axis=0))
    total = dot_nt(near, high[...]) + dot_nt(far, high[...]) + dot_nt(near, low[...])
    for m, part in enumerate(unfold([total[k * rows : (k + 1) * rows] for k in range(RADIX)])):
        columns = slice(m * step, (m + 1) * step)
        out[:, columns] = part * mask[:, columns].astype(jnp.float32)


def cost(microseconds):
    return pl.CostEstimate(flops=0, bytes_accessed=3_000_000 * microseconds, transcendentals=0)


def hbm(values):
    return pltpu.with_memory_space_constraint(values, pltpu.HBM)


def shards(initial_displacement, force, viscosity, layer_index, response, ocean_mask):
    components, shells, rows, count = initial_displacement.shape
    radial, lateral = lax.axis_size("radial"), lax.axis_size("lateral")
    f32 = functools.partial(jax.ShapeDtypeStruct, dtype=jnp.float32)
    scratch = lambda *shape: pltpu.VMEM(shape, jnp.float32)
    in_hbm = lambda *shape: pltpu.HBM(shape, jnp.float32)
    width = 2 * MODES // (lateral * radial)
    first = [(i, i + 1) for i in range(lateral - 1)]
    second = [(i + 1, i) for i in range(lateral - 1)]
    both = ("lateral", "radial")
    top_only = lambda pairs: [(i * radial + radial - 1, j * radial + radial - 1) for i, j in pairs]

    lower_only = lambda pairs: [(i * radial + k, j * radial + k) for i, j in pairs for k in range(radial - 1)]
    swap = [(i, radial - 1 - i) for i in range(radial)]
    tensors = [hbm(a) for a in (initial_displacement, force, layer_index)]
    viscosity = hbm(viscosity)
    message = f32((2 * (components + 1) * shells, count))
    sides = lambda *shape: scratch(2, *shape)
    mine = pl.pallas_call(
        message_kernel,
        in_specs=[HBM] * 4,
        out_specs=[VMEM] * 2,
        out_shape=[message] * 2,
        scratch_shapes=[
            sides(components, shells, TILE, count),
            sides(components, shells, TILE, count),
            pltpu.VMEM((2, shells, TILE, count), jnp.int32),
            scratch(3 * components + 2, 2 * shells, count),
            pltpu.SMEM(viscosity.shape, jnp.float32),
            pltpu.SemaphoreType.DMA((7,)),
        ],
        compiler_params=params(16),
        cost_estimate=cost(20),
    )(viscosity, *tensors)
    two = lax.ppermute(mine[1], both, top_only(second))
    one = lax.ppermute(mine[0], both, top_only(first))
    high, low = longitude_tables(count, MODES)
    high, low = hbm(jnp.asarray(high)), hbm(jnp.asarray(low))
    eta, early, *surface, table = pl.pallas_call(
        viscosity_kernel,
        in_specs=[HBM] * 4 + [ANY, HBM],
        out_specs=[HBM, HBM, VMEM, VMEM, VMEM, VMEM],
        out_shape=[
            in_hbm(shells, rows, count),
            in_hbm(components, EARLY, rows, count),
            f32((2, rows, count)),
            f32((2, rows, count)),
            f32((rows, count)),
            jax.ShapeDtypeStruct(high.shape, high.dtype),
        ],
        scratch_shapes=[
            pltpu.VMEM(layer_index.shape, jnp.int32),
            scratch(shells + 1, rows + 2 * TILE, count),
            scratch(components, EARLY + 2, rows + 2 * TILE, count),
            scratch(components, EARLY, rows, count),
            scratch(components, EARLY, rows, count),
            pltpu.SMEM(viscosity.shape, jnp.float32),
            pltpu.SemaphoreType.DMA((2 + shells,)),
            pltpu.SemaphoreType.DMA((3 * EARLY + 1 + shells,)),
        ],
        compiler_params=params(24),
        cost_estimate=cost(20),
    )(viscosity, *tensors, mine[0], high)
    lower_one, lower_two, eta = lax.optimization_barrier((*mine, eta))
    lower_one = lax.ppermute(lower_one, both, lower_only(first))
    lower_two = lax.ppermute(lower_two, both, lower_only(second))

    packed = (lateral * radial, rows * width // max(128, width), max(128, width))
    orders = pl.pallas_call(
        functools.partial(surface_kernel, components=components),
        in_specs=[VMEM] * 8 + [HBM],
        out_specs=VMEM,
        out_shape=f32(packed),
        scratch_shapes=[
            scratch(3, rows + 2 * TILE, count),
            scratch(3, rows + 2 * TILE, count),
            scratch(rows, count),
            pltpu.VMEM(low.shape, low.dtype),
            pltpu.SemaphoreType.DMA,
        ],
        compiler_params=params(16),
        cost_estimate=cost(200),
    )(*surface, *mine, one, two, table, low)
    eta, _ = lax.optimization_barrier((eta, orders))
    orders = lax.all_to_all(orders, both, split_axis=0, concat_axis=0, tiled=True)
    eta = hbm(eta)

    sweep_scratch = [
        scratch(components, shells + 2, rows + 2 * TILE, count),
        scratch(shells + 2, rows + 2 * TILE, count),
        scratch(components, shells, rows, count),
        scratch(components, shells, rows, count),
    ]
    sweep_sems = pltpu.SemaphoreType.DMA((shells, 4))
    point_high, point_low = colatitude_tables(rows * lateral, MODES)
    stages = [jnp.asarray(point_high), jnp.asarray(point_low)] + [response]
    ring_rows = 2 * (components + 1) * (rows + 1)
    sweep_scratch += [
        sides(*message.shape),
        scratch(2 * (components + 1), count),
    ]
    own_shape = (2, *message.shape)
    late, diagonal, ring, own, beside, *staged = pl.pallas_call(
        first_kernel,
        in_specs=[HBM] * 3 + [ANY] * 6 + [HBM] * len(stages),
        out_specs=[HBM] * 5 + [VMEM] * len(stages),
        out_shape=[
            in_hbm(components, shells - EARLY, rows, count),
            in_hbm(rows, count),
            in_hbm(ring_rows, count),
            in_hbm(*own_shape),
            in_hbm(2, *message.shape),
            *(jax.ShapeDtypeStruct(a.shape, a.dtype) for a in stages),
        ],
        scratch_shapes=[
            *sweep_scratch,
            scratch(rows, count),
            sweep_sems,
            pltpu.SemaphoreType.DMA((8 + 3 * components + len(stages),)),
        ],
        compiler_params=params(28),
        cost_estimate=cost(50),
    )(*tensors[:2], hbm(eta), one, two, lower_one, lower_two, *mine, *(hbm(a) for a in stages))
    ring, orders = lax.optimization_barrier((ring, orders))
    ring = lax.ppermute(ring, "radial", swap)
    coefficients, load = pl.pallas_call(
        spectrum_kernel,
        in_specs=[VMEM] * 4,
        out_specs=[VMEM, VMEM],
        out_shape=[f32((width, MODES)), f32(packed)],
        compiler_params=params(16),
        cost_estimate=cost(200),
    )(orders, *staged)
    eta, load = lax.optimization_barrier((eta, load))
    load = lax.all_to_all(load, both, split_axis=0, concat_axis=0, tiled=True)

    stages = [high, low]
    displacement, token, mask, *staged = pl.pallas_call(
        second_kernel,
        in_specs=[HBM] * 6 + [ANY] + [HBM] * (3 + len(stages)),
        out_specs=[HBM, VMEM, VMEM] + [VMEM] * len(stages),
        out_shape=[
            in_hbm(*initial_displacement.shape),
            f32((TILE, 128)),
            jax.ShapeDtypeStruct(ocean_mask.shape, jnp.bfloat16),
            *(jax.ShapeDtypeStruct(a.shape, a.dtype) for a in stages),
        ],
        scratch_shapes=[
            *sweep_scratch,
            scratch(*own_shape),
            scratch(rows, count),
            scratch(2 * components, rows, count),
            scratch(rows, count),
            pltpu.VMEM(ocean_mask.shape, ocean_mask.dtype),
            scratch(components, 2 * shells, count),
            sweep_sems,
            pltpu.SemaphoreType.DMA((8 + 2 * components + len(stages),)),
        ],
        compiler_params=params(28),
        cost_estimate=cost(50),
    )(
        *(hbm(a) for a in (early, late, tensors[1], eta, tensors[0], diagonal)),
        ring,
        *(hbm(a) for a in (beside, own, ocean_mask)),
        *stages,
    )

    sea_load = pl.pallas_call(
        load_kernel,
        in_specs=[VMEM] * 4,
        out_specs=VMEM,
        out_shape=f32((rows, count)),
        compiler_params=params(20),
        cost_estimate=cost(3),
    )(load, *staged, mask)
    return (displacement, coefficients.T, sea_load)


def solution(mesh):
    in_specs = (
        P("member", "radial", "lateral", None),
        P("member", "radial", "lateral", None),
        P("member"),
        P("radial", "lateral", None),
        P(None, "lateral"),
        P("lateral", None),
    )
    out_specs = (
        P("member", "radial", "lateral", None),
        P("member", ("lateral", "radial")),
        P("lateral", "member"),
    )
    return jax.shard_map(shards, mesh=mesh, in_specs=in_specs, out_specs=out_specs, check_vma=False)
```

```python
import functools
import math

import jax
import jax.numpy as jnp
import ml_dtypes
import numpy as np
from jax import lax
from jax.experimental import pallas as pl
from jax.experimental.pallas import tpu as pltpu
from jax.sharding import PartitionSpec as P

MODES = 512
RELAXATION = 0.8
TILE = 8
RADIX = 8
EARLY = 2
MIB = 1 << 20
ANY = pl.BlockSpec(memory_space=pl.ANY)
HBM = pl.BlockSpec(memory_space=pltpu.HBM)
SMEM = pl.BlockSpec(memory_space=pltpu.SMEM)
VMEM = pl.BlockSpec(memory_space=pltpu.VMEM)


def params(mib):
    return pltpu.CompilerParams(vmem_limit_bytes=mib * MIB)


def halves(table):
    high = table.astype(ml_dtypes.bfloat16)
    low = (table - high.astype(np.float64)).astype(ml_dtypes.bfloat16)
    return high, low


@functools.lru_cache
def longitude_tables(count, modes):
    points = np.arange(count // RADIX, dtype=np.int64)[:, None]
    orders = np.arange(modes, dtype=np.int64)[None, :]
    angle = (2.0 * math.pi / count) * (points * orders % count)
    table = np.concatenate([np.cos(angle), np.sin(angle)], axis=1) * math.sqrt(2.0 / count)
    return halves(table)


@functools.lru_cache
def colatitude_tables(count, modes):
    points = np.arange(count, dtype=np.int64)[:, None]
    waves = np.arange(modes, dtype=np.int64)[None, :]
    phase = waves * (2 * points + 1) % (4 * count)
    return halves(np.cos(math.pi / (2 * count) * phase) * math.sqrt(2.0 / count))


def split(values):
    high = values.astype(jnp.bfloat16)
    return high, (values - high.astype(jnp.float32)).astype(jnp.bfloat16)


def dot(a, b):
    return jnp.dot(a, b, preferred_element_type=jnp.float32)


def pack(block):
    rows, width = block.shape
    groups = max(1, 128 // width)
    rows //= groups
    return jnp.concatenate([block[k * rows : (k + 1) * rows] for k in range(groups)], axis=1)


def unpack(block, width):
    groups = max(1, 128 // width)
    return jnp.concatenate([block[:, k * width : (k + 1) * width] for k in range(groups)], axis=0)


def weighted_sum(terms):
    total = None
    for factor, values in terms:
        factor = round(factor, 15)
        if factor == 0.0:
            continue
        part = values if abs(factor) == 1.0 else abs(factor) * values
        if total is None:
            total = part if factor > 0 else -part
        else:
            total = total + part if factor > 0 else total - part
    return total


def turn(number):
    angle = 2.0 * math.pi * (number % RADIX) / RADIX
    return math.cos(angle), math.sin(angle)


def fold(values):
    step = values.shape[1] // RADIX
    parts = [values[:, m * step : (m + 1) * step] for m in range(RADIX)]
    cosines = [[(turn(k * m)[0], part) for m, part in enumerate(parts)] for k in range(RADIX // 2 + 1)]
    sines = [[(turn(k * m)[1], part) for m, part in enumerate(parts)] for k in range(1, RADIX // 2)]
    return [weighted_sum(terms) for terms in cosines + sines]


def unfold(blocks):
    cosines, sines = blocks[: RADIX // 2 + 1], blocks[RADIX // 2 + 1 :]
    return [
        weighted_sum(
            [(turn(k * m)[0], block) for k, block in enumerate(cosines)]
            + [(turn(k * m)[1], block) for k, block in enumerate(sines, 1)]
        )
        for m in range(RADIX)
    ]


def order_class(shape):
    order = lax.broadcasted_iota(jnp.int32, shape, len(shape) - 1) % RADIX
    mirrored = order > RADIX // 2
    return jnp.where(mirrored, RADIX - order, order), mirrored


def three_pass(product, near, far, high, low):
    both = product(jnp.concatenate([near, far], axis=0), high[...])
    return both[: near.shape[0]] + both[near.shape[0] :] + product(near, low[...])


def dot_nt(a, b):
    return lax.dot_general(a, b, (((1,), (1,)), ((), ())), preferred_element_type=jnp.float32)


def half_viscosity(index, viscosity_ref):
    values = [0.5 * viscosity_ref[k] for k in range(viscosity_ref.shape[0])]
    bit = 1
    while len(values) > 1:
        odd = (index & bit) != 0
        if len(values) % 2:
            values.append(values[-1])
        values = [jnp.where(odd, b, a) for a, b in zip(values[::2], values[1::2])]
        bit *= 2
    return values[0]


def row_number(shape):
    return lax.broadcasted_iota(jnp.int32, shape, 0)


def north_of(above, middle):
    return pltpu.roll(jnp.where(row_number(middle.shape) == TILE - 1, above, middle), 1, 0)


def south_of(below, middle):
    return pltpu.roll(jnp.where(row_number(middle.shape) == 0, below, middle), TILE - 1, 0)


def east_of(values):
    return pltpu.roll(values, values.shape[-1] - 1, values.ndim - 1)


def west_of(values):
    return pltpu.roll(values, 1, values.ndim - 1)


def relax_weights(middle, others):
    weights = [middle + other for other in others]
    diagonal = 1.0 + functools.reduce(jnp.add, weights)
    return weights, RELAXATION / diagonal


def relax(weights, factor, middle, others, force):
    total = force
    for weight, other in zip(weights, others):
        total = total + weight * other
    return (1.0 - RELAXATION) * middle + factor * total


def around(ref, lead, shell, start):
    rows = lambda first: pl.ds(pl.multiple_of(first, TILE), TILE)
    middle = ref[(*lead, shell, rows(start))]
    return middle, [
        ref[(*lead, shell + 1, rows(start))],
        ref[(*lead, shell - 1, rows(start))],
        south_of(ref[(*lead, shell, rows(start + TILE))], middle),
        north_of(ref[(*lead, shell, rows(start - TILE))], middle),
        west_of(middle),
        east_of(middle),
    ]


def message_kernel(viscosity_from, d, f, index, one, two, fields, forces, layers, rows_of, viscosity, sems):
    components, shells, rows, count = d.shape
    copies = [pltpu.make_async_copy(viscosity_from, viscosity, sems.at[0])]
    for side, start in enumerate((0, rows - TILE)):
        part = pl.ds(start, TILE)
        copies += [
            pltpu.make_async_copy(index.at[:, part], layers.at[side], sems.at[1 + side]),
            pltpu.make_async_copy(d.at[:, :, part], fields.at[side], sems.at[3 + side]),
            pltpu.make_async_copy(f.at[:, :, part], forces.at[side], sems.at[5 + side]),
        ]
    layer_copies, field_copies, force_copies = copies[1::3], copies[2::3], copies[3::3]
    start_all(copies[:1] + layer_copies + field_copies + force_copies)
    for copy in copies[:1] + layer_copies:
        copy.wait()
    near_eta, far_eta = 2 * components, 2 * components + 1
    for side, near, far in ((0, 0, 1), (1, TILE - 1, TILE - 2)):
        for s in range(shells):
            eta = half_viscosity(layers[side, s], viscosity)
            rows_of[near_eta, side * shells + s] = eta[near]
            rows_of[far_eta, side * shells + s] = eta[far]
    for copy in field_copies:
        copy.wait()
    for side, near, far in ((0, 0, 1), (1, TILE - 1, TILE - 2)):
        for s in range(shells):
            for c in range(components):
                rows_of[c, side * shells + s] = fields[side, c, s, near]
                rows_of[components + c, side * shells + s] = fields[side, c, s, far]
    for copy in force_copies:
        copy.wait()
    for side, near in ((0, 0), (1, TILE - 1)):
        for s in range(shells):
            for c in range(components):
                rows_of[far_eta + 1 + c, side * shells + s] = forces[side, c, s, near]
    radial = lax.axis_index("radial")
    place = row_number((2 * shells, count)) % shells
    highest, lowest = place == shells - 1, place == 0
    zero = jnp.zeros((2 * shells, count), jnp.float32)

    def beside(near, far):
        middle = rows_of[near]
        return middle, [
            jnp.where(highest, zero, pltpu.roll(middle, 2 * shells - 1, 0)),
            jnp.where(lowest, zero, pltpu.roll(middle, 1, 0)),
            rows_of[far],
            west_of(middle),
            east_of(middle),
        ]

    eta, others = beside(near_eta, far_eta)
    weights = [eta + other for other in others]
    inside = (radial < lax.axis_size("radial") - 1, radial > 0)
    weights[0] = jnp.where(jnp.logical_and(highest, inside[0]), zero, weights[0])
    weights[1] = jnp.where(jnp.logical_and(lowest, inside[1]), zero, weights[1])
    diagonal = 1.0 + functools.reduce(jnp.add, weights)
    values, sums = [], []
    for c in range(components):
        middle, others = beside(c, components + c)
        total = rows_of[far_eta + 1 + c]
        for weight, other in zip(weights, others):
            total = total + weight * other
        values.append(middle)
        sums.append(total)
    for place, field in enumerate(values + [eta] + sums + [diagonal]):
        both = pltpu.roll(field, shells, 0)
        one[pl.ds(place * shells, shells)] = both[:shells]
        two[pl.ds(place * shells, shells)] = both[shells:]


def shell_order(shells):
    lower = lax.axis_index("radial") == 0
    return lambda k: jnp.where(lower, k, shells - 1 - k)


def viscosity_kernel(
    viscosity_from, d, f, index_from, token, table_from, eta_out, out, surface_swept, surface_eta, surface_force, table,
    index, eta, field, force, result, viscosity, sems, more_sems,
):
    del token
    _, shells, rows, count = d.shape
    components = d.shape[0]
    block = pl.ds(TILE, rows)
    shell = shell_order(shells)
    value_copy = pltpu.make_async_copy(viscosity_from, viscosity, sems.at[shells])
    layers = [pltpu.make_async_copy(index_from.at[shell(k)], index.at[k], sems.at[k]) for k in range(shells)]
    fields = [
        pltpu.make_async_copy(d.at[:, shell(k)], field.at[:, k + 1, block], more_sems.at[k]) for k in range(EARLY + 1)
    ]
    forces = [
        pltpu.make_async_copy(f.at[:, shell(k)], force.at[:, k], more_sems.at[EARLY + 1 + k]) for k in range(EARLY)
    ]
    table_copy = pltpu.make_async_copy(table_from, table, sems.at[shells + 1])
    start_all([value_copy, *layers, *fields, *forces])
    zeros = jnp.zeros((rows, count), jnp.float32)
    for c in range(components):
        field[c, 0, block] = zeros
    eta[0, block] = zeros
    value_copy.wait()
    stores = start_all([table_copy])
    for k in range(shells):
        layers[k].wait()

        def lookup(step, _):
            start = pl.multiple_of(step * TILE, TILE)
            eta[k + 1, pl.ds(start + TILE, TILE)] = half_viscosity(index[k, pl.ds(start, TILE)], viscosity)
            return 0

        lax.fori_loop(0, rows // TILE, lookup, 0, unroll=2)
        stores += start_all(
            [pltpu.make_async_copy(eta.at[k + 1, block], eta_out.at[shell(k)], more_sems.at[2 * EARLY + 1 + k])]
        )
    for k in range(EARLY):
        for copy in (fields[: EARLY + 1] if k == 0 else []) + forces[k : k + 1]:
            copy.wait()

        def sweep(step, _):
            start = pl.multiple_of(step * TILE, TILE)
            part = pl.ds(start, TILE)
            weights, factor = relax_weights(*around(eta, (), k + 1, start + TILE))
            for c in range(components):
                middle, others = around(field, (c,), k + 1, start + TILE)
                result[c, k, part] = relax(weights, factor, middle, others, force[c, k, part])
            surface_swept[1 - k, part] = result[0, k, part]
            surface_eta[1 - k, part] = eta[k + 1, pl.ds(start + TILE, TILE)]
            if k == 0:
                surface_force[part] = force[0, 0, part]
            sem = more_sems.at[2 * EARLY + 1 + shells + k]
            pltpu.make_async_copy(result.at[:, k, part], out.at[:, k, part], sem).start()
            return 0

        lax.fori_loop(0, rows // TILE, sweep, 0, unroll=2)
        stores.append(pltpu.make_async_copy(result.at[:, k], out.at[:, k], more_sems.at[2 * EARLY + 1 + shells + k]))
    for copy in stores:
        copy.wait()


def surface_kernel(
    surface_swept, surface_eta, force, own_one, own_two, one, two, high, low_from, out,
    swept, eta, surface, low, sem, components,
):
    rows, count = force.shape

    @pl.when(lax.axis_index("radial") == lax.axis_size("radial") - 1)
    def _():
        low_copy = pltpu.make_async_copy(low_from, low, sem)
        low_copy.start()
        block = pl.ds(TILE, rows)
        for k in range(2):
            swept[k, block] = surface_swept[k]
            eta[k, block] = surface_eta[k]
        swept[2, block] = jnp.zeros((rows, count), jnp.float32)
        eta[2, block] = jnp.zeros((rows, count), jnp.float32)
        fields = one.shape[0]
        shells = fields // (2 * (components + 1))
        lateral = lax.axis_index("lateral")
        inside = (lateral > 0, lateral < lax.axis_size("lateral") - 1)
        for beside, own, place, own_place, there in zip(
            (one[...], two[...]), (own_two[...], own_one[...]), (TILE - 1, rows + TILE), (TILE, rows + TILE - 1), inside
        ):
            for k in range(2):
                row = lambda message, kind: message[kind * shells + shells - 2 + k : kind * shells + shells - 1 + k]
                weight = row(beside, components) + row(own, components)

                def finish(message, other):
                    total = row(message, components + 1) + weight * row(other, 0)
                    factor = RELAXATION / (row(message, 2 * components + 1) + weight)
                    return (1.0 - RELAXATION) * row(message, 0) + factor * total

                swept[k, pl.ds(own_place, 1)] = finish(own, beside)
                if k == 1:
                    edge = finish(beside, own)
                    swept[k, pl.ds(place, 1)] = jnp.where(there, edge, jnp.zeros_like(edge))
                    eta[k, pl.ds(place, 1)] = row(beside, components)

        def second(step, _):
            start = pl.multiple_of(step * TILE, TILE)
            weights, factor = relax_weights(*around(eta, (), 1, start + TILE))
            middle, others = around(swept, (), 1, start + TILE)
            surface[pl.ds(start, TILE)] = relax(weights, factor, middle, others, force[pl.ds(start, TILE)])
            return 0

        lax.fori_loop(0, rows // TILE, second, 0, unroll=2)
        near, far = split(jnp.concatenate(fold(surface[...]), axis=0))
        total = dot(near, high[...]) + dot(far, high[...])
        low_copy.wait()
        total = total + dot(near, low[...])
        blocks = [total[k * rows : (k + 1) * rows] for k in range(RADIX)]
        kind, mirrored = order_class((1, total.shape[1]))
        cosine, sine = blocks[0], jnp.zeros_like(blocks[0])
        for k in range(1, RADIX // 2 + 1):
            cosine = jnp.where(kind == k, blocks[k], cosine)
        for k in range(1, RADIX // 2):
            sine = jnp.where(kind == k, blocks[RADIX // 2 + k], sine)
        sine = jnp.where(mirrored, -sine, sine)
        modes = total.shape[1] // 2
        fourier = jnp.concatenate(
            [cosine[:, :modes] - sine[:, modes:], cosine[:, modes:] + sine[:, :modes]], axis=1
        )
        blocks = out.shape[0]
        width = fourier.shape[1] // blocks
        for block in range(blocks):
            out[block] = pack(fourier[:, block * width : (block + 1) * width])


def sweep_shells(
    begin, source, f, h, store, field, eta, force, result, sems, before_first, last_loads, arrived, finish, after_shell
):
    components, shells, rows, count = f.shape
    inner = pl.ds(TILE, rows)
    shell = shell_order(shells)

    def field_loads(k):
        s = shell(k)
        return [
            pltpu.make_async_copy(source(k), field.at[:, s + 1, inner], sems.at[k, 0]),
            pltpu.make_async_copy(h.at[s], eta.at[s + 1, inner], sems.at[k, 1]),
            *(last_loads if k == shells - 1 else []),
        ]

    def force_load(k):
        return [pltpu.make_async_copy(f.at[:, shell(k)], force.at[:, shell(k)], sems.at[k, 2])]

    loads = {k: start_all(field_loads(k)) for k in range(max(begin - 1, 0), begin + 2)}
    forces = {begin: start_all(force_load(begin))}
    if begin == 0:
        nothing = jnp.where(lax.axis_index("radial") == 0, 0, shells + 1)
        zeros = jnp.zeros((rows, count), jnp.float32)
        for c in range(components):
            field[c, nothing, inner] = zeros
        eta[nothing, inner] = zeros

    def start_until(k):
        for ahead in range(begin, shells):
            if ahead <= k and ahead not in loads:
                loads[ahead] = start_all(field_loads(ahead))
            if ahead < k and ahead not in forces:
                forces[ahead] = start_all(force_load(ahead))

    start_until(begin + 2)
    before_first()
    stores, there = [], set()
    for k in range(begin, shells):
        s = shell(k)
        start_until(k + 3)
        for near in range(max(k - 1, 0), min(k + 2, shells)):
            if near not in there:
                there.add(near)
                for copy in loads[near]:
                    copy.wait()
                arrived(near)
        for copy in forces[k]:
            copy.wait()

        def tile(step, _):
            first = pl.multiple_of(step * TILE, TILE)
            part = pl.ds(first, TILE)
            if k == shells - 1:
                finish(s, first)
            else:
                weights, factor = relax_weights(*around(eta, (), s + 1, first + TILE))
                for c in range(components):
                    middle, others = around(field, (c,), s + 1, first + TILE)
                    result[c, s, part] = relax(weights, factor, middle, others, force[c, s, part])
            pltpu.make_async_copy(result.at[:, s, part], store(k).at[:, part], sems.at[k, 3]).start()
            return 0

        lax.fori_loop(0, rows // TILE, tile, 0, unroll=2)
        stores.append(pltpu.make_async_copy(result.at[:, s], store(k), sems.at[k, 3]))
        after_shell(s, k)
    for copy in stores:
        copy.wait()


def set_edge(ref, lead, shells, rows, before, after):
    for s in range(shells):
        ref[(*lead, s + 1, TILE - 1)] = before(s)
        ref[(*lead, s + 1, rows + TILE)] = after(s)


def start_all(copies):
    for copy in copies:
        copy.start()
    return copies


def load_messages(sources, lower_sources, slots, sems):
    lower = lax.axis_index("radial") < lax.axis_size("radial") - 1
    copies = lambda refs: [pltpu.make_async_copy(ref, slots.at[k], sems.at[k]) for k, ref in enumerate(refs)]
    pl.when(lower)(lambda: [copy.start() for copy in copies(lower_sources)] and None)
    pl.when(jnp.logical_not(lower))(lambda: [copy.start() for copy in copies(sources)] and None)
    return copies(sources)


def first_kernel(d, f, h, one, two, lower_one, lower_two, mine_one, mine_two, *refs):
    components, shells, rows, count = d.shape
    staged = (len(refs) - 13) // 2
    sources, refs = refs[:staged], refs[staged:]
    out, diagonal_out, ring_out, own_out, beside_out, *targets = refs[: 5 + staged]
    field, eta, force, result, messages, edges, diagonal, sems, more_sems = refs[5 + staged :]
    arrivals = load_messages((one, two), (lower_one, lower_two), messages, more_sems)
    lower = lax.axis_index("radial") == 0
    last, beyond = jnp.where(lower, shells - 1, 0), jnp.where(lower, shells + 1, 0)
    values = pl.ds(0, own_out.shape[1])
    copies = []
    own_copies = lambda: start_all(
        [
            pltpu.make_async_copy(mine.at[values], own_out.at[k], more_sems.at[4 + components + k])
            for k, mine in enumerate((mine_one, mine_two))
        ]
    )

    def before_first():
        block = pl.ds(TILE, rows)
        zeros = jnp.zeros((rows, count), jnp.float32)
        for c in range(components):
            field[c, beyond, block] = zeros
        eta[beyond, block] = zeros
        for copy in arrivals:
            copy.wait()
        before, after = messages[0], messages[1]
        row = lambda message, kind: lambda s: message[kind * shells + s]
        for c in range(components):
            set_edge(field, (c,), shells, rows, row(before, c), row(after, c))
        set_edge(eta, (), shells, rows, row(before, components), row(after, components))
        for side, message in enumerate((before, after)):
            for k in range(components + 1):
                edges[side * (components + 1) + k] = jnp.where(
                    lower, message[(k + 1) * shells - 1], message[k * shells]
                )
        tail = ring_out.at[pl.ds(2 * (components + 1) * rows, edges.shape[0])]
        copies.extend(
            start_all(
                [
                    pltpu.make_async_copy(edges, tail, more_sems.at[2]),
                ]
            )
        )

    def arrived(k):
        if k < shells - 1:
            return
        block = pl.ds(TILE, rows)
        sources = [field.at[c, last + 1, block] for c in range(components)] + [eta.at[last + 1, block]]
        copies.extend(
            start_all(
                [
                    pltpu.make_async_copy(source, ring_out.at[pl.ds(k * rows, rows)], more_sems.at[6 + components + k])
                    for k, source in enumerate(sources)
                ]
            )
        )

    def finish(s, first):
        part = pl.ds(first, TILE)
        middle, others = around(eta, (), s + 1, first + TILE)
        weights = [middle + other for other in others]
        zero = jnp.zeros_like(middle)
        weights[0] = jnp.where(lower, zero, weights[0])
        weights[1] = jnp.where(lower, weights[1], zero)
        diagonal[part] = 1.0 + functools.reduce(jnp.add, weights)
        for c in range(components):
            total = force[c, s, part]
            for weight, other in zip(weights, around(field, (c,), s + 1, first + TILE)[1]):
                total = total + weight * other
            result[c, s, part] = total

    def after_shell(s, k):
        if k == EARLY:
            copies.extend(own_copies())
            copies.extend(start_all([pltpu.make_async_copy(messages, beside_out, more_sems.at[3])]))
            copies.extend(
                start_all(
                    [
                        pltpu.make_async_copy(source, target, more_sems.at[8 + 3 * components + n])
                        for n, (source, target) in enumerate(zip(sources, targets))
                    ]
                )
            )
        if k == shells - 1:
            sums = [result.at[c, s] for c in range(components)] + [diagonal]
            copies.extend(
                start_all(
                    [
                        pltpu.make_async_copy(
                            source,
                            ring_out.at[pl.ds((components + 1 + n) * rows, rows)],
                            more_sems.at[7 + 2 * components + n],
                        )
                        for n, source in enumerate(sums)
                    ]
                    + [pltpu.make_async_copy(diagonal, diagonal_out, more_sems.at[0])]
                )
            )

    shell = shell_order(shells)
    sweep_shells(
        EARLY, lambda k: d.at[:, shell(k)], f, h, lambda k: out.at[:, k - EARLY],
        field, eta, force, result, sems, before_first, [], arrived, finish, after_shell,
    )
    for copy in copies:
        copy.wait()


def second_kernel(early, late, f, h, start, diagonal_from, ring, beside, own_from, *refs):
    components, shells, rows, count = f.shape
    staged = (len(refs) - 18) // 2
    mask_from, *sources = refs[: 1 + staged]
    out, token, mask_out, *targets = refs[1 + staged : 4 + 2 * staged]
    (
        field, eta, force, result, messages, edges, own, diagonal, raw, ring_diagonal, mask, ends, sems, more_sems
    ) = refs[4 + 2 * staged :]
    token[...] = jnp.zeros_like(token)
    tail = ring.at[pl.ds(2 * (components + 1) * rows, edges.shape[0])]
    arrivals = start_all(
        [
            pltpu.make_async_copy(beside, messages, more_sems.at[0]),
            pltpu.make_async_copy(tail, edges, more_sems.at[1]),
            pltpu.make_async_copy(own_from, own, more_sems.at[2]),
        ]
    )
    radial, lateral = lax.axis_index("radial"), lax.axis_index("lateral")
    lower = radial == 0
    last, beyond = jnp.where(lower, shells - 1, 0), jnp.where(lower, shells + 1, 0)
    block = pl.ds(TILE, rows)
    shell = shell_order(shells)
    from_ring = lambda k, target, sem: pltpu.make_async_copy(
        ring.at[pl.ds(k * rows, rows)], target, more_sems.at[sem]
    )
    last_loads = [
        pltpu.make_async_copy(start.at[:, last], raw.at[pl.ds(0, components)], more_sems.at[3]),
        pltpu.make_async_copy(diagonal_from, diagonal, more_sems.at[4]),
        *(from_ring(c, raw.at[components + c], 5 + c) for c in range(components)),
        from_ring(components, eta.at[beyond, block], 5 + components),
        *(
            from_ring(components + 1 + c, field.at[c, beyond, block], 6 + components + c)
            for c in range(components)
        ),
        from_ring(2 * components + 1, ring_diagonal, 6 + 2 * components),
    ]
    copies = []
    mask_copy = pltpu.make_async_copy(mask_from, mask, more_sems.at[7 + 2 * components])

    def before_first():
        for copy in arrivals:
            copy.wait()
        before, after = messages[0], messages[1]
        pair = lambda k: jnp.concatenate(
            [before[k * shells : (k + 1) * shells], after[k * shells : (k + 1) * shells]], axis=0
        )
        place = row_number((2 * shells, count))
        zero = jnp.zeros((2 * shells, count), jnp.float32)
        shared = place % shells == last
        across_of = lambda k: jnp.where(
            place < shells, edges[pl.ds(k, 1)], edges[pl.ds(components + 1 + k, 1)]
        )
        inside = jnp.where(place < shells, lateral, lax.axis_size("lateral") - 1 - lateral) > 0
        mine = (own[1], own[0])
        own_row = lambda k: jnp.concatenate([part[k * shells : (k + 1) * shells] for part in mine], axis=0)
        middle = pair(components)
        weight = middle + own_row(components)
        across = jnp.where(shared, middle + across_of(components), zero)
        factor = RELAXATION / (pair(2 * components + 1) + weight + across)
        own_factor = RELAXATION / (own_row(2 * components + 1) + weight)
        for c in range(components):
            total = pair(components + 1 + c) + weight * own_row(c) + across * across_of(c)
            edge = jnp.where(inside, (1.0 - RELAXATION) * pair(c) + factor * total, zero)
            total = own_row(components + 1 + c) + weight * pair(c)
            ends[c] = (1.0 - RELAXATION) * own_row(c) + own_factor * total
            set_edge(field, (c,), shells, rows, lambda s: edge[s], lambda s: edge[shells + s])
        set_edge(eta, (), shells, rows, lambda s: middle[s], lambda s: middle[shells + s])

    def arrived(k):
        if k < EARLY:
            s = shell(k)
            for side, place in enumerate((TILE, TILE + rows - 1)):
                for c in range(components):
                    field[c, s + 1, pl.ds(place, 1)] = ends[c, pl.ds(side * shells + s, 1)]
        if k < shells - 1:
            return

        def tile(step, _):
            first = pl.multiple_of(step * TILE, TILE)
            part, place = pl.ds(first, TILE), pl.ds(first + TILE, TILE)
            weight = eta[last + 1, place] + eta[beyond, place]
            here, there = RELAXATION / (diagonal[part] + weight), RELAXATION / (ring_diagonal[part] + weight)
            for c in range(components):
                mine, other = raw[c, part], raw[components + c, part]
                field[c, last + 1, place] = (1.0 - RELAXATION) * mine + here * (
                    field[c, last + 1, place] + weight * other
                )
                field[c, beyond, place] = (1.0 - RELAXATION) * other + there * (
                    field[c, beyond, place] + weight * mine
                )
            return 0

        lax.fori_loop(0, rows // TILE, tile, 0)

    def finish(s, first):
        part = pl.ds(first, TILE)
        weights, factor = relax_weights(*around(eta, (), s + 1, first + TILE))
        for c in range(components):
            middle, others = around(field, (c,), s + 1, first + TILE)
            result[c, s, part] = relax(weights, factor, middle, others, force[c, s, part])

    def after_shell(s, k):
        if k == shells - 2:
            copies.extend(
                start_all(
                    [
                        pltpu.make_async_copy(source, target, more_sems.at[8 + 2 * components + n])
                        for n, (source, target) in enumerate(zip(sources, targets))
                    ]
                )
            )
            mask_copy.start()
        if k == shells - 1:
            mask_copy.wait()
            mask_out[...] = mask[...].astype(jnp.float32).astype(jnp.bfloat16)

    sweep_shells(
        0, lambda k: early.at[:, k] if k < EARLY else late.at[:, k - EARLY], f, h, lambda k: out.at[:, shell(k)],
        field, eta, force, result, sems, before_first, last_loads, arrived, finish, after_shell,
    )
    for copy in copies:
        copy.wait()


def spectrum_kernel(orders, high, low, response, coefficients, out):
    radial = lax.axis_size("radial")
    width = coefficients.shape[0]
    bands, rows = orders.shape[0] // radial, high.shape[0] * radial // orders.shape[0]
    fourier = jnp.concatenate([unpack(orders[band * radial + radial - 1], width) for band in range(bands)], axis=0)
    near, far = split(fourier.T)
    spectrum = three_pass(dot, near, far, high, low)
    coefficients[...] = spectrum
    own = response[:, :width]
    for place in range(1, radial):
        own = jnp.where(
            lax.axis_index("radial") == place, response[:, place * width : (place + 1) * width], own
        )
    near, far = split(own.T * spectrum)
    load = three_pass(dot_nt, near, far, high, low).T
    for band in range(bands):
        block = pack(load[band * rows : (band + 1) * rows])
        for place in range(radial):
            out[band * radial + place] = block


def load_kernel(load, high, low, mask, out):
    blocks, rows = load.shape[0], out.shape[0]
    step, width = out.shape[1] // RADIX, high.shape[1] // blocks
    values = jnp.concatenate([unpack(load[block], width) for block in range(blocks)], axis=1)
    modes = values.shape[1] // 2
    kind, mirrored = order_class((1, values.shape[1]))
    crossed = jnp.concatenate([values[:, modes:], -values[:, :modes]], axis=1)
    crossed = jnp.where(mirrored, -crossed, crossed)
    zero = jnp.zeros_like(values)
    stack = [jnp.where(kind == k, values, zero) for k in range(RADIX // 2 + 1)]
    stack += [jnp.where(kind == k, crossed, zero) for k in range(1, RADIX // 2)]
    near, far = split(jnp.concatenate(stack, axis=0))
    total = dot_nt(near, high[...]) + dot_nt(far, high[...]) + dot_nt(near, low[...])
    for m, part in enumerate(unfold([total[k * rows : (k + 1) * rows] for k in range(RADIX)])):
        columns = slice(m * step, (m + 1) * step)
        out[:, columns] = part * mask[:, columns].astype(jnp.float32)


def cost(microseconds):
    return pl.CostEstimate(flops=0, bytes_accessed=3_000_000 * microseconds, transcendentals=0)


def hbm(values):
    return pltpu.with_memory_space_constraint(values, pltpu.HBM)


def shards(initial_displacement, force, viscosity, layer_index, response, ocean_mask):
    components, shells, rows, count = initial_displacement.shape
    radial, lateral = lax.axis_size("radial"), lax.axis_size("lateral")
    f32 = functools.partial(jax.ShapeDtypeStruct, dtype=jnp.float32)
    scratch = lambda *shape: pltpu.VMEM(shape, jnp.float32)
    in_hbm = lambda *shape: pltpu.HBM(shape, jnp.float32)
    width = 2 * MODES // (lateral * radial)
    first = [(i, i + 1) for i in range(lateral - 1)]
    second = [(i + 1, i) for i in range(lateral - 1)]
    both = ("lateral", "radial")
    top_only = lambda pairs: [(i * radial + radial - 1, j * radial + radial - 1) for i, j in pairs]

    lower_only = lambda pairs: [(i * radial + k, j * radial + k) for i, j in pairs for k in range(radial - 1)]
    swap = [(i, radial - 1 - i) for i in range(radial)]
    tensors = [hbm(a) for a in (initial_displacement, force, layer_index)]
    viscosity = hbm(viscosity)
    message = f32((2 * (components + 1) * shells, count))
    sides = lambda *shape: scratch(2, *shape)
    mine = pl.pallas_call(
        message_kernel,
        in_specs=[HBM] * 4,
        out_specs=[VMEM] * 2,
        out_shape=[message] * 2,
        scratch_shapes=[
            sides(components, shells, TILE, count),
            sides(components, shells, TILE, count),
            pltpu.VMEM((2, shells, TILE, count), jnp.int32),
            scratch(3 * components + 2, 2 * shells, count),
            pltpu.SMEM(viscosity.shape, jnp.float32),
            pltpu.SemaphoreType.DMA((7,)),
        ],
        compiler_params=params(16),
        cost_estimate=cost(20),
    )(viscosity, *tensors)
    two = lax.ppermute(mine[1], both, top_only(second))
    one = lax.ppermute(mine[0], both, top_only(first))
    high, low = longitude_tables(count, MODES)
    high, low = hbm(jnp.asarray(high)), hbm(jnp.asarray(low))
    eta, early, *surface, table = pl.pallas_call(
        viscosity_kernel,
        in_specs=[HBM] * 4 + [ANY, HBM],
        out_specs=[HBM, HBM, VMEM, VMEM, VMEM, VMEM],
        out_shape=[
            in_hbm(shells, rows, count),
            in_hbm(components, EARLY, rows, count),
            f32((2, rows, count)),
            f32((2, rows, count)),
            f32((rows, count)),
            jax.ShapeDtypeStruct(high.shape, high.dtype),
        ],
        scratch_shapes=[
            pltpu.VMEM(layer_index.shape, jnp.int32),
            scratch(shells + 1, rows + 2 * TILE, count),
            scratch(components, EARLY + 2, rows + 2 * TILE, count),
            scratch(components, EARLY, rows, count),
            scratch(components, EARLY, rows, count),
            pltpu.SMEM(viscosity.shape, jnp.float32),
            pltpu.SemaphoreType.DMA((2 + shells,)),
            pltpu.SemaphoreType.DMA((3 * EARLY + 1 + shells,)),
        ],
        compiler_params=params(24),
        cost_estimate=cost(20),
    )(viscosity, *tensors, mine[0], high)
    lower_one, lower_two, eta = lax.optimization_barrier((*mine, eta))
    lower_one = lax.ppermute(lower_one, both, lower_only(first))
    lower_two = lax.ppermute(lower_two, both, lower_only(second))

    packed = (lateral * radial, rows * width // max(128, width), max(128, width))
    orders = pl.pallas_call(
        functools.partial(surface_kernel, components=components),
        in_specs=[VMEM] * 8 + [HBM],
        out_specs=VMEM,
        out_shape=f32(packed),
        scratch_shapes=[
            scratch(3, rows + 2 * TILE, count),
            scratch(3, rows + 2 * TILE, count),
            scratch(rows, count),
            pltpu.VMEM(low.shape, low.dtype),
            pltpu.SemaphoreType.DMA,
        ],
        compiler_params=params(16),
        cost_estimate=cost(200),
    )(*surface, *mine, one, two, table, low)
    eta, _ = lax.optimization_barrier((eta, orders))
    orders = lax.all_to_all(orders, both, split_axis=0, concat_axis=0, tiled=True)
    eta = hbm(eta)

    sweep_scratch = [
        scratch(components, shells + 2, rows + 2 * TILE, count),
        scratch(shells + 2, rows + 2 * TILE, count),
        scratch(components, shells, rows, count),
        scratch(components, shells, rows, count),
    ]
    sweep_sems = pltpu.SemaphoreType.DMA((shells, 4))
    point_high, point_low = colatitude_tables(rows * lateral, MODES)
    stages = [jnp.asarray(point_high), jnp.asarray(point_low)] + [response]
    ring_rows = 2 * (components + 1) * (rows + 1)
    sweep_scratch += [
        sides(*message.shape),
        scratch(2 * (components + 1), count),
    ]
    own_shape = (2, *message.shape)
    late, diagonal, ring, own, beside, *staged = pl.pallas_call(
        first_kernel,
        in_specs=[HBM] * 3 + [ANY] * 6 + [HBM] * len(stages),
        out_specs=[HBM] * 5 + [VMEM] * len(stages),
        out_shape=[
            in_hbm(components, shells - EARLY, rows, count),
            in_hbm(rows, count),
            in_hbm(ring_rows, count),
            in_hbm(*own_shape),
            in_hbm(2, *message.shape),
            *(jax.ShapeDtypeStruct(a.shape, a.dtype) for a in stages),
        ],
        scratch_shapes=[
            *sweep_scratch,
            scratch(rows, count),
            sweep_sems,
            pltpu.SemaphoreType.DMA((8 + 3 * components + len(stages),)),
        ],
        compiler_params=params(28),
        cost_estimate=cost(50),
    )(*tensors[:2], hbm(eta), one, two, lower_one, lower_two, *mine, *(hbm(a) for a in stages))
    ring, orders = lax.optimization_barrier((ring, orders))
    ring = lax.ppermute(ring, "radial", swap)
    coefficients, load = pl.pallas_call(
        spectrum_kernel,
        in_specs=[VMEM] * 4,
        out_specs=[VMEM, VMEM],
        out_shape=[f32((width, MODES)), f32(packed)],
        compiler_params=params(16),
        cost_estimate=cost(200),
    )(orders, *staged)
    eta, load = lax.optimization_barrier((eta, load))
    load = lax.all_to_all(load, both, split_axis=0, concat_axis=0, tiled=True)

    stages = [high, low]
    displacement, token, mask, *staged = pl.pallas_call(
        second_kernel,
        in_specs=[HBM] * 6 + [ANY] + [HBM] * (3 + len(stages)),
        out_specs=[HBM, VMEM, VMEM] + [VMEM] * len(stages),
        out_shape=[
            in_hbm(*initial_displacement.shape),
            f32((TILE, 128)),
            jax.ShapeDtypeStruct(ocean_mask.shape, jnp.bfloat16),
            *(jax.ShapeDtypeStruct(a.shape, a.dtype) for a in stages),
        ],
        scratch_shapes=[
            *sweep_scratch,
            scratch(*own_shape),
            scratch(rows, count),
            scratch(2 * components, rows, count),
            scratch(rows, count),
            pltpu.VMEM(ocean_mask.shape, ocean_mask.dtype),
            scratch(components, 2 * shells, count),
            sweep_sems,
            pltpu.SemaphoreType.DMA((8 + 2 * components + len(stages),)),
        ],
        compiler_params=params(28),
        cost_estimate=cost(50),
    )(
        *(hbm(a) for a in (early, late, tensors[1], eta, tensors[0], diagonal)),
        ring,
        *(hbm(a) for a in (beside, own, ocean_mask)),
        *stages,
    )

    sea_load = pl.pallas_call(
        load_kernel,
        in_specs=[VMEM] * 4,
        out_specs=VMEM,
        out_shape=f32((rows, count)),
        compiler_params=params(20),
        cost_estimate=cost(3),
    )(load, *staged, mask)
    return (displacement, coefficients.T, sea_load)


def solution(mesh):
    in_specs = (
        P("member", "radial", "lateral", None),
        P("member", "radial", "lateral", None),
        P("member"),
        P("radial", "lateral", None),
        P(None, "lateral"),
        P("lateral", None),
    )
    out_specs = (
        P("member", "radial", "lateral", None),
        P("member", ("lateral", "radial")),
        P("lateral", "member"),
    )
    return jax.shard_map(shards, mesh=mesh, in_specs=in_specs, out_specs=out_specs, check_vma=False)
```

```python
import functools
import math

import jax
import jax.numpy as jnp
import ml_dtypes
import numpy as np
from jax import lax
from jax.experimental import pallas as pl
from jax.experimental.pallas import tpu as pltpu
from jax.sharding import PartitionSpec as P

MODES = 512
RELAXATION = 0.8
TILE = 8
RADIX = 8
EARLY = 2
MIB = 1 << 20
ANY = pl.BlockSpec(memory_space=pl.ANY)
HBM = pl.BlockSpec(memory_space=pltpu.HBM)
SMEM = pl.BlockSpec(memory_space=pltpu.SMEM)
VMEM = pl.BlockSpec(memory_space=pltpu.VMEM)


def params(mib):
    return pltpu.CompilerParams(vmem_limit_bytes=mib * MIB)


def halves(table):
    high = table.astype(ml_dtypes.bfloat16)
    low = (table - high.astype(np.float64)).astype(ml_dtypes.bfloat16)
    return high, low


@functools.lru_cache
def longitude_tables(count, modes):
    points = np.arange(count // RADIX, dtype=np.int64)[:, None]
    orders = np.arange(modes, dtype=np.int64)[None, :]
    angle = (2.0 * math.pi / count) * (points * orders % count)
    table = np.concatenate([np.cos(angle), np.sin(angle)], axis=1) * math.sqrt(2.0 / count)
    return halves(table)


@functools.lru_cache
def colatitude_tables(count, modes):
    points = np.arange(count, dtype=np.int64)[:, None]
    waves = np.arange(modes, dtype=np.int64)[None, :]
    phase = waves * (2 * points + 1) % (4 * count)
    return halves(np.cos(math.pi / (2 * count) * phase) * math.sqrt(2.0 / count))


def split(values):
    high = values.astype(jnp.bfloat16)
    return high, (values - high.astype(jnp.float32)).astype(jnp.bfloat16)


def dot(a, b):
    return jnp.dot(a, b, preferred_element_type=jnp.float32)


def pack(block):
    rows, width = block.shape
    groups = max(1, 128 // width)
    rows //= groups
    return jnp.concatenate([block[k * rows : (k + 1) * rows] for k in range(groups)], axis=1)


def unpack(block, width):
    groups = max(1, 128 // width)
    return jnp.concatenate([block[:, k * width : (k + 1) * width] for k in range(groups)], axis=0)


def weighted_sum(terms):
    total = None
    for factor, values in terms:
        factor = round(factor, 15)
        if factor == 0.0:
            continue
        part = values if abs(factor) == 1.0 else abs(factor) * values
        if total is None:
            total = part if factor > 0 else -part
        else:
            total = total + part if factor > 0 else total - part
    return total


def turn(number):
    angle = 2.0 * math.pi * (number % RADIX) / RADIX
    return math.cos(angle), math.sin(angle)


def fold(values):
    step = values.shape[1] // RADIX
    parts = [values[:, m * step : (m + 1) * step] for m in range(RADIX)]
    cosines = [[(turn(k * m)[0], part) for m, part in enumerate(parts)] for k in range(RADIX // 2 + 1)]
    sines = [[(turn(k * m)[1], part) for m, part in enumerate(parts)] for k in range(1, RADIX // 2)]
    return [weighted_sum(terms) for terms in cosines + sines]


def unfold(blocks):
    cosines, sines = blocks[: RADIX // 2 + 1], blocks[RADIX // 2 + 1 :]
    return [
        weighted_sum(
            [(turn(k * m)[0], block) for k, block in enumerate(cosines)]
            + [(turn(k * m)[1], block) for k, block in enumerate(sines, 1)]
        )
        for m in range(RADIX)
    ]


def order_class(shape):
    order = lax.broadcasted_iota(jnp.int32, shape, len(shape) - 1) % RADIX
    mirrored = order > RADIX // 2
    return jnp.where(mirrored, RADIX - order, order), mirrored


def three_pass(product, near, far, high, low):
    both = product(jnp.concatenate([near, far], axis=0), high[...])
    return both[: near.shape[0]] + both[near.shape[0] :] + product(near, low[...])


def dot_nt(a, b):
    return lax.dot_general(a, b, (((1,), (1,)), ((), ())), preferred_element_type=jnp.float32)


def half_viscosity(index, viscosity_ref):
    values = [0.5 * viscosity_ref[k] for k in range(viscosity_ref.shape[0])]
    bit = 1
    while len(values) > 1:
        odd = (index & bit) != 0
        if len(values) % 2:
            values.append(values[-1])
        values = [jnp.where(odd, b, a) for a, b in zip(values[::2], values[1::2])]
        bit *= 2
    return values[0]


def row_number(shape):
    return lax.broadcasted_iota(jnp.int32, shape, 0)


def north_of(above, middle):
    return pltpu.roll(jnp.where(row_number(middle.shape) == TILE - 1, above, middle), 1, 0)


def south_of(below, middle):
    return pltpu.roll(jnp.where(row_number(middle.shape) == 0, below, middle), TILE - 1, 0)


def east_of(values):
    return pltpu.roll(values, values.shape[-1] - 1, values.ndim - 1)


def west_of(values):
    return pltpu.roll(values, 1, values.ndim - 1)


def relax_weights(middle, others):
    weights = [middle + other for other in others]
    diagonal = 1.0 + functools.reduce(jnp.add, weights)
    return weights, RELAXATION / diagonal


def relax(weights, factor, middle, others, force):
    total = force
    for weight, other in zip(weights, others):
        total = total + weight * other
    return (1.0 - RELAXATION) * middle + factor * total


def around(ref, lead, shell, start):
    rows = lambda first: pl.ds(pl.multiple_of(first, TILE), TILE)
    middle = ref[(*lead, shell, rows(start))]
    return middle, [
        ref[(*lead, shell + 1, rows(start))],
        ref[(*lead, shell - 1, rows(start))],
        south_of(ref[(*lead, shell, rows(start + TILE))], middle),
        north_of(ref[(*lead, shell, rows(start - TILE))], middle),
        west_of(middle),
        east_of(middle),
    ]


def message_kernel(viscosity_from, d, f, index, one, two, fields, forces, layers, rows_of, viscosity, sems):
    components, shells, rows, count = d.shape
    copies = [pltpu.make_async_copy(viscosity_from, viscosity, sems.at[0])]
    for side, start in enumerate((0, rows - TILE)):
        part = pl.ds(start, TILE)
        copies += [
            pltpu.make_async_copy(index.at[:, part], layers.at[side], sems.at[1 + side]),
            pltpu.make_async_copy(d.at[:, :, part], fields.at[side], sems.at[3 + side]),
            pltpu.make_async_copy(f.at[:, :, part], forces.at[side], sems.at[5 + side]),
        ]
    layer_copies, field_copies, force_copies = copies[1::3], copies[2::3], copies[3::3]
    start_all(copies[:1] + layer_copies + field_copies + force_copies)
    for copy in copies[:1] + layer_copies:
        copy.wait()
    near_eta, far_eta = 2 * components, 2 * components + 1
    for side, near, far in ((0, 0, 1), (1, TILE - 1, TILE - 2)):
        for s in range(shells):
            eta = half_viscosity(layers[side, s], viscosity)
            rows_of[near_eta, side * shells + s] = eta[near]
            rows_of[far_eta, side * shells + s] = eta[far]
    for copy in field_copies:
        copy.wait()
    for side, near, far in ((0, 0, 1), (1, TILE - 1, TILE - 2)):
        for s in range(shells):
            for c in range(components):
                rows_of[c, side * shells + s] = fields[side, c, s, near]
                rows_of[components + c, side * shells + s] = fields[side, c, s, far]
    for copy in force_copies:
        copy.wait()
    for side, near in ((0, 0), (1, TILE - 1)):
        for s in range(shells):
            for c in range(components):
                rows_of[far_eta + 1 + c, side * shells + s] = forces[side, c, s, near]
    radial = lax.axis_index("radial")
    place = row_number((2 * shells, count)) % shells
    highest, lowest = place == shells - 1, place == 0
    zero = jnp.zeros((2 * shells, count), jnp.float32)

    def beside(near, far):
        middle = rows_of[near]
        return middle, [
            jnp.where(highest, zero, pltpu.roll(middle, 2 * shells - 1, 0)),
            jnp.where(lowest, zero, pltpu.roll(middle, 1, 0)),
            rows_of[far],
            west_of(middle),
            east_of(middle),
        ]

    eta, others = beside(near_eta, far_eta)
    weights = [eta + other for other in others]
    inside = (radial < lax.axis_size("radial") - 1, radial > 0)
    weights[0] = jnp.where(jnp.logical_and(highest, inside[0]), zero, weights[0])
    weights[1] = jnp.where(jnp.logical_and(lowest, inside[1]), zero, weights[1])
    diagonal = 1.0 + functools.reduce(jnp.add, weights)
    values, sums = [], []
    for c in range(components):
        middle, others = beside(c, components + c)
        total = rows_of[far_eta + 1 + c]
        for weight, other in zip(weights, others):
            total = total + weight * other
        values.append(middle)
        sums.append(total)
    for place, field in enumerate(values + [eta] + sums + [diagonal]):
        both = pltpu.roll(field, shells, 0)
        one[pl.ds(place * shells, shells)] = both[:shells]
        two[pl.ds(place * shells, shells)] = both[shells:]


def shell_order(shells):
    lower = lax.axis_index("radial") == 0
    return lambda k: jnp.where(lower, k, shells - 1 - k)


def viscosity_kernel(
    viscosity_from, d, f, index_from, token, table_from, eta_out, out, surface_swept, surface_eta, surface_force, table,
    index, eta, field, force, result, viscosity, sems, more_sems,
):
    del token
    _, shells, rows, count = d.shape
    components = d.shape[0]
    block = pl.ds(TILE, rows)
    shell = shell_order(shells)
    value_copy = pltpu.make_async_copy(viscosity_from, viscosity, sems.at[shells])
    layers = [pltpu.make_async_copy(index_from.at[shell(k)], index.at[k], sems.at[k]) for k in range(shells)]
    fields = [
        pltpu.make_async_copy(d.at[:, shell(k)], field.at[:, k + 1, block], more_sems.at[k]) for k in range(EARLY + 1)
    ]
    forces = [
        pltpu.make_async_copy(f.at[:, shell(k)], force.at[:, k], more_sems.at[EARLY + 1 + k]) for k in range(EARLY)
    ]
    table_copy = pltpu.make_async_copy(table_from, table, sems.at[shells + 1])
    start_all([value_copy, *layers, *fields, *forces])
    zeros = jnp.zeros((rows, count), jnp.float32)
    for c in range(components):
        field[c, 0, block] = zeros
    eta[0, block] = zeros
    value_copy.wait()
    stores = start_all([table_copy])
    for k in range(shells):
        layers[k].wait()

        def lookup(step, _):
            start = pl.multiple_of(step * TILE, TILE)
            eta[k + 1, pl.ds(start + TILE, TILE)] = half_viscosity(index[k, pl.ds(start, TILE)], viscosity)
            return 0

        lax.fori_loop(0, rows // TILE, lookup, 0, unroll=2)
        stores += start_all(
            [pltpu.make_async_copy(eta.at[k + 1, block], eta_out.at[shell(k)], more_sems.at[2 * EARLY + 1 + k])]
        )
    for k in range(EARLY):
        for copy in (fields[: EARLY + 1] if k == 0 else []) + forces[k : k + 1]:
            copy.wait()

        def sweep(step, _):
            start = pl.multiple_of(step * TILE, TILE)
            part = pl.ds(start, TILE)
            weights, factor = relax_weights(*around(eta, (), k + 1, start + TILE))
            for c in range(components):
                middle, others = around(field, (c,), k + 1, start + TILE)
                result[c, k, part] = relax(weights, factor, middle, others, force[c, k, part])
            surface_swept[1 - k, part] = result[0, k, part]
            surface_eta[1 - k, part] = eta[k + 1, pl.ds(start + TILE, TILE)]
            if k == 0:
                surface_force[part] = force[0, 0, part]
            sem = more_sems.at[2 * EARLY + 1 + shells + k]
            pltpu.make_async_copy(result.at[:, k, part], out.at[:, k, part], sem).start()
            return 0

        lax.fori_loop(0, rows // TILE, sweep, 0, unroll=2)
        stores.append(pltpu.make_async_copy(result.at[:, k], out.at[:, k], more_sems.at[2 * EARLY + 1 + shells + k]))
    for copy in stores:
        copy.wait()


def surface_kernel(
    surface_swept, surface_eta, force, own_one, own_two, one, two, high, low_from, out,
    swept, eta, surface, low, sem, components,
):
    rows, count = force.shape

    @pl.when(lax.axis_index("radial") == lax.axis_size("radial") - 1)
    def _():
        low_copy = pltpu.make_async_copy(low_from, low, sem)
        low_copy.start()
        block = pl.ds(TILE, rows)
        for k in range(2):
            swept[k, block] = surface_swept[k]
            eta[k, block] = surface_eta[k]
        swept[2, block] = jnp.zeros((rows, count), jnp.float32)
        eta[2, block] = jnp.zeros((rows, count), jnp.float32)
        fields = one.shape[0]
        shells = fields // (2 * (components + 1))
        lateral = lax.axis_index("lateral")
        inside = (lateral > 0, lateral < lax.axis_size("lateral") - 1)
        for beside, own, place, own_place, there in zip(
            (one[...], two[...]), (own_two[...], own_one[...]), (TILE - 1, rows + TILE), (TILE, rows + TILE - 1), inside
        ):
            for k in range(2):
                row = lambda message, kind: message[kind * shells + shells - 2 + k : kind * shells + shells - 1 + k]
                weight = row(beside, components) + row(own, components)

                def finish(message, other):
                    total = row(message, components + 1) + weight * row(other, 0)
                    factor = RELAXATION / (row(message, 2 * components + 1) + weight)
                    return (1.0 - RELAXATION) * row(message, 0) + factor * total

                swept[k, pl.ds(own_place, 1)] = finish(own, beside)
                if k == 1:
                    edge = finish(beside, own)
                    swept[k, pl.ds(place, 1)] = jnp.where(there, edge, jnp.zeros_like(edge))
                    eta[k, pl.ds(place, 1)] = row(beside, components)

        def second(step, _):
            start = pl.multiple_of(step * TILE, TILE)
            weights, factor = relax_weights(*around(eta, (), 1, start + TILE))
            middle, others = around(swept, (), 1, start + TILE)
            surface[pl.ds(start, TILE)] = relax(weights, factor, middle, others, force[pl.ds(start, TILE)])
            return 0

        lax.fori_loop(0, rows // TILE, second, 0, unroll=2)
        near, far = split(jnp.concatenate(fold(surface[...]), axis=0))
        total = dot(near, high[...]) + dot(far, high[...])
        low_copy.wait()
        total = total + dot(near, low[...])
        blocks = [total[k * rows : (k + 1) * rows] for k in range(RADIX)]
        kind, mirrored = order_class((1, total.shape[1]))
        cosine, sine = blocks[0], jnp.zeros_like(blocks[0])
        for k in range(1, RADIX // 2 + 1):
            cosine = jnp.where(kind == k, blocks[k], cosine)
        for k in range(1, RADIX // 2):
            sine = jnp.where(kind == k, blocks[RADIX // 2 + k], sine)
        sine = jnp.where(mirrored, -sine, sine)
        modes = total.shape[1] // 2
        fourier = jnp.concatenate(
            [cosine[:, :modes] - sine[:, modes:], cosine[:, modes:] + sine[:, :modes]], axis=1
        )
        blocks = out.shape[0]
        width = fourier.shape[1] // blocks
        for block in range(blocks):
            out[block] = pack(fourier[:, block * width : (block + 1) * width])


def sweep_shells(
    begin, source, f, h, store, field, eta, force, result, sems, before_first, last_loads, arrived, finish, after_shell
):
    components, shells, rows, count = f.shape
    inner = pl.ds(TILE, rows)
    shell = shell_order(shells)

    def field_loads(k):
        s = shell(k)
        return [
            pltpu.make_async_copy(source(k), field.at[:, s + 1, inner], sems.at[k, 0]),
            pltpu.make_async_copy(h.at[s], eta.at[s + 1, inner], sems.at[k, 1]),
            *(last_loads if k == shells - 1 else []),
        ]

    def force_load(k):
        return [pltpu.make_async_copy(f.at[:, shell(k)], force.at[:, shell(k)], sems.at[k, 2])]

    loads = {k: start_all(field_loads(k)) for k in range(max(begin - 1, 0), begin + 2)}
    forces = {begin: start_all(force_load(begin))}
    if begin == 0:
        nothing = jnp.where(lax.axis_index("radial") == 0, 0, shells + 1)
        zeros = jnp.zeros((rows, count), jnp.float32)
        for c in range(components):
            field[c, nothing, inner] = zeros
        eta[nothing, inner] = zeros

    def start_until(k):
        for ahead in range(begin, shells):
            if ahead <= k and ahead not in loads:
                loads[ahead] = start_all(field_loads(ahead))
            if ahead < k and ahead not in forces:
                forces[ahead] = start_all(force_load(ahead))

    start_until(begin + 2)
    before_first()
    stores, there = [], set()
    for k in range(begin, shells):
        s = shell(k)
        start_until(k + 3)
        for near in range(max(k - 1, 0), min(k + 2, shells)):
            if near not in there:
                there.add(near)
                for copy in loads[near]:
                    copy.wait()
                arrived(near)
        for copy in forces[k]:
            copy.wait()

        def tile(step, _):
            first = pl.multiple_of(step * TILE, TILE)
            part = pl.ds(first, TILE)
            if k == shells - 1:
                finish(s, first)
            else:
                weights, factor = relax_weights(*around(eta, (), s + 1, first + TILE))
                for c in range(components):
                    middle, others = around(field, (c,), s + 1, first + TILE)
                    result[c, s, part] = relax(weights, factor, middle, others, force[c, s, part])
            pltpu.make_async_copy(result.at[:, s, part], store(k).at[:, part], sems.at[k, 3]).start()
            return 0

        lax.fori_loop(0, rows // TILE, tile, 0, unroll=2)
        stores.append(pltpu.make_async_copy(result.at[:, s], store(k), sems.at[k, 3]))
        after_shell(s, k)
    for copy in stores:
        copy.wait()


def set_edge(ref, lead, shells, rows, before, after):
    for s in range(shells):
        ref[(*lead, s + 1, TILE - 1)] = before(s)
        ref[(*lead, s + 1, rows + TILE)] = after(s)


def start_all(copies):
    for copy in copies:
        copy.start()
    return copies


def load_messages(sources, lower_sources, slots, sems):
    lower = lax.axis_index("radial") < lax.axis_size("radial") - 1
    copies = lambda refs: [pltpu.make_async_copy(ref, slots.at[k], sems.at[k]) for k, ref in enumerate(refs)]
    pl.when(lower)(lambda: [copy.start() for copy in copies(lower_sources)] and None)
    pl.when(jnp.logical_not(lower))(lambda: [copy.start() for copy in copies(sources)] and None)
    return copies(sources)


def first_kernel(d, f, h, one, two, lower_one, lower_two, mine_one, mine_two, *refs):
    components, shells, rows, count = d.shape
    staged = (len(refs) - 13) // 2
    sources, refs = refs[:staged], refs[staged:]
    out, diagonal_out, ring_out, own_out, beside_out, *targets = refs[: 5 + staged]
    field, eta, force, result, messages, edges, diagonal, sems, more_sems = refs[5 + staged :]
    arrivals = load_messages((one, two), (lower_one, lower_two), messages, more_sems)
    lower = lax.axis_index("radial") == 0
    last, beyond = jnp.where(lower, shells - 1, 0), jnp.where(lower, shells + 1, 0)
    values = pl.ds(0, own_out.shape[1])
    copies = []
    own_copies = lambda: start_all(
        [
            pltpu.make_async_copy(mine.at[values], own_out.at[k], more_sems.at[4 + components + k])
            for k, mine in enumerate((mine_one, mine_two))
        ]
    )

    def before_first():
        block = pl.ds(TILE, rows)
        zeros = jnp.zeros((rows, count), jnp.float32)
        for c in range(components):
            field[c, beyond, block] = zeros
        eta[beyond, block] = zeros
        for copy in arrivals:
            copy.wait()
        before, after = messages[0], messages[1]
        row = lambda message, kind: lambda s: message[kind * shells + s]
        for c in range(components):
            set_edge(field, (c,), shells, rows, row(before, c), row(after, c))
        set_edge(eta, (), shells, rows, row(before, components), row(after, components))
        for side, message in enumerate((before, after)):
            for k in range(components + 1):
                edges[side * (components + 1) + k] = jnp.where(
                    lower, message[(k + 1) * shells - 1], message[k * shells]
                )
        tail = ring_out.at[pl.ds(2 * (components + 1) * rows, edges.shape[0])]
        copies.extend(
            start_all(
                [
                    pltpu.make_async_copy(edges, tail, more_sems.at[2]),
                ]
            )
        )

    def arrived(k):
        if k < shells - 1:
            return
        block = pl.ds(TILE, rows)
        sources = [field.at[c, last + 1, block] for c in range(components)] + [eta.at[last + 1, block]]
        copies.extend(
            start_all(
                [
                    pltpu.make_async_copy(source, ring_out.at[pl.ds(k * rows, rows)], more_sems.at[6 + components + k])
                    for k, source in enumerate(sources)
                ]
            )
        )

    def finish(s, first):
        part = pl.ds(first, TILE)
        middle, others = around(eta, (), s + 1, first + TILE)
        weights = [middle + other for other in others]
        zero = jnp.zeros_like(middle)
        weights[0] = jnp.where(lower, zero, weights[0])
        weights[1] = jnp.where(lower, weights[1], zero)
        diagonal[part] = 1.0 + functools.reduce(jnp.add, weights)
        for c in range(components):
            total = force[c, s, part]
            for weight, other in zip(weights, around(field, (c,), s + 1, first + TILE)[1]):
                total = total + weight * other
            result[c, s, part] = total

    def after_shell(s, k):
        if k == EARLY:
            copies.extend(own_copies())
            copies.extend(start_all([pltpu.make_async_copy(messages, beside_out, more_sems.at[3])]))
            copies.extend(
                start_all(
                    [
                        pltpu.make_async_copy(source, target, more_sems.at[8 + 3 * components + n])
                        for n, (source, target) in enumerate(zip(sources, targets))
                    ]
                )
            )
        if k == shells - 1:
            sums = [result.at[c, s] for c in range(components)] + [diagonal]
            copies.extend(
                start_all(
                    [
                        pltpu.make_async_copy(
                            source,
                            ring_out.at[pl.ds((components + 1 + n) * rows, rows)],
                            more_sems.at[7 + 2 * components + n],
                        )
                        for n, source in enumerate(sums)
                    ]
                    + [pltpu.make_async_copy(diagonal, diagonal_out, more_sems.at[0])]
                )
            )

    shell = shell_order(shells)
    sweep_shells(
        EARLY, lambda k: d.at[:, shell(k)], f, h, lambda k: out.at[:, k - EARLY],
        field, eta, force, result, sems, before_first, [], arrived, finish, after_shell,
    )
    for copy in copies:
        copy.wait()


def second_kernel(early, late, f, h, start, diagonal_from, ring, beside, own_from, *refs):
    components, shells, rows, count = f.shape
    staged = (len(refs) - 18) // 2
    mask_from, *sources = refs[: 1 + staged]
    out, token, mask_out, *targets = refs[1 + staged : 4 + 2 * staged]
    (
        field, eta, force, result, messages, edges, own, diagonal, raw, ring_diagonal, mask, ends, sems, more_sems
    ) = refs[4 + 2 * staged :]
    token[...] = jnp.zeros_like(token)
    tail = ring.at[pl.ds(2 * (components + 1) * rows, edges.shape[0])]
    arrivals = start_all(
        [
            pltpu.make_async_copy(beside, messages, more_sems.at[0]),
            pltpu.make_async_copy(tail, edges, more_sems.at[1]),
            pltpu.make_async_copy(own_from, own, more_sems.at[2]),
        ]
    )
    radial, lateral = lax.axis_index("radial"), lax.axis_index("lateral")
    lower = radial == 0
    last, beyond = jnp.where(lower, shells - 1, 0), jnp.where(lower, shells + 1, 0)
    block = pl.ds(TILE, rows)
    shell = shell_order(shells)
    from_ring = lambda k, target, sem: pltpu.make_async_copy(
        ring.at[pl.ds(k * rows, rows)], target, more_sems.at[sem]
    )
    last_loads = [
        pltpu.make_async_copy(start.at[:, last], raw.at[pl.ds(0, components)], more_sems.at[3]),
        pltpu.make_async_copy(diagonal_from, diagonal, more_sems.at[4]),
        *(from_ring(c, raw.at[components + c], 5 + c) for c in range(components)),
        from_ring(components, eta.at[beyond, block], 5 + components),
        *(
            from_ring(components + 1 + c, field.at[c, beyond, block], 6 + components + c)
            for c in range(components)
        ),
        from_ring(2 * components + 1, ring_diagonal, 6 + 2 * components),
    ]
    copies = []
    mask_copy = pltpu.make_async_copy(mask_from, mask, more_sems.at[7 + 2 * components])

    def before_first():
        for copy in arrivals:
            copy.wait()
        before, after = messages[0], messages[1]
        pair = lambda k: jnp.concatenate(
            [before[k * shells : (k + 1) * shells], after[k * shells : (k + 1) * shells]], axis=0
        )
        place = row_number((2 * shells, count))
        zero = jnp.zeros((2 * shells, count), jnp.float32)
        shared = place % shells == last
        across_of = lambda k: jnp.where(
            place < shells, edges[pl.ds(k, 1)], edges[pl.ds(components + 1 + k, 1)]
        )
        inside = jnp.where(place < shells, lateral, lax.axis_size("lateral") - 1 - lateral) > 0
        mine = (own[1], own[0])
        own_row = lambda k: jnp.concatenate([part[k * shells : (k + 1) * shells] for part in mine], axis=0)
        middle = pair(components)
        weight = middle + own_row(components)
        across = jnp.where(shared, middle + across_of(components), zero)
        factor = RELAXATION / (pair(2 * components + 1) + weight + across)
        own_factor = RELAXATION / (own_row(2 * components + 1) + weight)
        for c in range(components):
            total = pair(components + 1 + c) + weight * own_row(c) + across * across_of(c)
            edge = jnp.where(inside, (1.0 - RELAXATION) * pair(c) + factor * total, zero)
            total = own_row(components + 1 + c) + weight * pair(c)
            ends[c] = (1.0 - RELAXATION) * own_row(c) + own_factor * total
            set_edge(field, (c,), shells, rows, lambda s: edge[s], lambda s: edge[shells + s])
        set_edge(eta, (), shells, rows, lambda s: middle[s], lambda s: middle[shells + s])

    def arrived(k):
        if k < EARLY:
            s = shell(k)
            for side, place in enumerate((TILE, TILE + rows - 1)):
                for c in range(components):
                    field[c, s + 1, pl.ds(place, 1)] = ends[c, pl.ds(side * shells + s, 1)]
        if k < shells - 1:
            return

        def tile(step, _):
            first = pl.multiple_of(step * TILE, TILE)
            part, place = pl.ds(first, TILE), pl.ds(first + TILE, TILE)
            weight = eta[last + 1, place] + eta[beyond, place]
            here, there = RELAXATION / (diagonal[part] + weight), RELAXATION / (ring_diagonal[part] + weight)
            for c in range(components):
                mine, other = raw[c, part], raw[components + c, part]
                field[c, last + 1, place] = (1.0 - RELAXATION) * mine + here * (
                    field[c, last + 1, place] + weight * other
                )
                field[c, beyond, place] = (1.0 - RELAXATION) * other + there * (
                    field[c, beyond, place] + weight * mine
                )
            return 0

        lax.fori_loop(0, rows // TILE, tile, 0, unroll=2)

    def finish(s, first):
        part = pl.ds(first, TILE)
        weights, factor = relax_weights(*around(eta, (), s + 1, first + TILE))
        for c in range(components):
            middle, others = around(field, (c,), s + 1, first + TILE)
            result[c, s, part] = relax(weights, factor, middle, others, force[c, s, part])

    def after_shell(s, k):
        if k == 0:
            copies.extend(
                start_all(
                    [
                        pltpu.make_async_copy(source, target, more_sems.at[8 + 2 * components + n])
                        for n, (source, target) in enumerate(zip(sources, targets))
                    ]
                )
            )
            mask_copy.start()
        if k == shells - 1:
            mask_copy.wait()
            mask_out[...] = mask[...].astype(jnp.float32).astype(jnp.bfloat16)

    sweep_shells(
        0, lambda k: early.at[:, k] if k < EARLY else late.at[:, k - EARLY], f, h, lambda k: out.at[:, shell(k)],
        field, eta, force, result, sems, before_first, last_loads, arrived, finish, after_shell,
    )
    for copy in copies:
        copy.wait()


def spectrum_kernel(orders, high, low, response, coefficients, out):
    radial = lax.axis_size("radial")
    width = coefficients.shape[0]
    bands, rows = orders.shape[0] // radial, high.shape[0] * radial // orders.shape[0]
    fourier = jnp.concatenate([unpack(orders[band * radial + radial - 1], width) for band in range(bands)], axis=0)
    near, far = split(fourier.T)
    spectrum = three_pass(dot, near, far, high, low)
    coefficients[...] = spectrum
    own = response[:, :width]
    for place in range(1, radial):
        own = jnp.where(
            lax.axis_index("radial") == place, response[:, place * width : (place + 1) * width], own
        )
    near, far = split(own.T * spectrum)
    load = three_pass(dot_nt, near, far, high, low).T
    for band in range(bands):
        block = pack(load[band * rows : (band + 1) * rows])
        for place in range(radial):
            out[band * radial + place] = block


def load_kernel(load, high, low, mask, out):
    blocks, rows = load.shape[0], out.shape[0]
    step, width = out.shape[1] // RADIX, high.shape[1] // blocks
    values = jnp.concatenate([unpack(load[block], width) for block in range(blocks)], axis=1)
    modes = values.shape[1] // 2
    kind, mirrored = order_class((1, values.shape[1]))
    crossed = jnp.concatenate([values[:, modes:], -values[:, :modes]], axis=1)
    crossed = jnp.where(mirrored, -crossed, crossed)
    zero = jnp.zeros_like(values)
    stack = [jnp.where(kind == k, values, zero) for k in range(RADIX // 2 + 1)]
    stack += [jnp.where(kind == k, crossed, zero) for k in range(1, RADIX // 2)]
    near, far = split(jnp.concatenate(stack, axis=0))
    total = dot_nt(near, high[...]) + dot_nt(far, high[...]) + dot_nt(near, low[...])
    for m, part in enumerate(unfold([total[k * rows : (k + 1) * rows] for k in range(RADIX)])):
        columns = slice(m * step, (m + 1) * step)
        out[:, columns] = part * mask[:, columns].astype(jnp.float32)


def cost(microseconds):
    return pl.CostEstimate(flops=0, bytes_accessed=3_000_000 * microseconds, transcendentals=0)


def hbm(values):
    return pltpu.with_memory_space_constraint(values, pltpu.HBM)


def shards(initial_displacement, force, viscosity, layer_index, response, ocean_mask):
    components, shells, rows, count = initial_displacement.shape
    radial, lateral = lax.axis_size("radial"), lax.axis_size("lateral")
    f32 = functools.partial(jax.ShapeDtypeStruct, dtype=jnp.float32)
    scratch = lambda *shape: pltpu.VMEM(shape, jnp.float32)
    in_hbm = lambda *shape: pltpu.HBM(shape, jnp.float32)
    width = 2 * MODES // (lateral * radial)
    first = [(i, i + 1) for i in range(lateral - 1)]
    second = [(i + 1, i) for i in range(lateral - 1)]
    both = ("lateral", "radial")
    top_only = lambda pairs: [(i * radial + radial - 1, j * radial + radial - 1) for i, j in pairs]

    lower_only = lambda pairs: [(i * radial + k, j * radial + k) for i, j in pairs for k in range(radial - 1)]
    swap = [(i, radial - 1 - i) for i in range(radial)]
    tensors = [hbm(a) for a in (initial_displacement, force, layer_index)]
    viscosity = hbm(viscosity)
    message = f32((2 * (components + 1) * shells, count))
    sides = lambda *shape: scratch(2, *shape)
    mine = pl.pallas_call(
        message_kernel,
        in_specs=[HBM] * 4,
        out_specs=[VMEM] * 2,
        out_shape=[message] * 2,
        scratch_shapes=[
            sides(components, shells, TILE, count),
            sides(components, shells, TILE, count),
            pltpu.VMEM((2, shells, TILE, count), jnp.int32),
            scratch(3 * components + 2, 2 * shells, count),
            pltpu.SMEM(viscosity.shape, jnp.float32),
            pltpu.SemaphoreType.DMA((7,)),
        ],
        compiler_params=params(16),
        cost_estimate=cost(20),
    )(viscosity, *tensors)
    two = lax.ppermute(mine[1], both, top_only(second))
    one = lax.ppermute(mine[0], both, top_only(first))
    high, low = longitude_tables(count, MODES)
    high, low = hbm(jnp.asarray(high)), hbm(jnp.asarray(low))
    eta, early, *surface, table = pl.pallas_call(
        viscosity_kernel,
        in_specs=[HBM] * 4 + [ANY, HBM],
        out_specs=[HBM, HBM, VMEM, VMEM, VMEM, VMEM],
        out_shape=[
            in_hbm(shells, rows, count),
            in_hbm(components, EARLY, rows, count),
            f32((2, rows, count)),
            f32((2, rows, count)),
            f32((rows, count)),
            jax.ShapeDtypeStruct(high.shape, high.dtype),
        ],
        scratch_shapes=[
            pltpu.VMEM(layer_index.shape, jnp.int32),
            scratch(shells + 1, rows + 2 * TILE, count),
            scratch(components, EARLY + 2, rows + 2 * TILE, count),
            scratch(components, EARLY, rows, count),
            scratch(components, EARLY, rows, count),
            pltpu.SMEM(viscosity.shape, jnp.float32),
            pltpu.SemaphoreType.DMA((2 + shells,)),
            pltpu.SemaphoreType.DMA((3 * EARLY + 1 + shells,)),
        ],
        compiler_params=params(24),
        cost_estimate=cost(20),
    )(viscosity, *tensors, mine[0], high)
    lower_one, lower_two, eta = lax.optimization_barrier((*mine, eta))
    lower_one = lax.ppermute(lower_one, both, lower_only(first))
    lower_two = lax.ppermute(lower_two, both, lower_only(second))

    packed = (lateral * radial, rows * width // max(128, width), max(128, width))
    orders = pl.pallas_call(
        functools.partial(surface_kernel, components=components),
        in_specs=[VMEM] * 8 + [HBM],
        out_specs=VMEM,
        out_shape=f32(packed),
        scratch_shapes=[
            scratch(3, rows + 2 * TILE, count),
            scratch(3, rows + 2 * TILE, count),
            scratch(rows, count),
            pltpu.VMEM(low.shape, low.dtype),
            pltpu.SemaphoreType.DMA,
        ],
        compiler_params=params(16),
        cost_estimate=cost(200),
    )(*surface, *mine, one, two, table, low)
    eta, _ = lax.optimization_barrier((eta, orders))
    orders = lax.all_to_all(orders, both, split_axis=0, concat_axis=0, tiled=True)
    eta = hbm(eta)

    sweep_scratch = [
        scratch(components, shells + 2, rows + 2 * TILE, count),
        scratch(shells + 2, rows + 2 * TILE, count),
        scratch(components, shells, rows, count),
        scratch(components, shells, rows, count),
    ]
    sweep_sems = pltpu.SemaphoreType.DMA((shells, 4))
    point_high, point_low = colatitude_tables(rows * lateral, MODES)
    stages = [jnp.asarray(point_high), jnp.asarray(point_low)] + [response]
    ring_rows = 2 * (components + 1) * (rows + 1)
    sweep_scratch += [
        sides(*message.shape),
        scratch(2 * (components + 1), count),
    ]
    own_shape = (2, *message.shape)
    late, diagonal, ring, own, beside, *staged = pl.pallas_call(
        first_kernel,
        in_specs=[HBM] * 3 + [ANY] * 6 + [HBM] * len(stages),
        out_specs=[HBM] * 5 + [VMEM] * len(stages),
        out_shape=[
            in_hbm(components, shells - EARLY, rows, count),
            in_hbm(rows, count),
            in_hbm(ring_rows, count),
            in_hbm(*own_shape),
            in_hbm(2, *message.shape),
            *(jax.ShapeDtypeStruct(a.shape, a.dtype) for a in stages),
        ],
        scratch_shapes=[
            *sweep_scratch,
            scratch(rows, count),
            sweep_sems,
            pltpu.SemaphoreType.DMA((8 + 3 * components + len(stages),)),
        ],
        compiler_params=params(28),
        cost_estimate=cost(50),
    )(*tensors[:2], hbm(eta), one, two, lower_one, lower_two, *mine, *(hbm(a) for a in stages))
    ring, orders = lax.optimization_barrier((ring, orders))
    ring = lax.ppermute(ring, "radial", swap)
    coefficients, load = pl.pallas_call(
        spectrum_kernel,
        in_specs=[VMEM] * 4,
        out_specs=[VMEM, VMEM],
        out_shape=[f32((width, MODES)), f32(packed)],
        compiler_params=params(16),
        cost_estimate=cost(200),
    )(orders, *staged)
    eta, load = lax.optimization_barrier((eta, load))
    load = lax.all_to_all(load, both, split_axis=0, concat_axis=0, tiled=True)

    stages = [high, low]
    displacement, token, mask, *staged = pl.pallas_call(
        second_kernel,
        in_specs=[HBM] * 6 + [ANY] + [HBM] * (3 + len(stages)),
        out_specs=[HBM, VMEM, VMEM] + [VMEM] * len(stages),
        out_shape=[
            in_hbm(*initial_displacement.shape),
            f32((TILE, 128)),
            jax.ShapeDtypeStruct(ocean_mask.shape, jnp.bfloat16),
            *(jax.ShapeDtypeStruct(a.shape, a.dtype) for a in stages),
        ],
        scratch_shapes=[
            *sweep_scratch,
            scratch(*own_shape),
            scratch(rows, count),
            scratch(2 * components, rows, count),
            scratch(rows, count),
            pltpu.VMEM(ocean_mask.shape, ocean_mask.dtype),
            scratch(components, 2 * shells, count),
            sweep_sems,
            pltpu.SemaphoreType.DMA((8 + 2 * components + len(stages),)),
        ],
        compiler_params=params(28),
        cost_estimate=cost(50),
    )(
        *(hbm(a) for a in (early, late, tensors[1], eta, tensors[0], diagonal)),
        ring,
        *(hbm(a) for a in (beside, own, ocean_mask)),
        *stages,
    )

    sea_load = pl.pallas_call(
        load_kernel,
        in_specs=[VMEM] * 4,
        out_specs=VMEM,
        out_shape=f32((rows, count)),
        compiler_params=params(20),
        cost_estimate=cost(3),
    )(load, *staged, mask)
    return (displacement, coefficients.T, sea_load)


def solution(mesh):
    in_specs = (
        P("member", "radial", "lateral", None),
        P("member", "radial", "lateral", None),
        P("member"),
        P("radial", "lateral", None),
        P(None, "lateral"),
        P("lateral", None),
    )
    out_specs = (
        P("member", "radial", "lateral", None),
        P("member", ("lateral", "radial")),
        P("lateral", "member"),
    )
    return jax.shard_map(shards, mesh=mesh, in_specs=in_specs, out_specs=out_specs, check_vma=False)
```
